32 devices in a mesh: gx: 4 (over z), gy: 8 (over y, x, core).
Axes of the slice: x: 2, y: 2, z: 4, core: 2. Of those that a mesh axis runs over, the one named last changes fastest.
Arguments:
- populations: float32 [27, 128, 8192], P(None, 'gx', 'gy'), may hold values from 0.002 to 0.42, as said below
- adjoint_in: float32 [27, 128, 8192], P(None, 'gx', 'gy'), may hold values from -6 to 6
- porosity: float32 [128, 8192], P('gx', 'gy'), may hold values from 0.1 to 10
- solid: int32 [128, 8192], P('gx', 'gy'), may hold values 0 or 1
- labels: int32 [128, 8192], P('gx', 'gy'), may hold values from 0 to 2
Outputs:
- final_pops: float32 [27, 128, 8192], P(None, 'gx', 'gy')
- adjoint_out: float32 [27, 128, 8192], P(None, 'gx', 'gy')
- sensitivity: float32 [128, 8192], P('gx', 'gy')
The draws below stay inside these ranges and needn't reach their ends.
Inputs may be any that keep to these rules, and one draw needn't show every extreme that they name: `populations`: every population is between 0.6 and 1.4 times its weight w_i.
All inputs are finite; a program needn't handle non-finite values. Where the reference program divides by a largest or mean magnitude, that divisor is 1e-20 or more. No bound on the sum of `solid` on one device may be relied on, other than what follows from the above.
Results may differ from the reference program's by a relative error of at most 0.0001.
Values sent between devices are 32-bit elements; how exact they have to be, the bound alone decides.
No kernel may reach another device: no remote copies, remote signals or barrier semaphores. Data moves between devices by JAX's collectives and lax.ppermute only.
A program may use at most 128 MiB of HBM per device.

```python
import math
import jax
import jax.numpy as jnp
from jax import lax

NZ = 64
STEPS = 2
NX = 128
NY = 128


def draw_populations(key, part):
    key = jax.random.fold_in(key, 7)
    velocity_vectors = [(a, b, c) for a in (-1, 0, 1) for b in (-1, 0, 1) for c in (-1, 0, 1)]
    wts = jnp.asarray([[8.0 / 27, 2.0 / 27, 1.0 / 54, 1.0 / 216][abs(v[0]) + abs(v[1]) + abs(v[2])] for v in velocity_vectors], jnp.float32)
    shape = (27, NX, NY * NZ)
    factor = jax.random.uniform(key, shape, jnp.float32, 0.6, 1.4)
    return (wts[:, None, None] * factor).astype(jnp.float32)


def touch_ends(entries, stream_key, least, high):
    extent = entries.shape
    spot = [jax.random.randint(jax.random.fold_in(stream_key, axis), (), 0, extent[axis]) for axis in range(len(extent))]
    entries = entries.at[tuple(spot)].set(least)
    longest = extent.index(max(extent))
    spot[longest] = (spot[longest] + 1) % extent[longest]
    return entries.at[tuple(spot)].set(high)


def shard_levels(stream_key, extent, pieces, smallest, top_value):
    gain = 1.0
    for dim, shards_of in pieces:
        steps = jax.random.uniform(jax.random.fold_in(jax.random.fold_in(stream_key, 6), dim), (shards_of,), jnp.float32, smallest / len(pieces), top_value / len(pieces))
        gain = gain * jnp.repeat(jnp.exp(steps), extent[dim] // shards_of).reshape((-1,) + (1,) * (len(extent) - 1 - dim))
    return gain


def gaussian(key, shape, scale, limit, pieces=(), kind=jnp.bfloat16):
    drawn = scale * jax.random.normal(key, shape, jnp.float32)
    if pieces:
        drawn = drawn * shard_levels(key, shape, pieces, -0.22, 0.18)
    return jnp.clip(drawn, -limit, limit).astype(kind)


def setup_inputs(seed: int = 0) -> dict:
    arg_keys = jax.random.split(jax.random.key(seed), 6)
    populations = draw_populations(jax.random.fold_in(arg_keys[5], 71), 0)
    adjoint_in = gaussian(arg_keys[1], (27, NX, NY * NZ), 1.0, 6.0, ((1, 4), (2, 8)), jnp.float32)
    porosity = jnp.clip(jnp.exp(math.log(10.0) - 4.6051702 * jax.random.uniform(arg_keys[2], (NX, NY * NZ), jnp.float32) ** shard_levels(arg_keys[2], (NX, NY * NZ), ((0, 4), (1, 8)), -0.2, 0.2)), 0.1, 10.0)
    solid = touch_ends((jax.random.randint(arg_keys[3], (NX, NY * NZ), 0, 5) < 1).astype(jnp.int32), jax.random.fold_in(arg_keys[3], 1), 0, 1)
    labels = touch_ends(jax.random.randint(arg_keys[4], (NX, NY * NZ), 0, 3), jax.random.fold_in(arg_keys[4], 1), 0, 2).astype(jnp.int32)
    return dict(populations=populations, adjoint_in=adjoint_in, porosity=porosity, solid=solid, labels=labels)


RELAX = 0.8
PUSH = 0.2
EPS = 1e-06
velocity_vectors = [(a, b, c) for a in (-1, 0, 1) for b in (-1, 0, 1) for c in (-1, 0, 1)]
vel_x = [float(v[0]) for v in velocity_vectors]
vel_y = [float(v[1]) for v in velocity_vectors]
vel_z = [float(v[2]) for v in velocity_vectors]
weight_table = [[8.0 / 27, 2.0 / 27, 1.0 / 54, 1.0 / 216][abs(v[0]) + abs(v[1]) + abs(v[2])] for v in velocity_vectors]

def column(table):
    return jnp.asarray(table, jnp.float32)[:, None, None]

def collide(pops, porosity, solid, drive):
    dir_x, dir_y, dir_z, wts = (column(vel_x), column(vel_y), column(vel_z), column(weight_table))
    fluid_density = lax.optimization_barrier(jnp.sum(pops, 0))
    damp = 1.0 / (1.0 + porosity)
    vel_u = (lax.optimization_barrier(jnp.sum(dir_x * pops, 0)) / fluid_density + PUSH * drive) * damp
    vel_v = lax.optimization_barrier(jnp.sum(dir_y * pops, 0)) / fluid_density * damp
    vel_w = lax.optimization_barrier(jnp.sum(dir_z * pops, 0)) / fluid_density * damp
    along = dir_x * vel_u + dir_y * vel_v + dir_z * vel_w
    usq = vel_u * vel_u + vel_v * vel_v + vel_w * vel_w
    equil = wts * fluid_density * (1.0 + 3.0 * along + 4.5 * along * along - 1.5 * usq)
    fluid = pops - (pops - equil) / RELAX
    return jnp.where(solid[None] == 1, pops[::-1], fluid)

def energy(pops):
    fluid_density = lax.optimization_barrier(jnp.sum(pops, 0))
    total_sum = jnp.zeros((), pops.dtype)
    for table in (vel_x, vel_y, vel_z):
        speed = lax.optimization_barrier(jnp.sum(column(table) * pops, 0)) / fluid_density
        total_sum = total_sum + 0.5 * jnp.sum(speed * speed)
    return total_sum

def stream(pops, sign):
    grid = pops.reshape(27, NX, NY, NZ)
    moved = []
    for index in range(27):
        a, b, c = velocity_vectors[index]
        moved.append(jnp.roll(grid[index], (sign * a, sign * b, sign * c), axis=(0, 1, 2)))
    return jnp.stack(moved).reshape(27, NX, NY * NZ)

def reference(populations, adjoint_in, porosity, solid, labels):
    drive = (labels == 1).astype(jnp.float32) - (labels == 2).astype(jnp.float32)
    states = []
    current = populations
    for step in range(STEPS):
        states.append(current)
        current = stream(collide(current, porosity, solid, drive), 1)
    final_pops = current
    adjoint_field = adjoint_in + jax.grad(energy)(final_pops)
    total_sum = jnp.zeros_like(porosity)
    for step in range(STEPS - 1, -1, -1):
        pulled_values = stream(adjoint_field, -1)
        unused, backward_sweep = jax.vjp(lambda p, q: collide(p, q, solid, drive), states[step], porosity)
        adjoint_field, porosity_gradient = backward_sweep(pulled_values)
        total_sum = total_sum + porosity_gradient
    peak = jnp.max(jnp.abs(total_sum))
    return (final_pops, adjoint_field, total_sum / (peak + EPS))
```

```python
import functools

import jax
import jax.numpy as jnp
from jax import lax
from jax.experimental import pallas as pl
from jax.experimental.pallas import tpu as pltpu
from jax.sharding import PartitionSpec as P

NZ = 64
RELAX = 0.8
PUSH = 0.2
EPS = 1e-06
LANES = 128
VELOCITY = [(a, b, c) for a in (-1, 0, 1) for b in (-1, 0, 1) for c in (-1, 0, 1)]
INDEX = {v: i for i, v in enumerate(VELOCITY)}
WEIGHT = [
    [8.0 / 27, 2.0 / 27, 1.0 / 54, 1.0 / 216][abs(v[0]) + abs(v[1]) + abs(v[2])]
    for v in VELOCITY
]
NORM = [abs(v[0]) + abs(v[1]) + abs(v[2]) for v in VELOCITY]
F32 = jnp.float32
VMEM_LIMIT = 20 * 1024 * 1024
CORNERS = [(1, 1), (1, -1), (-1, 1), (-1, -1)]


class Grid:
    def __init__(self, rows, width):
        self.rows = rows
        self.cols = width // LANES
        self.tiles = rows // 8
        self.panel = rows + 16
        self.padded = (27 * (self.cols + 1) * self.panel, LANES)

    def at(self, i, c, r):
        return (i * (self.cols + 1) + c) * self.panel + 8 + r


def scaled(d, sign):
    return (sign * d[0], sign * d[1], sign * d[2])


def lane_masks():
    lane = lax.broadcasted_iota(jnp.int32, (8, LANES), 1)
    return lane >= NZ, lane % NZ == 0, lane % NZ == NZ - 1


def pull(g, buf, i, d, c, r, masks):
    high, first, last = masks
    dx, dy, dz = d
    here = buf[pl.ds(g.at(i, c, r - dx), 8), :]
    if dy == 1:
        before = jnp.where(c == 0, g.cols, c - 1)
        here = jnp.where(high, buf[pl.ds(g.at(i, before, r - dx), 8), :], here)
    elif dy == -1:
        here = jnp.where(high, here, buf[pl.ds(g.at(i, c + 1, r - dx), 8), :])
    if dz == 0:
        return here if dy == 0 else pltpu.roll(here, NZ, 1)
    if dz == 1:
        one, other, edge = 1, NZ + 1, first
    else:
        one, other, edge = LANES - 1, NZ - 1, last
    inner, wrapped = (one, other) if dy == 0 else (other, one)
    return jnp.where(edge, pltpu.roll(here, wrapped, 1), pltpu.roll(here, inner, 1))


def moments(f):
    flat = {}
    along_z = None
    for a in (-1, 0, 1):
        for b in (-1, 0, 1):
            lo, mid, hi = (f[INDEX[(a, b, c)]] for c in (-1, 0, 1))
            flat[a, b] = lo + mid + hi
            diff = hi - lo
            along_z = diff if along_z is None else along_z + diff
    line = {}
    along_y = None
    for a in (-1, 0, 1):
        line[a] = flat[a, -1] + flat[a, 0] + flat[a, 1]
        diff = flat[a, 1] - flat[a, -1]
        along_y = diff if along_y is None else along_y + diff
    return line[-1] + line[0] + line[1], line[1] - line[-1], along_y, along_z


def combos(x, y, z):
    plane = {}
    for a in (-1, 0, 1):
        for b in (-1, 0, 1):
            if (a, b) > (0, 0):
                continue
            if a == 0:
                plane[a, b] = -y if b else None
            else:
                plane[a, b] = -x if b == 0 else (-x - y if b < 0 else y - x)
    out = []
    for a, b, c in VELOCITY[:13]:
        base = plane[a, b]
        if base is None:
            out.append(-z)
        else:
            out.append(base if c == 0 else (base - z if c < 0 else base + z))
    return out


def relax(f, rho, wx, wy, wz, damp, push, solid):
    ux, uy, uz = (wx + push) * damp, wy * damp, wz * damp
    base = 1.0 - 1.5 * (ux * ux + uy * uy + uz * uz)
    keep = 1.0 - 1.0 / RELAX
    gain = rho * (1.0 / RELAX)
    level = [gain * w for w in (8.0 / 27, 2.0 / 27, 1.0 / 54, 1.0 / 216)]
    along = combos(3.0 * ux, 3.0 * uy, 3.0 * uz)
    out = [None] * 27
    for i in range(13):
        j = 26 - i
        even = base + 0.5 * (along[i] * along[i])
        lift = level[NORM[i]]
        out[i] = jnp.where(solid, f[j], keep * f[i] + lift * (even + along[i]))
        out[j] = jnp.where(solid, f[i], keep * f[j] + lift * (even - along[i]))
    out[13] = jnp.where(solid, f[13], keep * f[13] + level[0] * base)
    return out


def pulled_moments(p):
    first = {}
    for a in (-1, 0, 1):
        for b in (-1, 0, 1):
            lo, mid, hi = (p[INDEX[(a, b, c)]] for c in (-1, 0, 1))
            both = lo + hi
            first[a, b] = (4.0 * mid + both, hi - lo, both)
    second = {}
    for a in (-1, 0, 1):
        lo, mid, hi = (first[a, b] for b in (-1, 0, 1))
        b0 = lo[0] + hi[0]
        b1 = lo[1] + hi[1]
        second[a] = dict(
            one=4.0 * mid[0] + b0,
            y=hi[0] - lo[0],
            yy=b0,
            z=4.0 * mid[1] + b1,
            yz=hi[1] - lo[1],
            zz=4.0 * mid[2] + lo[2] + hi[2],
        )
    lo, mid, hi = (second[a] for a in (-1, 0, 1))

    def full(key):
        return 4.0 * mid[key] + lo[key] + hi[key]

    xx = lo["one"] + hi["one"]
    return dict(
        one=4.0 * mid["one"] + xx,
        x=hi["one"] - lo["one"],
        xx=xx,
        y=full("y"),
        xy=hi["y"] - lo["y"],
        yy=full("yy"),
        z=full("z"),
        xz=hi["z"] - lo["z"],
        yz=full("yz"),
        zz=full("zz"),
    )


def adjoint_scalars(p, rho, wx, wy, wz, damp, push, solid):
    ux, uy, uz = (wx + push) * damp, wy * damp, wz * damp
    s = pulled_moments(p)
    scale = 1.0 / (216.0 * RELAX)
    one = s["one"] * scale
    b = [s[k] * (3.0 * scale) for k in ("x", "y", "z")]
    d = {k: s[k] * (9.0 * scale) for k in ("xx", "xy", "yy", "xz", "yz", "zz")}
    qx = d["xx"] * ux + d["xy"] * uy + d["xz"] * uz
    qy = d["xy"] * ux + d["yy"] * uy + d["yz"] * uz
    qz = d["xz"] * ux + d["yz"] * uy + d["zz"] * uz
    linear = b[0] * ux + b[1] * uy + b[2] * uz
    square = ux * ux + uy * uy + uz * uz
    even = one + linear + 0.5 * (qx * ux + qy * uy + qz * uz) - 1.5 * one * square
    three = 3.0 * one
    gx = (b[0] + qx - three * ux) * damp
    gy = (b[1] + qy - three * uy) * damp
    gz = (b[2] + qz - three * uz) * damp
    even = even - (gx * wx + gy * wy + gz * wz)
    porous = jnp.where(solid, 0.0, -rho * (gx * ux + gy * uy + gz * uz))
    return even, gx, gy, gz, porous


def adjoint_spread(p, even, gx, gy, gz, solid):
    keep = 1.0 - 1.0 / RELAX
    along = combos(gx, gy, gz)
    out = [None] * 27
    for i in range(13):
        j = 26 - i
        out[i] = jnp.where(solid, p[j], keep * p[i] + (even + along[i]))
        out[j] = jnp.where(solid, p[i], keep * p[j] + (even - along[i]))
    out[13] = jnp.where(solid, p[13], keep * p[13] + even)
    return out


def faces(sign, axis, side):
    return [i for i, v in enumerate(VELOCITY) if sign * v[axis] == side]


def corner(sign, sx, sy):
    return [i for i, v in enumerate(VELOCITY) if sign * v[0] == sx and sign * v[1] == sy]


def fill_sends(g, buf, sign, sends, high):
    x_up, x_down, y_up, y_down = sends[:4]
    for side, ref in ((1, x_up), (-1, x_down)):
        row = g.rows - 1 if side == 1 else 0
        for k, i in enumerate(faces(sign, 0, side)):
            ref[k * g.cols : (k + 1) * g.cols, :] = buf[
                pl.ds(g.at(i, 0, row), g.cols, stride=g.panel), :
            ]
    for side, ref in ((1, y_up), (-1, y_down)):
        col = g.cols - 1 if side == 1 else 0
        pops = faces(sign, 1, side)
        for k in range(5):
            for a in range(g.tiles):
                value = buf[pl.ds(g.at(pops[k], col, 8 * a), 8), :]
                if k < 4:
                    other = pltpu.roll(buf[pl.ds(g.at(pops[5 + k], col, 8 * a), 8), :], NZ, 1)
                    pair = (value, other) if side == 1 else (other, value)
                    value = jnp.where(high, *pair)
                ref[k * g.rows + 8 * a : k * g.rows + 8 * a + 8, :] = value
    for (sx, sy), ref in zip(CORNERS, sends[4:]):
        row = g.rows - 1 if sx == 1 else 0
        col = g.cols - 1 if sy == 1 else 0
        ref[...] = jnp.zeros((8, LANES), F32)
        for k, i in enumerate(corner(sign, sx, sy)):
            ref[k : k + 1, :] = buf[pl.ds(g.at(i, col, row), 1), :]


def fill_halo(g, buf, sign, parcels):
    x_up, x_down, y_up, y_down = parcels[:4]
    for side, ref in ((1, x_up), (-1, x_down)):
        row = -1 if side == 1 else g.rows
        for k, i in enumerate(faces(sign, 0, side)):
            buf[pl.ds(g.at(i, 0, row), g.cols, stride=g.panel), :] = ref[
                k * g.cols : (k + 1) * g.cols, :
            ]
    for side, ref in ((1, y_up), (-1, y_down)):
        pops = faces(sign, 1, side)
        for k in range(5):
            for a in range(g.tiles):
                value = ref[k * g.rows + 8 * a : k * g.rows + 8 * a + 8, :]
                buf[pl.ds(g.at(pops[k], g.cols, 8 * a), 8), :] = value
                if k < 4:
                    buf[pl.ds(g.at(pops[5 + k], g.cols, 8 * a), 8), :] = pltpu.roll(value, NZ, 1)
    for (sx, sy), ref in zip(CORNERS, parcels[4:]):
        row = -1 if sx == 1 else g.rows
        for k, i in enumerate(corner(sign, sx, sy)):
            buf[pl.ds(g.at(i, g.cols, row), 1), :] = ref[k : k + 1, :]


def tile_of(g, ref, k, c, r):
    return ref[pl.ds((k * g.cols + c) * g.rows + r, 8), :]


def put_tile(g, ref, k, c, r, value):
    ref[pl.ds((k * g.cols + c) * g.rows + r, 8), :] = value


def over_tiles(g, body, before=None, after=None):
    def column(c, carry):
        if before is not None:
            before(c)

        def tile(a, inner):
            body(c, pl.multiple_of(a * 8, 8))
            return inner

        lax.fori_loop(0, g.tiles, tile, 0)
        if after is not None:
            after(c)
        return carry

    lax.fori_loop(0, g.cols, column, 0)


def save_state(g, ref, c, r, rho, wx, wy, wz):
    for k, value in enumerate((rho, wx, wy, wz)):
        put_tile(g, ref, k, c, r, value)


def read_aux(g, aux, c, r):
    return tile_of(g, aux, 0, c, r), tile_of(g, aux, 1, c, r), tile_of(g, aux, 2, c, r) > 0.5


def first_kernel(g, pops, porosity, solid, labels, out, state, aux, *rest):
    sends, (stage, sems) = rest[:8], rest[8:]
    high = lane_masks()[0]

    def copy(c):
        source = pops.at[:, :, pl.ds(pl.multiple_of(c * LANES, LANES), LANES)]
        return pltpu.make_async_copy(source, stage.at[c], sems.at[c])

    for c in range(g.cols):
        copy(c).start()

    def body(c, r):
        f = [stage[c, i, pl.ds(r, 8), :] for i in range(27)]
        spot = (pl.ds(r, 8), pl.ds(pl.multiple_of(c * LANES, LANES), LANES))
        wall = solid[spot]
        label = labels[spot]
        damp = 1.0 / (1.0 + porosity[spot])
        push = jnp.where(label == 1, PUSH, jnp.where(label == 2, -PUSH, 0.0))
        put_tile(g, aux, 0, c, r, damp)
        put_tile(g, aux, 1, c, r, push)
        put_tile(g, aux, 2, c, r, wall.astype(F32))
        rho, mx, my, mz = moments(f)
        inverse = 1.0 / rho
        wx, wy, wz = mx * inverse, my * inverse, mz * inverse
        save_state(g, state, c, r, rho, wx, wy, wz)
        for i, value in enumerate(relax(f, rho, wx, wy, wz, damp, push, wall == 1)):
            out[pl.ds(g.at(i, c, r), 8), :] = value

    over_tiles(g, body, before=lambda c: copy(c).wait())
    fill_sends(g, out, 1, sends, high)


def second_kernel(g, padded, aux, *rest):
    parcels, (buf, out, state), sends = rest[:8], rest[8:11], rest[11:19]
    del padded
    masks = lane_masks()
    fill_halo(g, buf, 1, parcels)

    def body(c, r):
        f = [pull(g, buf, i, VELOCITY[i], c, r, masks) for i in range(27)]
        damp, push, wall = read_aux(g, aux, c, r)
        rho, mx, my, mz = moments(f)
        inverse = 1.0 / rho
        wx, wy, wz = mx * inverse, my * inverse, mz * inverse
        save_state(g, state, c, r, rho, wx, wy, wz)
        for i, value in enumerate(relax(f, rho, wx, wy, wz, damp, push, wall)):
            out[pl.ds(g.at(i, c, r), 8), :] = value

    over_tiles(g, body)
    fill_sends(g, out, 1, sends, masks[0])


def third_kernel(g, padded, adjoint, *rest):
    parcels, (final, buf, out), sends = rest[:8], rest[8:11], rest[11:19]
    stage_out, stage_in, sems_out, sems_in = rest[19:]
    del padded
    masks = lane_masks()

    def block(ref, c):
        return ref.at[:, :, pl.ds(pl.multiple_of(c * LANES, LANES), LANES)]

    def copy_in(c):
        return pltpu.make_async_copy(block(adjoint, c), stage_in.at[c], sems_in.at[c])

    def copy_out(c):
        return pltpu.make_async_copy(stage_out.at[c], block(final, c), sems_out.at[c])

    for c in range(g.cols):
        copy_in(c).start()
    fill_halo(g, buf, 1, parcels)

    def body(c, r):
        f = [pull(g, buf, i, VELOCITY[i], c, r, masks) for i in range(27)]
        for i in range(27):
            stage_out[c, i, pl.ds(r, 8), :] = f[i]
        rho, mx, my, mz = moments(f)
        inverse = 1.0 / rho
        wx, wy, wz = mx * inverse, my * inverse, mz * inverse
        even = -(wx * wx + wy * wy + wz * wz) * inverse
        along = combos(wx * inverse, wy * inverse, wz * inverse)
        for i in range(27):
            value = stage_in[c, i, pl.ds(r, 8), :] + even
            if i < 13:
                value = value + along[i]
            elif i > 13:
                value = value - along[26 - i]
            out[pl.ds(g.at(i, c, r), 8), :] = value

    over_tiles(
        g, body, before=lambda c: copy_in(c).wait(), after=lambda c: copy_out(c).start()
    )
    fill_sends(g, out, -1, sends, masks[0])
    for c in range(g.cols):
        copy_out(c).wait()


def fourth_kernel(g, padded, state, aux, *rest):
    parcels, (buf, out, total), sends = rest[:8], rest[8:11], rest[11:19]
    del padded
    masks = lane_masks()
    fill_halo(g, buf, -1, parcels)

    def body(c, r):
        p = [pull(g, buf, i, scaled(VELOCITY[i], -1), c, r, masks) for i in range(27)]
        damp, push, wall = read_aux(g, aux, c, r)
        rho, wx, wy, wz = (tile_of(g, state, k, c, r) for k in range(4))
        even, gx, gy, gz, porous = adjoint_scalars(p, rho, wx, wy, wz, damp, push, wall)
        put_tile(g, total, 0, c, r, porous)
        for i, value in enumerate(adjoint_spread(p, even, gx, gy, gz, wall)):
            out[pl.ds(g.at(i, c, r), 8), :] = value

    over_tiles(g, body)
    fill_sends(g, out, -1, sends, masks[0])


def fifth_kernel(g, padded, state, aux, before, *rest):
    parcels, (result, buf, total, peak) = rest[:8], rest[8:12]
    stage_out, sems_out = rest[12:]
    del padded
    masks = lane_masks()

    def copy_out(c):
        target = result.at[:, :, pl.ds(pl.multiple_of(c * LANES, LANES), LANES)]
        return pltpu.make_async_copy(stage_out.at[c], target, sems_out.at[c])

    fill_halo(g, buf, -1, parcels)
    peak[...] = jnp.zeros((8, LANES), F32)

    def body(c, r):
        p = [pull(g, buf, i, scaled(VELOCITY[i], -1), c, r, masks) for i in range(27)]
        damp, push, wall = read_aux(g, aux, c, r)
        rho, wx, wy, wz = (tile_of(g, state, k, c, r) for k in range(4))
        even, gx, gy, gz, porous = adjoint_scalars(p, rho, wx, wy, wz, damp, push, wall)
        here = tile_of(g, before, 0, c, r) + porous
        put_tile(g, total, 0, c, r, here)
        peak[...] = jnp.maximum(peak[...], jnp.abs(here))
        for i, value in enumerate(adjoint_spread(p, even, gx, gy, gz, wall)):
            stage_out[c, i, pl.ds(r, 8), :] = value

    over_tiles(g, body, after=lambda c: copy_out(c).start())
    for c in range(g.cols):
        copy_out(c).wait()


def scale_kernel(g, total, peak, out):
    largest = jnp.max(peak[...])
    factor = 1.0 / (jnp.full((8, LANES), largest, F32) + EPS)

    for c in range(g.cols):
        for a in range(g.tiles):
            out[8 * a : 8 * a + 8, c * LANES : (c + 1) * LANES] = (
                tile_of(g, total, 0, c, 8 * a) * factor
            )


def ring(mesh_axes, sizes, shift):
    nx, ny = sizes
    sx, sy = shift
    if mesh_axes == "gx":
        return [(i, (i + sx) % nx) for i in range(nx)]
    if mesh_axes == "gy":
        return [(i, (i + sy) % ny) for i in range(ny)]
    return [
        (x * ny + y, ((x + sx) % nx) * ny + (y + sy) % ny)
        for x in range(nx)
        for y in range(ny)
    ]


def exchange(sends, sizes):
    moves = [("gx", (1, 0)), ("gx", (-1, 0)), ("gy", (0, 1)), ("gy", (0, -1))]
    moves += [(("gx", "gy"), shift) for shift in CORNERS]
    return [
        lax.ppermute(parcel, axes, ring(axes, sizes, shift))
        for parcel, (axes, shift) in zip(sends, moves)
    ]


def largest_of_all(peak, sizes):
    nx, ny = sizes
    for axis, count in (("gy", ny), ("gx", nx)):
        parts = [peak]
        for k in range(1, count):
            parts.append(lax.ppermute(peak, axis, ring(axis, sizes, (k, k))))
        peak = functools.reduce(jnp.maximum, parts)
    return peak


def on_device(sizes, populations, adjoint_in, porosity, solid, labels):
    rows, width = porosity.shape
    g = Grid(rows, width)
    in_vmem = pl.BlockSpec(memory_space=pltpu.VMEM)
    anywhere = pl.BlockSpec(memory_space=pl.ANY)
    hbm = pl.BlockSpec(memory_space=pltpu.HBM)
    padded = pltpu.VMEM(g.padded, F32)

    def fields(count):
        return pltpu.VMEM((count * g.cols * rows, LANES), F32)

    parcel_shapes = [
        pltpu.VMEM((9 * g.cols, LANES), F32),
        pltpu.VMEM((9 * g.cols, LANES), F32),
        pltpu.VMEM((5 * rows, LANES), F32),
        pltpu.VMEM((5 * rows, LANES), F32),
    ] + [pltpu.VMEM((8, LANES), F32)] * 4
    whole = jax.ShapeDtypeStruct(populations.shape, F32)
    stage = pltpu.VMEM((g.cols, 27, rows, LANES), F32)
    sems = pltpu.SemaphoreType.DMA((g.cols,))

    def call(kernel, in_specs, out_shape, out_specs, scratch=(), aliases=None, name=None):
        return pl.pallas_call(
            functools.partial(kernel, g),
            in_specs=in_specs,
            out_shape=out_shape,
            out_specs=out_specs,
            scratch_shapes=list(scratch),
            input_output_aliases=aliases or {},
            compiler_params=pltpu.CompilerParams(vmem_limit_bytes=VMEM_LIMIT),
            name=name,
        )

    def pin(x):
        return pltpu.with_memory_space_constraint(x, pltpu.VMEM)

    post, state0, aux, *sends = call(
        first_kernel,
        [anywhere, in_vmem, in_vmem, in_vmem],
        [padded, fields(4), fields(3)] + parcel_shapes,
        [in_vmem] * 11,
        [stage, sems],
        name="collide_first",
    )(populations, porosity, solid, labels)
    parcels = exchange(sends, sizes)

    _, post, state1, *sends = call(
        second_kernel,
        [in_vmem] * 10,
        [padded, padded, fields(4)] + parcel_shapes,
        [in_vmem] * 11,
        aliases={0: 0},
        name="collide_second",
    )(pin(post), pin(aux), *parcels)
    parcels = exchange(sends, sizes)

    final, _, field, *sends = call(
        third_kernel,
        [in_vmem, anywhere] + [in_vmem] * 8,
        [whole, padded, padded] + parcel_shapes,
        [hbm] + [in_vmem] * 10,
        [stage, stage, sems, sems],
        aliases={0: 1},
        name="stream_and_seed",
    )(pin(post), adjoint_in, *parcels)
    parcels = exchange(sends, sizes)

    _, field, total, *sends = call(
        fourth_kernel,
        [in_vmem] * 11,
        [padded, padded, fields(1)] + parcel_shapes,
        [in_vmem] * 11,
        aliases={0: 0},
        name="adjoint_second",
    )(pin(field), pin(state1), pin(aux), *parcels)
    parcels = exchange(sends, sizes)

    adjoint_out, _, total, peak = call(
        fifth_kernel,
        [in_vmem] * 12,
        [whole, padded, fields(1), pltpu.VMEM((8, LANES), F32)],
        [hbm] + [in_vmem] * 3,
        [stage, sems],
        aliases={0: 1},
        name="adjoint_first",
    )(pin(field), pin(state0), pin(aux), pin(total), *parcels)

    peak = largest_of_all(peak, sizes)
    sensitivity = call(
        scale_kernel,
        [in_vmem, in_vmem],
        jax.ShapeDtypeStruct(porosity.shape, F32),
        in_vmem,
        name="normalize",
    )(pin(total), peak)
    return final, adjoint_out, sensitivity


def solution(mesh):
    sizes = (mesh.shape["gx"], mesh.shape["gy"])
    whole, flat = P(None, "gx", "gy"), P("gx", "gy")
    return jax.shard_map(
        functools.partial(on_device, sizes),
        mesh=mesh,
        in_specs=(whole, whole, flat, flat, flat),
        out_specs=(whole, whole, flat),
        check_vma=False,
    )
```

```python
import functools

import jax
import jax.numpy as jnp
from jax import lax
from jax.experimental import pallas as pl
from jax.experimental.pallas import tpu as pltpu
from jax.sharding import PartitionSpec as P

NZ = 64
RELAX = 0.8
PUSH = 0.2
EPS = 1e-06
LANES = 128
VELOCITY = [(a, b, c) for a in (-1, 0, 1) for b in (-1, 0, 1) for c in (-1, 0, 1)]
INDEX = {v: i for i, v in enumerate(VELOCITY)}
WEIGHT = [
    [8.0 / 27, 2.0 / 27, 1.0 / 54, 1.0 / 216][abs(v[0]) + abs(v[1]) + abs(v[2])]
    for v in VELOCITY
]
NORM = [abs(v[0]) + abs(v[1]) + abs(v[2]) for v in VELOCITY]
F32 = jnp.float32
VMEM_LIMIT = 20 * 1024 * 1024


class Grid:
    def __init__(self, rows, width):
        self.rows = rows
        self.cols = width // LANES
        self.tiles = rows // 8
        self.panel = rows + 16
        self.halo = self.cols + 1
        self.local = self.cols * self.tiles
        self.extended = self.halo * self.tiles + 3

    def at(self, i, k, r):
        return (i * (self.cols + 2) + k) * self.panel + 8 + r

    def padded(self, fields):
        return (fields * (self.cols + 2) * self.panel + 8, LANES)


def velocity(i, sign):
    return tuple(sign * n for n in VELOCITY[i]) if i < 27 else (0, 0, 0)


def moving(fields, sign, axis, side):
    return [i for i in range(fields) if velocity(i, sign)[axis] == side]


def lane_masks():
    lane = lax.broadcasted_iota(jnp.int32, (8, LANES), 1)
    return lane >= NZ, lane % NZ == 0, lane % NZ == NZ - 1


def shift_lanes(here, d, masks):
    first, last = masks[1:]
    dy, dz = d[1:]
    if dz == 0:
        return here if dy == 0 else pltpu.roll(here, NZ, 1)
    if dz == 1:
        one, other, edge = 1, NZ + 1, first
    else:
        one, other, edge = LANES - 1, NZ - 1, last
    inner, wrapped = (one, other) if dy == 0 else (other, one)
    return jnp.where(edge, pltpu.roll(here, wrapped, 1), pltpu.roll(here, inner, 1))


def pull(load, d, masks):
    high = masks[0]
    here = load(0)
    if d[1] == 1:
        here = jnp.where(high, load(-1), here)
    elif d[1] == -1:
        here = jnp.where(high, here, load(1))
    return shift_lanes(here, d, masks)


def pull_block(g, buf, sign, k, r, masks, fields=27):
    after = jnp.where(k == g.halo, 1, k + 1)
    out = []
    for i in range(fields):
        d = velocity(i, sign)

        def load(n, i=i, d=d):
            panel = {-1: k - 1, 0: k, 1: after}[n]
            return buf[pl.ds(g.at(i, panel, r - d[0]), 8), :]

        out.append(pull(load, d, masks))
    return out


def pull_edge(g, buf, sign, side, masks, fields=27):
    out = []
    for i in range(fields):
        d = velocity(i, sign)
        if side == 1:
            row = g.rows - d[0]
        else:
            row = {1: g.rows, 0: g.rows + 1, -1: 0}[d[0]]

        def load(n, i=i, row=row):
            return buf[pl.ds(g.at(i, 1 + n, row), g.cols, stride=g.panel), :]

        out.append(pull(load, d, masks))
    return out


def moments(f):
    flat = {}
    along_z = None
    for a in (-1, 0, 1):
        for b in (-1, 0, 1):
            lo, mid, hi = (f[INDEX[(a, b, c)]] for c in (-1, 0, 1))
            flat[a, b] = lo + mid + hi
            diff = hi - lo
            along_z = diff if along_z is None else along_z + diff
    line = {}
    along_y = None
    for a in (-1, 0, 1):
        line[a] = flat[a, -1] + flat[a, 0] + flat[a, 1]
        diff = flat[a, 1] - flat[a, -1]
        along_y = diff if along_y is None else along_y + diff
    return line[-1] + line[0] + line[1], line[1] - line[-1], along_y, along_z


def combos(x, y, z):
    plane = {}
    for a in (-1, 0, 1):
        for b in (-1, 0, 1):
            if (a, b) > (0, 0):
                continue
            if a == 0:
                plane[a, b] = -y if b else None
            else:
                plane[a, b] = -x if b == 0 else (-x - y if b < 0 else y - x)
    out = []
    for a, b, c in VELOCITY[:13]:
        base = plane[a, b]
        if base is None:
            out.append(-z)
        else:
            out.append(base if c == 0 else (base - z if c < 0 else base + z))
    return out


def relax(f, rho, wx, wy, wz, damp, push, solid):
    ux, uy, uz = (wx + push) * damp, wy * damp, wz * damp
    base = 1.0 - 1.5 * (ux * ux + uy * uy + uz * uz)
    keep = 1.0 - 1.0 / RELAX
    gain = rho * (1.0 / RELAX)
    level = [gain * w for w in (8.0 / 27, 2.0 / 27, 1.0 / 54, 1.0 / 216)]
    along = combos(3.0 * ux, 3.0 * uy, 3.0 * uz)
    out = [None] * 27
    for i in range(13):
        j = 26 - i
        even = base + 0.5 * (along[i] * along[i])
        lift = level[NORM[i]]
        out[i] = jnp.where(solid, f[j], keep * f[i] + lift * (even + along[i]))
        out[j] = jnp.where(solid, f[i], keep * f[j] + lift * (even - along[i]))
    out[13] = jnp.where(solid, f[13], keep * f[13] + level[0] * base)
    return out


def pulled_moments(p):
    first = {}
    for a in (-1, 0, 1):
        for b in (-1, 0, 1):
            lo, mid, hi = (p[INDEX[(a, b, c)]] for c in (-1, 0, 1))
            both = lo + hi
            first[a, b] = (4.0 * mid + both, hi - lo, both)
    second = {}
    for a in (-1, 0, 1):
        lo, mid, hi = (first[a, b] for b in (-1, 0, 1))
        b0 = lo[0] + hi[0]
        b1 = lo[1] + hi[1]
        second[a] = dict(
            one=4.0 * mid[0] + b0,
            y=hi[0] - lo[0],
            yy=b0,
            z=4.0 * mid[1] + b1,
            yz=hi[1] - lo[1],
            zz=4.0 * mid[2] + lo[2] + hi[2],
        )
    lo, mid, hi = (second[a] for a in (-1, 0, 1))

    def full(key):
        return 4.0 * mid[key] + lo[key] + hi[key]

    xx = lo["one"] + hi["one"]
    return dict(
        one=4.0 * mid["one"] + xx,
        x=hi["one"] - lo["one"],
        xx=xx,
        y=full("y"),
        xy=hi["y"] - lo["y"],
        yy=full("yy"),
        z=full("z"),
        xz=hi["z"] - lo["z"],
        yz=full("yz"),
        zz=full("zz"),
    )


def adjoint_scalars(p, rho, wx, wy, wz, damp, push, solid):
    ux, uy, uz = (wx + push) * damp, wy * damp, wz * damp
    s = pulled_moments(p)
    scale = 1.0 / (216.0 * RELAX)
    one = s["one"] * scale
    b = [s[k] * (3.0 * scale) for k in ("x", "y", "z")]
    d = {k: s[k] * (9.0 * scale) for k in ("xx", "xy", "yy", "xz", "yz", "zz")}
    qx = d["xx"] * ux + d["xy"] * uy + d["xz"] * uz
    qy = d["xy"] * ux + d["yy"] * uy + d["yz"] * uz
    qz = d["xz"] * ux + d["yz"] * uy + d["zz"] * uz
    linear = b[0] * ux + b[1] * uy + b[2] * uz
    square = ux * ux + uy * uy + uz * uz
    even = one + linear + 0.5 * (qx * ux + qy * uy + qz * uz) - 1.5 * one * square
    three = 3.0 * one
    gx = (b[0] + qx - three * ux) * damp
    gy = (b[1] + qy - three * uy) * damp
    gz = (b[2] + qz - three * uz) * damp
    even = even - (gx * wx + gy * wy + gz * wz)
    porous = jnp.where(solid, 0.0, -rho * (gx * ux + gy * uy + gz * uz))
    return even, gx, gy, gz, porous


def adjoint_spread(p, even, gx, gy, gz, solid):
    keep = 1.0 - 1.0 / RELAX
    along = combos(gx, gy, gz)
    out = [None] * 27
    for i in range(13):
        j = 26 - i
        out[i] = jnp.where(solid, p[j], keep * p[i] + (even + along[i]))
        out[j] = jnp.where(solid, p[i], keep * p[j] + (even - along[i]))
    out[13] = jnp.where(solid, p[13], keep * p[13] + even)
    return out


def pack_x(g, buf, sign, fields, up, down):
    for side, ref in ((1, up), (-1, down)):
        edge, inner = (g.rows - 1, g.rows - 2) if side == 1 else (0, 1)
        lines = [(i, r) for i in moving(fields, sign, 0, side) for r in (edge, inner)]
        lines += [(i, edge) for i in moving(fields, sign, 0, 0)]
        for n, (i, r) in enumerate(lines):
            ref[n * g.cols : (n + 1) * g.cols, :] = buf[
                pl.ds(g.at(i, 1, r), g.cols, stride=g.panel), :
            ]


def unpack_x(g, buf, sign, fields, up, down):
    for side, ref in ((1, up), (-1, down)):
        lines = []
        for i in moving(fields, sign, 0, side):
            if side == 1:
                lines += [(i, (-1, g.rows + 1)), (i, (g.rows,))]
            else:
                lines += [(i, (g.rows,)), (i, (g.rows + 1,))]
        for i in moving(fields, sign, 0, 0):
            lines.append((i, (g.rows + 1 if side == 1 else g.rows,)))
        for n, (i, targets) in enumerate(lines):
            value = ref[n * g.cols : (n + 1) * g.cols, :]
            for r in targets:
                buf[pl.ds(g.at(i, 1, r), g.cols, stride=g.panel), :] = value
    for i in moving(fields, sign, 0, -1):
        buf[pl.ds(g.at(i, 1, g.rows + 2), g.cols, stride=g.panel), :] = buf[
            pl.ds(g.at(i, 1, 0), g.cols, stride=g.panel), :
        ]


def slot_rows(g, slots, n):
    pieces = [(n * g.rows + 8 * a, 8 * a, 8) for a in range(g.tiles)]
    return pieces + [(slots * g.rows + 2 * n, g.rows, 2)]


def still_pairs(fields, sign):
    still = moving(fields, sign, 1, 0)
    half = (len(still) + 1) // 2
    return [(still[n], still[n + half] if n + half < len(still) else None) for n in range(half)]


def y_slots(fields, sign):
    return 9 + len(still_pairs(fields, sign))


def pack_y(g, buf, sign, fields, up, down, high):
    slots = y_slots(fields, sign)
    for side, ref in ((1, up), (-1, down)):
        k = g.cols if side == 1 else 1
        for n, i in enumerate(moving(fields, sign, 1, side)):
            for to, r, count in slot_rows(g, slots, n):
                ref[to : to + count, :] = buf[pl.ds(g.at(i, k, r), count), :]
        for n, (i, j) in enumerate(still_pairs(fields, sign)):
            for to, r, count in slot_rows(g, slots, 9 + n):
                value = buf[pl.ds(g.at(i, k, r), count), :]
                if j is not None:
                    other = pltpu.roll(buf[pl.ds(g.at(j, k, r), count), :], NZ, 1)
                    pair = (value, other) if side == 1 else (other, value)
                    value = jnp.where(high[:count], *pair)
                ref[to : to + count, :] = value


def unpack_y(g, buf, sign, fields, up, down, high):
    slots = y_slots(fields, sign)
    for side, ref in ((1, up), (-1, down)):
        for n, i in enumerate(moving(fields, sign, 1, side)):
            for to, r, count in slot_rows(g, slots, n):
                value = ref[to : to + count, :]
                for k in (0, g.halo) if side == 1 else (g.halo,):
                    buf[pl.ds(g.at(i, k, r), count), :] = value
    for n, (i, j) in enumerate(still_pairs(fields, sign)):
        for to, r, count in slot_rows(g, slots, 9 + n):
            before, after = up[to : to + count, :], down[to : to + count, :]
            mask = high[:count]
            buf[pl.ds(g.at(i, g.halo, r), count), :] = jnp.where(mask, before, after)
            if j is not None:
                buf[pl.ds(g.at(j, g.halo, r), count), :] = pltpu.roll(
                    jnp.where(mask, after, before), NZ, 1
                )
    for i in moving(fields, sign, 0, 1):
        for k in (0, g.halo) if velocity(i, sign)[1] == 1 else (g.halo,):
            buf[pl.ds(g.at(i, k, -1), 1), :] = buf[pl.ds(g.at(i, k, g.rows + 1), 1), :]
    for i in moving(fields, sign, 0, -1):
        for k in (0, g.halo) if velocity(i, sign)[1] == 1 else (g.halo,):
            buf[pl.ds(g.at(i, k, g.rows + 2), 1), :] = buf[pl.ds(g.at(i, k, 0), 1), :]


def by_parity(axis, first, second, act):
    even = lax.rem(lax.axis_index(axis), 2) == 0

    @pl.when(even)
    def _():
        act(first, second)

    @pl.when(jnp.logical_not(even))
    def _():
        act(second, first)


def load_fields(ref, tiles, t, count):
    return [ref[pl.ds((n * tiles + t) * 8, 8), :] for n in range(count)]


def save_fields(ref, tiles, t, values):
    for n, value in enumerate(values):
        ref[pl.ds((n * tiles + t) * 8, 8), :] = value


def over_tiles(g, panels, body, before=None, after=None):
    def column(k, carry):
        if before is not None:
            before(k)

        def tile(a, inner):
            body(k, pl.multiple_of(a * 8, 8), (k - 1) * g.tiles + a)
            return inner

        lax.fori_loop(0, g.tiles, tile, 0)
        if after is not None:
            after(k)
        return carry

    lax.fori_loop(1, panels + 1, column, 0)


def over_extended(g, buf, out, sign, fields, masks, compute):
    def body(k, r, t):
        values = compute(pull_block(g, buf, sign, k, r, masks, fields), t)
        for i in range(27):
            out[pl.ds(g.at(i, k, r), 8), :] = values[i]

    over_tiles(g, g.halo, body)
    t = g.halo * g.tiles
    values = compute(pull_block(g, buf, sign, g.halo, g.rows, masks, fields), t)
    for i in range(27):
        dx = velocity(i, sign)[0]
        if dx == -1:
            out[pl.ds(g.at(i, g.halo, g.rows), 1), :] = values[i][0:1]
        elif dx == 1:
            out[pl.ds(g.at(i, g.halo, -1), 1), :] = values[i][1:2]
    for n, side in ((1, 1), (2, -1)):
        values = compute(pull_edge(g, buf, sign, side, masks, fields), t + n)
        for i in moving(27, sign, 0, -side):
            row = g.rows if side == 1 else -1
            out[pl.ds(g.at(i, 1, row), g.cols, stride=g.panel), :] = values[i]
    for i in moving(27, sign, 1, 1):
        for a in range(g.tiles):
            out[pl.ds(g.at(i, 0, 8 * a), 8), :] = out[pl.ds(g.at(i, g.halo, 8 * a), 8), :]
        for r in (-1, g.rows):
            out[pl.ds(g.at(i, 0, r), 1), :] = out[pl.ds(g.at(i, g.halo, r), 1), :]


def block_of(ref, k):
    return ref.at[:, :, pl.ds(pl.multiple_of((k - 1) * LANES, LANES), LANES)]


def first_kernel(g, pops, porosity, solid, labels, out, state, x_first, x_second, stage, sems):
    def copy(k):
        return pltpu.make_async_copy(block_of(pops, k), stage.at[k - 1], sems.at[k - 1])

    for k in range(1, g.cols + 1):
        copy(k).start()

    def body(k, r, t):
        f = [stage[k - 1, i, pl.ds(r, 8), :] for i in range(27)]
        spot = (pl.ds(r, 8), pl.ds(pl.multiple_of((k - 1) * LANES, LANES), LANES))
        wall = solid[spot]
        label = labels[spot]
        damp = 1.0 / (1.0 + porosity[spot])
        push = jnp.where(label == 1, PUSH, jnp.where(label == 2, -PUSH, 0.0))
        rho, mx, my, mz = moments(f)
        inverse = 1.0 / rho
        flow = (rho, mx * inverse, my * inverse, mz * inverse, damp, push)
        extra = (damp, push, wall.astype(F32))
        save_fields(state, g.local, t, flow + extra[2:])
        values = relax(f, *flow, wall == 1)
        for i, value in enumerate(tuple(values) + extra):
            out[pl.ds(g.at(i, k, r), 8), :] = value

    over_tiles(g, g.cols, body, before=lambda k: copy(k).wait())
    by_parity("gx", x_first, x_second, functools.partial(pack_x, g, out, 1, 30))


def relay_kernel(g, sign, fields, padded, x_first, x_second, buf, y_first, y_second):
    del padded
    high = lane_masks()[0]
    by_parity("gx", x_second, x_first, functools.partial(unpack_x, g, buf, sign, fields))
    by_parity(
        "gy",
        y_first,
        y_second,
        lambda up, down: pack_y(g, buf, sign, fields, up, down, high),
    )


def second_kernel(g, padded, y_first, y_second, buf, out, state):
    del padded
    masks = lane_masks()
    by_parity(
        "gy", y_second, y_first, lambda up, down: unpack_y(g, buf, 1, 30, up, down, masks[0])
    )

    def compute(values, t):
        f, (damp, push, wall) = values[:27], values[27:]
        rho, mx, my, mz = moments(f)
        inverse = 1.0 / rho
        flow = (rho, mx * inverse, my * inverse, mz * inverse, damp, push)
        save_fields(state, g.extended, t, flow + (wall,))
        return relax(f, *flow, wall > 0.5)

    over_extended(g, buf, out, 1, 30, masks, compute)


def third_kernel(g, buf, adjoint, final, out, x_first, x_second, stage_out, stage_in, *sems):
    sems_out, sems_in = sems
    masks = lane_masks()

    def copy_in(k):
        return pltpu.make_async_copy(block_of(adjoint, k), stage_in.at[k - 1], sems_in.at[k - 1])

    def copy_out(k):
        return pltpu.make_async_copy(stage_out.at[k - 1], block_of(final, k), sems_out.at[k - 1])

    for k in range(1, g.cols + 1):
        copy_in(k).start()

    def body(k, r, t):
        f = pull_block(g, buf, 1, k, r, masks)
        for i in range(27):
            stage_out[k - 1, i, pl.ds(r, 8), :] = f[i]
        rho, mx, my, mz = moments(f)
        inverse = 1.0 / rho
        wx, wy, wz = mx * inverse, my * inverse, mz * inverse
        even = -(wx * wx + wy * wy + wz * wz) * inverse
        along = combos(wx * inverse, wy * inverse, wz * inverse)
        for i in range(27):
            value = stage_in[k - 1, i, pl.ds(r, 8), :] + even
            if i < 13:
                value = value + along[i]
            elif i > 13:
                value = value - along[26 - i]
            out[pl.ds(g.at(i, k, r), 8), :] = value

    over_tiles(
        g,
        g.cols,
        body,
        before=lambda k: copy_in(k).wait(),
        after=lambda k: copy_out(k).start(),
    )
    by_parity("gx", x_first, x_second, functools.partial(pack_x, g, out, -1, 27))
    for k in range(1, g.cols + 1):
        copy_out(k).wait()


def fourth_kernel(g, padded, state, y_first, y_second, buf, out, total):
    del padded
    masks = lane_masks()
    by_parity(
        "gy", y_second, y_first, lambda up, down: unpack_y(g, buf, -1, 27, up, down, masks[0])
    )

    def compute(p, t):
        *flow, wall = load_fields(state, g.extended, t, 7)
        even, gx, gy, gz, porous = adjoint_scalars(p, *flow, wall > 0.5)
        save_fields(total, g.extended, t, [porous])
        return adjoint_spread(p, even, gx, gy, gz, wall > 0.5)

    over_extended(g, buf, out, -1, 27, masks, compute)


def fifth_kernel(g, buf, state, before, result, total, peak, stage_out, sems_out):
    masks = lane_masks()

    def copy_out(k):
        return pltpu.make_async_copy(stage_out.at[k - 1], block_of(result, k), sems_out.at[k - 1])

    peak[...] = jnp.zeros((8, LANES), F32)

    def body(k, r, t):
        p = pull_block(g, buf, -1, k, r, masks)
        *flow, wall = load_fields(state, g.local, t, 7)
        even, gx, gy, gz, porous = adjoint_scalars(p, *flow, wall > 0.5)
        here = load_fields(before, g.extended, t, 1)[0] + porous
        save_fields(total, g.local, t, [here])
        peak[...] = jnp.maximum(peak[...], jnp.abs(here))
        for i, value in enumerate(adjoint_spread(p, even, gx, gy, gz, wall > 0.5)):
            stage_out[k - 1, i, pl.ds(r, 8), :] = value

    over_tiles(g, g.cols, body, after=lambda k: copy_out(k).start())
    for k in range(1, g.cols + 1):
        copy_out(k).wait()


def scale_kernel(g, total, peak, out):
    largest = jnp.max(peak[...])
    factor = 1.0 / (jnp.full((8, LANES), largest, F32) + EPS)
    for c in range(g.cols):
        for a in range(g.tiles):
            value = load_fields(total, g.local, c * g.tiles + a, 1)[0] * factor
            out[8 * a : 8 * a + 8, c * LANES : (c + 1) * LANES] = value


def swap_pairs(count, start):
    pairs = []
    for i in range(start, count, 2):
        j = (i + 1) % count
        pairs += [(i, j), (j, i)]
    return pairs


def swap(axis, count, first, second):
    return (
        lax.ppermute(first, axis, swap_pairs(count, 0)),
        lax.ppermute(second, axis, swap_pairs(count, 1)),
    )


def largest_of_all(peak, sizes):
    for axis, count in (("gy", sizes[1]), ("gx", sizes[0])):
        step = 1
        while step < count:
            other = lax.ppermute(peak, axis, [(i, i ^ step) for i in range(count)])
            peak = jnp.maximum(peak, other)
            step *= 2
    return peak


def on_device(sizes, populations, adjoint_in, porosity, solid, labels):
    rows, width = porosity.shape
    g = Grid(rows, width)
    in_vmem = pl.BlockSpec(memory_space=pltpu.VMEM)
    anywhere = pl.BlockSpec(memory_space=pl.ANY)
    hbm = pl.BlockSpec(memory_space=pltpu.HBM)
    nx, ny = sizes

    def vmem(*shape):
        return pltpu.VMEM(shape, F32)

    def fields(count, tiles):
        return vmem(count * tiles * 8, LANES)

    def padded(count):
        return vmem(*g.padded(count))

    def x_parcels(count):
        return [vmem((count) * g.cols, LANES)] * 2

    def y_parcels(count, sign):
        slots = y_slots(count, sign)
        return [vmem(-(-slots * (rows + 2) // 8) * 8, LANES)] * 2

    whole = jax.ShapeDtypeStruct(populations.shape, F32)
    stage = pltpu.VMEM((g.cols, 27, rows, LANES), F32)
    sems = pltpu.SemaphoreType.DMA((g.cols,))

    def call(name, kernel, in_specs, out_shape, out_specs, scratch=(), aliases=None):
        return pl.pallas_call(
            functools.partial(kernel, g),
            in_specs=in_specs,
            out_shape=out_shape,
            out_specs=out_specs,
            scratch_shapes=list(scratch),
            input_output_aliases=aliases or {},
            compiler_params=pltpu.CompilerParams(vmem_limit_bytes=VMEM_LIMIT),
            name=name,
        )

    def pin(x):
        return pltpu.with_memory_space_constraint(x, pltpu.VMEM)

    def exchange(buf, parcels, sign, count):
        parcels = swap("gx", nx, *parcels)
        buf, *parcels = call(
            "relay",
            lambda grid, *refs: relay_kernel(grid, sign, count, *refs),
            [in_vmem] * 3,
            [padded(count)] + y_parcels(count, sign),
            [in_vmem] * 3,
            aliases={0: 0},
        )(pin(buf), *parcels)
        return buf, swap("gy", ny, *parcels)

    post, state0, *parcels = call(
        "collide_first",
        first_kernel,
        [anywhere, in_vmem, in_vmem, in_vmem],
        [padded(30), fields(7, g.local)] + x_parcels(30),
        [in_vmem] * 4,
        [stage, sems],
    )(populations, porosity, solid, labels)
    post, parcels = exchange(post, parcels, 1, 30)

    _, post, state1 = call(
        "collide_second",
        second_kernel,
        [in_vmem] * 3,
        [padded(30), padded(27), fields(7, g.extended)],
        [in_vmem] * 3,
        aliases={0: 0},
    )(pin(post), *parcels)

    final, field, *parcels = call(
        "stream_and_seed",
        third_kernel,
        [in_vmem, anywhere],
        [whole, padded(27)] + x_parcels(27),
        [hbm] + [in_vmem] * 3,
        [stage, stage, sems, sems],
    )(pin(post), adjoint_in)
    field, parcels = exchange(field, parcels, -1, 27)

    _, field, total = call(
        "adjoint_second",
        fourth_kernel,
        [in_vmem] * 4,
        [padded(27), padded(27), fields(1, g.extended)],
        [in_vmem] * 3,
        aliases={0: 0},
    )(pin(field), pin(state1), *parcels)

    adjoint_out, total, peak = call(
        "adjoint_first",
        fifth_kernel,
        [in_vmem] * 3,
        [whole, fields(1, g.local), vmem(8, LANES)],
        [hbm] + [in_vmem] * 2,
        [stage, sems],
    )(pin(field), pin(state0), pin(total))

    sensitivity = call(
        "normalize",
        scale_kernel,
        [in_vmem, in_vmem],
        jax.ShapeDtypeStruct(porosity.shape, F32),
        in_vmem,
    )(pin(total), largest_of_all(peak, sizes))
    return final, adjoint_out, sensitivity


def solution(mesh):
    sizes = (mesh.shape["gx"], mesh.shape["gy"])
    whole, flat = P(None, "gx", "gy"), P("gx", "gy")
    return jax.shard_map(
        functools.partial(on_device, sizes),
        mesh=mesh,
        in_specs=(whole, whole, flat, flat, flat),
        out_specs=(whole, whole, flat),
        check_vma=False,
    )
```

```python
import functools

import jax
import jax.numpy as jnp
from jax import lax
from jax.experimental import pallas as pl
from jax.experimental.pallas import tpu as pltpu
from jax.sharding import PartitionSpec as P

NZ = 64
RELAX = 0.8
PUSH = 0.2
EPS = 1e-06
LANES = 128
VELOCITY = [(a, b, c) for a in (-1, 0, 1) for b in (-1, 0, 1) for c in (-1, 0, 1)]
INDEX = {v: i for i, v in enumerate(VELOCITY)}
WEIGHT = [
    [8.0 / 27, 2.0 / 27, 1.0 / 54, 1.0 / 216][abs(v[0]) + abs(v[1]) + abs(v[2])]
    for v in VELOCITY
]
NORM = [abs(v[0]) + abs(v[1]) + abs(v[2]) for v in VELOCITY]
F32 = jnp.float32
VMEM_LIMIT = 20 * 1024 * 1024


class Grid:
    def __init__(self, rows, width):
        self.rows = rows
        self.cols = width // LANES
        self.tiles = rows // 8
        self.panel = rows + 16
        self.halo = self.cols + 1
        self.local = self.cols * self.tiles
        self.extended = self.halo * self.tiles + 3

    def at(self, i, k, r):
        return self.field(i) + k * self.panel + r

    def field(self, i):
        return i * (self.cols + 2) * self.panel + 8

    def padded(self, fields):
        return (fields * (self.cols + 2) * self.panel + 8, LANES)


def velocity(i, sign):
    return tuple(sign * n for n in VELOCITY[i]) if i < 27 else (0, 0, 0)


def moving(fields, sign, axis, side):
    return [i for i in range(fields) if velocity(i, sign)[axis] == side]


def lane_masks():
    lane = lax.broadcasted_iota(jnp.int32, (8, LANES), 1)
    return lane >= NZ, lane % NZ == 0, lane % NZ == NZ - 1


def shift_lanes(here, d, masks):
    first, last = masks[1:]
    dy, dz = d[1:]
    if dz == 0:
        return here if dy == 0 else pltpu.roll(here, NZ, 1)
    if dz == 1:
        one, other, edge = 1, NZ + 1, first
    else:
        one, other, edge = LANES - 1, NZ - 1, last
    inner, wrapped = (one, other) if dy == 0 else (other, one)
    return jnp.where(edge, pltpu.roll(here, wrapped, 1), pltpu.roll(here, inner, 1))


def pull(load, d, masks):
    high = masks[0]
    here = load(0)
    if d[1] == 1:
        here = jnp.where(high, load(-1), here)
    elif d[1] == -1:
        here = jnp.where(high, here, load(1))
    return shift_lanes(here, d, masks)


def pull_block(g, buf, sign, k, r, masks, fields=27):
    base = pl.multiple_of(k * g.panel + r, 8)
    after = pl.multiple_of(jnp.where(k == g.halo, g.panel + r, base + g.panel), 8)
    out = []
    for i in range(fields):
        d = velocity(i, sign)

        def load(n, i=i, d=d):
            start = {-1: base - g.panel, 0: base, 1: after}[n]
            return buf[pl.ds(start + (g.field(i) - d[0]), 8), :]

        out.append(pull(load, d, masks))
    return out


def pull_edge(g, buf, sign, side, masks, fields=27):
    out = []
    for i in range(fields):
        d = velocity(i, sign)
        if side == 1:
            row = g.rows - d[0]
        else:
            row = {1: g.rows, 0: g.rows + 1, -1: 0}[d[0]]

        def load(n, i=i, row=row):
            return buf[pl.ds(g.at(i, 1 + n, row), g.cols, stride=g.panel), :]

        out.append(pull(load, d, masks))
    return out


def moments(f):
    flat = {}
    along_z = None
    for a in (-1, 0, 1):
        for b in (-1, 0, 1):
            lo, mid, hi = (f[INDEX[(a, b, c)]] for c in (-1, 0, 1))
            flat[a, b] = lo + mid + hi
            diff = hi - lo
            along_z = diff if along_z is None else along_z + diff
    line = {}
    along_y = None
    for a in (-1, 0, 1):
        line[a] = flat[a, -1] + flat[a, 0] + flat[a, 1]
        diff = flat[a, 1] - flat[a, -1]
        along_y = diff if along_y is None else along_y + diff
    return line[-1] + line[0] + line[1], line[1] - line[-1], along_y, along_z


def combos(x, y, z):
    plane = {}
    for a in (-1, 0, 1):
        for b in (-1, 0, 1):
            if (a, b) > (0, 0):
                continue
            if a == 0:
                plane[a, b] = -y if b else None
            else:
                plane[a, b] = -x if b == 0 else (-x - y if b < 0 else y - x)
    out = []
    for a, b, c in VELOCITY[:13]:
        base = plane[a, b]
        if base is None:
            out.append(-z)
        else:
            out.append(base if c == 0 else (base - z if c < 0 else base + z))
    return out


def relax(f, rho, wx, wy, wz, damp, push, solid):
    ux, uy, uz = (wx + push) * damp, wy * damp, wz * damp
    base = 1.0 - 1.5 * (ux * ux + uy * uy + uz * uz)
    keep = 1.0 - 1.0 / RELAX
    gain = rho * (1.0 / RELAX)
    level = [gain * w for w in (8.0 / 27, 2.0 / 27, 1.0 / 54, 1.0 / 216)]
    along = combos(3.0 * ux, 3.0 * uy, 3.0 * uz)
    out = [None] * 27
    for i in range(13):
        j = 26 - i
        even = base + 0.5 * (along[i] * along[i])
        lift = level[NORM[i]]
        out[i] = jnp.where(solid, f[j], keep * f[i] + lift * (even + along[i]))
        out[j] = jnp.where(solid, f[i], keep * f[j] + lift * (even - along[i]))
    out[13] = jnp.where(solid, f[13], keep * f[13] + level[0] * base)
    return out


def pulled_moments(p):
    first = {}
    for a in (-1, 0, 1):
        for b in (-1, 0, 1):
            lo, mid, hi = (p[INDEX[(a, b, c)]] for c in (-1, 0, 1))
            both = lo + hi
            first[a, b] = (4.0 * mid + both, hi - lo, both)
    second = {}
    for a in (-1, 0, 1):
        lo, mid, hi = (first[a, b] for b in (-1, 0, 1))
        b0 = lo[0] + hi[0]
        b1 = lo[1] + hi[1]
        second[a] = dict(
            one=4.0 * mid[0] + b0,
            y=hi[0] - lo[0],
            yy=b0,
            z=4.0 * mid[1] + b1,
            yz=hi[1] - lo[1],
            zz=4.0 * mid[2] + lo[2] + hi[2],
        )
    lo, mid, hi = (second[a] for a in (-1, 0, 1))

    def full(key):
        return 4.0 * mid[key] + lo[key] + hi[key]

    xx = lo["one"] + hi["one"]
    return dict(
        one=4.0 * mid["one"] + xx,
        x=hi["one"] - lo["one"],
        xx=xx,
        y=full("y"),
        xy=hi["y"] - lo["y"],
        yy=full("yy"),
        z=full("z"),
        xz=hi["z"] - lo["z"],
        yz=full("yz"),
        zz=full("zz"),
    )


def adjoint_scalars(p, rho, wx, wy, wz, damp, push, solid):
    ux, uy, uz = (wx + push) * damp, wy * damp, wz * damp
    s = pulled_moments(p)
    scale = 1.0 / (216.0 * RELAX)
    one = s["one"] * scale
    b = [s[k] * (3.0 * scale) for k in ("x", "y", "z")]
    d = {k: s[k] * (9.0 * scale) for k in ("xx", "xy", "yy", "xz", "yz", "zz")}
    qx = d["xx"] * ux + d["xy"] * uy + d["xz"] * uz
    qy = d["xy"] * ux + d["yy"] * uy + d["yz"] * uz
    qz = d["xz"] * ux + d["yz"] * uy + d["zz"] * uz
    linear = b[0] * ux + b[1] * uy + b[2] * uz
    square = ux * ux + uy * uy + uz * uz
    even = one + linear + 0.5 * (qx * ux + qy * uy + qz * uz) - 1.5 * one * square
    three = 3.0 * one
    gx = (b[0] + qx - three * ux) * damp
    gy = (b[1] + qy - three * uy) * damp
    gz = (b[2] + qz - three * uz) * damp
    even = even - (gx * wx + gy * wy + gz * wz)
    porous = jnp.where(solid, 0.0, -rho * (gx * ux + gy * uy + gz * uz))
    return even, gx, gy, gz, porous


def adjoint_spread(p, even, gx, gy, gz, solid):
    keep = 1.0 - 1.0 / RELAX
    along = combos(gx, gy, gz)
    out = [None] * 27
    for i in range(13):
        j = 26 - i
        out[i] = jnp.where(solid, p[j], keep * p[i] + (even + along[i]))
        out[j] = jnp.where(solid, p[i], keep * p[j] + (even - along[i]))
    out[13] = jnp.where(solid, p[13], keep * p[13] + even)
    return out


def pack_x(g, buf, sign, fields, up, down):
    for side, ref in ((1, up), (-1, down)):
        edge, inner = (g.rows - 1, g.rows - 2) if side == 1 else (0, 1)
        lines = [(i, r) for i in moving(fields, sign, 0, side) for r in (edge, inner)]
        lines += [(i, edge) for i in moving(fields, sign, 0, 0)]
        for n, (i, r) in enumerate(lines):
            ref[n * g.cols : (n + 1) * g.cols, :] = buf[
                pl.ds(g.at(i, 1, r), g.cols, stride=g.panel), :
            ]


def unpack_x(g, buf, sign, fields, up, down):
    for side, ref in ((1, up), (-1, down)):
        lines = []
        for i in moving(fields, sign, 0, side):
            if side == 1:
                lines += [(i, (-1, g.rows + 1)), (i, (g.rows,))]
            else:
                lines += [(i, (g.rows,)), (i, (g.rows + 1,))]
        for i in moving(fields, sign, 0, 0):
            lines.append((i, (g.rows + 1 if side == 1 else g.rows,)))
        for n, (i, targets) in enumerate(lines):
            value = ref[n * g.cols : (n + 1) * g.cols, :]
            for r in targets:
                buf[pl.ds(g.at(i, 1, r), g.cols, stride=g.panel), :] = value
    for i in moving(fields, sign, 0, -1):
        buf[pl.ds(g.at(i, 1, g.rows + 2), g.cols, stride=g.panel), :] = buf[
            pl.ds(g.at(i, 1, 0), g.cols, stride=g.panel), :
        ]


def slot_rows(g, slots, n):
    pieces = [(n * g.rows + 8 * a, 8 * a, 8) for a in range(g.tiles)]
    return pieces + [(slots * g.rows + 2 * n, g.rows, 2)]


def still_pairs(fields, sign):
    still = moving(fields, sign, 1, 0)
    half = (len(still) + 1) // 2
    return [(still[n], still[n + half] if n + half < len(still) else None) for n in range(half)]


def y_slots(fields, sign):
    return 9 + len(still_pairs(fields, sign))


def pack_y(g, buf, sign, fields, up, down, high):
    slots = y_slots(fields, sign)
    for side, ref in ((1, up), (-1, down)):
        k = g.cols if side == 1 else 1
        for n, i in enumerate(moving(fields, sign, 1, side)):
            for to, r, count in slot_rows(g, slots, n):
                ref[to : to + count, :] = buf[pl.ds(g.at(i, k, r), count), :]
        for n, (i, j) in enumerate(still_pairs(fields, sign)):
            for to, r, count in slot_rows(g, slots, 9 + n):
                value = buf[pl.ds(g.at(i, k, r), count), :]
                if j is not None:
                    other = pltpu.roll(buf[pl.ds(g.at(j, k, r), count), :], NZ, 1)
                    pair = (value, other) if side == 1 else (other, value)
                    value = jnp.where(high[:count], *pair)
                ref[to : to + count, :] = value


def unpack_y(g, buf, sign, fields, up, down, high):
    slots = y_slots(fields, sign)
    for side, ref in ((1, up), (-1, down)):
        for n, i in enumerate(moving(fields, sign, 1, side)):
            for to, r, count in slot_rows(g, slots, n):
                value = ref[to : to + count, :]
                for k in (0, g.halo) if side == 1 else (g.halo,):
                    buf[pl.ds(g.at(i, k, r), count), :] = value
    for n, (i, j) in enumerate(still_pairs(fields, sign)):
        for to, r, count in slot_rows(g, slots, 9 + n):
            before, after = up[to : to + count, :], down[to : to + count, :]
            mask = high[:count]
            buf[pl.ds(g.at(i, g.halo, r), count), :] = jnp.where(mask, before, after)
            if j is not None:
                buf[pl.ds(g.at(j, g.halo, r), count), :] = pltpu.roll(
                    jnp.where(mask, after, before), NZ, 1
                )
    for i in moving(fields, sign, 0, 1):
        for k in (0, g.halo) if velocity(i, sign)[1] == 1 else (g.halo,):
            buf[pl.ds(g.at(i, k, -1), 1), :] = buf[pl.ds(g.at(i, k, g.rows + 1), 1), :]
    for i in moving(fields, sign, 0, -1):
        for k in (0, g.halo) if velocity(i, sign)[1] == 1 else (g.halo,):
            buf[pl.ds(g.at(i, k, g.rows + 2), 1), :] = buf[pl.ds(g.at(i, k, 0), 1), :]


def by_parity(axis, first, second, act):
    even = lax.rem(lax.axis_index(axis), 2) == 0

    @pl.when(even)
    def _():
        act(first, second)

    @pl.when(jnp.logical_not(even))
    def _():
        act(second, first)


def load_fields(ref, tiles, t, count):
    base = pl.multiple_of(t * 8, 8)
    return [ref[pl.ds(base + n * tiles * 8, 8), :] for n in range(count)]


def save_fields(ref, tiles, t, values):
    base = pl.multiple_of(t * 8, 8)
    for n, value in enumerate(values):
        ref[pl.ds(base + n * tiles * 8, 8), :] = value


def save_populations(g, out, k, r, values):
    base = pl.multiple_of(k * g.panel + r, 8)
    for i, value in enumerate(values):
        out[pl.ds(base + g.field(i), 8), :] = value


def over_tiles(g, panels, body, before=None, after=None):
    def column(k, carry):
        if before is not None:
            before(k)

        def tile(a, inner):
            body(k, pl.multiple_of(a * 8, 8), (k - 1) * g.tiles + a)
            return inner

        lax.fori_loop(0, g.tiles, tile, 0)
        if after is not None:
            after(k)
        return carry

    lax.fori_loop(1, panels + 1, column, 0)


def over_extended(g, buf, out, sign, fields, masks, compute):
    def body(k, r, t):
        values = compute(pull_block(g, buf, sign, k, r, masks, fields), t)
        save_populations(g, out, k, r, values)

    over_tiles(g, g.halo, body)
    t = g.halo * g.tiles
    values = compute(pull_block(g, buf, sign, g.halo, g.rows, masks, fields), t)
    for i in range(27):
        dx = velocity(i, sign)[0]
        if dx == -1:
            out[pl.ds(g.at(i, g.halo, g.rows), 1), :] = values[i][0:1]
        elif dx == 1:
            out[pl.ds(g.at(i, g.halo, -1), 1), :] = values[i][1:2]
    for n, side in ((1, 1), (2, -1)):
        values = compute(pull_edge(g, buf, sign, side, masks, fields), t + n)
        for i in moving(27, sign, 0, -side):
            row = g.rows if side == 1 else -1
            out[pl.ds(g.at(i, 1, row), g.cols, stride=g.panel), :] = values[i]
    for i in moving(27, sign, 1, 1):
        for a in range(g.tiles):
            out[pl.ds(g.at(i, 0, 8 * a), 8), :] = out[pl.ds(g.at(i, g.halo, 8 * a), 8), :]
        for r in (-1, g.rows):
            out[pl.ds(g.at(i, 0, r), 1), :] = out[pl.ds(g.at(i, g.halo, r), 1), :]


def block_of(ref, k):
    return ref.at[:, :, pl.ds(pl.multiple_of((k - 1) * LANES, LANES), LANES)]


def first_kernel(g, pops, *refs):
    flat, (out, state, x_first, x_second, stage, *near), sems, flat_sems = refs[:3], refs[3:-2], *refs[-2:]
    porosity, solid, labels = near

    def copy(k):
        return pltpu.make_async_copy(block_of(pops, k), stage.at[k - 1], sems.at[k - 1])

    flat_copies = [
        pltpu.make_async_copy(source, target, flat_sems.at[n])
        for n, (source, target) in enumerate(zip(flat, near))
    ]
    copy(1).start()
    for each in flat_copies:
        each.start()
    for k in range(2, g.cols + 1):
        copy(k).start()
    for each in flat_copies:
        each.wait()

    def body(k, r, t):
        f = [stage[k - 1, i, pl.ds(r, 8), :] for i in range(27)]
        spot = (pl.ds(r, 8), pl.ds(pl.multiple_of((k - 1) * LANES, LANES), LANES))
        wall = solid[spot]
        label = labels[spot]
        damp = 1.0 / (1.0 + porosity[spot])
        push = jnp.where(label == 1, PUSH, jnp.where(label == 2, -PUSH, 0.0))
        rho, mx, my, mz = moments(f)
        inverse = 1.0 / rho
        flow = (rho, mx * inverse, my * inverse, mz * inverse, damp, push)
        extra = (damp, push, wall.astype(F32))
        save_fields(state, g.local, t, flow + extra[2:])
        save_populations(g, out, k, r, tuple(relax(f, *flow, wall == 1)) + extra)

    over_tiles(g, g.cols, body, before=lambda k: copy(k).wait())
    by_parity("gx", x_first, x_second, functools.partial(pack_x, g, out, 1, 30))


def relay_kernel(g, sign, fields, padded, x_first, x_second, buf, y_first, y_second):
    del padded
    high = lane_masks()[0]
    by_parity("gx", x_second, x_first, functools.partial(unpack_x, g, buf, sign, fields))
    by_parity(
        "gy",
        y_first,
        y_second,
        lambda up, down: pack_y(g, buf, sign, fields, up, down, high),
    )


def second_kernel(g, padded, y_first, y_second, buf, out, state):
    del padded
    masks = lane_masks()
    by_parity(
        "gy", y_second, y_first, lambda up, down: unpack_y(g, buf, 1, 30, up, down, masks[0])
    )

    def compute(values, t):
        f, (damp, push, wall) = values[:27], values[27:]
        rho, mx, my, mz = moments(f)
        inverse = 1.0 / rho
        flow = (rho, mx * inverse, my * inverse, mz * inverse, damp, push)
        save_fields(state, g.extended, t, flow + (wall,))
        return relax(f, *flow, wall > 0.5)

    over_extended(g, buf, out, 1, 30, masks, compute)


def third_kernel(g, buf, adjoint, final, out, x_first, x_second, stage_out, stage_in, *sems):
    sems_out, sems_in = sems
    masks = lane_masks()

    def copy_in(k):
        return pltpu.make_async_copy(block_of(adjoint, k), stage_in.at[k - 1], sems_in.at[k - 1])

    def copy_out(k):
        return pltpu.make_async_copy(stage_out.at[k - 1], block_of(final, k), sems_out.at[k - 1])

    for k in range(1, g.cols + 1):
        copy_in(k).start()

    def body(k, r, t):
        f = pull_block(g, buf, 1, k, r, masks)
        for i in range(27):
            stage_out[k - 1, i, pl.ds(r, 8), :] = f[i]
        rho, mx, my, mz = moments(f)
        inverse = 1.0 / rho
        wx, wy, wz = mx * inverse, my * inverse, mz * inverse
        even = -(wx * wx + wy * wy + wz * wz) * inverse
        along = combos(wx * inverse, wy * inverse, wz * inverse)
        seeded = [stage_in[k - 1, i, pl.ds(r, 8), :] + even for i in range(27)]
        for i in range(13):
            seeded[i] = seeded[i] + along[i]
            seeded[26 - i] = seeded[26 - i] - along[i]
        save_populations(g, out, k, r, seeded)

    over_tiles(
        g,
        g.cols,
        body,
        before=lambda k: copy_in(k).wait(),
        after=lambda k: copy_out(k).start(),
    )
    by_parity("gx", x_first, x_second, functools.partial(pack_x, g, out, -1, 27))
    for k in range(1, g.cols + 1):
        copy_out(k).wait()


def fourth_kernel(g, padded, state, y_first, y_second, buf, out, total):
    del padded
    masks = lane_masks()
    by_parity(
        "gy", y_second, y_first, lambda up, down: unpack_y(g, buf, -1, 27, up, down, masks[0])
    )

    def compute(p, t):
        *flow, wall = load_fields(state, g.extended, t, 7)
        even, gx, gy, gz, porous = adjoint_scalars(p, *flow, wall > 0.5)
        save_fields(total, g.extended, t, [porous])
        return adjoint_spread(p, even, gx, gy, gz, wall > 0.5)

    over_extended(g, buf, out, -1, 27, masks, compute)


def fifth_kernel(g, buf, state, before, total, peak, parts):
    masks = lane_masks()
    peak[...] = jnp.zeros((8, LANES), F32)

    def body(k, r, t):
        p = pull_block(g, buf, -1, k, r, masks)
        *flow, wall = load_fields(state, g.local, t, 7)
        *spread, porous = adjoint_scalars(p, *flow, wall > 0.5)
        here = load_fields(before, g.extended, t, 1)[0] + porous
        save_fields(total, g.local, t, [here])
        save_fields(parts, g.local, t, spread + [wall])
        peak[...] = jnp.maximum(peak[...], jnp.abs(here))

    over_tiles(g, g.cols, body)


def sixth_kernel(g, buf, parts, result, stage_out, sems_out):
    masks = lane_masks()

    def copy_out(k):
        return pltpu.make_async_copy(stage_out.at[k - 1], block_of(result, k), sems_out.at[k - 1])

    def body(k, r, t):
        p = pull_block(g, buf, -1, k, r, masks)
        *spread, wall = load_fields(parts, g.local, t, 5)
        for i, value in enumerate(adjoint_spread(p, *spread, wall > 0.5)):
            stage_out[k - 1, i, pl.ds(r, 8), :] = value

    over_tiles(g, g.cols, body, after=lambda k: copy_out(k).start())
    for k in range(1, g.cols + 1):
        copy_out(k).wait()


def scale_kernel(g, total, peak, out):
    largest = jnp.max(peak[...])
    factor = 1.0 / (jnp.full((8, LANES), largest, F32) + EPS)
    for c in range(g.cols):
        for a in range(g.tiles):
            value = load_fields(total, g.local, c * g.tiles + a, 1)[0] * factor
            out[8 * a : 8 * a + 8, c * LANES : (c + 1) * LANES] = value


def swap_pairs(count, start):
    pairs = []
    for i in range(start, count, 2):
        j = (i + 1) % count
        pairs += [(i, j), (j, i)]
    return pairs


def swap(axis, count, first, second):
    return (
        lax.ppermute(first, axis, swap_pairs(count, 0)),
        lax.ppermute(second, axis, swap_pairs(count, 1)),
    )


def largest_of_all(peak):
    return lax.all_gather(peak, ("gx", "gy"), tiled=True)


def on_device(sizes, populations, adjoint_in, porosity, solid, labels):
    rows, width = porosity.shape
    g = Grid(rows, width)
    in_vmem = pl.BlockSpec(memory_space=pltpu.VMEM)
    anywhere = pl.BlockSpec(memory_space=pl.ANY)
    hbm = pl.BlockSpec(memory_space=pltpu.HBM)
    nx, ny = sizes

    def vmem(*shape):
        return pltpu.VMEM(shape, F32)

    def fields(count, tiles):
        return vmem(count * tiles * 8, LANES)

    def padded(count):
        return vmem(*g.padded(count))

    def x_parcels(count):
        return [vmem((count) * g.cols, LANES)] * 2

    def y_parcels(count, sign):
        slots = y_slots(count, sign)
        return [vmem(-(-slots * (rows + 2) // 8) * 8, LANES)] * 2

    whole = jax.ShapeDtypeStruct(populations.shape, F32)
    stage = pltpu.VMEM((g.cols, 27, rows, LANES), F32)
    sems = pltpu.SemaphoreType.DMA((g.cols,))

    def call(name, kernel, in_specs, out_shape, out_specs, scratch=(), aliases=None):
        return pl.pallas_call(
            functools.partial(kernel, g),
            in_specs=in_specs,
            out_shape=out_shape,
            out_specs=out_specs,
            scratch_shapes=list(scratch),
            input_output_aliases=aliases or {},
            compiler_params=pltpu.CompilerParams(vmem_limit_bytes=VMEM_LIMIT),
            name=name,
        )

    def pin(x):
        return pltpu.with_memory_space_constraint(x, pltpu.VMEM)

    def exchange(buf, parcels, sign, count):
        parcels = swap("gx", nx, *parcels)
        buf, *parcels = call(
            "relay",
            lambda grid, *refs: relay_kernel(grid, sign, count, *refs),
            [in_vmem] * 3,
            [padded(count)] + y_parcels(count, sign),
            [in_vmem] * 3,
            aliases={0: 0},
        )(pin(buf), *parcels)
        return buf, swap("gy", ny, *parcels)

    post, state0, *parcels = call(
        "collide_first",
        first_kernel,
        [hbm] * 4,
        [padded(30), fields(7, g.local)] + x_parcels(30),
        [in_vmem] * 4,
        [stage, vmem(*porosity.shape)]
        + [pltpu.VMEM(porosity.shape, jnp.int32)] * 2
        + [sems, pltpu.SemaphoreType.DMA((3,))],
    )(*(pltpu.with_memory_space_constraint(x, pltpu.HBM) for x in (populations, porosity, solid, labels)))
    post, parcels = exchange(post, parcels, 1, 30)

    _, post, state1 = call(
        "collide_second",
        second_kernel,
        [in_vmem] * 3,
        [padded(30), padded(27), fields(7, g.extended)],
        [in_vmem] * 3,
        aliases={0: 0},
    )(pin(post), *parcels)

    final, field, *parcels = call(
        "stream_and_seed",
        third_kernel,
        [in_vmem, anywhere],
        [whole, padded(27)] + x_parcels(27),
        [hbm] + [in_vmem] * 3,
        [stage, stage, sems, sems],
    )(pin(post), adjoint_in)
    field, parcels = exchange(field, parcels, -1, 27)

    _, field, total = call(
        "adjoint_second",
        fourth_kernel,
        [in_vmem] * 4,
        [padded(27), padded(27), fields(1, g.extended)],
        [in_vmem] * 3,
        aliases={0: 0},
    )(pin(field), pin(state1), *parcels)

    total, peak, parts = call(
        "adjoint_total",
        fifth_kernel,
        [in_vmem] * 3,
        [fields(1, g.local), vmem(8, LANES), fields(5, g.local)],
        [in_vmem] * 3,
    )(pin(field), pin(state0), pin(total))
    largest = largest_of_all(peak)

    adjoint_out = call(
        "adjoint_first",
        sixth_kernel,
        [in_vmem] * 2,
        whole,
        hbm,
        [stage, sems],
    )(pin(field), pin(parts))

    sensitivity = call(
        "normalize",
        scale_kernel,
        [in_vmem, in_vmem],
        jax.ShapeDtypeStruct(porosity.shape, F32),
        in_vmem,
    )(pin(total), largest)
    return final, adjoint_out, sensitivity


def solution(mesh):
    sizes = (mesh.shape["gx"], mesh.shape["gy"])
    whole, flat = P(None, "gx", "gy"), P("gx", "gy")
    return jax.shard_map(
        functools.partial(on_device, sizes),
        mesh=mesh,
        in_specs=(whole, whole, flat, flat, flat),
        out_specs=(whole, whole, flat),
        check_vma=False,
    )
```

```python
import functools

import jax
import jax.numpy as jnp
from jax import lax
from jax.experimental import pallas as pl
from jax.experimental.pallas import tpu as pltpu
from jax.sharding import PartitionSpec as P

NZ = 64
RELAX = 0.8
PUSH = 0.2
EPS = 1e-06
LANES = 128
VELOCITY = [(a, b, c) for a in (-1, 0, 1) for b in (-1, 0, 1) for c in (-1, 0, 1)]
INDEX = {v: i for i, v in enumerate(VELOCITY)}
WEIGHT = [
    [8.0 / 27, 2.0 / 27, 1.0 / 54, 1.0 / 216][abs(v[0]) + abs(v[1]) + abs(v[2])]
    for v in VELOCITY
]
NORM = [abs(v[0]) + abs(v[1]) + abs(v[2]) for v in VELOCITY]
F32 = jnp.float32
VMEM_LIMIT = 20 * 1024 * 1024


class Grid:
    def __init__(self, rows, width):
        self.rows = rows
        self.cols = width // LANES
        self.height = 16 if rows % 16 == 0 else 8
        self.tiles = rows // self.height
        self.panel = rows + 16
        self.halo = self.cols + 1
        self.local = self.cols * rows
        self.extended = self.halo * rows + 24

    def at(self, i, k, r):
        return self.field(i) + k * self.panel + r

    def field(self, i):
        return i * (self.cols + 2) * self.panel + 8

    def padded(self, fields):
        return (fields * (self.cols + 2) * self.panel + 8, LANES)


def velocity(i, sign):
    return tuple(sign * n for n in VELOCITY[i]) if i < 27 else (0, 0, 0)


def moving(fields, sign, axis, side):
    return [i for i in range(fields) if velocity(i, sign)[axis] == side]


def lane_masks(height):
    lane = lax.broadcasted_iota(jnp.int32, (height, LANES), 1)
    return lane >= NZ, lane % NZ == 0, lane % NZ == NZ - 1


def shift_lanes(here, d, masks):
    first, last = masks[1:]
    dy, dz = d[1:]
    if dz == 0:
        return here if dy == 0 else pltpu.roll(here, NZ, 1)
    if dz == 1:
        one, other, edge = 1, NZ + 1, first
    else:
        one, other, edge = LANES - 1, NZ - 1, last
    inner, wrapped = (one, other) if dy == 0 else (other, one)
    return jnp.where(edge, pltpu.roll(here, wrapped, 1), pltpu.roll(here, inner, 1))


def pull(load, d, masks):
    high = masks[0]
    here = load(0)
    if d[1] == 1:
        here = jnp.where(high, load(-1), here)
    elif d[1] == -1:
        here = jnp.where(high, here, load(1))
    return shift_lanes(here, d, masks)


def pull_block(g, buf, sign, k, r, masks, fields=27):
    height = masks[0].shape[0]
    base = pl.multiple_of(k * g.panel + r, 8)
    after = pl.multiple_of(jnp.where(k == g.halo, g.panel + r, base + g.panel), 8)
    out = []
    for i in range(fields):
        d = velocity(i, sign)

        def load(n, i=i, d=d):
            start = {-1: base - g.panel, 0: base, 1: after}[n]
            return buf[pl.ds(start + (g.field(i) - d[0]), height), :]

        out.append(pull(load, d, masks))
    return out


def pull_edge(g, buf, sign, side, masks, fields=27):
    out = []
    for i in range(fields):
        d = velocity(i, sign)
        if side == 1:
            row = g.rows - d[0]
        else:
            row = {1: g.rows, 0: g.rows + 1, -1: 0}[d[0]]

        def load(n, i=i, row=row):
            return buf[pl.ds(g.at(i, 1 + n, row), g.cols, stride=g.panel), :]

        out.append(pull(load, d, masks))
    return out


def moments(f):
    flat = {}
    along_z = None
    for a in (-1, 0, 1):
        for b in (-1, 0, 1):
            lo, mid, hi = (f[INDEX[(a, b, c)]] for c in (-1, 0, 1))
            flat[a, b] = lo + mid + hi
            diff = hi - lo
            along_z = diff if along_z is None else along_z + diff
    line = {}
    along_y = None
    for a in (-1, 0, 1):
        line[a] = flat[a, -1] + flat[a, 0] + flat[a, 1]
        diff = flat[a, 1] - flat[a, -1]
        along_y = diff if along_y is None else along_y + diff
    return line[-1] + line[0] + line[1], line[1] - line[-1], along_y, along_z


def combos(x, y, z):
    plane = {}
    for a in (-1, 0, 1):
        for b in (-1, 0, 1):
            if (a, b) > (0, 0):
                continue
            if a == 0:
                plane[a, b] = -y if b else None
            else:
                plane[a, b] = -x if b == 0 else (-x - y if b < 0 else y - x)
    out = []
    for a, b, c in VELOCITY[:13]:
        base = plane[a, b]
        if base is None:
            out.append(-z)
        else:
            out.append(base if c == 0 else (base - z if c < 0 else base + z))
    return out


def relax(f, rho, wx, wy, wz, damp, push, solid):
    ux, uy, uz = (wx + push) * damp, wy * damp, wz * damp
    base = 1.0 - 1.5 * (ux * ux + uy * uy + uz * uz)
    keep = 1.0 - 1.0 / RELAX
    gain = rho * (1.0 / RELAX)
    level = [gain * w for w in (8.0 / 27, 2.0 / 27, 1.0 / 54, 1.0 / 216)]
    along = combos(3.0 * ux, 3.0 * uy, 3.0 * uz)
    out = [None] * 27
    for i in range(13):
        j = 26 - i
        even = base + 0.5 * (along[i] * along[i])
        lift = level[NORM[i]]
        out[i] = jnp.where(solid, f[j], keep * f[i] + lift * (even + along[i]))
        out[j] = jnp.where(solid, f[i], keep * f[j] + lift * (even - along[i]))
    out[13] = jnp.where(solid, f[13], keep * f[13] + level[0] * base)
    return out


def pulled_moments(p):
    first = {}
    for a in (-1, 0, 1):
        for b in (-1, 0, 1):
            lo, mid, hi = (p[INDEX[(a, b, c)]] for c in (-1, 0, 1))
            both = lo + hi
            first[a, b] = (4.0 * mid + both, hi - lo, both)
    second = {}
    for a in (-1, 0, 1):
        lo, mid, hi = (first[a, b] for b in (-1, 0, 1))
        b0 = lo[0] + hi[0]
        b1 = lo[1] + hi[1]
        second[a] = dict(
            one=4.0 * mid[0] + b0,
            y=hi[0] - lo[0],
            yy=b0,
            z=4.0 * mid[1] + b1,
            yz=hi[1] - lo[1],
            zz=4.0 * mid[2] + lo[2] + hi[2],
        )
    lo, mid, hi = (second[a] for a in (-1, 0, 1))

    def full(key):
        return 4.0 * mid[key] + lo[key] + hi[key]

    xx = lo["one"] + hi["one"]
    return dict(
        one=4.0 * mid["one"] + xx,
        x=hi["one"] - lo["one"],
        xx=xx,
        y=full("y"),
        xy=hi["y"] - lo["y"],
        yy=full("yy"),
        z=full("z"),
        xz=hi["z"] - lo["z"],
        yz=full("yz"),
        zz=full("zz"),
    )


def adjoint_scalars(p, rho, wx, wy, wz, damp, push, solid):
    ux, uy, uz = (wx + push) * damp, wy * damp, wz * damp
    s = pulled_moments(p)
    scale = 1.0 / (216.0 * RELAX)
    one = s["one"] * scale
    b = [s[k] * (3.0 * scale) for k in ("x", "y", "z")]
    d = {k: s[k] * (9.0 * scale) for k in ("xx", "xy", "yy", "xz", "yz", "zz")}
    qx = d["xx"] * ux + d["xy"] * uy + d["xz"] * uz
    qy = d["xy"] * ux + d["yy"] * uy + d["yz"] * uz
    qz = d["xz"] * ux + d["yz"] * uy + d["zz"] * uz
    linear = b[0] * ux + b[1] * uy + b[2] * uz
    square = ux * ux + uy * uy + uz * uz
    even = one + linear + 0.5 * (qx * ux + qy * uy + qz * uz) - 1.5 * one * square
    three = 3.0 * one
    gx = (b[0] + qx - three * ux) * damp
    gy = (b[1] + qy - three * uy) * damp
    gz = (b[2] + qz - three * uz) * damp
    even = even - (gx * wx + gy * wy + gz * wz)
    porous = jnp.where(solid, 0.0, -rho * (gx * ux + gy * uy + gz * uz))
    return even, gx, gy, gz, porous


def adjoint_spread(p, even, gx, gy, gz, solid):
    keep = 1.0 - 1.0 / RELAX
    along = combos(gx, gy, gz)
    out = [None] * 27
    for i in range(13):
        j = 26 - i
        out[i] = jnp.where(solid, p[j], keep * p[i] + (even + along[i]))
        out[j] = jnp.where(solid, p[i], keep * p[j] + (even - along[i]))
    out[13] = jnp.where(solid, p[13], keep * p[13] + even)
    return out


def pack_x(g, buf, sign, fields, up, down):
    for side, ref in ((1, up), (-1, down)):
        edge, inner = (g.rows - 1, g.rows - 2) if side == 1 else (0, 1)
        lines = [(i, r) for i in moving(fields, sign, 0, side) for r in (edge, inner)]
        lines += [(i, edge) for i in moving(fields, sign, 0, 0)]
        for n, (i, r) in enumerate(lines):
            ref[n * g.cols : (n + 1) * g.cols, :] = buf[
                pl.ds(g.at(i, 1, r), g.cols, stride=g.panel), :
            ]


def unpack_x(g, buf, sign, fields, up, down):
    for side, ref in ((1, up), (-1, down)):
        lines = []
        for i in moving(fields, sign, 0, side):
            if side == 1:
                lines += [(i, (-1, g.rows + 1)), (i, (g.rows,))]
            else:
                lines += [(i, (g.rows,)), (i, (g.rows + 1,))]
        for i in moving(fields, sign, 0, 0):
            lines.append((i, (g.rows + 1 if side == 1 else g.rows,)))
        for n, (i, targets) in enumerate(lines):
            value = ref[n * g.cols : (n + 1) * g.cols, :]
            for r in targets:
                buf[pl.ds(g.at(i, 1, r), g.cols, stride=g.panel), :] = value
    for i in moving(fields, sign, 0, -1):
        buf[pl.ds(g.at(i, 1, g.rows + 2), g.cols, stride=g.panel), :] = buf[
            pl.ds(g.at(i, 1, 0), g.cols, stride=g.panel), :
        ]


def slot_rows(g, slots, n):
    pieces = [(n * g.rows + r, r, 8) for r in range(0, g.rows, 8)]
    return pieces + [(slots * g.rows + 2 * n, g.rows, 2)]


def still_pairs(fields, sign):
    still = moving(fields, sign, 1, 0)
    half = (len(still) + 1) // 2
    return [(still[n], still[n + half] if n + half < len(still) else None) for n in range(half)]


def y_slots(fields, sign):
    return 9 + len(still_pairs(fields, sign))


def pack_y(g, buf, sign, fields, up, down, high):
    slots = y_slots(fields, sign)
    for side, ref in ((1, up), (-1, down)):
        k = g.cols if side == 1 else 1
        for n, i in enumerate(moving(fields, sign, 1, side)):
            for to, r, count in slot_rows(g, slots, n):
                ref[to : to + count, :] = buf[pl.ds(g.at(i, k, r), count), :]
        for n, (i, j) in enumerate(still_pairs(fields, sign)):
            for to, r, count in slot_rows(g, slots, 9 + n):
                value = buf[pl.ds(g.at(i, k, r), count), :]
                if j is not None:
                    other = pltpu.roll(buf[pl.ds(g.at(j, k, r), count), :], NZ, 1)
                    pair = (value, other) if side == 1 else (other, value)
                    value = jnp.where(high[:count], *pair)
                ref[to : to + count, :] = value


def unpack_y(g, buf, sign, fields, up, down, high):
    slots = y_slots(fields, sign)
    for side, ref in ((1, up), (-1, down)):
        for n, i in enumerate(moving(fields, sign, 1, side)):
            for to, r, count in slot_rows(g, slots, n):
                value = ref[to : to + count, :]
                for k in (0, g.halo) if side == 1 else (g.halo,):
                    buf[pl.ds(g.at(i, k, r), count), :] = value
    for n, (i, j) in enumerate(still_pairs(fields, sign)):
        for to, r, count in slot_rows(g, slots, 9 + n):
            before, after = up[to : to + count, :], down[to : to + count, :]
            mask = high[:count]
            buf[pl.ds(g.at(i, g.halo, r), count), :] = jnp.where(mask, before, after)
            if j is not None:
                buf[pl.ds(g.at(j, g.halo, r), count), :] = pltpu.roll(
                    jnp.where(mask, after, before), NZ, 1
                )
    for i in moving(fields, sign, 0, 1):
        for k in (0, g.halo) if velocity(i, sign)[1] == 1 else (g.halo,):
            buf[pl.ds(g.at(i, k, -1), 1), :] = buf[pl.ds(g.at(i, k, g.rows + 1), 1), :]
    for i in moving(fields, sign, 0, -1):
        for k in (0, g.halo) if velocity(i, sign)[1] == 1 else (g.halo,):
            buf[pl.ds(g.at(i, k, g.rows + 2), 1), :] = buf[pl.ds(g.at(i, k, 0), 1), :]


def by_parity(axis, first, second, act):
    even = lax.rem(lax.axis_index(axis), 2) == 0

    @pl.when(even)
    def _():
        act(first, second)

    @pl.when(jnp.logical_not(even))
    def _():
        act(second, first)


def load_fields(ref, rows, start, count, height):
    return [ref[pl.ds(start + n * rows, height), :] for n in range(count)]


def save_fields(ref, rows, start, values):
    for n, value in enumerate(values):
        ref[pl.ds(start + n * rows, value.shape[0]), :] = value


def save_populations(g, out, k, r, values):
    base = pl.multiple_of(k * g.panel + r, 8)
    for i, value in enumerate(values):
        out[pl.ds(base + g.field(i), value.shape[0]), :] = value


def over_tiles(g, panels, body, before=None, after=None):
    def column(k, carry):
        if before is not None:
            before(k)

        def tile(a, inner):
            r = pl.multiple_of(a * g.height, g.height)
            body(k, r, pl.multiple_of((k - 1) * g.rows + r, g.height))
            return inner

        lax.fori_loop(0, g.tiles, tile, 0)
        if after is not None:
            after(k)
        return carry

    lax.fori_loop(1, panels + 1, column, 0)


def over_extended(g, buf, out, sign, fields, masks, compute):
    small = lane_masks(8)

    def body(k, r, t):
        values = compute(pull_block(g, buf, sign, k, r, masks, fields), t)
        save_populations(g, out, k, r, values)

    over_tiles(g, g.halo, body)
    t = g.halo * g.rows
    values = compute(pull_block(g, buf, sign, g.halo, g.rows, small, fields), t)
    for i in range(27):
        dx = velocity(i, sign)[0]
        if dx == -1:
            out[pl.ds(g.at(i, g.halo, g.rows), 1), :] = values[i][0:1]
        elif dx == 1:
            out[pl.ds(g.at(i, g.halo, -1), 1), :] = values[i][1:2]
    for n, side in ((1, 1), (2, -1)):
        values = compute(pull_edge(g, buf, sign, side, small, fields), t + 8 * n)
        for i in moving(27, sign, 0, -side):
            row = g.rows if side == 1 else -1
            out[pl.ds(g.at(i, 1, row), g.cols, stride=g.panel), :] = values[i]
    for i in moving(27, sign, 1, 1):
        out[pl.ds(g.at(i, 0, 0), g.rows), :] = out[pl.ds(g.at(i, g.halo, 0), g.rows), :]
        for r in (-1, g.rows):
            out[pl.ds(g.at(i, 0, r), 1), :] = out[pl.ds(g.at(i, g.halo, r), 1), :]


def block_of(ref, k):
    return ref.at[:, :, pl.ds(pl.multiple_of((k - 1) * LANES, LANES), LANES)]


def first_kernel(g, pops, *refs):
    flat, (out, state, x_first, x_second, stage, *near), sems, flat_sems = refs[:3], refs[3:-2], *refs[-2:]
    porosity, solid, labels = near

    def copy(k):
        return pltpu.make_async_copy(block_of(pops, k), stage.at[k - 1], sems.at[k - 1])

    flat_copies = [
        pltpu.make_async_copy(source, target, flat_sems.at[n])
        for n, (source, target) in enumerate(zip(flat, near))
    ]
    copy(1).start()
    for each in flat_copies:
        each.start()
    for k in range(2, g.cols + 1):
        copy(k).start()
    for each in flat_copies:
        each.wait()

    def body(k, r, t):
        f = [stage[k - 1, i, pl.ds(r, g.height), :] for i in range(27)]
        spot = (pl.ds(r, g.height), pl.ds(pl.multiple_of((k - 1) * LANES, LANES), LANES))
        wall = solid[spot]
        label = labels[spot]
        damp = 1.0 / (1.0 + porosity[spot])
        push = jnp.where(label == 1, PUSH, jnp.where(label == 2, -PUSH, 0.0))
        rho, mx, my, mz = moments(f)
        inverse = 1.0 / rho
        flow = (rho, mx * inverse, my * inverse, mz * inverse, damp, push)
        extra = (damp, push, wall.astype(F32))
        save_fields(state, g.local, t, flow + extra[2:])
        save_populations(g, out, k, r, tuple(relax(f, *flow, wall == 1)) + extra)

    over_tiles(g, g.cols, body, before=lambda k: copy(k).wait())
    by_parity("gx", x_first, x_second, functools.partial(pack_x, g, out, 1, 30))


def relay_kernel(g, sign, fields, padded, x_first, x_second, buf, y_first, y_second):
    del padded
    high = lane_masks(8)[0]
    by_parity("gx", x_second, x_first, functools.partial(unpack_x, g, buf, sign, fields))
    by_parity(
        "gy",
        y_first,
        y_second,
        lambda up, down: pack_y(g, buf, sign, fields, up, down, high),
    )


def second_kernel(g, padded, y_first, y_second, buf, out, state):
    del padded
    masks = lane_masks(g.height)
    by_parity(
        "gy", y_second, y_first, lambda up, down: unpack_y(g, buf, 1, 30, up, down, lane_masks(8)[0])
    )

    def compute(values, t):
        f, (damp, push, wall) = values[:27], values[27:]
        rho, mx, my, mz = moments(f)
        inverse = 1.0 / rho
        flow = (rho, mx * inverse, my * inverse, mz * inverse, damp, push)
        save_fields(state, g.extended, t, flow + (wall,))
        return relax(f, *flow, wall > 0.5)

    over_extended(g, buf, out, 1, 30, masks, compute)


def third_kernel(g, buf, adjoint, final, out, x_first, x_second, stage_out, stage_in, *sems):
    sems_out, sems_in = sems
    masks = lane_masks(g.height)

    def copy_in(k):
        return pltpu.make_async_copy(block_of(adjoint, k), stage_in.at[k - 1], sems_in.at[k - 1])

    def copy_out(k):
        return pltpu.make_async_copy(stage_out.at[k - 1], block_of(final, k), sems_out.at[k - 1])

    for k in range(1, g.cols + 1):
        copy_in(k).start()

    def body(k, r, t):
        f = pull_block(g, buf, 1, k, r, masks)
        for i in range(27):
            stage_out[k - 1, i, pl.ds(r, g.height), :] = f[i]
        rho, mx, my, mz = moments(f)
        inverse = 1.0 / rho
        wx, wy, wz = mx * inverse, my * inverse, mz * inverse
        even = -(wx * wx + wy * wy + wz * wz) * inverse
        along = combos(wx * inverse, wy * inverse, wz * inverse)
        seeded = [stage_in[k - 1, i, pl.ds(r, g.height), :] + even for i in range(27)]
        for i in range(13):
            seeded[i] = seeded[i] + along[i]
            seeded[26 - i] = seeded[26 - i] - along[i]
        save_populations(g, out, k, r, seeded)

    over_tiles(
        g,
        g.cols,
        body,
        before=lambda k: copy_in(k).wait(),
        after=lambda k: copy_out(k).start(),
    )
    by_parity("gx", x_first, x_second, functools.partial(pack_x, g, out, -1, 27))
    for k in range(1, g.cols + 1):
        copy_out(k).wait()


def fourth_kernel(g, padded, state, y_first, y_second, buf, out, total):
    del padded
    masks = lane_masks(g.height)
    by_parity(
        "gy", y_second, y_first, lambda up, down: unpack_y(g, buf, -1, 27, up, down, lane_masks(8)[0])
    )

    def compute(p, t):
        *flow, wall = load_fields(state, g.extended, t, 7, p[0].shape[0])
        even, gx, gy, gz, porous = adjoint_scalars(p, *flow, wall > 0.5)
        save_fields(total, g.extended, t, [porous])
        return adjoint_spread(p, even, gx, gy, gz, wall > 0.5)

    over_extended(g, buf, out, -1, 27, masks, compute)


def fifth_kernel(g, buf, state, before, total, peak, parts):
    masks = lane_masks(g.height)
    peak[...] = jnp.zeros((8, LANES), F32)

    def body(k, r, t):
        p = pull_block(g, buf, -1, k, r, masks)
        *flow, wall = load_fields(state, g.local, t, 7, g.height)
        *spread, porous = adjoint_scalars(p, *flow, wall > 0.5)
        here = load_fields(before, g.extended, t, 1, g.height)[0] + porous
        save_fields(total, g.local, t, [here])
        save_fields(parts, g.local, t, spread + [wall])
        peak[...] = jnp.maximum(peak[...], jnp.max(jnp.abs(here).reshape(-1, 8, LANES), 0))

    over_tiles(g, g.cols, body)


def sixth_kernel(g, buf, parts, result, stage_out, sems_out):
    masks = lane_masks(g.height)

    def copy_out(k):
        return pltpu.make_async_copy(stage_out.at[k - 1], block_of(result, k), sems_out.at[k - 1])

    def body(k, r, t):
        p = pull_block(g, buf, -1, k, r, masks)
        *spread, wall = load_fields(parts, g.local, t, 5, g.height)
        for i, value in enumerate(adjoint_spread(p, *spread, wall > 0.5)):
            stage_out[k - 1, i, pl.ds(r, g.height), :] = value

    over_tiles(g, g.cols, body, after=lambda k: copy_out(k).start())
    for k in range(1, g.cols + 1):
        copy_out(k).wait()


def scale_kernel(g, total, peak, out):
    largest = jnp.max(peak[...])
    factor = 1.0 / (jnp.full((g.height, LANES), largest, F32) + EPS)
    for c in range(g.cols):
        for a in range(g.tiles):
            r = a * g.height
            value = load_fields(total, g.local, c * g.rows + r, 1, g.height)[0] * factor
            out[r : r + g.height, c * LANES : (c + 1) * LANES] = value


def swap_pairs(count, start):
    pairs = []
    for i in range(start, count, 2):
        j = (i + 1) % count
        pairs += [(i, j), (j, i)]
    return pairs


def swap(axis, count, first, second):
    return (
        lax.ppermute(first, axis, swap_pairs(count, 0)),
        lax.ppermute(second, axis, swap_pairs(count, 1)),
    )


def largest_of_all(peak, sizes):
    for axis, count, widths in (("gy", sizes[1], (2, 4, 4)), ("gx", sizes[0], (4, 2))):
        step = 1
        for width in widths:
            width = min(width, count // step)
            parts = [peak]
            for n in range(1, width):
                pairs = [(i, i ^ (n * step)) for i in range(count)]
                parts.append(lax.ppermute(peak, axis, pairs))
            peak = functools.reduce(jnp.maximum, parts)
            step *= width
    return peak


def on_device(sizes, populations, adjoint_in, porosity, solid, labels):
    rows, width = porosity.shape
    g = Grid(rows, width)
    in_vmem = pl.BlockSpec(memory_space=pltpu.VMEM)
    anywhere = pl.BlockSpec(memory_space=pl.ANY)
    hbm = pl.BlockSpec(memory_space=pltpu.HBM)
    nx, ny = sizes

    def vmem(*shape):
        return pltpu.VMEM(shape, F32)

    def fields(count, size):
        return vmem(count * size, LANES)

    def padded(count):
        return vmem(*g.padded(count))

    def x_parcels(count):
        return [vmem((count) * g.cols, LANES)] * 2

    def y_parcels(count, sign):
        slots = y_slots(count, sign)
        return [vmem(-(-slots * (rows + 2) // 8) * 8, LANES)] * 2

    whole = jax.ShapeDtypeStruct(populations.shape, F32)
    stage = pltpu.VMEM((g.cols, 27, rows, LANES), F32)
    sems = pltpu.SemaphoreType.DMA((g.cols,))

    def call(name, kernel, in_specs, out_shape, out_specs, scratch=(), aliases=None):
        return pl.pallas_call(
            functools.partial(kernel, g),
            in_specs=in_specs,
            out_shape=out_shape,
            out_specs=out_specs,
            scratch_shapes=list(scratch),
            input_output_aliases=aliases or {},
            compiler_params=pltpu.CompilerParams(vmem_limit_bytes=VMEM_LIMIT),
            name=name,
        )

    def pin(x):
        return pltpu.with_memory_space_constraint(x, pltpu.VMEM)

    def exchange(buf, parcels, sign, count):
        parcels = swap("gx", nx, *parcels)
        buf, *parcels = call(
            "relay",
            lambda grid, *refs: relay_kernel(grid, sign, count, *refs),
            [in_vmem] * 3,
            [padded(count)] + y_parcels(count, sign),
            [in_vmem] * 3,
            aliases={0: 0},
        )(pin(buf), *parcels)
        return buf, swap("gy", ny, *parcels)

    post, state0, *parcels = call(
        "collide_first",
        first_kernel,
        [hbm] * 4,
        [padded(30), fields(7, g.local)] + x_parcels(30),
        [in_vmem] * 4,
        [stage, vmem(*porosity.shape)]
        + [pltpu.VMEM(porosity.shape, jnp.int32)] * 2
        + [sems, pltpu.SemaphoreType.DMA((3,))],
    )(*(pltpu.with_memory_space_constraint(x, pltpu.HBM) for x in (populations, porosity, solid, labels)))
    post, parcels = exchange(post, parcels, 1, 30)

    _, post, state1 = call(
        "collide_second",
        second_kernel,
        [in_vmem] * 3,
        [padded(30), padded(27), fields(7, g.extended)],
        [in_vmem] * 3,
        aliases={0: 0},
    )(pin(post), *parcels)

    final, field, *parcels = call(
        "stream_and_seed",
        third_kernel,
        [in_vmem, anywhere],
        [whole, padded(27)] + x_parcels(27),
        [hbm] + [in_vmem] * 3,
        [stage, stage, sems, sems],
    )(pin(post), adjoint_in)
    field, parcels = exchange(field, parcels, -1, 27)

    _, field, total = call(
        "adjoint_second",
        fourth_kernel,
        [in_vmem] * 4,
        [padded(27), padded(27), fields(1, g.extended)],
        [in_vmem] * 3,
        aliases={0: 0},
    )(pin(field), pin(state1), *parcels)

    total, peak, parts = call(
        "adjoint_total",
        fifth_kernel,
        [in_vmem] * 3,
        [fields(1, g.local), vmem(8, LANES), fields(5, g.local)],
        [in_vmem] * 3,
    )(pin(field), pin(state0), pin(total))
    largest = largest_of_all(peak, sizes)

    adjoint_out = call(
        "adjoint_first",
        sixth_kernel,
        [in_vmem] * 2,
        whole,
        hbm,
        [stage, sems],
    )(pin(field), pin(parts))

    sensitivity = call(
        "normalize",
        scale_kernel,
        [in_vmem, in_vmem],
        jax.ShapeDtypeStruct(porosity.shape, F32),
        in_vmem,
    )(pin(total), largest)
    return final, adjoint_out, sensitivity


def solution(mesh):
    sizes = (mesh.shape["gx"], mesh.shape["gy"])
    whole, flat = P(None, "gx", "gy"), P("gx", "gy")
    return jax.shard_map(
        functools.partial(on_device, sizes),
        mesh=mesh,
        in_specs=(whole, whole, flat, flat, flat),
        out_specs=(whole, whole, flat),
        check_vma=False,
    )
```

```python
import functools

import jax
import jax.numpy as jnp
from jax import lax
from jax.experimental import pallas as pl
from jax.experimental.pallas import tpu as pltpu
from jax.sharding import PartitionSpec as P

NZ = 64
RELAX = 0.8
PUSH = 0.2
EPS = 1e-06
LANES = 128
VELOCITY = [(a, b, c) for a in (-1, 0, 1) for b in (-1, 0, 1) for c in (-1, 0, 1)]
INDEX = {v: i for i, v in enumerate(VELOCITY)}
WEIGHT = [
    [8.0 / 27, 2.0 / 27, 1.0 / 54, 1.0 / 216][abs(v[0]) + abs(v[1]) + abs(v[2])]
    for v in VELOCITY
]
NORM = [abs(v[0]) + abs(v[1]) + abs(v[2]) for v in VELOCITY]
F32 = jnp.float32
VMEM_LIMIT = 6 * 1024 * 1024
FLIGHT = 12 * 1024 * 1024


class Grid:
    def __init__(self, rows, width):
        self.rows = rows
        self.cols = width // LANES
        self.panel = rows + 16
        self.halo = self.cols + 1
        self.local = self.cols * rows
        self.extended = self.halo * rows + 24
        self.outer = ((0, 8), (rows - 8, 8))
        self.inner = tuple(((r, 16),) for r in range(8, rows - 8, 16))

    def at(self, i, k, r):
        return self.field(i) + k * self.panel + r

    def field(self, i):
        return i * (self.cols + 2) * self.panel + 8

    def padded(self, fields):
        return (fields * (self.cols + 2) * self.panel + 8, LANES)


def velocity(i, sign):
    return tuple(sign * n for n in VELOCITY[i]) if i < 27 else (0, 0, 0)


def moving(fields, sign, axis, side):
    return [i for i in range(fields) if velocity(i, sign)[axis] == side]


def lane_masks(height):
    lane = lax.broadcasted_iota(jnp.int32, (height, LANES), 1)
    return lane >= NZ, lane % NZ == 0, lane % NZ == NZ - 1


def shift_lanes(here, d, masks):
    first, last = masks[1:]
    dy, dz = d[1:]
    if dz == 0:
        return here if dy == 0 else pltpu.roll(here, NZ, 1)
    if dz == 1:
        one, other, edge = 1, NZ + 1, first
    else:
        one, other, edge = LANES - 1, NZ - 1, last
    inner, wrapped = (one, other) if dy == 0 else (other, one)
    return jnp.where(edge, pltpu.roll(here, wrapped, 1), pltpu.roll(here, inner, 1))


def pull(load, d, masks):
    high = masks[0]
    here = load(0)
    if d[1] == 1:
        here = jnp.where(high, load(-1), here)
    elif d[1] == -1:
        here = jnp.where(high, here, load(1))
    return shift_lanes(here, d, masks)


def stacked(parts):
    return parts[0] if len(parts) == 1 else jnp.concatenate(parts, 0)


def read_rows(ref, base, pieces):
    return stacked([ref[pl.ds(base + r, n), :] for r, n in pieces])


def write_rows(ref, base, pieces, value):
    done = 0
    for r, n in pieces:
        ref[pl.ds(base + r, n), :] = value[done : done + n]
        done += n


def pull_block(g, buf, sign, k, pieces, masks, fields=27):
    base = pl.multiple_of(k * g.panel, 8)
    after = pl.multiple_of(jnp.where(k == g.halo, g.panel, base + g.panel), 8)
    out = []
    for i in range(fields):
        d = velocity(i, sign)

        def load(n, i=i, d=d):
            start = {-1: base - g.panel, 0: base, 1: after}[n]
            return read_rows(buf, start + (g.field(i) - d[0]), pieces)

        out.append(pull(load, d, masks))
    return out


def pull_edge(g, buf, sign, side, masks, fields=27):
    out = []
    for i in range(fields):
        d = velocity(i, sign)
        if side == 1:
            row = g.rows - d[0]
        else:
            row = {1: g.rows, 0: g.rows + 1, -1: 0}[d[0]]

        def load(n, i=i, row=row):
            return buf[pl.ds(g.at(i, 1 + n, row), g.cols, stride=g.panel), :]

        out.append(pull(load, d, masks))
    return out


def moments(f):
    flat = {}
    along_z = None
    for a in (-1, 0, 1):
        for b in (-1, 0, 1):
            lo, mid, hi = (f[INDEX[(a, b, c)]] for c in (-1, 0, 1))
            flat[a, b] = lo + mid + hi
            diff = hi - lo
            along_z = diff if along_z is None else along_z + diff
    line = {}
    along_y = None
    for a in (-1, 0, 1):
        line[a] = flat[a, -1] + flat[a, 0] + flat[a, 1]
        diff = flat[a, 1] - flat[a, -1]
        along_y = diff if along_y is None else along_y + diff
    return line[-1] + line[0] + line[1], line[1] - line[-1], along_y, along_z


def combos(x, y, z):
    plane = {}
    for a in (-1, 0, 1):
        for b in (-1, 0, 1):
            if (a, b) > (0, 0):
                continue
            if a == 0:
                plane[a, b] = -y if b else None
            else:
                plane[a, b] = -x if b == 0 else (-x - y if b < 0 else y - x)
    out = []
    for a, b, c in VELOCITY[:13]:
        base = plane[a, b]
        if base is None:
            out.append(-z)
        else:
            out.append(base if c == 0 else (base - z if c < 0 else base + z))
    return out


def relax(f, rho, wx, wy, wz, damp, push, solid):
    ux, uy, uz = (wx + push) * damp, wy * damp, wz * damp
    base = 1.0 - 1.5 * (ux * ux + uy * uy + uz * uz)
    keep = 1.0 - 1.0 / RELAX
    gain = rho * (1.0 / RELAX)
    level = [gain * w for w in (8.0 / 27, 2.0 / 27, 1.0 / 54, 1.0 / 216)]
    along = combos(3.0 * ux, 3.0 * uy, 3.0 * uz)
    out = [None] * 27
    for i in range(13):
        j = 26 - i
        even = base + 0.5 * (along[i] * along[i])
        lift = level[NORM[i]]
        out[i] = jnp.where(solid, f[j], keep * f[i] + lift * (even + along[i]))
        out[j] = jnp.where(solid, f[i], keep * f[j] + lift * (even - along[i]))
    out[13] = jnp.where(solid, f[13], keep * f[13] + level[0] * base)
    return out


def pulled_moments(p):
    first = {}
    for a in (-1, 0, 1):
        for b in (-1, 0, 1):
            lo, mid, hi = (p[INDEX[(a, b, c)]] for c in (-1, 0, 1))
            both = lo + hi
            first[a, b] = (4.0 * mid + both, hi - lo, both)
    second = {}
    for a in (-1, 0, 1):
        lo, mid, hi = (first[a, b] for b in (-1, 0, 1))
        b0 = lo[0] + hi[0]
        b1 = lo[1] + hi[1]
        second[a] = dict(
            one=4.0 * mid[0] + b0,
            y=hi[0] - lo[0],
            yy=b0,
            z=4.0 * mid[1] + b1,
            yz=hi[1] - lo[1],
            zz=4.0 * mid[2] + lo[2] + hi[2],
        )
    lo, mid, hi = (second[a] for a in (-1, 0, 1))

    def full(key):
        return 4.0 * mid[key] + lo[key] + hi[key]

    xx = lo["one"] + hi["one"]
    return dict(
        one=4.0 * mid["one"] + xx,
        x=hi["one"] - lo["one"],
        xx=xx,
        y=full("y"),
        xy=hi["y"] - lo["y"],
        yy=full("yy"),
        z=full("z"),
        xz=hi["z"] - lo["z"],
        yz=full("yz"),
        zz=full("zz"),
    )


def adjoint_scalars(p, rho, wx, wy, wz, damp, push, solid):
    ux, uy, uz = (wx + push) * damp, wy * damp, wz * damp
    s = pulled_moments(p)
    scale = 1.0 / (216.0 * RELAX)
    one = s["one"] * scale
    b = [s[k] * (3.0 * scale) for k in ("x", "y", "z")]
    d = {k: s[k] * (9.0 * scale) for k in ("xx", "xy", "yy", "xz", "yz", "zz")}
    qx = d["xx"] * ux + d["xy"] * uy + d["xz"] * uz
    qy = d["xy"] * ux + d["yy"] * uy + d["yz"] * uz
    qz = d["xz"] * ux + d["yz"] * uy + d["zz"] * uz
    linear = b[0] * ux + b[1] * uy + b[2] * uz
    square = ux * ux + uy * uy + uz * uz
    even = one + linear + 0.5 * (qx * ux + qy * uy + qz * uz) - 1.5 * one * square
    three = 3.0 * one
    gx = (b[0] + qx - three * ux) * damp
    gy = (b[1] + qy - three * uy) * damp
    gz = (b[2] + qz - three * uz) * damp
    even = even - (gx * wx + gy * wy + gz * wz)
    porous = jnp.where(solid, 0.0, -rho * (gx * ux + gy * uy + gz * uz))
    return even, gx, gy, gz, porous


def adjoint_spread(p, even, gx, gy, gz, solid):
    keep = 1.0 - 1.0 / RELAX
    along = combos(gx, gy, gz)
    out = [None] * 27
    for i in range(13):
        j = 26 - i
        out[i] = jnp.where(solid, p[j], keep * p[i] + (even + along[i]))
        out[j] = jnp.where(solid, p[i], keep * p[j] + (even - along[i]))
    out[13] = jnp.where(solid, p[13], keep * p[13] + even)
    return out


def pack_x(g, buf, sign, fields, up, down):
    for side, ref in ((1, up), (-1, down)):
        edge, inner = (g.rows - 1, g.rows - 2) if side == 1 else (0, 1)
        lines = [(i, r) for i in moving(fields, sign, 0, side) for r in (edge, inner)]
        lines += [(i, edge) for i in moving(fields, sign, 0, 0)]
        for n, (i, r) in enumerate(lines):
            ref[n * g.cols : (n + 1) * g.cols, :] = buf[
                pl.ds(g.at(i, 1, r), g.cols, stride=g.panel), :
            ]


def unpack_x(g, buf, sign, fields, up, down):
    for side, ref in ((1, up), (-1, down)):
        lines = []
        for i in moving(fields, sign, 0, side):
            if side == 1:
                lines += [(i, (-1, g.rows + 1)), (i, (g.rows,))]
            else:
                lines += [(i, (g.rows,)), (i, (g.rows + 1,))]
        for i in moving(fields, sign, 0, 0):
            lines.append((i, (g.rows + 1 if side == 1 else g.rows,)))
        for n, (i, targets) in enumerate(lines):
            value = ref[n * g.cols : (n + 1) * g.cols, :]
            for r in targets:
                buf[pl.ds(g.at(i, 1, r), g.cols, stride=g.panel), :] = value
    for i in moving(fields, sign, 0, -1):
        buf[pl.ds(g.at(i, 1, g.rows + 2), g.cols, stride=g.panel), :] = buf[
            pl.ds(g.at(i, 1, 0), g.cols, stride=g.panel), :
        ]


def slot_rows(g, n, part):
    if part == "corner":
        return [(2 * n, g.rows, 2)]
    return [(n * g.rows + r, r, 8) for r in range(0, g.rows, 8)]


def still_pairs(fields, sign):
    still = moving(fields, sign, 1, 0)
    half = (len(still) + 1) // 2
    return [(still[n], still[n + half] if n + half < len(still) else None) for n in range(half)]


def y_slots(fields, sign):
    return 9 + len(still_pairs(fields, sign))


def pack_y(g, buf, sign, fields, part, high, up, down):
    for side, ref in ((1, up), (-1, down)):
        k = g.cols if side == 1 else 1
        for n, i in enumerate(moving(fields, sign, 1, side)):
            for to, r, count in slot_rows(g, n, part):
                ref[to : to + count, :] = buf[pl.ds(g.at(i, k, r), count), :]
        for n, (i, j) in enumerate(still_pairs(fields, sign)):
            for to, r, count in slot_rows(g, 9 + n, part):
                value = buf[pl.ds(g.at(i, k, r), count), :]
                if j is not None:
                    other = pltpu.roll(buf[pl.ds(g.at(j, k, r), count), :], NZ, 1)
                    pair = (value, other) if side == 1 else (other, value)
                    value = jnp.where(high[:count], *pair)
                ref[to : to + count, :] = value


def unpack_y(g, buf, sign, fields, part, high, up, down):
    for side, ref in ((1, up), (-1, down)):
        for n, i in enumerate(moving(fields, sign, 1, side)):
            for to, r, count in slot_rows(g, n, part):
                value = ref[to : to + count, :]
                for k in (0, g.halo) if side == 1 else (g.halo,):
                    buf[pl.ds(g.at(i, k, r), count), :] = value
    for n, (i, j) in enumerate(still_pairs(fields, sign)):
        for to, r, count in slot_rows(g, 9 + n, part):
            before, after = up[to : to + count, :], down[to : to + count, :]
            mask = high[:count]
            buf[pl.ds(g.at(i, g.halo, r), count), :] = jnp.where(mask, before, after)
            if j is not None:
                buf[pl.ds(g.at(j, g.halo, r), count), :] = pltpu.roll(
                    jnp.where(mask, after, before), NZ, 1
                )
    if part != "corner":
        return
    for i in moving(fields, sign, 0, 1):
        for k in (0, g.halo) if velocity(i, sign)[1] == 1 else (g.halo,):
            buf[pl.ds(g.at(i, k, -1), 1), :] = buf[pl.ds(g.at(i, k, g.rows + 1), 1), :]
    for i in moving(fields, sign, 0, -1):
        for k in (0, g.halo) if velocity(i, sign)[1] == 1 else (g.halo,):
            buf[pl.ds(g.at(i, k, g.rows + 2), 1), :] = buf[pl.ds(g.at(i, k, 0), 1), :]


def by_parity(axis, first, second, act):
    even = lax.rem(lax.axis_index(axis), 2) == 0

    @pl.when(even)
    def _():
        act(first, second)

    @pl.when(jnp.logical_not(even))
    def _():
        act(second, first)


def load_fields(ref, rows, base, pieces, count):
    return [read_rows(ref, base + n * rows, pieces) for n in range(count)]


def save_fields(ref, rows, base, pieces, values):
    for n, value in enumerate(values):
        write_rows(ref, base + n * rows, pieces, value)


def save_populations(g, out, k, pieces, values):
    base = pl.multiple_of(k * g.panel, 8)
    for i, value in enumerate(values):
        write_rows(out, base + g.field(i), pieces, value)


def spot_of(g, k):
    return pl.multiple_of((k - 1) * g.rows, 8)


def lanes_of(k):
    return pl.ds(pl.multiple_of((k - 1) * LANES, LANES), LANES)


def every(first, last, act):
    def step(k, carry):
        act(k)
        return carry

    lax.fori_loop(first, last + 1, step, 0)


def side_panels(g, act, count):
    def step(n, carry):
        act(jnp.where(n == 0, 1, g.cols - 1 + n))
        return carry

    lax.fori_loop(0, count, step, 0)


def interior_tiles(g, act):
    for pieces in g.inner:
        every(2, g.cols - 1, functools.partial(act, pieces=pieces))


def middle_tiles(g, act):
    every(2, g.cols - 1, functools.partial(act, pieces=g.outer))
    for pieces in g.inner:
        side_panels(g, functools.partial(act, pieces=pieces), 3)


def rim_tiles(g, act):
    every(1, g.cols, functools.partial(act, pieces=g.outer))
    for pieces in g.inner:
        side_panels(g, functools.partial(act, pieces=pieces), 2)


def step_tile(g, buf, out, sign, fields, masks, compute):
    def act(k, pieces):
        values = compute(
            pull_block(g, buf, sign, k, pieces, masks, fields), spot_of(g, k), pieces
        )
        save_populations(g, out, k, pieces, values)

    return act


def corner_tiles(g, buf, out, sign, fields, masks, compute):
    small = tuple(mask[:8] for mask in masks)
    act = step_tile(g, buf, out, sign, fields, masks, compute)
    side_panels(g, functools.partial(act, pieces=g.outer), 3)
    spot = g.halo * g.rows
    pieces = ((g.rows, 8),)
    values = compute(pull_block(g, buf, sign, g.halo, pieces, small, fields), spot, ((0, 8),))
    for i in range(27):
        dx = velocity(i, sign)[0]
        if dx == -1:
            out[pl.ds(g.at(i, g.halo, g.rows), 1), :] = values[i][0:1]
        elif dx == 1:
            out[pl.ds(g.at(i, g.halo, -1), 1), :] = values[i][1:2]
    edges = [pull_edge(g, buf, sign, side, small, fields) for side in (1, -1)]
    both = [stacked(pair) for pair in zip(*edges)]
    values = compute(both, spot, ((8, 16),))
    for i in moving(27, sign, 0, -1):
        out[pl.ds(g.at(i, 1, g.rows), g.cols, stride=g.panel), :] = values[i][:8]
    for i in moving(27, sign, 0, 1):
        out[pl.ds(g.at(i, 1, -1), g.cols, stride=g.panel), :] = values[i][8:]
    for i in moving(27, sign, 1, 1):
        out[pl.ds(g.at(i, 0, 0), g.rows), :] = out[pl.ds(g.at(i, g.halo, 0), g.rows), :]
        for r in (-1, g.rows):
            out[pl.ds(g.at(i, 0, r), 1), :] = out[pl.ds(g.at(i, g.halo, r), 1), :]


def flow_of(f):
    rho, mx, my, mz = moments(f)
    inverse = 1.0 / rho
    return inverse, rho, mx * inverse, my * inverse, mz * inverse


def collide_first(g, state, out):
    def act(k, pieces, f):
        base = pl.multiple_of(k * g.panel, 8)
        damp, push, wall = (read_rows(out, base + g.field(i), pieces) for i in (27, 28, 29))
        flow = flow_of(f)[1:] + (damp, push)
        save_fields(state, g.local, spot_of(g, k), pieces, flow + (wall,))
        save_populations(g, out, k, pieces, relax(f, *flow, wall > 0.5))

    return act


def collide_second(g, state):
    def compute(values, spot, pieces):
        f, (damp, push, wall) = values[:27], values[27:]
        flow = flow_of(f)[1:] + (damp, push)
        save_fields(state, g.extended, spot, pieces, flow + (wall,))
        return relax(f, *flow, wall > 0.5)

    return compute


def adjoint_second(g, state, total):
    def compute(p, spot, pieces):
        *flow, wall = load_fields(state, g.extended, spot, pieces, 7)
        *spread, porous = adjoint_scalars(p, *flow, wall > 0.5)
        save_fields(total, g.extended, spot, pieces, [porous])
        return adjoint_spread(p, *spread, wall > 0.5)

    return compute


def seed_tile(g, buf, adjoint, stage, out, masks):
    def act(k, pieces):
        f = pull_block(g, buf, 1, k, pieces, masks)
        for i in range(27):
            write_rows(stage.at[k - 1, i], 0, pieces, f[i])
        inverse, _, wx, wy, wz = flow_of(f)
        even = -(wx * wx + wy * wy + wz * wz) * inverse
        along = combos(wx * inverse, wy * inverse, wz * inverse)
        lanes = lanes_of(k)
        seeded = [
            stacked([adjoint[i, pl.ds(r, n), lanes] for r, n in pieces]) + even for i in range(27)
        ]
        for i in range(13):
            seeded[i] = seeded[i] + along[i]
            seeded[26 - i] = seeded[26 - i] - along[i]
        save_populations(g, out, k, pieces, seeded)

    return act


def block_of(ref, k):
    return ref.at[:, :, lanes_of(k)]


def pack_faces(g, buf, sign, fields, x_first, x_second, y_first, y_second):
    high = lane_masks(8)[0]
    by_parity("gx", x_first, x_second, functools.partial(pack_x, g, buf, sign, fields))
    by_parity(
        "gy", y_first, y_second, functools.partial(pack_y, g, buf, sign, fields, "face", high)
    )


def rim_first_kernel(g, pops, *refs):
    flat, (out, state, stage, *faces), near, (sems, flat_sems) = (
        refs[:3],
        refs[3:10],
        refs[10:13],
        refs[13:],
    )
    porosity, solid, labels = near

    def copy(k):
        return pltpu.make_async_copy(block_of(pops, k), stage.at[k - 1], sems.at[k - 1])

    flat_copies = [
        pltpu.make_async_copy(source, target, flat_sems.at[n])
        for n, (source, target) in enumerate(zip(flat, near))
    ]
    for each in flat_copies:
        each.start()
    for k in range(1, g.cols + 1):
        copy(k).start()
    for each in flat_copies:
        each.wait()

    def fields_of(k):
        lanes = lanes_of(k)
        label = labels[:, lanes]
        damp = 1.0 / (1.0 + porosity[:, lanes])
        push = jnp.where(label == 1, PUSH, jnp.where(label == 2, -PUSH, 0.0))
        base = pl.multiple_of(k * g.panel, 8)
        for i, value in ((27, damp), (28, push), (29, solid[:, lanes].astype(F32))):
            out[pl.ds(base + g.field(i), g.rows), :] = value

    every(1, g.cols, fields_of)
    collide = collide_first(g, state, out)

    def act(k, pieces):
        collide(k, pieces, [read_rows(stage.at[k - 1, i], 0, pieces) for i in range(27)])

    def column(k):
        copy(k).wait()
        act(k, g.outer)

    every(1, g.cols, column)
    for pieces in g.inner:
        side_panels(g, functools.partial(act, pieces=pieces), 2)
    pack_faces(g, out, 1, 30, *faces)


def inner_first_kernel(g, _, _state, stage, post, state0, out, state1):
    masks = lane_masks(16)
    collide = collide_first(g, state0, post)

    def act(k, pieces):
        collide(k, pieces, [read_rows(stage.at[k - 1, i], 0, pieces) for i in range(27)])

    interior_tiles(g, act)
    interior_tiles(g, step_tile(g, post, out, 1, 30, masks, collide_second(g, state1)))


def relay_kernel(g, sign, fields, _, x_first, x_second, y_first, y_second, buf, first, second):
    high = lane_masks(8)[0]
    by_parity("gx", x_second, x_first, functools.partial(unpack_x, g, buf, sign, fields))
    by_parity(
        "gy", y_second, y_first, functools.partial(unpack_y, g, buf, sign, fields, "face", high)
    )
    by_parity(
        "gy", first, second, functools.partial(pack_y, g, buf, sign, fields, "corner", high)
    )


def unpack_corners(g, buf, sign, fields, first, second):
    high = lane_masks(8)[0]
    by_parity(
        "gy", second, first, functools.partial(unpack_y, g, buf, sign, fields, "corner", high)
    )


def middle_second_kernel(g, post, _out, _state, out, state1):
    masks = lane_masks(16)
    middle_tiles(g, step_tile(g, post, out, 1, 30, masks, collide_second(g, state1)))


def rim_seed_kernel(g, _post, _out, _state, first, second, adjoint, *refs):
    post, out, state1, stage, field, *faces = refs
    masks = lane_masks(16)
    unpack_corners(g, post, 1, 30, first, second)
    corner_tiles(g, post, out, 1, 30, masks, collide_second(g, state1))
    rim_tiles(g, seed_tile(g, out, adjoint, stage, field, masks))
    pack_faces(g, field, -1, 27, *faces)


def inner_seed_kernel(
    g, post, _stage, _field, state1, adjoint, stage, field, out, total, final, sems
):
    masks = lane_masks(16)

    def copy(k):
        return pltpu.make_async_copy(stage.at[k - 1], block_of(final, k), sems.at[k - 1])

    copy(1).start()
    copy(g.cols).start()
    seed = seed_tile(g, post, adjoint, stage, field, masks)

    def column(k):
        for pieces in g.inner:
            seed(k, pieces)
        copy(k).start()

    every(2, g.cols - 1, column)
    interior_tiles(g, step_tile(g, field, out, -1, 27, masks, adjoint_second(g, state1, total)))
    every(1, g.cols, lambda k: copy(k).wait())


def middle_adjoint_kernel(g, field, _out, _total, state1, out, total):
    masks = lane_masks(16)
    middle_tiles(g, step_tile(g, field, out, -1, 27, masks, adjoint_second(g, state1, total)))


def total_kernel(g, _field, out, before, state1, state0, first, second, *refs):
    field, out, before, total, peak, parts = refs
    masks = lane_masks(16)
    unpack_corners(g, field, -1, 27, first, second)
    corner_tiles(g, field, out, -1, 27, masks, adjoint_second(g, state1, before))
    peak[...] = jnp.zeros((8, LANES), F32)

    def act(k, pieces):
        p = pull_block(g, out, -1, k, pieces, masks)
        spot = spot_of(g, k)
        *flow, wall = load_fields(state0, g.local, spot, pieces, 7)
        *spread, porous = adjoint_scalars(p, *flow, wall > 0.5)
        here = load_fields(before, g.extended, spot, pieces, 1)[0] + porous
        save_fields(total, g.local, spot, pieces, [here])
        save_fields(parts, g.local, spot, pieces, spread + [wall])
        largest = jnp.maximum(jnp.abs(here[:8]), jnp.abs(here[8:]))
        peak[...] = jnp.maximum(peak[...], largest)

    for pieces in (g.outer,) + g.inner:
        every(1, g.cols, functools.partial(act, pieces=pieces))


def adjoint_kernel(g, buf, parts, result, stage, sems):
    masks = lane_masks(16)

    def copy(k):
        return pltpu.make_async_copy(stage.at[k - 1], block_of(result, k), sems.at[k - 1])

    def column(k):
        for pieces in (g.outer,) + g.inner:
            p = pull_block(g, buf, -1, k, pieces, masks)
            *spread, wall = load_fields(parts, g.local, spot_of(g, k), pieces, 5)
            for i, value in enumerate(adjoint_spread(p, *spread, wall > 0.5)):
                write_rows(stage.at[k - 1, i], 0, pieces, value)
        copy(k).start()

    every(1, g.cols, column)
    every(1, g.cols, lambda k: copy(k).wait())


def scale_kernel(g, total, peak, out):
    largest = jnp.max(peak[...])
    factor = 1.0 / (jnp.full((g.rows, LANES), largest, F32) + EPS)
    for c in range(g.cols):
        value = total[c * g.rows : (c + 1) * g.rows, :] * factor
        out[:, c * LANES : (c + 1) * LANES] = value


def swap_pairs(count, start):
    pairs = []
    for i in range(start, count, 2):
        j = (i + 1) % count
        pairs += [(i, j), (j, i)]
    return pairs


def swap(axis, count, first, second):
    return (
        lax.ppermute(first, axis, swap_pairs(count, 0)),
        lax.ppermute(second, axis, swap_pairs(count, 1)),
    )


def largest_of_all(peak, sizes):
    for axis, count, widths in (("gy", sizes[1], (2, 4, 4)), ("gx", sizes[0], (4, 2))):
        step = 1
        for width in widths:
            width = min(width, count // step)
            parts = [peak]
            for n in range(1, width):
                pairs = [(i, i ^ (n * step)) for i in range(count)]
                parts.append(lax.ppermute(peak, axis, pairs))
            peak = functools.reduce(jnp.maximum, parts)
            step *= width
    return peak


def on_device(sizes, populations, adjoint_in, porosity, solid, labels):
    rows, width = porosity.shape
    g = Grid(rows, width)
    in_vmem = pl.BlockSpec(memory_space=pltpu.VMEM)
    in_hbm = pl.BlockSpec(memory_space=pltpu.HBM)
    nx, ny = sizes

    def vmem(*shape):
        return pltpu.VMEM(shape, F32)

    def fields(count, size):
        return vmem(count * size, LANES)

    def padded(count):
        return vmem(*g.padded(count))

    def faces(count, sign):
        along_x = vmem(count * g.cols, LANES)
        along_y = vmem(y_slots(count, sign) * rows, LANES)
        return [along_x, along_x, along_y, along_y]

    def corners(count, sign):
        return [vmem(-(-2 * y_slots(count, sign) // 8) * 8, LANES)] * 2

    whole = pltpu.HBM(populations.shape, F32)
    stage = vmem(g.cols, 27, rows, LANES)
    sems = pltpu.SemaphoreType.DMA((g.cols,))

    def call(name, kernel, operands, out_shape, scratch=(), kept=0, load=0):
        out_shape = [pltpu.VMEM(x.shape, x.dtype) for x in operands[:kept]] + out_shape
        hbm = [x is whole for x in out_shape]
        pinned = [
            pltpu.with_memory_space_constraint(x, pltpu.HBM if name == "rim_first" else pltpu.VMEM)
            for x in operands
        ]
        return pl.pallas_call(
            functools.partial(kernel, g),
            in_specs=[in_hbm if name == "rim_first" else in_vmem] * len(operands),
            out_shape=out_shape,
            out_specs=[in_hbm if there else in_vmem for there in hbm],
            scratch_shapes=list(scratch),
            input_output_aliases={n: n for n in range(kept)},
            compiler_params=pltpu.CompilerParams(vmem_limit_bytes=VMEM_LIMIT),
            cost_estimate=pl.CostEstimate(flops=0, bytes_accessed=load, transcendentals=0)
            if load
            else None,
            name=name,
        )(*pinned)

    def swap_faces(parcels):
        return swap("gx", nx, *parcels[:2]) + swap("gy", ny, *parcels[2:])

    def relay(buf, parcels, sign, count):
        def kernel(grid, *refs):
            relay_kernel(grid, sign, count, *refs)

        buf, *parcels = call("relay", kernel, [buf, *parcels], corners(count, sign), kept=1)
        return buf, swap("gy", ny, *parcels)

    post, state0, staged, *parcels = call(
        "rim_first",
        rim_first_kernel,
        [populations, porosity, solid, labels],
        [padded(30), fields(7, g.local), stage] + faces(30, 1),
        [vmem(*porosity.shape)]
        + [pltpu.VMEM(porosity.shape, jnp.int32)] * 2
        + [sems, pltpu.SemaphoreType.DMA((3,))],
    )
    parcels = swap_faces(parcels)
    post, state0, second, state1 = call(
        "inner_first",
        inner_first_kernel,
        [post, state0, staged],
        [padded(27), fields(7, g.extended)],
        kept=2,
        load=FLIGHT,
    )
    post, parcels = relay(post, parcels, 1, 30)
    second, state1 = call(
        "middle_second",
        lambda grid, out, state, buf, *refs: middle_second_kernel(grid, buf, out, state, *refs),
        [second, state1, post],
        [],
        kept=2,
        load=FLIGHT,
    )
    _, second, state1, staged, field, *parcels = call(
        "rim_seed",
        rim_seed_kernel,
        [post, second, state1, *parcels, adjoint_in],
        [stage, padded(27)] + faces(27, -1),
        kept=3,
    )
    parcels = swap_faces(parcels)
    _, field, pulled, total, final = call(
        "inner_seed",
        lambda grid, kept, into, buf, *refs: inner_seed_kernel(grid, buf, kept, into, *refs),
        [staged, field, second, state1, adjoint_in],
        [padded(27), fields(1, g.extended), whole],
        [sems],
        kept=2,
        load=FLIGHT,
    )
    field, parcels = relay(field, parcels, -1, 27)
    pulled, total = call(
        "middle_adjoint",
        lambda grid, out, sums, buf, *refs: middle_adjoint_kernel(grid, buf, out, sums, *refs),
        [pulled, total, field, state1],
        [],
        kept=2,
        load=FLIGHT,
    )
    _, pulled, _, total, peak, parts = call(
        "total",
        total_kernel,
        [field, pulled, total, state1, state0, *parcels],
        [fields(1, g.local), vmem(8, LANES), fields(5, g.local)],
        kept=3,
    )
    largest = largest_of_all(peak, sizes)
    (adjoint_out,) = call(
        "adjoint_first", adjoint_kernel, [pulled, parts], [whole], [stage, sems], load=FLIGHT
    )
    (sensitivity,) = call(
        "normalize",
        scale_kernel,
        [total, largest],
        [jax.ShapeDtypeStruct(porosity.shape, F32)],
    )
    return final, adjoint_out, sensitivity


def solution(mesh):
    sizes = (mesh.shape["gx"], mesh.shape["gy"])
    whole, flat = P(None, "gx", "gy"), P("gx", "gy")
    return jax.shard_map(
        functools.partial(on_device, sizes),
        mesh=mesh,
        in_specs=(whole, whole, flat, flat, flat),
        out_specs=(whole, whole, flat),
        check_vma=False,
    )
```

```python
import functools

import jax
import jax.numpy as jnp
from jax import lax
from jax.experimental import pallas as pl
from jax.experimental.pallas import tpu as pltpu
from jax.sharding import PartitionSpec as P

NZ = 64
RELAX = 0.8
PUSH = 0.2
EPS = 1e-06
LANES = 128
VELOCITY = [(a, b, c) for a in (-1, 0, 1) for b in (-1, 0, 1) for c in (-1, 0, 1)]
INDEX = {v: i for i, v in enumerate(VELOCITY)}
WEIGHT = [
    [8.0 / 27, 2.0 / 27, 1.0 / 54, 1.0 / 216][abs(v[0]) + abs(v[1]) + abs(v[2])]
    for v in VELOCITY
]
NORM = [abs(v[0]) + abs(v[1]) + abs(v[2]) for v in VELOCITY]
F32 = jnp.float32
VMEM_LIMIT = 6 * 1024 * 1024
FLIGHT = 12 * 1024 * 1024


class Grid:
    def __init__(self, rows, width):
        self.rows = rows
        self.cols = width // LANES
        self.panel = rows + 16
        self.halo = self.cols + 1
        self.local = self.cols * rows
        self.extended = self.halo * rows + 24
        self.outer = ((0, 8), (rows - 8, 8))
        self.inner = tuple(((r, 16),) for r in range(8, rows - 8, 16))

    def at(self, i, k, r):
        return self.field(i) + k * self.panel + r

    def field(self, i):
        return i * (self.cols + 2) * self.panel + 8

    def padded(self, fields):
        return (fields * (self.cols + 2) * self.panel + 8, LANES)


def velocity(i, sign):
    return tuple(sign * n for n in VELOCITY[i]) if i < 27 else (0, 0, 0)


def moving(fields, sign, axis, side):
    return [i for i in range(fields) if velocity(i, sign)[axis] == side]


def lane_masks(height):
    lane = lax.broadcasted_iota(jnp.int32, (height, LANES), 1)
    return lane >= NZ, lane % NZ == 0, lane % NZ == NZ - 1


def shift_lanes(here, d, masks):
    first, last = masks[1:]
    dy, dz = d[1:]
    if dz == 0:
        return here if dy == 0 else pltpu.roll(here, NZ, 1)
    if dz == 1:
        one, other, edge = 1, NZ + 1, first
    else:
        one, other, edge = LANES - 1, NZ - 1, last
    inner, wrapped = (one, other) if dy == 0 else (other, one)
    return jnp.where(edge, pltpu.roll(here, wrapped, 1), pltpu.roll(here, inner, 1))


def pull(load, d, masks):
    high = masks[0]
    here = load(0)
    if d[1] == 1:
        here = jnp.where(high, load(-1), here)
    elif d[1] == -1:
        here = jnp.where(high, here, load(1))
    return shift_lanes(here, d, masks)


def stacked(parts):
    return parts[0] if len(parts) == 1 else jnp.concatenate(parts, 0)


def read_rows(ref, base, pieces):
    return stacked([ref[pl.ds(base + r, n), :] for r, n in pieces])


def write_rows(ref, base, pieces, value):
    done = 0
    for r, n in pieces:
        ref[pl.ds(base + r, n), :] = value[done : done + n]
        done += n


def pull_block(g, buf, sign, k, pieces, masks, fields=27):
    base = pl.multiple_of(k * g.panel, 8)
    after = pl.multiple_of(jnp.where(k == g.halo, g.panel, base + g.panel), 8)
    out = []
    for i in range(fields):
        d = velocity(i, sign)

        def load(n, i=i, d=d):
            start = {-1: base - g.panel, 0: base, 1: after}[n]
            return read_rows(buf, start + (g.field(i) - d[0]), pieces)

        out.append(pull(load, d, masks))
    return out


def pull_edge(g, buf, sign, side, masks, fields=27):
    out = []
    for i in range(fields):
        d = velocity(i, sign)
        if side == 1:
            row = g.rows - d[0]
        else:
            row = {1: g.rows, 0: g.rows + 1, -1: 0}[d[0]]

        def load(n, i=i, row=row):
            return buf[pl.ds(g.at(i, 1 + n, row), g.cols, stride=g.panel), :]

        out.append(pull(load, d, masks))
    return out


def moments(f):
    flat = {}
    along_z = None
    for a in (-1, 0, 1):
        for b in (-1, 0, 1):
            lo, mid, hi = (f[INDEX[(a, b, c)]] for c in (-1, 0, 1))
            flat[a, b] = lo + mid + hi
            diff = hi - lo
            along_z = diff if along_z is None else along_z + diff
    line = {}
    along_y = None
    for a in (-1, 0, 1):
        line[a] = flat[a, -1] + flat[a, 0] + flat[a, 1]
        diff = flat[a, 1] - flat[a, -1]
        along_y = diff if along_y is None else along_y + diff
    return line[-1] + line[0] + line[1], line[1] - line[-1], along_y, along_z


def combos(x, y, z):
    plane = {}
    for a in (-1, 0, 1):
        for b in (-1, 0, 1):
            if (a, b) > (0, 0):
                continue
            if a == 0:
                plane[a, b] = -y if b else None
            else:
                plane[a, b] = -x if b == 0 else (-x - y if b < 0 else y - x)
    out = []
    for a, b, c in VELOCITY[:13]:
        base = plane[a, b]
        if base is None:
            out.append(-z)
        else:
            out.append(base if c == 0 else (base - z if c < 0 else base + z))
    return out


def relax(f, rho, wx, wy, wz, damp, push, solid):
    ux, uy, uz = (wx + push) * damp, wy * damp, wz * damp
    base = 1.0 - 1.5 * (ux * ux + uy * uy + uz * uz)
    keep = 1.0 - 1.0 / RELAX
    gain = rho * (1.0 / RELAX)
    level = [gain * w for w in (8.0 / 27, 2.0 / 27, 1.0 / 54, 1.0 / 216)]
    along = combos(3.0 * ux, 3.0 * uy, 3.0 * uz)
    out = [None] * 27
    for i in range(13):
        j = 26 - i
        even = base + 0.5 * (along[i] * along[i])
        lift = level[NORM[i]]
        out[i] = jnp.where(solid, f[j], keep * f[i] + lift * (even + along[i]))
        out[j] = jnp.where(solid, f[i], keep * f[j] + lift * (even - along[i]))
    out[13] = jnp.where(solid, f[13], keep * f[13] + level[0] * base)
    return out


def pulled_moments(p):
    first = {}
    for a in (-1, 0, 1):
        for b in (-1, 0, 1):
            lo, mid, hi = (p[INDEX[(a, b, c)]] for c in (-1, 0, 1))
            both = lo + hi
            first[a, b] = (4.0 * mid + both, hi - lo, both)
    second = {}
    for a in (-1, 0, 1):
        lo, mid, hi = (first[a, b] for b in (-1, 0, 1))
        b0 = lo[0] + hi[0]
        b1 = lo[1] + hi[1]
        second[a] = dict(
            one=4.0 * mid[0] + b0,
            y=hi[0] - lo[0],
            yy=b0,
            z=4.0 * mid[1] + b1,
            yz=hi[1] - lo[1],
            zz=4.0 * mid[2] + lo[2] + hi[2],
        )
    lo, mid, hi = (second[a] for a in (-1, 0, 1))

    def full(key):
        return 4.0 * mid[key] + lo[key] + hi[key]

    xx = lo["one"] + hi["one"]
    return dict(
        one=4.0 * mid["one"] + xx,
        x=hi["one"] - lo["one"],
        xx=xx,
        y=full("y"),
        xy=hi["y"] - lo["y"],
        yy=full("yy"),
        z=full("z"),
        xz=hi["z"] - lo["z"],
        yz=full("yz"),
        zz=full("zz"),
    )


def adjoint_scalars(p, rho, wx, wy, wz, damp, push, solid):
    ux, uy, uz = (wx + push) * damp, wy * damp, wz * damp
    s = pulled_moments(p)
    scale = 1.0 / (216.0 * RELAX)
    one = s["one"] * scale
    b = [s[k] * (3.0 * scale) for k in ("x", "y", "z")]
    d = {k: s[k] * (9.0 * scale) for k in ("xx", "xy", "yy", "xz", "yz", "zz")}
    qx = d["xx"] * ux + d["xy"] * uy + d["xz"] * uz
    qy = d["xy"] * ux + d["yy"] * uy + d["yz"] * uz
    qz = d["xz"] * ux + d["yz"] * uy + d["zz"] * uz
    linear = b[0] * ux + b[1] * uy + b[2] * uz
    square = ux * ux + uy * uy + uz * uz
    even = one + linear + 0.5 * (qx * ux + qy * uy + qz * uz) - 1.5 * one * square
    three = 3.0 * one
    gx = (b[0] + qx - three * ux) * damp
    gy = (b[1] + qy - three * uy) * damp
    gz = (b[2] + qz - three * uz) * damp
    even = even - (gx * wx + gy * wy + gz * wz)
    porous = jnp.where(solid, 0.0, -rho * (gx * ux + gy * uy + gz * uz))
    return even, gx, gy, gz, porous


def adjoint_spread(p, even, gx, gy, gz, solid):
    keep = 1.0 - 1.0 / RELAX
    along = combos(gx, gy, gz)
    out = [None] * 27
    for i in range(13):
        j = 26 - i
        out[i] = jnp.where(solid, p[j], keep * p[i] + (even + along[i]))
        out[j] = jnp.where(solid, p[i], keep * p[j] + (even - along[i]))
    out[13] = jnp.where(solid, p[13], keep * p[13] + even)
    return out


def x_lines(g, sign, fields, side):
    lines = []
    for i in moving(fields, sign, 0, side):
        if side == 1:
            lines.append((i, g.rows - 1, (-1, g.rows + 1)))
            lines.append((i, g.rows - 2, (g.rows,)))
        else:
            lines += [(i, 0, (g.rows,)), (i, 1, (g.rows + 1,))]
    edge, target = (g.rows - 1, g.rows + 1) if side == 1 else (0, g.rows)
    return lines + [(i, edge, (target,)) for i in moving(fields, sign, 0, 0)]


def pack_x(g, buf, sign, fields, up, down):
    for side, ref in ((1, up), (-1, down)):
        for n, (i, r, _) in enumerate(x_lines(g, sign, fields, side)):
            ref[n * g.cols : (n + 1) * g.cols, :] = buf[
                pl.ds(g.at(i, 1, r), g.cols, stride=g.panel), :
            ]


def unpack_x(g, buf, sign, fields, up, down):
    for side, ref in ((1, up), (-1, down)):
        for n, (i, _, targets) in enumerate(x_lines(g, sign, fields, side)):
            value = ref[n * g.cols : (n + 1) * g.cols, :]
            for r in targets:
                buf[pl.ds(g.at(i, 1, r), g.cols, stride=g.panel), :] = value
    for i in moving(fields, sign, 0, -1):
        buf[pl.ds(g.at(i, 1, g.rows + 2), g.cols, stride=g.panel), :] = buf[
            pl.ds(g.at(i, 1, 0), g.cols, stride=g.panel), :
        ]


def halo_panels(g, i, sign):
    return (0, g.halo) if velocity(i, sign)[1] == 1 else (g.halo,)


def pack_corners(g, buf, sign, fields, up, down):
    for side, ref in ((1, up), (-1, down)):
        for n, (i, r, _) in enumerate(x_lines(g, sign, fields, side)):
            ref[n : n + 1, :] = buf[pl.ds(g.at(i, g.halo, r), 1), :]


def unpack_corners(g, buf, sign, fields, up, down):
    for side, ref in ((1, up), (-1, down)):
        for n, (i, _, targets) in enumerate(x_lines(g, sign, fields, side)):
            value = ref[n : n + 1, :]
            for r in targets:
                for k in halo_panels(g, i, sign):
                    buf[pl.ds(g.at(i, k, r), 1), :] = value
    for i in moving(fields, sign, 0, -1):
        for k in halo_panels(g, i, sign):
            buf[pl.ds(g.at(i, k, g.rows + 2), 1), :] = buf[pl.ds(g.at(i, k, 0), 1), :]


def still_pairs(fields, sign):
    still = moving(fields, sign, 1, 0)
    half = (len(still) + 1) // 2
    return [(still[n], still[n + half] if n + half < len(still) else None) for n in range(half)]


def y_slots(fields, sign):
    return 9 + len(still_pairs(fields, sign))


def pack_y(g, buf, sign, fields, high, up, down):
    for side, ref in ((1, up), (-1, down)):
        k = g.cols if side == 1 else 1
        for n, i in enumerate(moving(fields, sign, 1, side)):
            ref[n * g.rows : (n + 1) * g.rows, :] = buf[pl.ds(g.at(i, k, 0), g.rows), :]
        for n, (i, j) in enumerate(still_pairs(fields, sign)):
            value = buf[pl.ds(g.at(i, k, 0), g.rows), :]
            if j is not None:
                other = pltpu.roll(buf[pl.ds(g.at(j, k, 0), g.rows), :], NZ, 1)
                pair = (value, other) if side == 1 else (other, value)
                value = jnp.where(high, *pair)
            ref[(9 + n) * g.rows : (10 + n) * g.rows, :] = value


def unpack_y(g, buf, sign, fields, high, up, down):
    for side, ref in ((1, up), (-1, down)):
        for n, i in enumerate(moving(fields, sign, 1, side)):
            value = ref[n * g.rows : (n + 1) * g.rows, :]
            for k in halo_panels(g, i, sign):
                buf[pl.ds(g.at(i, k, 0), g.rows), :] = value
    for n, (i, j) in enumerate(still_pairs(fields, sign)):
        spot = slice((9 + n) * g.rows, (10 + n) * g.rows)
        before, after = up[spot, :], down[spot, :]
        buf[pl.ds(g.at(i, g.halo, 0), g.rows), :] = jnp.where(high, before, after)
        if j is not None:
            value = pltpu.roll(jnp.where(high, after, before), NZ, 1)
            buf[pl.ds(g.at(j, g.halo, 0), g.rows), :] = value


def by_parity(axis, first, second, act):
    even = lax.rem(lax.axis_index(axis), 2) == 0

    @pl.when(even)
    def _():
        act(first, second)

    @pl.when(jnp.logical_not(even))
    def _():
        act(second, first)


def load_fields(ref, rows, base, pieces, count):
    return [read_rows(ref, base + n * rows, pieces) for n in range(count)]


def save_fields(ref, rows, base, pieces, values):
    for n, value in enumerate(values):
        write_rows(ref, base + n * rows, pieces, value)


def save_populations(g, out, k, pieces, values):
    base = pl.multiple_of(k * g.panel, 8)
    for i, value in enumerate(values):
        write_rows(out, base + g.field(i), pieces, value)


def spot_of(g, k):
    return pl.multiple_of((k - 1) * g.rows, 8)


def lanes_of(k):
    return pl.ds(pl.multiple_of((k - 1) * LANES, LANES), LANES)


def every(first, last, act):
    def step(k, carry):
        act(k)
        return carry

    lax.fori_loop(first, last + 1, step, 0)


def side_panels(g, act, count):
    def step(n, carry):
        act(jnp.where(n == 0, 1, g.cols - 1 + n))
        return carry

    lax.fori_loop(0, count, step, 0)


def interior_tiles(g, act):
    for pieces in g.inner:
        every(2, g.cols - 1, functools.partial(act, pieces=pieces))


def middle_tiles(g, act):
    for pieces in g.inner:
        side_panels(g, functools.partial(act, pieces=pieces), 3)
    every(2, g.cols - 1, functools.partial(act, pieces=g.outer))


def rim_tiles(g, act):
    every(1, g.cols, functools.partial(act, pieces=g.outer))
    for pieces in g.inner:
        side_panels(g, functools.partial(act, pieces=pieces), 2)


def step_tile(g, buf, out, sign, fields, masks, compute):
    def act(k, pieces):
        values = compute(
            pull_block(g, buf, sign, k, pieces, masks, fields), spot_of(g, k), pieces
        )
        save_populations(g, out, k, pieces, values)

    return act


def corner_tiles(g, buf, out, sign, fields, masks, compute):
    small = tuple(mask[:8] for mask in masks)
    act = step_tile(g, buf, out, sign, fields, masks, compute)
    side_panels(g, functools.partial(act, pieces=g.outer), 3)
    spot = g.halo * g.rows
    pieces = ((g.rows, 8),)
    values = compute(pull_block(g, buf, sign, g.halo, pieces, small, fields), spot, ((0, 8),))
    for i in range(27):
        dx = velocity(i, sign)[0]
        if dx == -1:
            out[pl.ds(g.at(i, g.halo, g.rows), 1), :] = values[i][0:1]
        elif dx == 1:
            out[pl.ds(g.at(i, g.halo, -1), 1), :] = values[i][1:2]
    edges = [pull_edge(g, buf, sign, side, small, fields) for side in (1, -1)]
    both = [stacked(pair) for pair in zip(*edges)]
    values = compute(both, spot, ((8, 16),))
    for i in moving(27, sign, 0, -1):
        out[pl.ds(g.at(i, 1, g.rows), g.cols, stride=g.panel), :] = values[i][:8]
    for i in moving(27, sign, 0, 1):
        out[pl.ds(g.at(i, 1, -1), g.cols, stride=g.panel), :] = values[i][8:]
    for i in moving(27, sign, 1, 1):
        out[pl.ds(g.at(i, 0, 0), g.rows), :] = out[pl.ds(g.at(i, g.halo, 0), g.rows), :]
        for r in (-1, g.rows):
            out[pl.ds(g.at(i, 0, r), 1), :] = out[pl.ds(g.at(i, g.halo, r), 1), :]


def flow_of(f):
    rho, mx, my, mz = moments(f)
    inverse = 1.0 / rho
    return inverse, rho, mx * inverse, my * inverse, mz * inverse


def collide_first(g, state, out):
    def act(k, pieces, f):
        base = pl.multiple_of(k * g.panel, 8)
        damp, push, wall = (read_rows(out, base + g.field(i), pieces) for i in (27, 28, 29))
        flow = flow_of(f)[1:] + (damp, push)
        save_fields(state, g.local, spot_of(g, k), pieces, flow + (wall,))
        save_populations(g, out, k, pieces, relax(f, *flow, wall > 0.5))

    return act


def collide_second(g, state):
    def compute(values, spot, pieces):
        f, (damp, push, wall) = values[:27], values[27:]
        flow = flow_of(f)[1:] + (damp, push)
        save_fields(state, g.extended, spot, pieces, flow + (wall,))
        return relax(f, *flow, wall > 0.5)

    return compute


def adjoint_second(g, state, total):
    def compute(p, spot, pieces):
        *flow, wall = load_fields(state, g.extended, spot, pieces, 7)
        *spread, porous = adjoint_scalars(p, *flow, wall > 0.5)
        save_fields(total, g.extended, spot, pieces, [porous])
        return adjoint_spread(p, *spread, wall > 0.5)

    return compute


def seed_tile(g, buf, adjoint, stage, out, masks):
    def act(k, pieces):
        f = pull_block(g, buf, 1, k, pieces, masks)
        for i in range(27):
            write_rows(stage.at[k - 1, i], 0, pieces, f[i])
        inverse, _, wx, wy, wz = flow_of(f)
        even = -(wx * wx + wy * wy + wz * wz) * inverse
        along = combos(wx * inverse, wy * inverse, wz * inverse)
        lanes = lanes_of(k)
        seeded = [
            stacked([adjoint[i, pl.ds(r, n), lanes] for r, n in pieces]) + even for i in range(27)
        ]
        for i in range(13):
            seeded[i] = seeded[i] + along[i]
            seeded[26 - i] = seeded[26 - i] - along[i]
        save_populations(g, out, k, pieces, seeded)

    return act


def block_of(ref, k):
    return ref.at[:, :, lanes_of(k)]


def pack_faces(g, buf, sign, fields, x_first, x_second, y_first, y_second):
    high = lane_masks(g.rows)[0]
    by_parity("gx", x_first, x_second, functools.partial(pack_x, g, buf, sign, fields))
    by_parity("gy", y_first, y_second, functools.partial(pack_y, g, buf, sign, fields, high))


def rim_first_kernel(g, pops, *refs):
    flat, (out, state, stage, *faces), near, (sems, flat_sems) = (
        refs[:3],
        refs[3:10],
        refs[10:13],
        refs[13:],
    )
    porosity, solid, labels = near

    def copy(k):
        return pltpu.make_async_copy(block_of(pops, k), stage.at[k - 1], sems.at[k - 1])

    flat_copies = [
        pltpu.make_async_copy(source, target, flat_sems.at[n])
        for n, (source, target) in enumerate(zip(flat, near))
    ]
    for each in flat_copies:
        each.start()
    for k in range(1, g.cols + 1):
        copy(k).start()
    for each in flat_copies:
        each.wait()

    def fields_of(k):
        lanes = lanes_of(k)
        label = labels[:, lanes]
        damp = 1.0 / (1.0 + porosity[:, lanes])
        push = jnp.where(label == 1, PUSH, jnp.where(label == 2, -PUSH, 0.0))
        base = pl.multiple_of(k * g.panel, 8)
        for i, value in ((27, damp), (28, push), (29, solid[:, lanes].astype(F32))):
            out[pl.ds(base + g.field(i), g.rows), :] = value

    every(1, g.cols, fields_of)
    collide = collide_first(g, state, out)

    def act(k, pieces):
        collide(k, pieces, [read_rows(stage.at[k - 1, i], 0, pieces) for i in range(27)])

    def column(k):
        copy(k).wait()
        act(k, g.outer)

    every(1, g.cols, column)
    for pieces in g.inner:
        side_panels(g, functools.partial(act, pieces=pieces), 2)
    pack_faces(g, out, 1, 30, *faces)


def inner_first_kernel(g, _, _state, stage, post, state0, out, state1):
    masks = lane_masks(16)
    collide = collide_first(g, state0, post)

    def act(k, pieces):
        collide(k, pieces, [read_rows(stage.at[k - 1, i], 0, pieces) for i in range(27)])

    interior_tiles(g, act)
    interior_tiles(g, step_tile(g, post, out, 1, 30, masks, collide_second(g, state1)))


def relay_kernel(g, sign, fields, _, y_second, y_first, buf, first, second):
    high = lane_masks(g.rows)[0]
    by_parity("gy", y_second, y_first, functools.partial(unpack_y, g, buf, sign, fields, high))
    by_parity("gx", first, second, functools.partial(pack_corners, g, buf, sign, fields))


def middle_second_kernel(g, post, out, state1, x_second, x_first):
    masks = lane_masks(16)
    by_parity("gx", x_second, x_first, functools.partial(unpack_x, g, post, 1, 30))
    middle_tiles(g, step_tile(g, post, out, 1, 30, masks, collide_second(g, state1)))


def rim_seed_kernel(g, _post, _out, _state, first, second, adjoint, *refs):
    post, out, state1, stage, field, *faces = refs
    masks = lane_masks(16)
    by_parity("gx", second, first, functools.partial(unpack_corners, g, post, 1, 30))
    corner_tiles(g, post, out, 1, 30, masks, collide_second(g, state1))
    rim_tiles(g, seed_tile(g, out, adjoint, stage, field, masks))
    pack_faces(g, field, -1, 27, *faces)


def inner_seed_kernel(
    g, post, _stage, _field, state1, adjoint, stage, field, out, total, final, sems
):
    masks = lane_masks(16)

    def copy(k):
        return pltpu.make_async_copy(stage.at[k - 1], block_of(final, k), sems.at[k - 1])

    copy(1).start()
    copy(g.cols).start()
    seed = seed_tile(g, post, adjoint, stage, field, masks)

    def column(k):
        for pieces in g.inner:
            seed(k, pieces)
        copy(k).start()

    every(2, g.cols - 1, column)
    interior_tiles(g, step_tile(g, field, out, -1, 27, masks, adjoint_second(g, state1, total)))
    every(1, g.cols, lambda k: copy(k).wait())


def middle_adjoint_kernel(g, field, out, total, state1, x_second, x_first):
    masks = lane_masks(16)
    by_parity("gx", x_second, x_first, functools.partial(unpack_x, g, field, -1, 27))
    middle_tiles(g, step_tile(g, field, out, -1, 27, masks, adjoint_second(g, state1, total)))


def total_kernel(g, _field, out, before, state1, state0, first, second, *refs):
    field, out, before, total, peak, parts = refs
    masks = lane_masks(16)
    by_parity("gx", second, first, functools.partial(unpack_corners, g, field, -1, 27))
    corner_tiles(g, field, out, -1, 27, masks, adjoint_second(g, state1, before))
    peak[...] = jnp.zeros((8, LANES), F32)

    def act(k, pieces):
        p = pull_block(g, out, -1, k, pieces, masks)
        spot = spot_of(g, k)
        *flow, wall = load_fields(state0, g.local, spot, pieces, 7)
        *spread, porous = adjoint_scalars(p, *flow, wall > 0.5)
        here = load_fields(before, g.extended, spot, pieces, 1)[0] + porous
        save_fields(total, g.local, spot, pieces, [here])
        save_fields(parts, g.local, spot, pieces, spread + [wall])
        largest = jnp.maximum(jnp.abs(here[:8]), jnp.abs(here[8:]))
        peak[...] = jnp.maximum(peak[...], largest)

    for pieces in (g.outer,) + g.inner:
        every(1, g.cols, functools.partial(act, pieces=pieces))


def adjoint_kernel(g, first, last, buf, parts, result, stage, sems):
    masks = lane_masks(16)

    def copy(k):
        return pltpu.make_async_copy(stage.at[k - first], block_of(result, k), sems.at[k - first])

    def column(k):
        for pieces in (g.outer,) + g.inner:
            p = pull_block(g, buf, -1, k, pieces, masks)
            *spread, wall = load_fields(parts, g.local, spot_of(g, k), pieces, 5)
            for i, value in enumerate(adjoint_spread(p, *spread, wall > 0.5)):
                write_rows(stage.at[k - first, i], 0, pieces, value)
        copy(k).start()

    every(first, last, column)
    every(first, last, lambda k: copy(k).wait())


def scale_kernel(g, total, peak, out):
    largest = jnp.max(peak[...])
    factor = 1.0 / (jnp.full((g.rows, LANES), largest, F32) + EPS)
    for c in range(g.cols):
        value = total[c * g.rows : (c + 1) * g.rows, :] * factor
        out[:, c * LANES : (c + 1) * LANES] = value


def swap_pairs(count, start):
    pairs = []
    for i in range(start, count, 2):
        j = (i + 1) % count
        pairs += [(i, j), (j, i)]
    return pairs


def swap(axis, count, first, second):
    return (
        lax.ppermute(first, axis, swap_pairs(count, 0)),
        lax.ppermute(second, axis, swap_pairs(count, 1)),
    )


def largest_of_all(peak, sizes, beside):
    groups = 0
    for axis, count, widths in (("gy", sizes[1], (2, 4, 4)), ("gx", sizes[0], (4, 2))):
        step = 1
        for width in widths:
            width = min(width, count // step)
            parts = [
                lax.ppermute(peak, axis, [(i, i ^ (n * step)) for i in range(count)])
                for n in range(1, width)
            ]
            groups += 1
            if groups == 2:
                peak = beside(peak)
            peak = functools.reduce(jnp.maximum, parts, peak)
            step *= width
    return peak


def on_device(sizes, populations, adjoint_in, porosity, solid, labels):
    rows, width = porosity.shape
    g = Grid(rows, width)
    in_vmem = pl.BlockSpec(memory_space=pltpu.VMEM)
    in_hbm = pl.BlockSpec(memory_space=pltpu.HBM)
    nx, ny = sizes

    def vmem(*shape):
        return pltpu.VMEM(shape, F32)

    def fields(count, size):
        return vmem(count * size, LANES)

    def padded(count):
        return vmem(*g.padded(count))

    def faces(count, sign):
        along_x = vmem(count * g.cols, LANES)
        along_y = vmem(y_slots(count, sign) * rows, LANES)
        return [along_x, along_x, along_y, along_y]

    def corners(count):
        return [vmem(-(-count // 8) * 8, LANES)] * 2

    whole = pltpu.HBM(populations.shape, F32)
    stage = vmem(g.cols, 27, rows, LANES)
    sems = pltpu.SemaphoreType.DMA((g.cols,))

    def call(name, kernel, operands, out_shape, scratch=(), kept=0, load=0, result=None):
        out_shape = [pltpu.VMEM(x.shape, x.dtype) for x in operands[:kept]] + out_shape
        aliases = {n: n for n in range(kept)}
        space = pltpu.HBM if name == "rim_first" else pltpu.VMEM
        pinned = [pltpu.with_memory_space_constraint(x, space) for x in operands]
        in_specs = [pl.BlockSpec(memory_space=space)] * len(operands)
        if result is not None:
            aliases[len(operands)] = len(out_shape) - 1
            pinned.append(pltpu.with_memory_space_constraint(result, pltpu.HBM))
            in_specs.append(in_hbm)
        return pl.pallas_call(
            functools.partial(kernel, g),
            in_specs=in_specs,
            out_shape=out_shape,
            out_specs=[in_hbm if x is whole else in_vmem for x in out_shape],
            scratch_shapes=list(scratch),
            input_output_aliases=aliases,
            compiler_params=pltpu.CompilerParams(vmem_limit_bytes=VMEM_LIMIT),
            cost_estimate=pl.CostEstimate(flops=0, bytes_accessed=load, transcendentals=0)
            if load
            else None,
            name=name,
        )(*pinned)

    def swap_faces(parcels):
        x_first, x_second = swap("gx", nx, *parcels[:2])
        y_first, y_second = swap("gy", ny, *parcels[2:])
        return [x_second, x_first], [y_second, y_first]

    def relay(buf, parcels, sign, count):
        def kernel(grid, *refs):
            relay_kernel(grid, sign, count, *refs)

        buf, *parcels = call("relay", kernel, [buf, *parcels], corners(count), kept=1)
        return buf, swap("gx", nx, *parcels)

    post, state0, staged, *parcels = call(
        "rim_first",
        rim_first_kernel,
        [populations, porosity, solid, labels],
        [padded(30), fields(7, g.local), stage] + faces(30, 1),
        [vmem(*porosity.shape)]
        + [pltpu.VMEM(porosity.shape, jnp.int32)] * 2
        + [sems, pltpu.SemaphoreType.DMA((3,))],
    )
    along_x, along_y = swap_faces(parcels)
    post, state0, second, state1 = call(
        "inner_first",
        inner_first_kernel,
        [post, state0, staged],
        [padded(27), fields(7, g.extended)],
        kept=2,
        load=FLIGHT,
    )
    post, parcels = relay(post, along_y, 1, 30)
    post, second, state1 = call(
        "middle_second",
        lambda grid, _post, _out, _state, b, a, *refs: middle_second_kernel(grid, *refs, b, a),
        [post, second, state1, *along_x],
        [],
        kept=3,
        load=FLIGHT,
    )
    _, second, state1, staged, field, *parcels = call(
        "rim_seed",
        rim_seed_kernel,
        [post, second, state1, *parcels, adjoint_in],
        [stage, padded(27)] + faces(27, -1),
        kept=3,
    )
    along_x, along_y = swap_faces(parcels)
    _, field, pulled, total, final = call(
        "inner_seed",
        lambda grid, kept, into, buf, *refs: inner_seed_kernel(grid, buf, kept, into, *refs),
        [staged, field, second, state1, adjoint_in],
        [padded(27), fields(1, g.extended), whole],
        [sems],
        kept=2,
        load=FLIGHT,
    )
    field, parcels = relay(field, along_y, -1, 27)
    field, pulled, total = call(
        "middle_adjoint",
        lambda grid, _field, _out, _total, state, b, a, *refs: middle_adjoint_kernel(
            grid, *refs, state, b, a
        ),
        [field, pulled, total, state1, *along_x],
        [],
        kept=3,
        load=FLIGHT,
    )
    _, pulled, _, total, peak, parts = call(
        "total",
        total_kernel,
        [field, pulled, total, state1, state0, *parcels],
        [fields(1, g.local), vmem(8, LANES), fields(5, g.local)],
        kept=3,
    )
    half = g.cols // 2
    scratch = [vmem(half, 27, rows, LANES), pltpu.SemaphoreType.DMA((half,))]
    halves = []

    def first_half(peak):
        def kernel(grid, buf, fields, near, echo, *refs):
            echo[...] = near[...]
            adjoint_kernel(grid, 1, half, buf, fields, *refs)

        echo, result = call(
            "adjoint_low",
            kernel,
            [pulled, parts, peak],
            [vmem(8, LANES), whole],
            scratch,
            load=FLIGHT // 2,
        )
        halves.append(result)
        return echo

    largest = largest_of_all(peak, sizes, first_half)
    (adjoint_out,) = call(
        "adjoint_high",
        lambda grid, buf, fields, _, *refs: adjoint_kernel(
            grid, 1 + half, g.cols, buf, fields, *refs
        ),
        [pulled, parts],
        [whole],
        scratch,
        load=FLIGHT // 2,
        result=halves[0],
    )
    (sensitivity,) = call(
        "normalize",
        scale_kernel,
        [total, largest],
        [jax.ShapeDtypeStruct(porosity.shape, F32)],
    )
    return final, adjoint_out, sensitivity


def solution(mesh):
    sizes = (mesh.shape["gx"], mesh.shape["gy"])
    whole, flat = P(None, "gx", "gy"), P("gx", "gy")
    return jax.shard_map(
        functools.partial(on_device, sizes),
        mesh=mesh,
        in_specs=(whole, whole, flat, flat, flat),
        out_specs=(whole, whole, flat),
        check_vma=False,
    )
```

```python
import functools

import jax
import jax.numpy as jnp
from jax import lax
from jax.experimental import pallas as pl
from jax.experimental.pallas import tpu as pltpu
from jax.sharding import PartitionSpec as P

NZ = 64
RELAX = 0.8
PUSH = 0.2
EPS = 1e-06
LANES = 128
VELOCITY = [(a, b, c) for a in (-1, 0, 1) for b in (-1, 0, 1) for c in (-1, 0, 1)]
INDEX = {v: i for i, v in enumerate(VELOCITY)}
WEIGHT = [
    [8.0 / 27, 2.0 / 27, 1.0 / 54, 1.0 / 216][abs(v[0]) + abs(v[1]) + abs(v[2])]
    for v in VELOCITY
]
NORM = [abs(v[0]) + abs(v[1]) + abs(v[2]) for v in VELOCITY]
F32 = jnp.float32
VMEM_LIMIT = 6 * 1024 * 1024
FLIGHT = 12 * 1024 * 1024


class Grid:
    def __init__(self, rows, width):
        self.rows = rows
        self.cols = width // LANES
        self.panel = rows + 16
        self.halo = self.cols + 1
        self.local = self.cols * rows
        self.extended = self.halo * rows + 24
        self.outer = ((0, 8), (rows - 8, 8))
        self.inner = tuple(((r, 16),) for r in range(8, rows - 8, 16))

    def at(self, i, k, r):
        return self.field(i) + k * self.panel + r

    def field(self, i):
        return i * (self.cols + 2) * self.panel + 8

    def padded(self, fields):
        return (fields * (self.cols + 2) * self.panel + 8, LANES)


def velocity(i, sign):
    return tuple(sign * n for n in VELOCITY[i]) if i < 27 else (0, 0, 0)


def moving(fields, sign, axis, side):
    return [i for i in range(fields) if velocity(i, sign)[axis] == side]


def lane_masks(height):
    lane = lax.broadcasted_iota(jnp.int32, (height, LANES), 1)
    level = lane % NZ
    below = jnp.where(level == 0, lane + (NZ - 1), lane - 1)
    above = jnp.where(level == NZ - 1, lane - (NZ - 1), lane + 1)
    other = lane ^ NZ
    return lane >= NZ, below, above, below ^ NZ, above ^ NZ, other


def shift_lanes(here, d, masks):
    dy, dz = d[1:]
    if dz == 0:
        return here if dy == 0 else pltpu.roll(here, NZ, 1)
    source = masks[(1 if dz == 1 else 2) + (0 if dy == 0 else 2)]
    return jnp.take_along_axis(here, source, axis=1, mode="promise_in_bounds")


def pull(load, d, masks):
    high = masks[0]
    here = load(0)
    if d[1] == 1:
        here = jnp.where(high, load(-1), here)
    elif d[1] == -1:
        here = jnp.where(high, here, load(1))
    return shift_lanes(here, d, masks)


def stacked(parts):
    return parts[0] if len(parts) == 1 else jnp.concatenate(parts, 0)


def read_rows(ref, base, pieces):
    return stacked([ref[pl.ds(base + r, n), :] for r, n in pieces])


def write_rows(ref, base, pieces, value):
    done = 0
    for r, n in pieces:
        ref[pl.ds(base + r, n), :] = value[done : done + n]
        done += n


def pull_block(g, buf, sign, k, pieces, masks, fields=27):
    base = pl.multiple_of(k * g.panel, 8)
    after = pl.multiple_of(jnp.where(k == g.halo, g.panel, base + g.panel), 8)
    out = []
    for i in range(fields):
        d = velocity(i, sign)

        def load(n, i=i, d=d):
            start = {-1: base - g.panel, 0: base, 1: after}[n]
            return read_rows(buf, start + (g.field(i) - d[0]), pieces)

        out.append(pull(load, d, masks))
    return out


def pull_edge(g, buf, sign, side, masks, fields=27):
    out = []
    for i in range(fields):
        d = velocity(i, sign)
        if side == 1:
            row = g.rows - d[0]
        else:
            row = {1: g.rows, 0: g.rows + 1, -1: 0}[d[0]]

        def load(n, i=i, row=row):
            return buf[pl.ds(g.at(i, 1 + n, row), g.cols, stride=g.panel), :]

        out.append(pull(load, d, masks))
    return out


def moments(f):
    flat = {}
    along_z = None
    for a in (-1, 0, 1):
        for b in (-1, 0, 1):
            lo, mid, hi = (f[INDEX[(a, b, c)]] for c in (-1, 0, 1))
            flat[a, b] = lo + mid + hi
            diff = hi - lo
            along_z = diff if along_z is None else along_z + diff
    line = {}
    along_y = None
    for a in (-1, 0, 1):
        line[a] = flat[a, -1] + flat[a, 0] + flat[a, 1]
        diff = flat[a, 1] - flat[a, -1]
        along_y = diff if along_y is None else along_y + diff
    return line[-1] + line[0] + line[1], line[1] - line[-1], along_y, along_z


def combos(x, y, z):
    plane = {}
    for a in (-1, 0, 1):
        for b in (-1, 0, 1):
            if (a, b) > (0, 0):
                continue
            if a == 0:
                plane[a, b] = -y if b else None
            else:
                plane[a, b] = -x if b == 0 else (-x - y if b < 0 else y - x)
    out = []
    for a, b, c in VELOCITY[:13]:
        base = plane[a, b]
        if base is None:
            out.append(-z)
        else:
            out.append(base if c == 0 else (base - z if c < 0 else base + z))
    return out


def relax(f, rho, wx, wy, wz, damp, push, solid):
    ux, uy, uz = (wx + push) * damp, wy * damp, wz * damp
    base = 1.0 - 1.5 * (ux * ux + uy * uy + uz * uz)
    keep = 1.0 - 1.0 / RELAX
    gain = rho * (1.0 / RELAX)
    level = [gain * w for w in (8.0 / 27, 2.0 / 27, 1.0 / 54, 1.0 / 216)]
    along = combos(3.0 * ux, 3.0 * uy, 3.0 * uz)
    out = [None] * 27
    for i in range(13):
        j = 26 - i
        even = base + 0.5 * (along[i] * along[i])
        lift = level[NORM[i]]
        out[i] = jnp.where(solid, f[j], keep * f[i] + lift * (even + along[i]))
        out[j] = jnp.where(solid, f[i], keep * f[j] + lift * (even - along[i]))
    out[13] = jnp.where(solid, f[13], keep * f[13] + level[0] * base)
    return out


def pulled_moments(p):
    first = {}
    for a in (-1, 0, 1):
        for b in (-1, 0, 1):
            lo, mid, hi = (p[INDEX[(a, b, c)]] for c in (-1, 0, 1))
            both = lo + hi
            first[a, b] = (4.0 * mid + both, hi - lo, both)
    second = {}
    for a in (-1, 0, 1):
        lo, mid, hi = (first[a, b] for b in (-1, 0, 1))
        b0 = lo[0] + hi[0]
        b1 = lo[1] + hi[1]
        second[a] = dict(
            one=4.0 * mid[0] + b0,
            y=hi[0] - lo[0],
            yy=b0,
            z=4.0 * mid[1] + b1,
            yz=hi[1] - lo[1],
            zz=4.0 * mid[2] + lo[2] + hi[2],
        )
    lo, mid, hi = (second[a] for a in (-1, 0, 1))

    def full(key):
        return 4.0 * mid[key] + lo[key] + hi[key]

    xx = lo["one"] + hi["one"]
    return dict(
        one=4.0 * mid["one"] + xx,
        x=hi["one"] - lo["one"],
        xx=xx,
        y=full("y"),
        xy=hi["y"] - lo["y"],
        yy=full("yy"),
        z=full("z"),
        xz=hi["z"] - lo["z"],
        yz=full("yz"),
        zz=full("zz"),
    )


def adjoint_scalars(p, rho, wx, wy, wz, damp, push, solid):
    ux, uy, uz = (wx + push) * damp, wy * damp, wz * damp
    s = pulled_moments(p)
    scale = 1.0 / (216.0 * RELAX)
    one = s["one"] * scale
    b = [s[k] * (3.0 * scale) for k in ("x", "y", "z")]
    d = {k: s[k] * (9.0 * scale) for k in ("xx", "xy", "yy", "xz", "yz", "zz")}
    qx = d["xx"] * ux + d["xy"] * uy + d["xz"] * uz
    qy = d["xy"] * ux + d["yy"] * uy + d["yz"] * uz
    qz = d["xz"] * ux + d["yz"] * uy + d["zz"] * uz
    linear = b[0] * ux + b[1] * uy + b[2] * uz
    square = ux * ux + uy * uy + uz * uz
    even = one + linear + 0.5 * (qx * ux + qy * uy + qz * uz) - 1.5 * one * square
    three = 3.0 * one
    gx = (b[0] + qx - three * ux) * damp
    gy = (b[1] + qy - three * uy) * damp
    gz = (b[2] + qz - three * uz) * damp
    even = even - (gx * wx + gy * wy + gz * wz)
    porous = jnp.where(solid, 0.0, -rho * (gx * ux + gy * uy + gz * uz))
    return even, gx, gy, gz, porous


def adjoint_spread(p, even, gx, gy, gz, solid):
    keep = 1.0 - 1.0 / RELAX
    along = combos(gx, gy, gz)
    out = [None] * 27
    for i in range(13):
        j = 26 - i
        out[i] = jnp.where(solid, p[j], keep * p[i] + (even + along[i]))
        out[j] = jnp.where(solid, p[i], keep * p[j] + (even - along[i]))
    out[13] = jnp.where(solid, p[13], keep * p[13] + even)
    return out


def x_lines(g, sign, fields, side):
    lines = []
    for i in moving(fields, sign, 0, side):
        if side == 1:
            lines.append((i, g.rows - 1, (-1, g.rows + 1)))
            lines.append((i, g.rows - 2, (g.rows,)))
        else:
            lines += [(i, 0, (g.rows,)), (i, 1, (g.rows + 1,))]
    edge, target = (g.rows - 1, g.rows + 1) if side == 1 else (0, g.rows)
    return lines + [(i, edge, (target,)) for i in moving(fields, sign, 0, 0)]


def pack_x(g, buf, sign, fields, up, down):
    for side, ref in ((1, up), (-1, down)):
        for n, (i, r, _) in enumerate(x_lines(g, sign, fields, side)):
            ref[n * g.cols : (n + 1) * g.cols, :] = buf[
                pl.ds(g.at(i, 1, r), g.cols, stride=g.panel), :
            ]


def unpack_x(g, buf, sign, fields, up, down):
    for side, ref in ((1, up), (-1, down)):
        for n, (i, _, targets) in enumerate(x_lines(g, sign, fields, side)):
            value = ref[n * g.cols : (n + 1) * g.cols, :]
            for r in targets:
                buf[pl.ds(g.at(i, 1, r), g.cols, stride=g.panel), :] = value
    for i in moving(fields, sign, 0, -1):
        buf[pl.ds(g.at(i, 1, g.rows + 2), g.cols, stride=g.panel), :] = buf[
            pl.ds(g.at(i, 1, 0), g.cols, stride=g.panel), :
        ]


def halo_panels(g, i, sign):
    return (0, g.halo) if velocity(i, sign)[1] == 1 else (g.halo,)


def pack_corners(g, buf, sign, fields, up, down):
    for side, ref in ((1, up), (-1, down)):
        for n, (i, r, _) in enumerate(x_lines(g, sign, fields, side)):
            ref[n : n + 1, :] = buf[pl.ds(g.at(i, g.halo, r), 1), :]


def unpack_corners(g, buf, sign, fields, up, down):
    for side, ref in ((1, up), (-1, down)):
        for n, (i, _, targets) in enumerate(x_lines(g, sign, fields, side)):
            value = ref[n : n + 1, :]
            for r in targets:
                for k in halo_panels(g, i, sign):
                    buf[pl.ds(g.at(i, k, r), 1), :] = value
    for i in moving(fields, sign, 0, -1):
        for k in halo_panels(g, i, sign):
            buf[pl.ds(g.at(i, k, g.rows + 2), 1), :] = buf[pl.ds(g.at(i, k, 0), 1), :]


def still_pairs(fields, sign):
    still = moving(fields, sign, 1, 0)
    half = (len(still) + 1) // 2
    return [(still[n], still[n + half] if n + half < len(still) else None) for n in range(half)]


def y_slots(fields, sign):
    return 9 + len(still_pairs(fields, sign))


def pack_y(g, buf, sign, fields, high, up, down):
    for side, ref in ((1, up), (-1, down)):
        k = g.cols if side == 1 else 1
        for n, i in enumerate(moving(fields, sign, 1, side)):
            ref[n * g.rows : (n + 1) * g.rows, :] = buf[pl.ds(g.at(i, k, 0), g.rows), :]
        for n, (i, j) in enumerate(still_pairs(fields, sign)):
            value = buf[pl.ds(g.at(i, k, 0), g.rows), :]
            if j is not None:
                other = pltpu.roll(buf[pl.ds(g.at(j, k, 0), g.rows), :], NZ, 1)
                pair = (value, other) if side == 1 else (other, value)
                value = jnp.where(high, *pair)
            ref[(9 + n) * g.rows : (10 + n) * g.rows, :] = value


def unpack_y(g, buf, sign, fields, high, up, down):
    for side, ref in ((1, up), (-1, down)):
        for n, i in enumerate(moving(fields, sign, 1, side)):
            value = ref[n * g.rows : (n + 1) * g.rows, :]
            for k in halo_panels(g, i, sign):
                buf[pl.ds(g.at(i, k, 0), g.rows), :] = value
    for n, (i, j) in enumerate(still_pairs(fields, sign)):
        spot = slice((9 + n) * g.rows, (10 + n) * g.rows)
        before, after = up[spot, :], down[spot, :]
        buf[pl.ds(g.at(i, g.halo, 0), g.rows), :] = jnp.where(high, before, after)
        if j is not None:
            value = pltpu.roll(jnp.where(high, after, before), NZ, 1)
            buf[pl.ds(g.at(j, g.halo, 0), g.rows), :] = value


def by_parity(axis, first, second, act):
    even = lax.rem(lax.axis_index(axis), 2) == 0

    @pl.when(even)
    def _():
        act(first, second)

    @pl.when(jnp.logical_not(even))
    def _():
        act(second, first)


def load_fields(ref, rows, base, pieces, count):
    return [read_rows(ref, base + n * rows, pieces) for n in range(count)]


def save_fields(ref, rows, base, pieces, values):
    for n, value in enumerate(values):
        write_rows(ref, base + n * rows, pieces, value)


def save_populations(g, out, k, pieces, values):
    base = pl.multiple_of(k * g.panel, 8)
    for i, value in enumerate(values):
        write_rows(out, base + g.field(i), pieces, value)


def spot_of(g, k):
    return pl.multiple_of((k - 1) * g.rows, 8)


def lanes_of(k):
    return pl.ds(pl.multiple_of((k - 1) * LANES, LANES), LANES)


def every(first, last, act):
    def step(k, carry):
        act(k)
        return carry

    lax.fori_loop(first, last + 1, step, 0)


def side_panels(g, act, count):
    def step(n, carry):
        act(jnp.where(n == 0, 1, g.cols - 1 + n))
        return carry

    lax.fori_loop(0, count, step, 0)


def interior_tiles(g, act):
    for pieces in g.inner:
        every(2, g.cols - 1, functools.partial(act, pieces=pieces))


def middle_tiles(g, act):
    for pieces in g.inner:
        side_panels(g, functools.partial(act, pieces=pieces), 3)
    every(2, g.cols - 1, functools.partial(act, pieces=g.outer))


def rim_tiles(g, act):
    every(1, g.cols, functools.partial(act, pieces=g.outer))
    for pieces in g.inner:
        side_panels(g, functools.partial(act, pieces=pieces), 2)


def step_tile(g, buf, out, sign, fields, masks, compute):
    def act(k, pieces):
        values = compute(
            pull_block(g, buf, sign, k, pieces, masks, fields), spot_of(g, k), pieces
        )
        save_populations(g, out, k, pieces, values)

    return act


def corner_tiles(g, buf, out, sign, fields, masks, compute):
    small = tuple(mask[:8] for mask in masks)
    act = step_tile(g, buf, out, sign, fields, masks, compute)
    side_panels(g, functools.partial(act, pieces=g.outer), 3)
    spot = g.halo * g.rows
    pieces = ((g.rows, 8),)
    values = compute(pull_block(g, buf, sign, g.halo, pieces, small, fields), spot, ((0, 8),))
    for i in range(27):
        dx = velocity(i, sign)[0]
        if dx == -1:
            out[pl.ds(g.at(i, g.halo, g.rows), 1), :] = values[i][0:1]
        elif dx == 1:
            out[pl.ds(g.at(i, g.halo, -1), 1), :] = values[i][1:2]
    edges = [pull_edge(g, buf, sign, side, small, fields) for side in (1, -1)]
    both = [stacked(pair) for pair in zip(*edges)]
    values = compute(both, spot, ((8, 16),))
    for i in moving(27, sign, 0, -1):
        out[pl.ds(g.at(i, 1, g.rows), g.cols, stride=g.panel), :] = values[i][:8]
    for i in moving(27, sign, 0, 1):
        out[pl.ds(g.at(i, 1, -1), g.cols, stride=g.panel), :] = values[i][8:]
    for i in moving(27, sign, 1, 1):
        out[pl.ds(g.at(i, 0, 0), g.rows), :] = out[pl.ds(g.at(i, g.halo, 0), g.rows), :]
        for r in (-1, g.rows):
            out[pl.ds(g.at(i, 0, r), 1), :] = out[pl.ds(g.at(i, g.halo, r), 1), :]


def flow_of(f):
    rho, mx, my, mz = moments(f)
    inverse = 1.0 / rho
    return inverse, rho, mx * inverse, my * inverse, mz * inverse


def collide_first(g, state, out):
    def act(k, pieces, f):
        base = pl.multiple_of(k * g.panel, 8)
        damp, push, wall = (read_rows(out, base + g.field(i), pieces) for i in (27, 28, 29))
        flow = flow_of(f)[1:] + (damp, push)
        save_fields(state, g.local, spot_of(g, k), pieces, flow + (wall,))
        save_populations(g, out, k, pieces, relax(f, *flow, wall > 0.5))

    return act


def collide_second(g, state):
    def compute(values, spot, pieces):
        f, (damp, push, wall) = values[:27], values[27:]
        flow = flow_of(f)[1:] + (damp, push)
        save_fields(state, g.extended, spot, pieces, flow + (wall,))
        return relax(f, *flow, wall > 0.5)

    return compute


def adjoint_second(g, state, total):
    def compute(p, spot, pieces):
        *flow, wall = load_fields(state, g.extended, spot, pieces, 7)
        *spread, porous = adjoint_scalars(p, *flow, wall > 0.5)
        save_fields(total, g.extended, spot, pieces, [porous])
        return adjoint_spread(p, *spread, wall > 0.5)

    return compute


def seed_tile(g, buf, adjoint, stage, out, masks):
    def act(k, pieces):
        f = pull_block(g, buf, 1, k, pieces, masks)
        for i in range(27):
            write_rows(stage.at[k - 1, i], 0, pieces, f[i])
        inverse, _, wx, wy, wz = flow_of(f)
        even = -(wx * wx + wy * wy + wz * wz) * inverse
        along = combos(wx * inverse, wy * inverse, wz * inverse)
        lanes = lanes_of(k)
        seeded = [
            stacked([adjoint[i, pl.ds(r, n), lanes] for r, n in pieces]) + even for i in range(27)
        ]
        for i in range(13):
            seeded[i] = seeded[i] + along[i]
            seeded[26 - i] = seeded[26 - i] - along[i]
        save_populations(g, out, k, pieces, seeded)

    return act


def block_of(ref, k):
    return ref.at[:, :, lanes_of(k)]


def pack_faces(g, buf, sign, fields, x_first, x_second, y_first, y_second):
    high = lane_masks(g.rows)[0]
    by_parity("gx", x_first, x_second, functools.partial(pack_x, g, buf, sign, fields))
    by_parity("gy", y_first, y_second, functools.partial(pack_y, g, buf, sign, fields, high))


def rim_first_kernel(g, pops, *refs):
    flat, (out, state, stage, *faces), near, (sems, flat_sems) = (
        refs[:3],
        refs[3:10],
        refs[10:13],
        refs[13:],
    )
    porosity, solid, labels = near

    def copy(k):
        return pltpu.make_async_copy(block_of(pops, k), stage.at[k - 1], sems.at[k - 1])

    flat_copies = [
        pltpu.make_async_copy(source, target, flat_sems.at[n])
        for n, (source, target) in enumerate(zip(flat, near))
    ]
    for each in flat_copies:
        each.start()
    for k in range(1, g.cols + 1):
        copy(k).start()
    for each in flat_copies:
        each.wait()

    def fields_of(k):
        lanes = lanes_of(k)
        label = labels[:, lanes]
        damp = 1.0 / (1.0 + porosity[:, lanes])
        push = jnp.where(label == 1, PUSH, jnp.where(label == 2, -PUSH, 0.0))
        base = pl.multiple_of(k * g.panel, 8)
        for i, value in ((27, damp), (28, push), (29, solid[:, lanes].astype(F32))):
            out[pl.ds(base + g.field(i), g.rows), :] = value

    every(1, g.cols, fields_of)
    collide = collide_first(g, state, out)

    def act(k, pieces):
        collide(k, pieces, [read_rows(stage.at[k - 1, i], 0, pieces) for i in range(27)])

    def column(k):
        copy(k).wait()
        act(k, g.outer)

    every(1, g.cols, column)
    for pieces in g.inner:
        side_panels(g, functools.partial(act, pieces=pieces), 2)
    pack_faces(g, out, 1, 30, *faces)


def inner_first_kernel(g, _, _state, stage, post, state0, out, state1):
    masks = lane_masks(16)
    collide = collide_first(g, state0, post)

    def act(k, pieces):
        collide(k, pieces, [read_rows(stage.at[k - 1, i], 0, pieces) for i in range(27)])

    interior_tiles(g, act)
    interior_tiles(g, step_tile(g, post, out, 1, 30, masks, collide_second(g, state1)))


def relay_kernel(g, sign, fields, _, y_second, y_first, buf, first, second):
    high = lane_masks(g.rows)[0]
    by_parity("gy", y_second, y_first, functools.partial(unpack_y, g, buf, sign, fields, high))
    by_parity("gx", first, second, functools.partial(pack_corners, g, buf, sign, fields))


def middle_second_kernel(g, post, out, state1, x_second, x_first):
    masks = lane_masks(16)
    by_parity("gx", x_second, x_first, functools.partial(unpack_x, g, post, 1, 30))
    middle_tiles(g, step_tile(g, post, out, 1, 30, masks, collide_second(g, state1)))


def rim_seed_kernel(g, _post, _out, _state, first, second, adjoint, *refs):
    post, out, state1, stage, field, *faces = refs
    masks = lane_masks(16)
    by_parity("gx", second, first, functools.partial(unpack_corners, g, post, 1, 30))
    corner_tiles(g, post, out, 1, 30, masks, collide_second(g, state1))
    rim_tiles(g, seed_tile(g, out, adjoint, stage, field, masks))
    pack_faces(g, field, -1, 27, *faces)


def inner_seed_kernel(
    g, post, _stage, _field, state1, adjoint, stage, field, out, total, final, sems
):
    masks = lane_masks(16)

    def copy(k):
        return pltpu.make_async_copy(stage.at[k - 1], block_of(final, k), sems.at[k - 1])

    copy(1).start()
    copy(g.cols).start()
    seed = seed_tile(g, post, adjoint, stage, field, masks)

    def column(k):
        for pieces in g.inner:
            seed(k, pieces)
        copy(k).start()

    every(2, g.cols - 1, column)
    interior_tiles(g, step_tile(g, field, out, -1, 27, masks, adjoint_second(g, state1, total)))
    every(1, g.cols, lambda k: copy(k).wait())


def middle_adjoint_kernel(g, field, out, total, state1, x_second, x_first):
    masks = lane_masks(16)
    by_parity("gx", x_second, x_first, functools.partial(unpack_x, g, field, -1, 27))
    middle_tiles(g, step_tile(g, field, out, -1, 27, masks, adjoint_second(g, state1, total)))


def total_kernel(g, _field, out, before, state1, state0, first, second, *refs):
    field, out, before, total, peak, parts = refs
    masks = lane_masks(16)
    by_parity("gx", second, first, functools.partial(unpack_corners, g, field, -1, 27))
    corner_tiles(g, field, out, -1, 27, masks, adjoint_second(g, state1, before))
    peak[...] = jnp.zeros((8, LANES), F32)

    def act(k, pieces):
        p = pull_block(g, out, -1, k, pieces, masks)
        spot = spot_of(g, k)
        *flow, wall = load_fields(state0, g.local, spot, pieces, 7)
        *spread, porous = adjoint_scalars(p, *flow, wall > 0.5)
        here = load_fields(before, g.extended, spot, pieces, 1)[0] + porous
        save_fields(total, g.local, spot, pieces, [here])
        save_fields(parts, g.local, spot, pieces, spread + [wall])
        largest = jnp.maximum(jnp.abs(here[:8]), jnp.abs(here[8:]))
        peak[...] = jnp.maximum(peak[...], largest)

    for pieces in (g.outer,) + g.inner:
        every(1, g.cols, functools.partial(act, pieces=pieces))


def adjoint_kernel(g, first, last, buf, parts, result, stage, sems):
    masks = lane_masks(16)

    def copy(k):
        return pltpu.make_async_copy(stage.at[k - first], block_of(result, k), sems.at[k - first])

    def column(k):
        for pieces in (g.outer,) + g.inner:
            p = pull_block(g, buf, -1, k, pieces, masks)
            *spread, wall = load_fields(parts, g.local, spot_of(g, k), pieces, 5)
            for i, value in enumerate(adjoint_spread(p, *spread, wall > 0.5)):
                write_rows(stage.at[k - first, i], 0, pieces, value)
        copy(k).start()

    every(first, last, column)
    every(first, last, lambda k: copy(k).wait())


def scale_kernel(g, total, peak, out):
    largest = jnp.max(peak[...])
    factor = 1.0 / (jnp.full((g.rows, LANES), largest, F32) + EPS)
    for c in range(g.cols):
        value = total[c * g.rows : (c + 1) * g.rows, :] * factor
        out[:, c * LANES : (c + 1) * LANES] = value


def swap_pairs(count, start):
    pairs = []
    for i in range(start, count, 2):
        j = (i + 1) % count
        pairs += [(i, j), (j, i)]
    return pairs


def swap(axis, count, first, second):
    return (
        lax.ppermute(first, axis, swap_pairs(count, 0)),
        lax.ppermute(second, axis, swap_pairs(count, 1)),
    )


def largest_of_all(peak, sizes, beside):
    groups = 0
    for axis, count, widths in (("gy", sizes[1], (2, 4, 4)), ("gx", sizes[0], (4, 2))):
        step = 1
        for width in widths:
            width = min(width, count // step)
            parts = [
                lax.ppermute(peak, axis, [(i, i ^ (n * step)) for i in range(count)])
                for n in range(1, width)
            ]
            groups += 1
            if groups == 2:
                peak = beside(peak)
            peak = functools.reduce(jnp.maximum, parts, peak)
            step *= width
    return peak


def on_device(sizes, populations, adjoint_in, porosity, solid, labels):
    rows, width = porosity.shape
    g = Grid(rows, width)
    in_vmem = pl.BlockSpec(memory_space=pltpu.VMEM)
    in_hbm = pl.BlockSpec(memory_space=pltpu.HBM)
    nx, ny = sizes

    def vmem(*shape):
        return pltpu.VMEM(shape, F32)

    def fields(count, size):
        return vmem(count * size, LANES)

    def padded(count):
        return vmem(*g.padded(count))

    def faces(count, sign):
        along_x = vmem(count * g.cols, LANES)
        along_y = vmem(y_slots(count, sign) * rows, LANES)
        return [along_x, along_x, along_y, along_y]

    def corners(count):
        return [vmem(-(-count // 8) * 8, LANES)] * 2

    whole = pltpu.HBM(populations.shape, F32)
    stage = vmem(g.cols, 27, rows, LANES)
    sems = pltpu.SemaphoreType.DMA((g.cols,))

    def call(name, kernel, operands, out_shape, scratch=(), kept=0, load=0, result=None):
        out_shape = [pltpu.VMEM(x.shape, x.dtype) for x in operands[:kept]] + out_shape
        aliases = {n: n for n in range(kept)}
        space = pltpu.HBM if name == "rim_first" else pltpu.VMEM
        pinned = [pltpu.with_memory_space_constraint(x, space) for x in operands]
        in_specs = [pl.BlockSpec(memory_space=space)] * len(operands)
        if result is not None:
            aliases[len(operands)] = len(out_shape) - 1
            pinned.append(pltpu.with_memory_space_constraint(result, pltpu.HBM))
            in_specs.append(in_hbm)
        return pl.pallas_call(
            functools.partial(kernel, g),
            in_specs=in_specs,
            out_shape=out_shape,
            out_specs=[in_hbm if x is whole else in_vmem for x in out_shape],
            scratch_shapes=list(scratch),
            input_output_aliases=aliases,
            compiler_params=pltpu.CompilerParams(vmem_limit_bytes=VMEM_LIMIT),
            cost_estimate=pl.CostEstimate(flops=0, bytes_accessed=load, transcendentals=0)
            if load
            else None,
            name=name,
        )(*pinned)

    def swap_faces(parcels):
        x_first, x_second = swap("gx", nx, *parcels[:2])
        y_first, y_second = swap("gy", ny, *parcels[2:])
        return [x_second, x_first], [y_second, y_first]

    def relay(buf, parcels, sign, count):
        def kernel(grid, *refs):
            relay_kernel(grid, sign, count, *refs)

        buf, *parcels = call("relay", kernel, [buf, *parcels], corners(count), kept=1)
        return buf, swap("gx", nx, *parcels)

    post, state0, staged, *parcels = call(
        "rim_first",
        rim_first_kernel,
        [populations, porosity, solid, labels],
        [padded(30), fields(7, g.local), stage] + faces(30, 1),
        [vmem(*porosity.shape)]
        + [pltpu.VMEM(porosity.shape, jnp.int32)] * 2
        + [sems, pltpu.SemaphoreType.DMA((3,))],
    )
    along_x, along_y = swap_faces(parcels)
    post, state0, second, state1 = call(
        "inner_first",
        inner_first_kernel,
        [post, state0, staged],
        [padded(27), fields(7, g.extended)],
        kept=2,
        load=FLIGHT,
    )
    post, parcels = relay(post, along_y, 1, 30)
    post, second, state1 = call(
        "middle_second",
        lambda grid, _post, _out, _state, b, a, *refs: middle_second_kernel(grid, *refs, b, a),
        [post, second, state1, *along_x],
        [],
        kept=3,
        load=FLIGHT,
    )
    _, second, state1, staged, field, *parcels = call(
        "rim_seed",
        rim_seed_kernel,
        [post, second, state1, *parcels, adjoint_in],
        [stage, padded(27)] + faces(27, -1),
        kept=3,
    )
    along_x, along_y = swap_faces(parcels)
    _, field, pulled, total, final = call(
        "inner_seed",
        lambda grid, kept, into, buf, *refs: inner_seed_kernel(grid, buf, kept, into, *refs),
        [staged, field, second, state1, adjoint_in],
        [padded(27), fields(1, g.extended), whole],
        [sems],
        kept=2,
        load=FLIGHT,
    )
    field, parcels = relay(field, along_y, -1, 27)
    field, pulled, total = call(
        "middle_adjoint",
        lambda grid, _field, _out, _total, state, b, a, *refs: middle_adjoint_kernel(
            grid, *refs, state, b, a
        ),
        [field, pulled, total, state1, *along_x],
        [],
        kept=3,
        load=FLIGHT,
    )
    _, pulled, _, total, peak, parts = call(
        "total",
        total_kernel,
        [field, pulled, total, state1, state0, *parcels],
        [fields(1, g.local), vmem(8, LANES), fields(5, g.local)],
        kept=3,
    )
    half = g.cols // 2
    scratch = [vmem(half, 27, rows, LANES), pltpu.SemaphoreType.DMA((half,))]
    halves = []

    def first_half(peak):
        def kernel(grid, buf, fields, near, echo, *refs):
            echo[...] = near[...]
            adjoint_kernel(grid, 1, half, buf, fields, *refs)

        echo, result = call(
            "adjoint_low",
            kernel,
            [pulled, parts, peak],
            [vmem(8, LANES), whole],
            scratch,
            load=FLIGHT // 2,
        )
        halves.append(result)
        return echo

    largest = largest_of_all(peak, sizes, first_half)
    (adjoint_out,) = call(
        "adjoint_high",
        lambda grid, buf, fields, _, *refs: adjoint_kernel(
            grid, 1 + half, g.cols, buf, fields, *refs
        ),
        [pulled, parts],
        [whole],
        scratch,
        load=FLIGHT // 2,
        result=halves[0],
    )
    (sensitivity,) = call(
        "normalize",
        scale_kernel,
        [total, largest],
        [jax.ShapeDtypeStruct(porosity.shape, F32)],
    )
    return final, adjoint_out, sensitivity


def solution(mesh):
    sizes = (mesh.shape["gx"], mesh.shape["gy"])
    whole, flat = P(None, "gx", "gy"), P("gx", "gy")
    return jax.shard_map(
        functools.partial(on_device, sizes),
        mesh=mesh,
        in_specs=(whole, whole, flat, flat, flat),
        out_specs=(whole, whole, flat),
        check_vma=False,
    )
```

```python
import functools

import jax
import jax.numpy as jnp
from jax import lax
from jax.experimental import pallas as pl
from jax.experimental.pallas import tpu as pltpu
from jax.sharding import PartitionSpec as P

NZ = 64
RELAX = 0.8
PUSH = 0.2
EPS = 1e-06
LANES = 128
VELOCITY = [(a, b, c) for a in (-1, 0, 1) for b in (-1, 0, 1) for c in (-1, 0, 1)]
INDEX = {v: i for i, v in enumerate(VELOCITY)}
WEIGHT = [
    [8.0 / 27, 2.0 / 27, 1.0 / 54, 1.0 / 216][abs(v[0]) + abs(v[1]) + abs(v[2])]
    for v in VELOCITY
]
NORM = [abs(v[0]) + abs(v[1]) + abs(v[2]) for v in VELOCITY]
F32 = jnp.float32
VMEM_LIMIT = 6 * 1024 * 1024
FLIGHT = 12 * 1024 * 1024


class Grid:
    def __init__(self, rows, width):
        self.rows = rows
        self.cols = width // LANES
        self.panel = rows + 16
        self.halo = self.cols + 1
        self.local = self.cols * rows
        self.extended = self.halo * rows + 24
        self.outer = ((0, 8), (rows - 8, 8))
        self.inner = tuple(((r, 16),) for r in range(8, rows - 8, 16))

    def at(self, i, k, r):
        return self.field(i) + k * self.panel + r

    def field(self, i):
        return i * (self.cols + 2) * self.panel + 8

    def padded(self, fields):
        return (fields * (self.cols + 2) * self.panel + 8, LANES)


def velocity(i, sign):
    return tuple(sign * n for n in VELOCITY[i]) if i < 27 else (0, 0, 0)


def moving(fields, sign, axis, side):
    return [i for i in range(fields) if velocity(i, sign)[axis] == side]


def lane_masks(height):
    lane = lax.broadcasted_iota(jnp.int32, (height, LANES), 1)
    return lane >= NZ, lane % NZ == 0, lane % NZ == NZ - 1


def shift_lanes(here, d, masks):
    first, last = masks[1:]
    dy, dz = d[1:]
    if dz == 0:
        return here if dy == 0 else pltpu.roll(here, NZ, 1)
    if dz == 1:
        one, other, edge = 1, NZ + 1, first
    else:
        one, other, edge = LANES - 1, NZ - 1, last
    inner, wrapped = (one, other) if dy == 0 else (other, one)
    return jnp.where(edge, pltpu.roll(here, wrapped, 1), pltpu.roll(here, inner, 1))


def pull(load, d, masks):
    high = masks[0]
    here = load(0)
    if d[1] == 1:
        here = jnp.where(high, load(-1), here)
    elif d[1] == -1:
        here = jnp.where(high, here, load(1))
    return shift_lanes(here, d, masks)


def stacked(parts):
    return parts[0] if len(parts) == 1 else jnp.concatenate(parts, 0)


def read_rows(ref, base, pieces):
    return stacked([ref[pl.ds(base + r, n), :] for r, n in pieces])


def write_rows(ref, base, pieces, value):
    done = 0
    for r, n in pieces:
        ref[pl.ds(base + r, n), :] = value[done : done + n]
        done += n


def pull_block(g, buf, sign, k, pieces, masks, fields=27):
    base = pl.multiple_of(k * g.panel, 8)
    after = pl.multiple_of(jnp.where(k == g.halo, g.panel, base + g.panel), 8)
    out = []
    for i in range(fields):
        d = velocity(i, sign)

        def load(n, i=i, d=d):
            start = {-1: base - g.panel, 0: base, 1: after}[n]
            return read_rows(buf, start + (g.field(i) - d[0]), pieces)

        out.append(pull(load, d, masks))
    return out


def pull_edge(g, buf, sign, side, masks, fields=27):
    out = []
    for i in range(fields):
        d = velocity(i, sign)
        if side == 1:
            row = g.rows - d[0]
        else:
            row = {1: g.rows, 0: g.rows + 1, -1: 0}[d[0]]

        def load(n, i=i, row=row):
            return buf[pl.ds(g.at(i, 1 + n, row), g.cols, stride=g.panel), :]

        out.append(pull(load, d, masks))
    return out


def moments(f):
    flat = {}
    along_z = None
    for a in (-1, 0, 1):
        for b in (-1, 0, 1):
            lo, mid, hi = (f[INDEX[(a, b, c)]] for c in (-1, 0, 1))
            flat[a, b] = lo + mid + hi
            diff = hi - lo
            along_z = diff if along_z is None else along_z + diff
    line = {}
    along_y = None
    for a in (-1, 0, 1):
        line[a] = flat[a, -1] + flat[a, 0] + flat[a, 1]
        diff = flat[a, 1] - flat[a, -1]
        along_y = diff if along_y is None else along_y + diff
    return line[-1] + line[0] + line[1], line[1] - line[-1], along_y, along_z


def combos(x, y, z):
    plane = {}
    for a in (-1, 0, 1):
        for b in (-1, 0, 1):
            if (a, b) > (0, 0):
                continue
            if a == 0:
                plane[a, b] = -y if b else None
            else:
                plane[a, b] = -x if b == 0 else (-x - y if b < 0 else y - x)
    out = []
    for a, b, c in VELOCITY[:13]:
        base = plane[a, b]
        if base is None:
            out.append(-z)
        else:
            out.append(base if c == 0 else (base - z if c < 0 else base + z))
    return out


def relax(f, rho, wx, wy, wz, damp, push, solid):
    ux, uy, uz = (wx + push) * damp, wy * damp, wz * damp
    base = 1.0 - 1.5 * (ux * ux + uy * uy + uz * uz)
    keep = 1.0 - 1.0 / RELAX
    gain = rho * (1.0 / RELAX)
    level = [gain * w for w in (8.0 / 27, 2.0 / 27, 1.0 / 54, 1.0 / 216)]
    along = combos(3.0 * ux, 3.0 * uy, 3.0 * uz)
    out = [None] * 27
    for i in range(13):
        j = 26 - i
        even = base + 0.5 * (along[i] * along[i])
        lift = level[NORM[i]]
        out[i] = jnp.where(solid, f[j], keep * f[i] + lift * (even + along[i]))
        out[j] = jnp.where(solid, f[i], keep * f[j] + lift * (even - along[i]))
    out[13] = jnp.where(solid, f[13], keep * f[13] + level[0] * base)
    return out


def pulled_moments(p):
    first = {}
    for a in (-1, 0, 1):
        for b in (-1, 0, 1):
            lo, mid, hi = (p[INDEX[(a, b, c)]] for c in (-1, 0, 1))
            both = lo + hi
            first[a, b] = (4.0 * mid + both, hi - lo, both)
    second = {}
    for a in (-1, 0, 1):
        lo, mid, hi = (first[a, b] for b in (-1, 0, 1))
        b0 = lo[0] + hi[0]
        b1 = lo[1] + hi[1]
        second[a] = dict(
            one=4.0 * mid[0] + b0,
            y=hi[0] - lo[0],
            yy=b0,
            z=4.0 * mid[1] + b1,
            yz=hi[1] - lo[1],
            zz=4.0 * mid[2] + lo[2] + hi[2],
        )
    lo, mid, hi = (second[a] for a in (-1, 0, 1))

    def full(key):
        return 4.0 * mid[key] + lo[key] + hi[key]

    xx = lo["one"] + hi["one"]
    return dict(
        one=4.0 * mid["one"] + xx,
        x=hi["one"] - lo["one"],
        xx=xx,
        y=full("y"),
        xy=hi["y"] - lo["y"],
        yy=full("yy"),
        z=full("z"),
        xz=hi["z"] - lo["z"],
        yz=full("yz"),
        zz=full("zz"),
    )


def adjoint_scalars(p, rho, wx, wy, wz, damp, push, solid):
    ux, uy, uz = (wx + push) * damp, wy * damp, wz * damp
    s = pulled_moments(p)
    scale = 1.0 / (216.0 * RELAX)
    one = s["one"] * scale
    b = [s[k] * (3.0 * scale) for k in ("x", "y", "z")]
    d = {k: s[k] * (9.0 * scale) for k in ("xx", "xy", "yy", "xz", "yz", "zz")}
    qx = d["xx"] * ux + d["xy"] * uy + d["xz"] * uz
    qy = d["xy"] * ux + d["yy"] * uy + d["yz"] * uz
    qz = d["xz"] * ux + d["yz"] * uy + d["zz"] * uz
    linear = b[0] * ux + b[1] * uy + b[2] * uz
    square = ux * ux + uy * uy + uz * uz
    even = one + linear + 0.5 * (qx * ux + qy * uy + qz * uz) - 1.5 * one * square
    three = 3.0 * one
    gx = (b[0] + qx - three * ux) * damp
    gy = (b[1] + qy - three * uy) * damp
    gz = (b[2] + qz - three * uz) * damp
    even = even - (gx * wx + gy * wy + gz * wz)
    porous = jnp.where(solid, 0.0, -rho * (gx * ux + gy * uy + gz * uz))
    return even, gx, gy, gz, porous


def adjoint_spread(p, even, gx, gy, gz, solid):
    keep = 1.0 - 1.0 / RELAX
    along = combos(gx, gy, gz)
    out = [None] * 27
    for i in range(13):
        j = 26 - i
        out[i] = jnp.where(solid, p[j], keep * p[i] + (even + along[i]))
        out[j] = jnp.where(solid, p[i], keep * p[j] + (even - along[i]))
    out[13] = jnp.where(solid, p[13], keep * p[13] + even)
    return out


def x_lines(g, sign, fields, side):
    lines = []
    for i in moving(fields, sign, 0, side):
        if side == 1:
            lines.append((i, g.rows - 1, (-1, g.rows + 1)))
            lines.append((i, g.rows - 2, (g.rows,)))
        else:
            lines += [(i, 0, (g.rows,)), (i, 1, (g.rows + 1,))]
    edge, target = (g.rows - 1, g.rows + 1) if side == 1 else (0, g.rows)
    return lines + [(i, edge, (target,)) for i in moving(fields, sign, 0, 0)]


def pack_x(g, buf, sign, fields, up, down):
    for side, ref in ((1, up), (-1, down)):
        for n, (i, r, _) in enumerate(x_lines(g, sign, fields, side)):
            ref[n * g.cols : (n + 1) * g.cols, :] = buf[
                pl.ds(g.at(i, 1, r), g.cols, stride=g.panel), :
            ]


def unpack_x(g, buf, sign, fields, up, down):
    for side, ref in ((1, up), (-1, down)):
        for n, (i, _, targets) in enumerate(x_lines(g, sign, fields, side)):
            value = ref[n * g.cols : (n + 1) * g.cols, :]
            for r in targets:
                buf[pl.ds(g.at(i, 1, r), g.cols, stride=g.panel), :] = value
    for i in moving(fields, sign, 0, -1):
        buf[pl.ds(g.at(i, 1, g.rows + 2), g.cols, stride=g.panel), :] = buf[
            pl.ds(g.at(i, 1, 0), g.cols, stride=g.panel), :
        ]


def halo_panels(g, i, sign):
    return (0, g.halo) if velocity(i, sign)[1] == 1 else (g.halo,)


def pack_corners(g, buf, sign, fields, up, down):
    for side, ref in ((1, up), (-1, down)):
        for n, (i, r, _) in enumerate(x_lines(g, sign, fields, side)):
            ref[n : n + 1, :] = buf[pl.ds(g.at(i, g.halo, r), 1), :]


def unpack_corners(g, buf, sign, fields, up, down):
    for side, ref in ((1, up), (-1, down)):
        for n, (i, _, targets) in enumerate(x_lines(g, sign, fields, side)):
            value = ref[n : n + 1, :]
            for r in targets:
                for k in halo_panels(g, i, sign):
                    buf[pl.ds(g.at(i, k, r), 1), :] = value
    for i in moving(fields, sign, 0, -1):
        for k in halo_panels(g, i, sign):
            buf[pl.ds(g.at(i, k, g.rows + 2), 1), :] = buf[pl.ds(g.at(i, k, 0), 1), :]


def still_pairs(fields, sign):
    still = moving(fields, sign, 1, 0)
    half = (len(still) + 1) // 2
    return [(still[n], still[n + half] if n + half < len(still) else None) for n in range(half)]


def y_slots(fields, sign):
    return 9 + len(still_pairs(fields, sign))


def pack_y(g, buf, sign, fields, high, up, down):
    for side, ref in ((1, up), (-1, down)):
        k = g.cols if side == 1 else 1
        for n, i in enumerate(moving(fields, sign, 1, side)):
            ref[n * g.rows : (n + 1) * g.rows, :] = buf[pl.ds(g.at(i, k, 0), g.rows), :]
        for n, (i, j) in enumerate(still_pairs(fields, sign)):
            value = buf[pl.ds(g.at(i, k, 0), g.rows), :]
            if j is not None:
                other = pltpu.roll(buf[pl.ds(g.at(j, k, 0), g.rows), :], NZ, 1)
                pair = (value, other) if side == 1 else (other, value)
                value = jnp.where(high, *pair)
            ref[(9 + n) * g.rows : (10 + n) * g.rows, :] = value


def unpack_y(g, buf, sign, fields, high, up, down):
    for side, ref in ((1, up), (-1, down)):
        for n, i in enumerate(moving(fields, sign, 1, side)):
            value = ref[n * g.rows : (n + 1) * g.rows, :]
            for k in halo_panels(g, i, sign):
                buf[pl.ds(g.at(i, k, 0), g.rows), :] = value
    for n, (i, j) in enumerate(still_pairs(fields, sign)):
        spot = slice((9 + n) * g.rows, (10 + n) * g.rows)
        before, after = up[spot, :], down[spot, :]
        buf[pl.ds(g.at(i, g.halo, 0), g.rows), :] = jnp.where(high, before, after)
        if j is not None:
            value = pltpu.roll(jnp.where(high, after, before), NZ, 1)
            buf[pl.ds(g.at(j, g.halo, 0), g.rows), :] = value


def by_parity(axis, first, second, act):
    even = lax.rem(lax.axis_index(axis), 2) == 0

    @pl.when(even)
    def _():
        act(first, second)

    @pl.when(jnp.logical_not(even))
    def _():
        act(second, first)


def load_fields(ref, rows, base, pieces, count):
    return [read_rows(ref, base + n * rows, pieces) for n in range(count)]


def save_fields(ref, rows, base, pieces, values):
    for n, value in enumerate(values):
        write_rows(ref, base + n * rows, pieces, value)


def save_populations(g, out, k, pieces, values):
    base = pl.multiple_of(k * g.panel, 8)
    for i, value in enumerate(values):
        write_rows(out, base + g.field(i), pieces, value)


def spot_of(g, k):
    return pl.multiple_of((k - 1) * g.rows, 8)


def lanes_of(k):
    return pl.ds(pl.multiple_of((k - 1) * LANES, LANES), LANES)


def every(first, last, act):
    def step(k, carry):
        act(k)
        return carry

    lax.fori_loop(first, last + 1, step, 0, unroll=2 - (last + 1 - first) % 2)


def side_panels(g, act, count):
    def step(n, carry):
        act(jnp.where(n == 0, 1, g.cols - 1 + n))
        return carry

    lax.fori_loop(0, count, step, 0, unroll=count)


def interior_tiles(g, act):
    for pieces in g.inner:
        every(2, g.cols - 1, functools.partial(act, pieces=pieces))


def middle_tiles(g, act):
    for pieces in g.inner:
        side_panels(g, functools.partial(act, pieces=pieces), 3)
    every(2, g.cols - 1, functools.partial(act, pieces=g.outer))


def rim_tiles(g, act):
    every(1, g.cols, functools.partial(act, pieces=g.outer))
    for pieces in g.inner:
        side_panels(g, functools.partial(act, pieces=pieces), 2)


def step_tile(g, buf, out, sign, fields, masks, compute):
    def act(k, pieces):
        values = compute(
            pull_block(g, buf, sign, k, pieces, masks, fields), spot_of(g, k), pieces
        )
        save_populations(g, out, k, pieces, values)

    return act


def corner_tiles(g, buf, out, sign, fields, masks, compute):
    small = tuple(mask[:8] for mask in masks)
    act = step_tile(g, buf, out, sign, fields, masks, compute)
    side_panels(g, functools.partial(act, pieces=g.outer), 3)
    spot = g.halo * g.rows
    pieces = ((g.rows, 8),)
    values = compute(pull_block(g, buf, sign, g.halo, pieces, small, fields), spot, ((0, 8),))
    for i in range(27):
        dx = velocity(i, sign)[0]
        if dx == -1:
            out[pl.ds(g.at(i, g.halo, g.rows), 1), :] = values[i][0:1]
        elif dx == 1:
            out[pl.ds(g.at(i, g.halo, -1), 1), :] = values[i][1:2]
    edges = [pull_edge(g, buf, sign, side, small, fields) for side in (1, -1)]
    both = [stacked(pair) for pair in zip(*edges)]
    values = compute(both, spot, ((8, 16),))
    for i in moving(27, sign, 0, -1):
        out[pl.ds(g.at(i, 1, g.rows), g.cols, stride=g.panel), :] = values[i][:8]
    for i in moving(27, sign, 0, 1):
        out[pl.ds(g.at(i, 1, -1), g.cols, stride=g.panel), :] = values[i][8:]
    for i in moving(27, sign, 1, 1):
        out[pl.ds(g.at(i, 0, 0), g.rows), :] = out[pl.ds(g.at(i, g.halo, 0), g.rows), :]
        for r in (-1, g.rows):
            out[pl.ds(g.at(i, 0, r), 1), :] = out[pl.ds(g.at(i, g.halo, r), 1), :]


def flow_of(f):
    rho, mx, my, mz = moments(f)
    inverse = 1.0 / rho
    return inverse, rho, mx * inverse, my * inverse, mz * inverse


def collide_first(g, state, out):
    def act(k, pieces, f):
        base = pl.multiple_of(k * g.panel, 8)
        damp, push, wall = (read_rows(out, base + g.field(i), pieces) for i in (27, 28, 29))
        flow = flow_of(f)[1:] + (damp, push)
        save_fields(state, g.local, spot_of(g, k), pieces, flow + (wall,))
        save_populations(g, out, k, pieces, relax(f, *flow, wall > 0.5))

    return act


def collide_second(g, state):
    def compute(values, spot, pieces):
        f, (damp, push, wall) = values[:27], values[27:]
        flow = flow_of(f)[1:] + (damp, push)
        save_fields(state, g.extended, spot, pieces, flow + (wall,))
        return relax(f, *flow, wall > 0.5)

    return compute


def adjoint_second(g, state, total):
    def compute(p, spot, pieces):
        *flow, wall = load_fields(state, g.extended, spot, pieces, 7)
        *spread, porous = adjoint_scalars(p, *flow, wall > 0.5)
        save_fields(total, g.extended, spot, pieces, [porous])
        return adjoint_spread(p, *spread, wall > 0.5)

    return compute


def seed_tile(g, buf, adjoint, stage, out, masks):
    def act(k, pieces):
        f = pull_block(g, buf, 1, k, pieces, masks)
        for i in range(27):
            write_rows(stage.at[k - 1, i], 0, pieces, f[i])
        inverse, _, wx, wy, wz = flow_of(f)
        even = -(wx * wx + wy * wy + wz * wz) * inverse
        along = combos(wx * inverse, wy * inverse, wz * inverse)
        lanes = lanes_of(k)
        seeded = [
            stacked([adjoint[i, pl.ds(r, n), lanes] for r, n in pieces]) + even for i in range(27)
        ]
        for i in range(13):
            seeded[i] = seeded[i] + along[i]
            seeded[26 - i] = seeded[26 - i] - along[i]
        save_populations(g, out, k, pieces, seeded)

    return act


def block_of(ref, k):
    return ref.at[:, :, lanes_of(k)]


def pack_faces(g, buf, sign, fields, x_first, x_second, y_first, y_second):
    high = lane_masks(g.rows)[0]
    by_parity("gx", x_first, x_second, functools.partial(pack_x, g, buf, sign, fields))
    by_parity("gy", y_first, y_second, functools.partial(pack_y, g, buf, sign, fields, high))


def rim_first_kernel(g, pops, *refs):
    flat, (out, state, stage, *faces), near, (sems, flat_sems) = (
        refs[:3],
        refs[3:10],
        refs[10:13],
        refs[13:],
    )
    porosity, solid, labels = near

    def copy(k):
        return pltpu.make_async_copy(block_of(pops, k), stage.at[k - 1], sems.at[k - 1])

    flat_copies = [
        pltpu.make_async_copy(source, target, flat_sems.at[n])
        for n, (source, target) in enumerate(zip(flat, near))
    ]
    for each in flat_copies:
        each.start()
    for k in range(1, g.cols + 1):
        copy(k).start()
    for each in flat_copies:
        each.wait()

    def fields_of(k):
        lanes = lanes_of(k)
        label = labels[:, lanes]
        damp = 1.0 / (1.0 + porosity[:, lanes])
        push = jnp.where(label == 1, PUSH, jnp.where(label == 2, -PUSH, 0.0))
        base = pl.multiple_of(k * g.panel, 8)
        for i, value in ((27, damp), (28, push), (29, solid[:, lanes].astype(F32))):
            out[pl.ds(base + g.field(i), g.rows), :] = value

    every(1, g.cols, fields_of)
    collide = collide_first(g, state, out)

    def act(k, pieces):
        collide(k, pieces, [read_rows(stage.at[k - 1, i], 0, pieces) for i in range(27)])

    def column(k):
        copy(k).wait()
        act(k, g.outer)

    every(1, g.cols, column)
    for pieces in g.inner:
        side_panels(g, functools.partial(act, pieces=pieces), 2)
    pack_faces(g, out, 1, 30, *faces)


def inner_first_kernel(g, _, _state, stage, post, state0, out, state1):
    masks = lane_masks(16)
    collide = collide_first(g, state0, post)

    def act(k, pieces):
        collide(k, pieces, [read_rows(stage.at[k - 1, i], 0, pieces) for i in range(27)])

    interior_tiles(g, act)
    interior_tiles(g, step_tile(g, post, out, 1, 30, masks, collide_second(g, state1)))


def relay_kernel(g, sign, fields, _, y_second, y_first, buf, first, second):
    high = lane_masks(g.rows)[0]
    by_parity("gy", y_second, y_first, functools.partial(unpack_y, g, buf, sign, fields, high))
    by_parity("gx", first, second, functools.partial(pack_corners, g, buf, sign, fields))


def middle_second_kernel(g, post, out, state1, x_second, x_first):
    masks = lane_masks(16)
    by_parity("gx", x_second, x_first, functools.partial(unpack_x, g, post, 1, 30))
    middle_tiles(g, step_tile(g, post, out, 1, 30, masks, collide_second(g, state1)))


def rim_seed_kernel(g, _post, _out, _state, first, second, adjoint, *refs):
    post, out, state1, stage, field, *faces = refs
    masks = lane_masks(16)
    by_parity("gx", second, first, functools.partial(unpack_corners, g, post, 1, 30))
    corner_tiles(g, post, out, 1, 30, masks, collide_second(g, state1))
    rim_tiles(g, seed_tile(g, out, adjoint, stage, field, masks))
    pack_faces(g, field, -1, 27, *faces)


def inner_seed_kernel(
    g, post, _stage, _field, state1, adjoint, stage, field, out, total, final, sems
):
    masks = lane_masks(16)

    def copy(k):
        return pltpu.make_async_copy(stage.at[k - 1], block_of(final, k), sems.at[k - 1])

    copy(1).start()
    copy(g.cols).start()
    seed = seed_tile(g, post, adjoint, stage, field, masks)

    def column(k):
        for pieces in g.inner:
            seed(k, pieces)
        copy(k).start()

    every(2, g.cols - 1, column)
    interior_tiles(g, step_tile(g, field, out, -1, 27, masks, adjoint_second(g, state1, total)))
    every(1, g.cols, lambda k: copy(k).wait())


def middle_adjoint_kernel(g, field, out, total, state1, x_second, x_first):
    masks = lane_masks(16)
    by_parity("gx", x_second, x_first, functools.partial(unpack_x, g, field, -1, 27))
    middle_tiles(g, step_tile(g, field, out, -1, 27, masks, adjoint_second(g, state1, total)))


def total_kernel(g, _field, out, before, state1, state0, first, second, *refs):
    field, out, before, total, peak, parts = refs
    masks = lane_masks(16)
    by_parity("gx", second, first, functools.partial(unpack_corners, g, field, -1, 27))
    corner_tiles(g, field, out, -1, 27, masks, adjoint_second(g, state1, before))
    peak[...] = jnp.zeros((8, LANES), F32)

    def act(k, pieces):
        p = pull_block(g, out, -1, k, pieces, masks)
        spot = spot_of(g, k)
        *flow, wall = load_fields(state0, g.local, spot, pieces, 7)
        *spread, porous = adjoint_scalars(p, *flow, wall > 0.5)
        here = load_fields(before, g.extended, spot, pieces, 1)[0] + porous
        save_fields(total, g.local, spot, pieces, [here])
        save_fields(parts, g.local, spot, pieces, spread + [wall])
        largest = jnp.maximum(jnp.abs(here[:8]), jnp.abs(here[8:]))
        peak[...] = jnp.maximum(peak[...], largest)

    for pieces in (g.outer,) + g.inner:
        every(1, g.cols, functools.partial(act, pieces=pieces))


def adjoint_kernel(g, first, last, buf, parts, result, stage, sems):
    masks = lane_masks(16)

    def copy(k):
        return pltpu.make_async_copy(stage.at[k - first], block_of(result, k), sems.at[k - first])

    def column(k):
        for pieces in (g.outer,) + g.inner:
            p = pull_block(g, buf, -1, k, pieces, masks)
            *spread, wall = load_fields(parts, g.local, spot_of(g, k), pieces, 5)
            for i, value in enumerate(adjoint_spread(p, *spread, wall > 0.5)):
                write_rows(stage.at[k - first, i], 0, pieces, value)
        copy(k).start()

    every(first, last, column)
    every(first, last, lambda k: copy(k).wait())


def scale_kernel(g, total, peak, out):
    largest = jnp.max(peak[...])
    factor = 1.0 / (jnp.full((g.rows, LANES), largest, F32) + EPS)
    for c in range(g.cols):
        value = total[c * g.rows : (c + 1) * g.rows, :] * factor
        out[:, c * LANES : (c + 1) * LANES] = value


def swap_pairs(count, start):
    pairs = []
    for i in range(start, count, 2):
        j = (i + 1) % count
        pairs += [(i, j), (j, i)]
    return pairs


def swap(axis, count, first, second):
    return (
        lax.ppermute(first, axis, swap_pairs(count, 0)),
        lax.ppermute(second, axis, swap_pairs(count, 1)),
    )


def largest_of_all(peak, sizes, beside):
    groups = 0
    for axis, count, widths in (("gy", sizes[1], (2, 4, 4)), ("gx", sizes[0], (4, 2))):
        step = 1
        for width in widths:
            width = min(width, count // step)
            parts = [
                lax.ppermute(peak, axis, [(i, i ^ (n * step)) for i in range(count)])
                for n in range(1, width)
            ]
            groups += 1
            if groups == 2:
                peak = beside(peak)
            peak = functools.reduce(jnp.maximum, parts, peak)
            step *= width
    return peak


def on_device(sizes, populations, adjoint_in, porosity, solid, labels):
    rows, width = porosity.shape
    g = Grid(rows, width)
    in_vmem = pl.BlockSpec(memory_space=pltpu.VMEM)
    in_hbm = pl.BlockSpec(memory_space=pltpu.HBM)
    nx, ny = sizes

    def vmem(*shape):
        return pltpu.VMEM(shape, F32)

    def fields(count, size):
        return vmem(count * size, LANES)

    def padded(count):
        return vmem(*g.padded(count))

    def faces(count, sign):
        along_x = vmem(count * g.cols, LANES)
        along_y = vmem(y_slots(count, sign) * rows, LANES)
        return [along_x, along_x, along_y, along_y]

    def corners(count):
        return [vmem(-(-count // 8) * 8, LANES)] * 2

    whole = pltpu.HBM(populations.shape, F32)
    stage = vmem(g.cols, 27, rows, LANES)
    sems = pltpu.SemaphoreType.DMA((g.cols,))

    def call(name, kernel, operands, out_shape, scratch=(), kept=0, load=0, result=None):
        out_shape = [pltpu.VMEM(x.shape, x.dtype) for x in operands[:kept]] + out_shape
        aliases = {n: n for n in range(kept)}
        space = pltpu.HBM if name == "rim_first" else pltpu.VMEM
        pinned = [pltpu.with_memory_space_constraint(x, space) for x in operands]
        in_specs = [pl.BlockSpec(memory_space=space)] * len(operands)
        if result is not None:
            aliases[len(operands)] = len(out_shape) - 1
            pinned.append(pltpu.with_memory_space_constraint(result, pltpu.HBM))
            in_specs.append(in_hbm)
        return pl.pallas_call(
            functools.partial(kernel, g),
            in_specs=in_specs,
            out_shape=out_shape,
            out_specs=[in_hbm if x is whole else in_vmem for x in out_shape],
            scratch_shapes=list(scratch),
            input_output_aliases=aliases,
            compiler_params=pltpu.CompilerParams(vmem_limit_bytes=VMEM_LIMIT),
            cost_estimate=pl.CostEstimate(flops=0, bytes_accessed=load, transcendentals=0)
            if load
            else None,
            name=name,
        )(*pinned)

    def swap_faces(parcels):
        x_first, x_second = swap("gx", nx, *parcels[:2])
        y_first, y_second = swap("gy", ny, *parcels[2:])
        return [x_second, x_first], [y_second, y_first]

    def relay(buf, parcels, sign, count):
        def kernel(grid, *refs):
            relay_kernel(grid, sign, count, *refs)

        buf, *parcels = call("relay", kernel, [buf, *parcels], corners(count), kept=1)
        return buf, swap("gx", nx, *parcels)

    post, state0, staged, *parcels = call(
        "rim_first",
        rim_first_kernel,
        [populations, porosity, solid, labels],
        [padded(30), fields(7, g.local), stage] + faces(30, 1),
        [vmem(*porosity.shape)]
        + [pltpu.VMEM(porosity.shape, jnp.int32)] * 2
        + [sems, pltpu.SemaphoreType.DMA((3,))],
    )
    along_x, along_y = swap_faces(parcels)
    post, state0, second, state1 = call(
        "inner_first",
        inner_first_kernel,
        [post, state0, staged],
        [padded(27), fields(7, g.extended)],
        kept=2,
        load=FLIGHT,
    )
    post, parcels = relay(post, along_y, 1, 30)
    post, second, state1 = call(
        "middle_second",
        lambda grid, _post, _out, _state, b, a, *refs: middle_second_kernel(grid, *refs, b, a),
        [post, second, state1, *along_x],
        [],
        kept=3,
        load=FLIGHT,
    )
    _, second, state1, staged, field, *parcels = call(
        "rim_seed",
        rim_seed_kernel,
        [post, second, state1, *parcels, adjoint_in],
        [stage, padded(27)] + faces(27, -1),
        kept=3,
    )
    along_x, along_y = swap_faces(parcels)
    _, field, pulled, total, final = call(
        "inner_seed",
        lambda grid, kept, into, buf, *refs: inner_seed_kernel(grid, buf, kept, into, *refs),
        [staged, field, second, state1, adjoint_in],
        [padded(27), fields(1, g.extended), whole],
        [sems],
        kept=2,
        load=FLIGHT,
    )
    field, parcels = relay(field, along_y, -1, 27)
    field, pulled, total = call(
        "middle_adjoint",
        lambda grid, _field, _out, _total, state, b, a, *refs: middle_adjoint_kernel(
            grid, *refs, state, b, a
        ),
        [field, pulled, total, state1, *along_x],
        [],
        kept=3,
        load=FLIGHT,
    )
    _, pulled, _, total, peak, parts = call(
        "total",
        total_kernel,
        [field, pulled, total, state1, state0, *parcels],
        [fields(1, g.local), vmem(8, LANES), fields(5, g.local)],
        kept=3,
    )
    half = g.cols // 2
    scratch = [vmem(half, 27, rows, LANES), pltpu.SemaphoreType.DMA((half,))]
    halves = []

    def first_half(peak):
        def kernel(grid, buf, fields, near, echo, *refs):
            echo[...] = near[...]
            adjoint_kernel(grid, 1, half, buf, fields, *refs)

        echo, result = call(
            "adjoint_low",
            kernel,
            [pulled, parts, peak],
            [vmem(8, LANES), whole],
            scratch,
            load=FLIGHT // 2,
        )
        halves.append(result)
        return echo

    largest = largest_of_all(peak, sizes, first_half)
    (adjoint_out,) = call(
        "adjoint_high",
        lambda grid, buf, fields, _, *refs: adjoint_kernel(
            grid, 1 + half, g.cols, buf, fields, *refs
        ),
        [pulled, parts],
        [whole],
        scratch,
        load=FLIGHT // 2,
        result=halves[0],
    )
    (sensitivity,) = call(
        "normalize",
        scale_kernel,
        [total, largest],
        [jax.ShapeDtypeStruct(porosity.shape, F32)],
    )
    return final, adjoint_out, sensitivity


def solution(mesh):
    sizes = (mesh.shape["gx"], mesh.shape["gy"])
    whole, flat = P(None, "gx", "gy"), P("gx", "gy")
    return jax.shard_map(
        functools.partial(on_device, sizes),
        mesh=mesh,
        in_specs=(whole, whole, flat, flat, flat),
        out_specs=(whole, whole, flat),
        check_vma=False,
    )
```

```python
import functools

import jax
import jax.numpy as jnp
from jax import lax
from jax.experimental import pallas as pl
from jax.experimental.pallas import tpu as pltpu
from jax.sharding import PartitionSpec as P

NZ = 64
RELAX = 0.8
PUSH = 0.2
EPS = 1e-06
LANES = 128
VELOCITY = [(a, b, c) for a in (-1, 0, 1) for b in (-1, 0, 1) for c in (-1, 0, 1)]
INDEX = {v: i for i, v in enumerate(VELOCITY)}
WEIGHT = [
    [8.0 / 27, 2.0 / 27, 1.0 / 54, 1.0 / 216][abs(v[0]) + abs(v[1]) + abs(v[2])]
    for v in VELOCITY
]
NORM = [abs(v[0]) + abs(v[1]) + abs(v[2]) for v in VELOCITY]
F32 = jnp.float32
VMEM_LIMIT = 6 * 1024 * 1024
FLIGHT = 12 * 1024 * 1024


class Grid:
    def __init__(self, rows, width):
        self.rows = rows
        self.cols = width // LANES
        self.panel = rows + 16
        self.halo = self.cols + 1
        self.local = self.cols * rows
        self.extended = self.halo * rows + 24
        self.outer = ((0, 8), (rows - 8, 8))
        self.inner = tuple(((r, 16),) for r in range(8, rows - 8, 16))

    def at(self, i, k, r):
        return self.field(i) + k * self.panel + r

    def field(self, i):
        return i * (self.cols + 2) * self.panel + 8

    def padded(self, fields):
        return (fields * (self.cols + 2) * self.panel + 8, LANES)


def velocity(i, sign):
    return tuple(sign * n for n in VELOCITY[i]) if i < 27 else (0, 0, 0)


def moving(fields, sign, axis, side):
    return [i for i in range(fields) if velocity(i, sign)[axis] == side]


def lane_masks(height):
    lane = lax.broadcasted_iota(jnp.int32, (height, LANES), 1)
    return lane >= NZ, lane % NZ == 0, lane % NZ == NZ - 1


def shift_lanes(here, d, masks):
    first, last = masks[1:]
    dy, dz = d[1:]
    if dz == 0:
        return here if dy == 0 else pltpu.roll(here, NZ, 1)
    if dz == 1:
        one, other, edge = 1, NZ + 1, first
    else:
        one, other, edge = LANES - 1, NZ - 1, last
    inner, wrapped = (one, other) if dy == 0 else (other, one)
    return jnp.where(edge, pltpu.roll(here, wrapped, 1), pltpu.roll(here, inner, 1))


def pull(load, d, masks):
    high = masks[0]
    here = load(0)
    if d[1] == 1:
        here = jnp.where(high, load(-1), here)
    elif d[1] == -1:
        here = jnp.where(high, here, load(1))
    return shift_lanes(here, d, masks)


def stacked(parts):
    return parts[0] if len(parts) == 1 else jnp.concatenate(parts, 0)


def read_rows(ref, base, pieces):
    return stacked([ref[pl.ds(base + r, n), :] for r, n in pieces])


def write_rows(ref, base, pieces, value):
    done = 0
    for r, n in pieces:
        ref[pl.ds(base + r, n), :] = value[done : done + n]
        done += n


def pull_block(g, buf, sign, k, pieces, masks, fields=27):
    base = pl.multiple_of(k * g.panel, 8)
    after = pl.multiple_of(jnp.where(k == g.halo, g.panel, base + g.panel), 8)
    out = []
    for i in range(fields):
        d = velocity(i, sign)

        def load(n, i=i, d=d):
            start = {-1: base - g.panel, 0: base, 1: after}[n]
            return read_rows(buf, start + (g.field(i) - d[0]), pieces)

        out.append(pull(load, d, masks))
    return out


def pull_edge(g, buf, sign, side, masks, fields=27):
    out = []
    for i in range(fields):
        d = velocity(i, sign)
        if side == 1:
            row = g.rows - d[0]
        else:
            row = {1: g.rows, 0: g.rows + 1, -1: 0}[d[0]]

        def load(n, i=i, row=row):
            return buf[pl.ds(g.at(i, 1 + n, row), g.cols, stride=g.panel), :]

        out.append(pull(load, d, masks))
    return out


def moments(f):
    flat = {}
    along_z = None
    for a in (-1, 0, 1):
        for b in (-1, 0, 1):
            lo, mid, hi = (f[INDEX[(a, b, c)]] for c in (-1, 0, 1))
            flat[a, b] = lo + mid + hi
            diff = hi - lo
            along_z = diff if along_z is None else along_z + diff
    line = {}
    along_y = None
    for a in (-1, 0, 1):
        line[a] = flat[a, -1] + flat[a, 0] + flat[a, 1]
        diff = flat[a, 1] - flat[a, -1]
        along_y = diff if along_y is None else along_y + diff
    return line[-1] + line[0] + line[1], line[1] - line[-1], along_y, along_z


def combos(x, y, z):
    plane = {}
    for a in (-1, 0, 1):
        for b in (-1, 0, 1):
            if (a, b) > (0, 0):
                continue
            if a == 0:
                plane[a, b] = -y if b else None
            else:
                plane[a, b] = -x if b == 0 else (-x - y if b < 0 else y - x)
    out = []
    for a, b, c in VELOCITY[:13]:
        base = plane[a, b]
        if base is None:
            out.append(-z)
        else:
            out.append(base if c == 0 else (base - z if c < 0 else base + z))
    return out


def relax(f, rho, wx, wy, wz, damp, push, solid):
    ux, uy, uz = (wx + push) * damp, wy * damp, wz * damp
    base = 1.0 - 1.5 * (ux * ux + uy * uy + uz * uz)
    keep = 1.0 - 1.0 / RELAX
    gain = rho * (1.0 / RELAX)
    level = [gain * w for w in (8.0 / 27, 2.0 / 27, 1.0 / 54, 1.0 / 216)]
    along = combos(3.0 * ux, 3.0 * uy, 3.0 * uz)
    out = [None] * 27
    for i in range(13):
        j = 26 - i
        even = base + 0.5 * (along[i] * along[i])
        lift = level[NORM[i]]
        out[i] = jnp.where(solid, f[j], keep * f[i] + lift * (even + along[i]))
        out[j] = jnp.where(solid, f[i], keep * f[j] + lift * (even - along[i]))
    out[13] = jnp.where(solid, f[13], keep * f[13] + level[0] * base)
    return out


def pulled_moments(p):
    first = {}
    for a in (-1, 0, 1):
        for b in (-1, 0, 1):
            lo, mid, hi = (p[INDEX[(a, b, c)]] for c in (-1, 0, 1))
            both = lo + hi
            first[a, b] = (4.0 * mid + both, hi - lo, both)
    second = {}
    for a in (-1, 0, 1):
        lo, mid, hi = (first[a, b] for b in (-1, 0, 1))
        b0 = lo[0] + hi[0]
        b1 = lo[1] + hi[1]
        second[a] = dict(
            one=4.0 * mid[0] + b0,
            y=hi[0] - lo[0],
            yy=b0,
            z=4.0 * mid[1] + b1,
            yz=hi[1] - lo[1],
            zz=4.0 * mid[2] + lo[2] + hi[2],
        )
    lo, mid, hi = (second[a] for a in (-1, 0, 1))

    def full(key):
        return 4.0 * mid[key] + lo[key] + hi[key]

    xx = lo["one"] + hi["one"]
    return dict(
        one=4.0 * mid["one"] + xx,
        x=hi["one"] - lo["one"],
        xx=xx,
        y=full("y"),
        xy=hi["y"] - lo["y"],
        yy=full("yy"),
        z=full("z"),
        xz=hi["z"] - lo["z"],
        yz=full("yz"),
        zz=full("zz"),
    )


def adjoint_scalars(p, rho, wx, wy, wz, damp, push, solid):
    ux, uy, uz = (wx + push) * damp, wy * damp, wz * damp
    s = pulled_moments(p)
    scale = 1.0 / (216.0 * RELAX)
    one = s["one"] * scale
    b = [s[k] * (3.0 * scale) for k in ("x", "y", "z")]
    d = {k: s[k] * (9.0 * scale) for k in ("xx", "xy", "yy", "xz", "yz", "zz")}
    qx = d["xx"] * ux + d["xy"] * uy + d["xz"] * uz
    qy = d["xy"] * ux + d["yy"] * uy + d["yz"] * uz
    qz = d["xz"] * ux + d["yz"] * uy + d["zz"] * uz
    linear = b[0] * ux + b[1] * uy + b[2] * uz
    square = ux * ux + uy * uy + uz * uz
    even = one + linear + 0.5 * (qx * ux + qy * uy + qz * uz) - 1.5 * one * square
    three = 3.0 * one
    gx = (b[0] + qx - three * ux) * damp
    gy = (b[1] + qy - three * uy) * damp
    gz = (b[2] + qz - three * uz) * damp
    even = even - (gx * wx + gy * wy + gz * wz)
    porous = jnp.where(solid, 0.0, -rho * (gx * ux + gy * uy + gz * uz))
    return even, gx, gy, gz, porous


def adjoint_spread(p, even, gx, gy, gz, solid):
    keep = 1.0 - 1.0 / RELAX
    along = combos(gx, gy, gz)
    out = [None] * 27
    for i in range(13):
        j = 26 - i
        out[i] = jnp.where(solid, p[j], keep * p[i] + (even + along[i]))
        out[j] = jnp.where(solid, p[i], keep * p[j] + (even - along[i]))
    out[13] = jnp.where(solid, p[13], keep * p[13] + even)
    return out


def x_lines(g, sign, fields, side):
    lines = []
    for i in moving(fields, sign, 0, side):
        if side == 1:
            lines.append((i, g.rows - 1, (-1, g.rows + 1)))
            lines.append((i, g.rows - 2, (g.rows,)))
        else:
            lines += [(i, 0, (g.rows,)), (i, 1, (g.rows + 1,))]
    edge, target = (g.rows - 1, g.rows + 1) if side == 1 else (0, g.rows)
    return lines + [(i, edge, (target,)) for i in moving(fields, sign, 0, 0)]


def pack_x(g, buf, sign, fields, up, down):
    for side, ref in ((1, up), (-1, down)):
        for n, (i, r, _) in enumerate(x_lines(g, sign, fields, side)):
            ref[n * g.cols : (n + 1) * g.cols, :] = buf[
                pl.ds(g.at(i, 1, r), g.cols, stride=g.panel), :
            ]


def unpack_x(g, buf, sign, fields, up, down):
    for side, ref in ((1, up), (-1, down)):
        for n, (i, _, targets) in enumerate(x_lines(g, sign, fields, side)):
            value = ref[n * g.cols : (n + 1) * g.cols, :]
            for r in targets:
                buf[pl.ds(g.at(i, 1, r), g.cols, stride=g.panel), :] = value
    for i in moving(fields, sign, 0, -1):
        buf[pl.ds(g.at(i, 1, g.rows + 2), g.cols, stride=g.panel), :] = buf[
            pl.ds(g.at(i, 1, 0), g.cols, stride=g.panel), :
        ]


def halo_panels(g, i, sign):
    return (0, g.halo) if velocity(i, sign)[1] == 1 else (g.halo,)


def pack_corners(g, buf, sign, fields, up, down):
    for side, ref in ((1, up), (-1, down)):
        for n, (i, r, _) in enumerate(x_lines(g, sign, fields, side)):
            ref[n : n + 1, :] = buf[pl.ds(g.at(i, g.halo, r), 1), :]


def unpack_corners(g, buf, sign, fields, up, down):
    for side, ref in ((1, up), (-1, down)):
        for n, (i, _, targets) in enumerate(x_lines(g, sign, fields, side)):
            value = ref[n : n + 1, :]
            for r in targets:
                for k in halo_panels(g, i, sign):
                    buf[pl.ds(g.at(i, k, r), 1), :] = value
    for i in moving(fields, sign, 0, -1):
        for k in halo_panels(g, i, sign):
            buf[pl.ds(g.at(i, k, g.rows + 2), 1), :] = buf[pl.ds(g.at(i, k, 0), 1), :]


def still_pairs(fields, sign):
    still = moving(fields, sign, 1, 0)
    half = (len(still) + 1) // 2
    return [(still[n], still[n + half] if n + half < len(still) else None) for n in range(half)]


def y_slots(fields, sign):
    return 9 + len(still_pairs(fields, sign))


def pack_y(g, buf, sign, fields, high, up, down):
    for side, ref in ((1, up), (-1, down)):
        k = g.cols if side == 1 else 1
        for n, i in enumerate(moving(fields, sign, 1, side)):
            ref[n * g.rows : (n + 1) * g.rows, :] = buf[pl.ds(g.at(i, k, 0), g.rows), :]
        for n, (i, j) in enumerate(still_pairs(fields, sign)):
            value = buf[pl.ds(g.at(i, k, 0), g.rows), :]
            if j is not None:
                other = pltpu.roll(buf[pl.ds(g.at(j, k, 0), g.rows), :], NZ, 1)
                pair = (value, other) if side == 1 else (other, value)
                value = jnp.where(high, *pair)
            ref[(9 + n) * g.rows : (10 + n) * g.rows, :] = value


def unpack_y(g, buf, sign, fields, high, up, down):
    for side, ref in ((1, up), (-1, down)):
        for n, i in enumerate(moving(fields, sign, 1, side)):
            value = ref[n * g.rows : (n + 1) * g.rows, :]
            for k in halo_panels(g, i, sign):
                buf[pl.ds(g.at(i, k, 0), g.rows), :] = value
    for n, (i, j) in enumerate(still_pairs(fields, sign)):
        spot = slice((9 + n) * g.rows, (10 + n) * g.rows)
        before, after = up[spot, :], down[spot, :]
        buf[pl.ds(g.at(i, g.halo, 0), g.rows), :] = jnp.where(high, before, after)
        if j is not None:
            value = pltpu.roll(jnp.where(high, after, before), NZ, 1)
            buf[pl.ds(g.at(j, g.halo, 0), g.rows), :] = value


def by_parity(axis, first, second, act):
    even = lax.rem(lax.axis_index(axis), 2) == 0

    @pl.when(even)
    def _():
        act(first, second)

    @pl.when(jnp.logical_not(even))
    def _():
        act(second, first)


def load_fields(ref, rows, base, pieces, count):
    return [read_rows(ref, base + n * rows, pieces) for n in range(count)]


def save_fields(ref, rows, base, pieces, values):
    for n, value in enumerate(values):
        write_rows(ref, base + n * rows, pieces, value)


def save_populations(g, out, k, pieces, values):
    base = pl.multiple_of(k * g.panel, 8)
    for i, value in enumerate(values):
        write_rows(out, base + g.field(i), pieces, value)


def spot_of(g, k):
    return pl.multiple_of((k - 1) * g.rows, 8)


def lanes_of(k):
    return pl.ds(pl.multiple_of((k - 1) * LANES, LANES), LANES)


def every(first, last, act):
    def step(k, carry):
        act(k)
        return carry

    count = last + 1 - first
    unroll = max(n for n in (1, 2, 3, 4) if count % n == 0)
    lax.fori_loop(first, last + 1, step, 0, unroll=unroll)


def side_panels(g, act, count):
    def step(n, carry):
        act(jnp.where(n == 0, 1, g.cols - 1 + n))
        return carry

    lax.fori_loop(0, count, step, 0, unroll=count)


def interior_tiles(g, act):
    for pieces in g.inner:
        every(2, g.cols - 1, functools.partial(act, pieces=pieces))


def middle_tiles(g, act):
    for pieces in g.inner:
        side_panels(g, functools.partial(act, pieces=pieces), 3)
    every(2, g.cols - 1, functools.partial(act, pieces=g.outer))


def core_tiles(g, act):
    for pieces in g.inner:
        every(3, g.cols - 2, functools.partial(act, pieces=pieces))


def near_core_tiles(g, act):
    def step(n, carry):
        for pieces in g.inner:
            act(jnp.where(n == 0, 2, g.cols - 1), pieces=pieces)
        return carry

    lax.fori_loop(0, 2, step, 0, unroll=2)


def rim_tiles(g, act):
    every(1, g.cols, functools.partial(act, pieces=g.outer))
    for pieces in g.inner:
        side_panels(g, functools.partial(act, pieces=pieces), 2)


def step_tile(g, buf, out, sign, fields, masks, compute):
    def act(k, pieces):
        values = compute(
            pull_block(g, buf, sign, k, pieces, masks, fields), spot_of(g, k), pieces
        )
        save_populations(g, out, k, pieces, values)

    return act


def corner_tiles(g, buf, out, sign, fields, masks, compute):
    small = tuple(mask[:8] for mask in masks)
    act = step_tile(g, buf, out, sign, fields, masks, compute)
    side_panels(g, functools.partial(act, pieces=g.outer), 3)
    spot = g.halo * g.rows
    pieces = ((g.rows, 8),)
    values = compute(pull_block(g, buf, sign, g.halo, pieces, small, fields), spot, ((0, 8),))
    for i in range(27):
        dx = velocity(i, sign)[0]
        if dx == -1:
            out[pl.ds(g.at(i, g.halo, g.rows), 1), :] = values[i][0:1]
        elif dx == 1:
            out[pl.ds(g.at(i, g.halo, -1), 1), :] = values[i][1:2]
    edges = [pull_edge(g, buf, sign, side, small, fields) for side in (1, -1)]
    both = [stacked(pair) for pair in zip(*edges)]
    values = compute(both, spot, ((8, 16),))
    for i in moving(27, sign, 0, -1):
        out[pl.ds(g.at(i, 1, g.rows), g.cols, stride=g.panel), :] = values[i][:8]
    for i in moving(27, sign, 0, 1):
        out[pl.ds(g.at(i, 1, -1), g.cols, stride=g.panel), :] = values[i][8:]
    for i in moving(27, sign, 1, 1):
        out[pl.ds(g.at(i, 0, 0), g.rows), :] = out[pl.ds(g.at(i, g.halo, 0), g.rows), :]
        for r in (-1, g.rows):
            out[pl.ds(g.at(i, 0, r), 1), :] = out[pl.ds(g.at(i, g.halo, r), 1), :]


def flow_of(f):
    rho, mx, my, mz = moments(f)
    inverse = 1.0 / rho
    return inverse, rho, mx * inverse, my * inverse, mz * inverse


def collide_first(g, state, out):
    def act(k, pieces, f):
        base = pl.multiple_of(k * g.panel, 8)
        damp, push, wall = (read_rows(out, base + g.field(i), pieces) for i in (27, 28, 29))
        flow = flow_of(f)[1:] + (damp, push)
        save_fields(state, g.local, spot_of(g, k), pieces, flow + (wall,))
        save_populations(g, out, k, pieces, relax(f, *flow, wall > 0.5))

    return act


def collide_second(g, state):
    def compute(values, spot, pieces):
        f, (damp, push, wall) = values[:27], values[27:]
        flow = flow_of(f)[1:] + (damp, push)
        save_fields(state, g.extended, spot, pieces, flow + (wall,))
        return relax(f, *flow, wall > 0.5)

    return compute


def adjoint_second(g, state, total):
    def compute(p, spot, pieces):
        *flow, wall = load_fields(state, g.extended, spot, pieces, 7)
        *spread, porous = adjoint_scalars(p, *flow, wall > 0.5)
        save_fields(total, g.extended, spot, pieces, [porous])
        return adjoint_spread(p, *spread, wall > 0.5)

    return compute


def seed_tile(g, buf, adjoint, stage, out, masks):
    def act(k, pieces):
        f = pull_block(g, buf, 1, k, pieces, masks)
        for i in range(27):
            write_rows(stage.at[k - 1, i], 0, pieces, f[i])
        inverse, _, wx, wy, wz = flow_of(f)
        even = -(wx * wx + wy * wy + wz * wz) * inverse
        along = combos(wx * inverse, wy * inverse, wz * inverse)
        lanes = lanes_of(k)
        seeded = [
            stacked([adjoint[i, pl.ds(r, n), lanes] for r, n in pieces]) + even for i in range(27)
        ]
        for i in range(13):
            seeded[i] = seeded[i] + along[i]
            seeded[26 - i] = seeded[26 - i] - along[i]
        save_populations(g, out, k, pieces, seeded)

    return act


def block_of(ref, k):
    return ref.at[:, :, lanes_of(k)]


def pack_faces(g, buf, sign, fields, x_first, x_second, y_first, y_second):
    high = lane_masks(g.rows)[0]
    by_parity("gx", x_first, x_second, functools.partial(pack_x, g, buf, sign, fields))
    by_parity("gy", y_first, y_second, functools.partial(pack_y, g, buf, sign, fields, high))


def rim_first_kernel(g, pops, *refs):
    flat, (out, state, stage, *faces), near, (sems, flat_sems) = (
        refs[:3],
        refs[3:10],
        refs[10:13],
        refs[13:],
    )
    porosity, solid, labels = near

    def copy(k, r, n):
        rows = pl.ds(r, n)
        source = pops.at[:, rows, lanes_of(k)]
        part = 0 if r == 0 else 2 if r + n == g.rows else 1
        return pltpu.make_async_copy(source, stage.at[k - 1, :, rows], sems.at[k - 1, part])

    middle = (8, g.rows - 16)
    flat_copies = [
        pltpu.make_async_copy(source, target, flat_sems.at[n])
        for n, (source, target) in enumerate(zip(flat, near))
    ]
    for each in flat_copies:
        each.start()
    for k in range(1, g.cols + 1):
        for piece in g.outer:
            copy(k, *piece).start()
    for k in (1, g.cols, *range(2, g.cols)):
        copy(k, *middle).start()
    for each in flat_copies:
        each.wait()

    def fields_of(k):
        lanes = lanes_of(k)
        label = labels[:, lanes]
        damp = 1.0 / (1.0 + porosity[:, lanes])
        push = jnp.where(label == 1, PUSH, jnp.where(label == 2, -PUSH, 0.0))
        base = pl.multiple_of(k * g.panel, 8)
        for i, value in ((27, damp), (28, push), (29, solid[:, lanes].astype(F32))):
            out[pl.ds(base + g.field(i), g.rows), :] = value

    every(1, g.cols, fields_of)
    collide = collide_first(g, state, out)

    def act(k, pieces):
        collide(k, pieces, [read_rows(stage.at[k - 1, i], 0, pieces) for i in range(27)])

    def column(k):
        for piece in g.outer:
            copy(k, *piece).wait()
        act(k, g.outer)

    every(1, g.cols, column)
    for k in (1, g.cols):
        copy(k, *middle).wait()
    for pieces in g.inner:
        side_panels(g, functools.partial(act, pieces=pieces), 2)
    pack_faces(g, out, 1, 30, *faces)
    for k in range(2, g.cols):
        copy(k, *middle).wait()


def inner_first_kernel(g, _, _state, stage, post, state0, out, state1):
    masks = lane_masks(16)
    collide = collide_first(g, state0, post)

    def act(k, pieces):
        collide(k, pieces, [read_rows(stage.at[k - 1, i], 0, pieces) for i in range(27)])

    interior_tiles(g, act)
    interior_tiles(g, step_tile(g, post, out, 1, 30, masks, collide_second(g, state1)))


def relay_kernel(g, sign, fields, _, y_second, y_first, buf, first, second):
    high = lane_masks(g.rows)[0]
    by_parity("gy", y_second, y_first, functools.partial(unpack_y, g, buf, sign, fields, high))
    by_parity("gx", first, second, functools.partial(pack_corners, g, buf, sign, fields))


def middle_second_kernel(g, adjoint, post, out, state1, stage, field, x_second, x_first):
    masks = lane_masks(16)
    by_parity("gx", x_second, x_first, functools.partial(unpack_x, g, post, 1, 30))
    middle_tiles(g, step_tile(g, post, out, 1, 30, masks, collide_second(g, state1)))
    core_tiles(g, seed_tile(g, out, adjoint, stage, field, masks))


def rim_seed_kernel(g, _post, _out, _state, _stage, _field, first, second, adjoint, *refs):
    post, out, state1, stage, field, *faces = refs
    masks = lane_masks(16)
    by_parity("gx", second, first, functools.partial(unpack_corners, g, post, 1, 30))
    corner_tiles(g, post, out, 1, 30, masks, collide_second(g, state1))
    rim_tiles(g, seed_tile(g, out, adjoint, stage, field, masks))
    pack_faces(g, field, -1, 27, *faces)


def inner_seed_kernel(
    g, post, _stage, _field, state1, adjoint, stage, field, out, total, final, sems
):
    masks = lane_masks(16)

    def copy(k):
        return pltpu.make_async_copy(stage.at[k - 1], block_of(final, k), sems.at[k - 1])

    copy(1).start()
    copy(g.cols).start()
    seed = seed_tile(g, post, adjoint, stage, field, masks)

    near_core_tiles(g, seed)
    every(2, g.cols - 1, lambda k: copy(k).start())
    interior_tiles(g, step_tile(g, field, out, -1, 27, masks, adjoint_second(g, state1, total)))
    every(1, g.cols, lambda k: copy(k).wait())


def total_tile(g, out, before, state0, total, parts, masks):
    def act(k, pieces):
        p = pull_block(g, out, -1, k, pieces, masks)
        spot = spot_of(g, k)
        *flow, wall = load_fields(state0, g.local, spot, pieces, 7)
        *spread, porous = adjoint_scalars(p, *flow, wall > 0.5)
        here = load_fields(before, g.extended, spot, pieces, 1)[0] + porous
        save_fields(total, g.local, spot, pieces, [here])
        save_fields(parts, g.local, spot, pieces, spread + [wall])

    return act


def middle_adjoint_kernel(g, field, out, before, total, parts, state1, state0, x_second, x_first):
    masks = lane_masks(16)
    by_parity("gx", x_second, x_first, functools.partial(unpack_x, g, field, -1, 27))
    middle_tiles(g, step_tile(g, field, out, -1, 27, masks, adjoint_second(g, state1, before)))
    core_tiles(g, total_tile(g, out, before, state0, total, parts, masks))


def total_kernel(g, *refs):
    state1, state0, first, second, field, out, before, total, parts, peak = refs[5:]
    masks = lane_masks(16)
    by_parity("gx", second, first, functools.partial(unpack_corners, g, field, -1, 27))
    corner_tiles(g, field, out, -1, 27, masks, adjoint_second(g, state1, before))
    act = total_tile(g, out, before, state0, total, parts, masks)
    near_core_tiles(g, act)
    rim_tiles(g, act)
    size = 8 * (g.local // 64)
    largest = jnp.zeros((8, LANES), F32)
    for start in range(0, g.local, size):
        value = jnp.abs(total[start : start + size, :]).reshape(-1, 8, LANES)
        largest = jnp.maximum(largest, jnp.max(value, 0))
    peak[...] = largest


def adjoint_kernel(g, first, last, buf, parts, result, stage, sems):
    masks = lane_masks(16)

    def copy(k):
        return pltpu.make_async_copy(stage.at[k - first], block_of(result, k), sems.at[k - first])

    def column(k):
        for pieces in (g.outer,) + g.inner:
            p = pull_block(g, buf, -1, k, pieces, masks)
            *spread, wall = load_fields(parts, g.local, spot_of(g, k), pieces, 5)
            for i, value in enumerate(adjoint_spread(p, *spread, wall > 0.5)):
                write_rows(stage.at[k - first, i], 0, pieces, value)
        copy(k).start()

    every(first, last, column)
    every(first, last, lambda k: copy(k).wait())


def scale_kernel(g, total, peak, out):
    largest = jnp.max(peak[...])
    factor = 1.0 / (jnp.full((g.rows, LANES), largest, F32) + EPS)
    for c in range(g.cols):
        value = total[c * g.rows : (c + 1) * g.rows, :] * factor
        out[:, c * LANES : (c + 1) * LANES] = value


def swap_pairs(count, start):
    pairs = []
    for i in range(start, count, 2):
        j = (i + 1) % count
        pairs += [(i, j), (j, i)]
    return pairs


def swap(axis, count, first, second):
    return (
        lax.ppermute(first, axis, swap_pairs(count, 0)),
        lax.ppermute(second, axis, swap_pairs(count, 1)),
    )


def largest_of_all(peak, sizes, beside):
    groups = 0
    for axis, count, widths in (("gy", sizes[1], (2, 4, 4)), ("gx", sizes[0], (4, 2))):
        step = 1
        for width in widths:
            width = min(width, count // step)
            parts = [
                lax.ppermute(peak, axis, [(i, i ^ (n * step)) for i in range(count)])
                for n in range(1, width)
            ]
            groups += 1
            if groups == 2:
                peak = beside(peak)
            peak = functools.reduce(jnp.maximum, parts, peak)
            step *= width
    return peak


def on_device(sizes, populations, adjoint_in, porosity, solid, labels):
    rows, width = porosity.shape
    g = Grid(rows, width)
    in_vmem = pl.BlockSpec(memory_space=pltpu.VMEM)
    in_hbm = pl.BlockSpec(memory_space=pltpu.HBM)
    nx, ny = sizes

    def vmem(*shape):
        return pltpu.VMEM(shape, F32)

    def fields(count, size):
        return vmem(count * size, LANES)

    def padded(count):
        return vmem(*g.padded(count))

    def faces(count, sign):
        along_x = vmem(count * g.cols, LANES)
        along_y = vmem(y_slots(count, sign) * rows, LANES)
        return [along_x, along_x, along_y, along_y]

    def corners(count):
        return [vmem(-(-count // 8) * 8, LANES)] * 2

    whole = pltpu.HBM(populations.shape, F32)
    stage = vmem(g.cols, 27, rows, LANES)
    sems = pltpu.SemaphoreType.DMA((g.cols,))

    def call(name, kernel, operands, out_shape, scratch=(), kept=0, load=0, result=None):
        out_shape = [pltpu.VMEM(x.shape, x.dtype) for x in operands[:kept]] + out_shape
        aliases = {n: n for n in range(kept)}
        space = pltpu.HBM if name == "rim_first" else pltpu.VMEM
        pinned = [pltpu.with_memory_space_constraint(x, space) for x in operands]
        in_specs = [pl.BlockSpec(memory_space=space)] * len(operands)
        if result is not None:
            aliases[len(operands)] = len(out_shape) - 1
            pinned.append(pltpu.with_memory_space_constraint(result, pltpu.HBM))
            in_specs.append(in_hbm)
        return pl.pallas_call(
            functools.partial(kernel, g),
            in_specs=in_specs,
            out_shape=out_shape,
            out_specs=[in_hbm if x is whole else in_vmem for x in out_shape],
            scratch_shapes=list(scratch),
            input_output_aliases=aliases,
            compiler_params=pltpu.CompilerParams(vmem_limit_bytes=VMEM_LIMIT),
            cost_estimate=pl.CostEstimate(flops=0, bytes_accessed=load, transcendentals=0)
            if load
            else None,
            name=name,
        )(*pinned)

    def swap_faces(parcels):
        x_first, x_second = swap("gx", nx, *parcels[:2])
        y_first, y_second = swap("gy", ny, *parcels[2:])
        return [x_second, x_first], [y_second, y_first]

    def relay(buf, parcels, sign, count):
        def kernel(grid, *refs):
            relay_kernel(grid, sign, count, *refs)

        buf, *parcels = call("relay", kernel, [buf, *parcels], corners(count), kept=1)
        return buf, swap("gx", nx, *parcels)

    post, state0, staged, *parcels = call(
        "rim_first",
        rim_first_kernel,
        [populations, porosity, solid, labels],
        [padded(30), fields(7, g.local), stage] + faces(30, 1),
        [vmem(*porosity.shape)]
        + [pltpu.VMEM(porosity.shape, jnp.int32)] * 2
        + [pltpu.SemaphoreType.DMA((g.cols, 3)), pltpu.SemaphoreType.DMA((3,))],
    )
    along_x, along_y = swap_faces(parcels)
    post, state0, second, state1 = call(
        "inner_first",
        inner_first_kernel,
        [post, state0, staged],
        [padded(27), fields(7, g.extended)],
        kept=2,
        load=FLIGHT,
    )
    post, parcels = relay(post, along_y, 1, 30)
    post, second, state1, staged, field = call(
        "middle_second",
        lambda grid, _post, _out, _state, b, a, source, *refs: middle_second_kernel(
            grid, source, *refs, b, a
        ),
        [post, second, state1, *along_x, adjoint_in],
        [stage, padded(27)],
        kept=3,
        load=FLIGHT,
    )
    _, second, state1, staged, field, *parcels = call(
        "rim_seed",
        rim_seed_kernel,
        [post, second, state1, staged, field, *parcels, adjoint_in],
        faces(27, -1),
        kept=5,
    )
    along_x, along_y = swap_faces(parcels)
    _, field, pulled, before, final = call(
        "inner_seed",
        lambda grid, kept, into, buf, *refs: inner_seed_kernel(grid, buf, kept, into, *refs),
        [staged, field, second, state1, adjoint_in],
        [padded(27), fields(1, g.extended), whole],
        [sems],
        kept=2,
        load=FLIGHT,
    )
    field, parcels = relay(field, along_y, -1, 27)
    field, pulled, before, total, parts = call(
        "middle_adjoint",
        lambda grid, _field, _out, _before, near, far, b, a, *refs: middle_adjoint_kernel(
            grid, *refs, near, far, b, a
        ),
        [field, pulled, before, state1, state0, *along_x],
        [fields(1, g.local), fields(5, g.local)],
        kept=3,
        load=FLIGHT,
    )
    _, pulled, _, total, parts, peak = call(
        "total",
        total_kernel,
        [field, pulled, before, total, parts, state1, state0, *parcels],
        [vmem(8, LANES)],
        kept=5,
    )
    half = g.cols // 2
    scratch = [vmem(half, 27, rows, LANES), pltpu.SemaphoreType.DMA((half,))]
    halves = []

    def first_half(peak):
        def kernel(grid, buf, fields, near, echo, *refs):
            echo[...] = near[...]
            adjoint_kernel(grid, 1, half, buf, fields, *refs)

        echo, result = call(
            "adjoint_low",
            kernel,
            [pulled, parts, peak],
            [vmem(8, LANES), whole],
            scratch,
            load=FLIGHT // 2,
        )
        halves.append(result)
        return echo

    largest = largest_of_all(peak, sizes, first_half)
    (adjoint_out,) = call(
        "adjoint_high",
        lambda grid, buf, fields, _, *refs: adjoint_kernel(
            grid, 1 + half, g.cols, buf, fields, *refs
        ),
        [pulled, parts],
        [whole],
        scratch,
        load=FLIGHT // 2,
        result=halves[0],
    )
    (sensitivity,) = call(
        "normalize",
        scale_kernel,
        [total, largest],
        [jax.ShapeDtypeStruct(porosity.shape, F32)],
    )
    return final, adjoint_out, sensitivity


def solution(mesh):
    sizes = (mesh.shape["gx"], mesh.shape["gy"])
    whole, flat = P(None, "gx", "gy"), P("gx", "gy")
    return jax.shard_map(
        functools.partial(on_device, sizes),
        mesh=mesh,
        in_specs=(whole, whole, flat, flat, flat),
        out_specs=(whole, whole, flat),
        check_vma=False,
    )
```

```python
import functools

import jax
import jax.numpy as jnp
from jax import lax
from jax.experimental import pallas as pl
from jax.experimental.pallas import tpu as pltpu
from jax.sharding import PartitionSpec as P

NZ = 64
RELAX = 0.8
PUSH = 0.2
EPS = 1e-06
LANES = 128
VELOCITY = [(a, b, c) for a in (-1, 0, 1) for b in (-1, 0, 1) for c in (-1, 0, 1)]
INDEX = {v: i for i, v in enumerate(VELOCITY)}
WEIGHT = [
    [8.0 / 27, 2.0 / 27, 1.0 / 54, 1.0 / 216][abs(v[0]) + abs(v[1]) + abs(v[2])]
    for v in VELOCITY
]
NORM = [abs(v[0]) + abs(v[1]) + abs(v[2]) for v in VELOCITY]
F32 = jnp.float32
VMEM_LIMIT = 6 * 1024 * 1024
FLIGHT = 12 * 1024 * 1024


class Grid:
    def __init__(self, rows, width):
        self.rows = rows
        self.cols = width // LANES
        self.panel = rows + 16
        self.halo = self.cols + 1
        self.local = self.cols * rows
        self.extended = self.halo * rows + 24
        self.outer = ((0, 8), (rows - 8, 8))
        self.inner = tuple(((r, 16),) for r in range(8, rows - 8, 16))

    def at(self, i, k, r):
        return self.field(i) + k * self.panel + r

    def field(self, i):
        return i * (self.cols + 2) * self.panel + 8

    def padded(self, fields):
        return (fields * (self.cols + 2) * self.panel + 8, LANES)


def velocity(i, sign):
    return tuple(sign * n for n in VELOCITY[i]) if i < 27 else (0, 0, 0)


def moving(fields, sign, axis, side):
    return [i for i in range(fields) if velocity(i, sign)[axis] == side]


def lane_masks(height):
    lane = lax.broadcasted_iota(jnp.int32, (height, LANES), 1)
    return lane >= NZ, lane % NZ == 0, lane % NZ == NZ - 1


def shift_lanes(here, d, masks):
    first, last = masks[1:]
    dy, dz = d[1:]
    if dz == 0:
        return here if dy == 0 else pltpu.roll(here, NZ, 1)
    if dz == 1:
        one, other, edge = 1, NZ + 1, first
    else:
        one, other, edge = LANES - 1, NZ - 1, last
    inner, wrapped = (one, other) if dy == 0 else (other, one)
    return jnp.where(edge, pltpu.roll(here, wrapped, 1), pltpu.roll(here, inner, 1))


def pull(load, d, masks):
    high = masks[0]
    here = load(0)
    if d[1] == 1:
        here = jnp.where(high, load(-1), here)
    elif d[1] == -1:
        here = jnp.where(high, here, load(1))
    return shift_lanes(here, d, masks)


def stacked(parts):
    return parts[0] if len(parts) == 1 else jnp.concatenate(parts, 0)


def read_rows(ref, base, pieces):
    return stacked([ref[pl.ds(base + r, n), :] for r, n in pieces])


def write_rows(ref, base, pieces, value):
    done = 0
    for r, n in pieces:
        ref[pl.ds(base + r, n), :] = value[done : done + n]
        done += n


def pull_block(g, buf, sign, k, pieces, masks, fields=27):
    base = pl.multiple_of(k * g.panel, 8)
    after = pl.multiple_of(jnp.where(k == g.halo, g.panel, base + g.panel), 8)
    out = []
    for i in range(fields):
        d = velocity(i, sign)

        def load(n, i=i, d=d):
            start = {-1: base - g.panel, 0: base, 1: after}[n]
            return read_rows(buf, start + (g.field(i) - d[0]), pieces)

        out.append(pull(load, d, masks))
    return out


def pull_edge(g, buf, sign, side, masks, fields=27):
    out = []
    for i in range(fields):
        d = velocity(i, sign)
        if side == 1:
            row = g.rows - d[0]
        else:
            row = {1: g.rows, 0: g.rows + 1, -1: 0}[d[0]]

        def load(n, i=i, row=row):
            return buf[pl.ds(g.at(i, 1 + n, row), g.cols, stride=g.panel), :]

        out.append(pull(load, d, masks))
    return out


def moments(f):
    flat = {}
    along_z = None
    for a in (-1, 0, 1):
        for b in (-1, 0, 1):
            lo, mid, hi = (f[INDEX[(a, b, c)]] for c in (-1, 0, 1))
            flat[a, b] = lo + mid + hi
            diff = hi - lo
            along_z = diff if along_z is None else along_z + diff
    line = {}
    along_y = None
    for a in (-1, 0, 1):
        line[a] = flat[a, -1] + flat[a, 0] + flat[a, 1]
        diff = flat[a, 1] - flat[a, -1]
        along_y = diff if along_y is None else along_y + diff
    return line[-1] + line[0] + line[1], line[1] - line[-1], along_y, along_z


def combos(x, y, z):
    plane = {}
    for a in (-1, 0, 1):
        for b in (-1, 0, 1):
            if (a, b) > (0, 0):
                continue
            if a == 0:
                plane[a, b] = -y if b else None
            else:
                plane[a, b] = -x if b == 0 else (-x - y if b < 0 else y - x)
    out = []
    for a, b, c in VELOCITY[:13]:
        base = plane[a, b]
        if base is None:
            out.append(-z)
        else:
            out.append(base if c == 0 else (base - z if c < 0 else base + z))
    return out


def relax(f, rho, wx, wy, wz, damp, push, solid):
    ux, uy, uz = (wx + push) * damp, wy * damp, wz * damp
    base = 1.0 - 1.5 * (ux * ux + uy * uy + uz * uz)
    keep = 1.0 - 1.0 / RELAX
    gain = rho * (1.0 / RELAX)
    level = [gain * w for w in (8.0 / 27, 2.0 / 27, 1.0 / 54, 1.0 / 216)]
    along = combos(3.0 * ux, 3.0 * uy, 3.0 * uz)
    out = [None] * 27
    for i in range(13):
        j = 26 - i
        even = base + 0.5 * (along[i] * along[i])
        lift = level[NORM[i]]
        out[i] = jnp.where(solid, f[j], keep * f[i] + lift * (even + along[i]))
        out[j] = jnp.where(solid, f[i], keep * f[j] + lift * (even - along[i]))
    out[13] = jnp.where(solid, f[13], keep * f[13] + level[0] * base)
    return out


def pulled_moments(p):
    first = {}
    for a in (-1, 0, 1):
        for b in (-1, 0, 1):
            lo, mid, hi = (p[INDEX[(a, b, c)]] for c in (-1, 0, 1))
            both = lo + hi
            first[a, b] = (4.0 * mid + both, hi - lo, both)
    second = {}
    for a in (-1, 0, 1):
        lo, mid, hi = (first[a, b] for b in (-1, 0, 1))
        b0 = lo[0] + hi[0]
        b1 = lo[1] + hi[1]
        second[a] = dict(
            one=4.0 * mid[0] + b0,
            y=hi[0] - lo[0],
            yy=b0,
            z=4.0 * mid[1] + b1,
            yz=hi[1] - lo[1],
            zz=4.0 * mid[2] + lo[2] + hi[2],
        )
    lo, mid, hi = (second[a] for a in (-1, 0, 1))

    def full(key):
        return 4.0 * mid[key] + lo[key] + hi[key]

    xx = lo["one"] + hi["one"]
    return dict(
        one=4.0 * mid["one"] + xx,
        x=hi["one"] - lo["one"],
        xx=xx,
        y=full("y"),
        xy=hi["y"] - lo["y"],
        yy=full("yy"),
        z=full("z"),
        xz=hi["z"] - lo["z"],
        yz=full("yz"),
        zz=full("zz"),
    )


def adjoint_scalars(p, rho, wx, wy, wz, damp, push, solid):
    ux, uy, uz = (wx + push) * damp, wy * damp, wz * damp
    s = pulled_moments(p)
    scale = 1.0 / (216.0 * RELAX)
    one = s["one"] * scale
    b = [s[k] * (3.0 * scale) for k in ("x", "y", "z")]
    d = {k: s[k] * (9.0 * scale) for k in ("xx", "xy", "yy", "xz", "yz", "zz")}
    qx = d["xx"] * ux + d["xy"] * uy + d["xz"] * uz
    qy = d["xy"] * ux + d["yy"] * uy + d["yz"] * uz
    qz = d["xz"] * ux + d["yz"] * uy + d["zz"] * uz
    linear = b[0] * ux + b[1] * uy + b[2] * uz
    square = ux * ux + uy * uy + uz * uz
    even = one + linear + 0.5 * (qx * ux + qy * uy + qz * uz) - 1.5 * one * square
    three = 3.0 * one
    gx = (b[0] + qx - three * ux) * damp
    gy = (b[1] + qy - three * uy) * damp
    gz = (b[2] + qz - three * uz) * damp
    even = even - (gx * wx + gy * wy + gz * wz)
    porous = jnp.where(solid, 0.0, -rho * (gx * ux + gy * uy + gz * uz))
    return even, gx, gy, gz, porous


def adjoint_spread(p, even, gx, gy, gz, solid):
    keep = 1.0 - 1.0 / RELAX
    along = combos(gx, gy, gz)
    out = [None] * 27
    for i in range(13):
        j = 26 - i
        out[i] = jnp.where(solid, p[j], keep * p[i] + (even + along[i]))
        out[j] = jnp.where(solid, p[i], keep * p[j] + (even - along[i]))
    out[13] = jnp.where(solid, p[13], keep * p[13] + even)
    return out


def x_lines(g, sign, fields, side):
    lines = []
    for i in moving(fields, sign, 0, side):
        if side == 1:
            lines.append((i, g.rows - 1, (-1, g.rows + 1)))
            lines.append((i, g.rows - 2, (g.rows,)))
        else:
            lines += [(i, 0, (g.rows,)), (i, 1, (g.rows + 1,))]
    edge, target = (g.rows - 1, g.rows + 1) if side == 1 else (0, g.rows)
    return lines + [(i, edge, (target,)) for i in moving(fields, sign, 0, 0)]


def pack_x(g, buf, sign, fields, up, down):
    for side, ref in ((1, up), (-1, down)):
        for n, (i, r, _) in enumerate(x_lines(g, sign, fields, side)):
            ref[n * g.cols : (n + 1) * g.cols, :] = buf[
                pl.ds(g.at(i, 1, r), g.cols, stride=g.panel), :
            ]


def unpack_x(g, buf, sign, fields, up, down):
    for side, ref in ((1, up), (-1, down)):
        for n, (i, _, targets) in enumerate(x_lines(g, sign, fields, side)):
            value = ref[n * g.cols : (n + 1) * g.cols, :]
            for r in targets:
                buf[pl.ds(g.at(i, 1, r), g.cols, stride=g.panel), :] = value
    for i in moving(fields, sign, 0, -1):
        buf[pl.ds(g.at(i, 1, g.rows + 2), g.cols, stride=g.panel), :] = buf[
            pl.ds(g.at(i, 1, 0), g.cols, stride=g.panel), :
        ]


def halo_panels(g, i, sign):
    return (0, g.halo) if velocity(i, sign)[1] == 1 else (g.halo,)


def still_pairs(fields, sign):
    still = moving(fields, sign, 1, 0)
    half = (len(still) + 1) // 2
    return [(still[n], still[n + half] if n + half < len(still) else None) for n in range(half)]


def y_slots(fields, sign):
    return 9 + len(still_pairs(fields, sign))


def y_slot(g, n, part):
    return (2 * n, g.rows, 2) if part == "corner" else (n * g.rows, 0, g.rows)


def pack_y(g, buf, sign, fields, part, up, down):
    for side, ref in ((1, up), (-1, down)):
        k = g.cols if side == 1 else 1
        for n, i in enumerate(moving(fields, sign, 1, side)):
            to, r, count = y_slot(g, n, part)
            ref[to : to + count, :] = buf[pl.ds(g.at(i, k, r), count), :]
        for n, (i, j) in enumerate(still_pairs(fields, sign)):
            to, r, count = y_slot(g, 9 + n, part)
            value = buf[pl.ds(g.at(i, k, r), count), :]
            if j is not None:
                other = pltpu.roll(buf[pl.ds(g.at(j, k, r), count), :], NZ, 1)
                pair = (value, other) if side == 1 else (other, value)
                value = jnp.where(lane_masks(count)[0], *pair)
            ref[to : to + count, :] = value


def unpack_y(g, buf, sign, fields, part, up, down):
    for side, ref in ((1, up), (-1, down)):
        for n, i in enumerate(moving(fields, sign, 1, side)):
            to, r, count = y_slot(g, n, part)
            value = ref[to : to + count, :]
            for k in halo_panels(g, i, sign):
                buf[pl.ds(g.at(i, k, r), count), :] = value
    for n, (i, j) in enumerate(still_pairs(fields, sign)):
        to, r, count = y_slot(g, 9 + n, part)
        high = lane_masks(count)[0]
        before, after = up[to : to + count, :], down[to : to + count, :]
        buf[pl.ds(g.at(i, g.halo, r), count), :] = jnp.where(high, before, after)
        if j is not None:
            value = pltpu.roll(jnp.where(high, after, before), NZ, 1)
            buf[pl.ds(g.at(j, g.halo, r), count), :] = value
    if part != "corner":
        return
    for i in moving(fields, sign, 0, 1):
        for k in halo_panels(g, i, sign):
            buf[pl.ds(g.at(i, k, -1), 1), :] = buf[pl.ds(g.at(i, k, g.rows + 1), 1), :]
    for i in moving(fields, sign, 0, -1):
        for k in halo_panels(g, i, sign):
            buf[pl.ds(g.at(i, k, g.rows + 2), 1), :] = buf[pl.ds(g.at(i, k, 0), 1), :]


def by_parity(axis, first, second, act):
    even = lax.rem(lax.axis_index(axis), 2) == 0

    @pl.when(even)
    def _():
        act(first, second)

    @pl.when(jnp.logical_not(even))
    def _():
        act(second, first)


def load_fields(ref, rows, base, pieces, count):
    return [read_rows(ref, base + n * rows, pieces) for n in range(count)]


def save_fields(ref, rows, base, pieces, values):
    for n, value in enumerate(values):
        write_rows(ref, base + n * rows, pieces, value)


def save_populations(g, out, k, pieces, values):
    base = pl.multiple_of(k * g.panel, 8)
    for i, value in enumerate(values):
        write_rows(out, base + g.field(i), pieces, value)


def spot_of(g, k):
    return pl.multiple_of((k - 1) * g.rows, 8)


def lanes_of(k):
    return pl.ds(pl.multiple_of((k - 1) * LANES, LANES), LANES)


def every(first, last, act):
    def step(k, carry):
        act(k)
        return carry

    count = last + 1 - first
    unroll = max(n for n in (1, 2, 3, 4) if count % n == 0)
    lax.fori_loop(first, last + 1, step, 0, unroll=unroll)


def side_panels(g, act, count):
    def step(n, carry):
        act(jnp.where(n == 0, 1, g.cols - 1 + n))
        return carry

    lax.fori_loop(0, count, step, 0, unroll=count)


def interior_tiles(g, act):
    for pieces in g.inner:
        every(2, g.cols - 1, functools.partial(act, pieces=pieces))


def middle_tiles(g, act):
    for pieces in g.inner:
        side_panels(g, functools.partial(act, pieces=pieces), 3)
    every(2, g.cols - 1, functools.partial(act, pieces=g.outer))


def core_tiles(g, act):
    for pieces in g.inner:
        every(3, g.cols - 2, functools.partial(act, pieces=pieces))


def near_core_tiles(g, act):
    def step(n, carry):
        for pieces in g.inner:
            act(jnp.where(n == 0, 2, g.cols - 1), pieces=pieces)
        return carry

    lax.fori_loop(0, 2, step, 0, unroll=2)


def rim_tiles(g, act):
    every(1, g.cols, functools.partial(act, pieces=g.outer))
    for pieces in g.inner:
        side_panels(g, functools.partial(act, pieces=pieces), 2)


def step_tile(g, buf, out, sign, fields, masks, compute):
    def act(k, pieces):
        values = compute(
            pull_block(g, buf, sign, k, pieces, masks, fields), spot_of(g, k), pieces
        )
        save_populations(g, out, k, pieces, values)

    return act


def corner_tiles(g, buf, out, sign, fields, masks, compute):
    small = tuple(mask[:8] for mask in masks)
    act = step_tile(g, buf, out, sign, fields, masks, compute)
    side_panels(g, functools.partial(act, pieces=g.outer), 3)
    spot = g.halo * g.rows
    pieces = ((g.rows, 8),)
    values = compute(pull_block(g, buf, sign, g.halo, pieces, small, fields), spot, ((0, 8),))
    for i in range(27):
        dx = velocity(i, sign)[0]
        if dx == -1:
            out[pl.ds(g.at(i, g.halo, g.rows), 1), :] = values[i][0:1]
        elif dx == 1:
            out[pl.ds(g.at(i, g.halo, -1), 1), :] = values[i][1:2]
    edges = [pull_edge(g, buf, sign, side, small, fields) for side in (1, -1)]
    both = [stacked(pair) for pair in zip(*edges)]
    values = compute(both, spot, ((8, 16),))
    for i in moving(27, sign, 0, -1):
        out[pl.ds(g.at(i, 1, g.rows), g.cols, stride=g.panel), :] = values[i][:8]
    for i in moving(27, sign, 0, 1):
        out[pl.ds(g.at(i, 1, -1), g.cols, stride=g.panel), :] = values[i][8:]
    for i in moving(27, sign, 1, 1):
        out[pl.ds(g.at(i, 0, 0), g.rows), :] = out[pl.ds(g.at(i, g.halo, 0), g.rows), :]
        for r in (-1, g.rows):
            out[pl.ds(g.at(i, 0, r), 1), :] = out[pl.ds(g.at(i, g.halo, r), 1), :]


def flow_of(f):
    rho, mx, my, mz = moments(f)
    inverse = 1.0 / rho
    return inverse, rho, mx * inverse, my * inverse, mz * inverse


def collide_first(g, state, out):
    def act(k, pieces, f):
        base = pl.multiple_of(k * g.panel, 8)
        damp, push, wall = (read_rows(out, base + g.field(i), pieces) for i in (27, 28, 29))
        flow = flow_of(f)[1:] + (damp, push)
        save_fields(state, g.local, spot_of(g, k), pieces, flow + (wall,))
        save_populations(g, out, k, pieces, relax(f, *flow, wall > 0.5))

    return act


def collide_second(g, state):
    def compute(values, spot, pieces):
        f, (damp, push, wall) = values[:27], values[27:]
        flow = flow_of(f)[1:] + (damp, push)
        save_fields(state, g.extended, spot, pieces, flow + (wall,))
        return relax(f, *flow, wall > 0.5)

    return compute


def adjoint_second(g, state, total):
    def compute(p, spot, pieces):
        *flow, wall = load_fields(state, g.extended, spot, pieces, 7)
        *spread, porous = adjoint_scalars(p, *flow, wall > 0.5)
        save_fields(total, g.extended, spot, pieces, [porous])
        return adjoint_spread(p, *spread, wall > 0.5)

    return compute


def seed_tile(g, buf, adjoint, stage, out, masks):
    def act(k, pieces):
        f = pull_block(g, buf, 1, k, pieces, masks)
        for i in range(27):
            write_rows(stage.at[k - 1, i], 0, pieces, f[i])
        inverse, _, wx, wy, wz = flow_of(f)
        even = -(wx * wx + wy * wy + wz * wz) * inverse
        along = combos(wx * inverse, wy * inverse, wz * inverse)
        lanes = lanes_of(k)
        seeded = [
            stacked([adjoint[i, pl.ds(r, n), lanes] for r, n in pieces]) + even for i in range(27)
        ]
        for i in range(13):
            seeded[i] = seeded[i] + along[i]
            seeded[26 - i] = seeded[26 - i] - along[i]
        save_populations(g, out, k, pieces, seeded)

    return act


def block_of(ref, k):
    return ref.at[:, :, lanes_of(k)]


def pack_faces(g, buf, sign, fields, x_first, x_second, y_first, y_second):
    by_parity("gx", x_first, x_second, functools.partial(pack_x, g, buf, sign, fields))
    by_parity("gy", y_first, y_second, functools.partial(pack_y, g, buf, sign, fields, "face"))


def rim_first_kernel(g, pops, *refs):
    flat, (out, state, stage, *faces), near, (sems, flat_sems) = (
        refs[:3],
        refs[3:10],
        refs[10:13],
        refs[13:],
    )
    porosity, solid, labels = near

    def copy(k, r, n):
        rows = pl.ds(r, n)
        source = pops.at[:, rows, lanes_of(k)]
        part = 0 if r == 0 else 2 if r + n == g.rows else 1
        return pltpu.make_async_copy(source, stage.at[k - 1, :, rows], sems.at[k - 1, part])

    middle = (8, g.rows - 16)
    flat_copies = [
        pltpu.make_async_copy(source, target, flat_sems.at[n])
        for n, (source, target) in enumerate(zip(flat, near))
    ]
    for each in flat_copies:
        each.start()
    for k in range(1, g.cols + 1):
        for piece in g.outer:
            copy(k, *piece).start()
    for k in (1, g.cols, *range(2, g.cols)):
        copy(k, *middle).start()
    for each in flat_copies:
        each.wait()

    def fields_of(k):
        lanes = lanes_of(k)
        label = labels[:, lanes]
        damp = 1.0 / (1.0 + porosity[:, lanes])
        push = jnp.where(label == 1, PUSH, jnp.where(label == 2, -PUSH, 0.0))
        base = pl.multiple_of(k * g.panel, 8)
        for i, value in ((27, damp), (28, push), (29, solid[:, lanes].astype(F32))):
            out[pl.ds(base + g.field(i), g.rows), :] = value

    every(1, g.cols, fields_of)
    collide = collide_first(g, state, out)

    def act(k, pieces):
        collide(k, pieces, [read_rows(stage.at[k - 1, i], 0, pieces) for i in range(27)])

    def column(k):
        for piece in g.outer:
            copy(k, *piece).wait()
        act(k, g.outer)

    every(1, g.cols, column)
    for k in (1, g.cols):
        copy(k, *middle).wait()
    for pieces in g.inner:
        side_panels(g, functools.partial(act, pieces=pieces), 2)
    pack_faces(g, out, 1, 30, *faces)
    for k in range(2, g.cols):
        copy(k, *middle).wait()


def inner_first_kernel(g, _, _state, stage, post, state0, out, state1):
    masks = lane_masks(16)
    collide = collide_first(g, state0, post)

    def act(k, pieces):
        collide(k, pieces, [read_rows(stage.at[k - 1, i], 0, pieces) for i in range(27)])

    interior_tiles(g, act)
    interior_tiles(g, step_tile(g, post, out, 1, 30, masks, collide_second(g, state1)))


def relay_kernel(g, sign, fields, _, x_second, x_first, y_second, y_first, buf, first, second):
    by_parity("gx", x_second, x_first, functools.partial(unpack_x, g, buf, sign, fields))
    by_parity("gy", y_second, y_first, functools.partial(unpack_y, g, buf, sign, fields, "face"))
    by_parity("gy", first, second, functools.partial(pack_y, g, buf, sign, fields, "corner"))


def middle_second_kernel(g, _out, _state, post, adjoint, out, state1, stage, field):
    masks = lane_masks(16)
    middle_tiles(g, step_tile(g, post, out, 1, 30, masks, collide_second(g, state1)))
    core_tiles(g, seed_tile(g, out, adjoint, stage, field, masks))


def rim_seed_kernel(g, _post, _out, _state, _stage, _field, first, second, adjoint, *refs):
    post, out, state1, stage, field, *faces = refs
    masks = lane_masks(16)
    by_parity("gy", second, first, functools.partial(unpack_y, g, post, 1, 30, "corner"))
    corner_tiles(g, post, out, 1, 30, masks, collide_second(g, state1))
    rim_tiles(g, seed_tile(g, out, adjoint, stage, field, masks))
    pack_faces(g, field, -1, 27, *faces)


def inner_seed_kernel(
    g, post, _stage, _field, state1, adjoint, stage, field, out, total, final, sems
):
    masks = lane_masks(16)

    def copy(k):
        return pltpu.make_async_copy(stage.at[k - 1], block_of(final, k), sems.at[k - 1])

    copy(1).start()
    copy(g.cols).start()
    seed = seed_tile(g, post, adjoint, stage, field, masks)

    near_core_tiles(g, seed)
    every(2, g.cols - 1, lambda k: copy(k).start())
    interior_tiles(g, step_tile(g, field, out, -1, 27, masks, adjoint_second(g, state1, total)))
    every(1, g.cols, lambda k: copy(k).wait())


def total_tile(g, out, before, state0, total, parts, masks):
    def act(k, pieces):
        p = pull_block(g, out, -1, k, pieces, masks)
        spot = spot_of(g, k)
        *flow, wall = load_fields(state0, g.local, spot, pieces, 7)
        *spread, porous = adjoint_scalars(p, *flow, wall > 0.5)
        here = load_fields(before, g.extended, spot, pieces, 1)[0] + porous
        save_fields(total, g.local, spot, pieces, [here])
        save_fields(parts, g.local, spot, pieces, spread + [wall])

    return act


def middle_adjoint_kernel(g, _out, _before, field, state1, state0, out, before, total, parts):
    masks = lane_masks(16)
    middle_tiles(g, step_tile(g, field, out, -1, 27, masks, adjoint_second(g, state1, before)))
    core_tiles(g, total_tile(g, out, before, state0, total, parts, masks))


def total_kernel(g, *refs):
    state1, state0, first, second, field, out, before, total, parts, peak = refs[5:]
    masks = lane_masks(16)
    by_parity("gy", second, first, functools.partial(unpack_y, g, field, -1, 27, "corner"))
    corner_tiles(g, field, out, -1, 27, masks, adjoint_second(g, state1, before))
    act = total_tile(g, out, before, state0, total, parts, masks)
    near_core_tiles(g, act)
    rim_tiles(g, act)
    size = 8 * (g.local // 64)
    largest = jnp.zeros((8, LANES), F32)
    for start in range(0, g.local, size):
        value = jnp.abs(total[start : start + size, :]).reshape(-1, 8, LANES)
        largest = jnp.maximum(largest, jnp.max(value, 0))
    peak[...] = largest


def adjoint_kernel(g, first, last, buf, parts, result, stage, sems):
    masks = lane_masks(16)

    def copy(k):
        return pltpu.make_async_copy(stage.at[k - first], block_of(result, k), sems.at[k - first])

    def column(k):
        for pieces in (g.outer,) + g.inner:
            p = pull_block(g, buf, -1, k, pieces, masks)
            *spread, wall = load_fields(parts, g.local, spot_of(g, k), pieces, 5)
            for i, value in enumerate(adjoint_spread(p, *spread, wall > 0.5)):
                write_rows(stage.at[k - first, i], 0, pieces, value)
        copy(k).start()

    every(first, last, column)
    every(first, last, lambda k: copy(k).wait())


def scale_kernel(g, total, peak, out):
    largest = jnp.max(peak[...])
    factor = 1.0 / (jnp.full((g.rows, LANES), largest, F32) + EPS)
    for c in range(g.cols):
        value = total[c * g.rows : (c + 1) * g.rows, :] * factor
        out[:, c * LANES : (c + 1) * LANES] = value


def swap_pairs(count, start):
    pairs = []
    for i in range(start, count, 2):
        j = (i + 1) % count
        pairs += [(i, j), (j, i)]
    return pairs


def swap(axis, count, first, second):
    return (
        lax.ppermute(first, axis, swap_pairs(count, 0)),
        lax.ppermute(second, axis, swap_pairs(count, 1)),
    )


def largest_of_all(peak, sizes, beside):
    nx, ny = sizes
    peak = jnp.maximum(peak, lax.ppermute(peak, "gy", [(i, i + 1) for i in range(0, ny, 2)]))
    groups = 0
    for axis, count, first, widths in (("gy", ny, 2, (4, 4)), ("gx", nx, 1, (4, 2))):
        step = first
        for width in widths:
            width = min(width, count // step)
            parts = []
            for n in range(1, width):
                pairs = [(i, i ^ (n * step)) for i in range(count)]
                if axis == "gy":
                    parts.append(lax.ppermute(peak, "gy", [(i, j) for i, j in pairs if i % 2]))
                else:
                    pairs = [(i * ny + y, j * ny + y) for i, j in pairs for y in range(1, ny, 2)]
                    parts.append(lax.ppermute(peak, ("gx", "gy"), pairs))
            groups += 1
            if groups <= 2:
                peak = beside(peak, groups)
            peak = functools.reduce(jnp.maximum, parts, peak)
            step *= width
    return jnp.maximum(peak, lax.ppermute(peak, "gy", [(i + 1, i) for i in range(0, ny, 2)]))


def on_device(sizes, populations, adjoint_in, porosity, solid, labels):
    rows, width = porosity.shape
    g = Grid(rows, width)
    in_vmem = pl.BlockSpec(memory_space=pltpu.VMEM)
    in_hbm = pl.BlockSpec(memory_space=pltpu.HBM)
    nx, ny = sizes

    def vmem(*shape):
        return pltpu.VMEM(shape, F32)

    def fields(count, size):
        return vmem(count * size, LANES)

    def padded(count):
        return vmem(*g.padded(count))

    def faces(count, sign):
        along_x = vmem(count * g.cols, LANES)
        along_y = vmem(y_slots(count, sign) * rows, LANES)
        return [along_x, along_x, along_y, along_y]

    def corners(count, sign):
        return [vmem(-(-2 * y_slots(count, sign) // 8) * 8, LANES)] * 2

    whole = pltpu.HBM(populations.shape, F32)
    stage = vmem(g.cols, 27, rows, LANES)
    sems = pltpu.SemaphoreType.DMA((g.cols,))

    def call(name, kernel, operands, out_shape, scratch=(), kept=0, load=0, result=None):
        out_shape = [pltpu.VMEM(x.shape, x.dtype) for x in operands[:kept]] + out_shape
        aliases = {n: n for n in range(kept)}
        space = pltpu.HBM if name == "rim_first" else pltpu.VMEM
        pinned = [pltpu.with_memory_space_constraint(x, space) for x in operands]
        in_specs = [pl.BlockSpec(memory_space=space)] * len(operands)
        if result is not None:
            aliases[len(operands)] = len(out_shape) - 1
            pinned.append(pltpu.with_memory_space_constraint(result, pltpu.HBM))
            in_specs.append(in_hbm)
        return pl.pallas_call(
            functools.partial(kernel, g),
            in_specs=in_specs,
            out_shape=out_shape,
            out_specs=[in_hbm if x is whole else in_vmem for x in out_shape],
            scratch_shapes=list(scratch),
            input_output_aliases=aliases,
            compiler_params=pltpu.CompilerParams(vmem_limit_bytes=VMEM_LIMIT),
            cost_estimate=pl.CostEstimate(flops=0, bytes_accessed=load, transcendentals=0)
            if load
            else None,
            name=name,
        )(*pinned)

    def swap_faces(parcels):
        x_first, x_second = swap("gx", nx, *parcels[:2])
        y_first, y_second = swap("gy", ny, *parcels[2:])
        return [x_second, x_first, y_second, y_first]

    def relay(buf, parcels, sign, count):
        def kernel(grid, *refs):
            relay_kernel(grid, sign, count, *refs)

        buf, *parcels = call("relay", kernel, [buf, *parcels], corners(count, sign), kept=1)
        return buf, swap("gy", ny, *parcels)

    post, state0, staged, *parcels = call(
        "rim_first",
        rim_first_kernel,
        [populations, porosity, solid, labels],
        [padded(30), fields(7, g.local), stage] + faces(30, 1),
        [vmem(*porosity.shape)]
        + [pltpu.VMEM(porosity.shape, jnp.int32)] * 2
        + [pltpu.SemaphoreType.DMA((g.cols, 3)), pltpu.SemaphoreType.DMA((3,))],
    )
    parcels = swap_faces(parcels)
    post, state0, second, state1 = call(
        "inner_first",
        inner_first_kernel,
        [post, state0, staged],
        [padded(27), fields(7, g.extended)],
        kept=2,
        load=FLIGHT,
    )
    post, parcels = relay(post, parcels, 1, 30)
    second, state1, staged, field = call(
        "middle_second",
        middle_second_kernel,
        [second, state1, post, adjoint_in],
        [stage, padded(27)],
        kept=2,
        load=FLIGHT,
    )
    _, second, state1, staged, field, *parcels = call(
        "rim_seed",
        rim_seed_kernel,
        [post, second, state1, staged, field, *parcels, adjoint_in],
        faces(27, -1),
        kept=5,
    )
    parcels = swap_faces(parcels)
    _, field, pulled, before, final = call(
        "inner_seed",
        lambda grid, kept, into, buf, *refs: inner_seed_kernel(grid, buf, kept, into, *refs),
        [staged, field, second, state1, adjoint_in],
        [padded(27), fields(1, g.extended), whole],
        [sems],
        kept=2,
        load=FLIGHT,
    )
    field, parcels = relay(field, parcels, -1, 27)
    pulled, before, total, parts = call(
        "middle_adjoint",
        middle_adjoint_kernel,
        [pulled, before, field, state1, state0],
        [fields(1, g.local), fields(5, g.local)],
        kept=2,
        load=FLIGHT,
    )
    _, pulled, _, total, parts, peak = call(
        "total",
        total_kernel,
        [field, pulled, before, total, parts, state1, state0, *parcels],
        [vmem(8, LANES)],
        kept=5,
    )
    half = g.cols // 2
    scratch = [vmem(half, 27, rows, LANES), pltpu.SemaphoreType.DMA((half,))]
    halves = [None]

    def run_half(peak, n):
        first, last = ((1, half), (1 + half, g.cols))[n - 1]

        def kernel(grid, buf, fields, near, *refs):
            echo, *refs = refs[-4:]
            echo[...] = near[...]
            adjoint_kernel(grid, first, last, buf, fields, *refs)

        echo, result = call(
            ("adjoint_low", "adjoint_high")[n - 1],
            kernel,
            [pulled, parts, peak],
            [vmem(8, LANES), whole],
            scratch,
            load=FLIGHT // 2,
            result=halves[-1],
        )
        halves.append(result)
        return echo

    largest = largest_of_all(peak, sizes, run_half)
    adjoint_out = halves[-1]
    (sensitivity,) = call(
        "normalize",
        scale_kernel,
        [total, largest],
        [jax.ShapeDtypeStruct(porosity.shape, F32)],
    )
    return final, adjoint_out, sensitivity


def solution(mesh):
    sizes = (mesh.shape["gx"], mesh.shape["gy"])
    whole, flat = P(None, "gx", "gy"), P("gx", "gy")
    return jax.shard_map(
        functools.partial(on_device, sizes),
        mesh=mesh,
        in_specs=(whole, whole, flat, flat, flat),
        out_specs=(whole, whole, flat),
        check_vma=False,
    )
```

```python
import functools

import jax
import jax.numpy as jnp
from jax import lax
from jax.experimental import pallas as pl
from jax.experimental.pallas import tpu as pltpu
from jax.sharding import PartitionSpec as P

NZ = 64
RELAX = 0.8
PUSH = 0.2
EPS = 1e-06
LANES = 128
VELOCITY = [(a, b, c) for a in (-1, 0, 1) for b in (-1, 0, 1) for c in (-1, 0, 1)]
INDEX = {v: i for i, v in enumerate(VELOCITY)}
WEIGHT = [
    [8.0 / 27, 2.0 / 27, 1.0 / 54, 1.0 / 216][abs(v[0]) + abs(v[1]) + abs(v[2])]
    for v in VELOCITY
]
NORM = [abs(v[0]) + abs(v[1]) + abs(v[2]) for v in VELOCITY]
F32 = jnp.float32
VMEM_LIMIT = 6 * 1024 * 1024
FLIGHT = 12 * 1024 * 1024


class Grid:
    def __init__(self, rows, width):
        self.rows = rows
        self.cols = width // LANES
        self.panel = rows + 16
        self.halo = self.cols + 1
        self.local = self.cols * rows
        self.extended = self.halo * rows + 24
        self.outer = ((0, 8), (rows - 8, 8))
        self.inner = tuple(((r, 16),) for r in range(8, rows - 8, 16))

    def at(self, i, k, r):
        return self.field(i) + k * self.panel + r

    def field(self, i):
        return i * (self.cols + 2) * self.panel + 8

    def padded(self, fields):
        return (fields * (self.cols + 2) * self.panel + 8, LANES)


def velocity(i, sign):
    return tuple(sign * n for n in VELOCITY[i]) if i < 27 else (0, 0, 0)


def moving(fields, sign, axis, side):
    return [i for i in range(fields) if velocity(i, sign)[axis] == side]


def lane_masks(height):
    lane = lax.broadcasted_iota(jnp.int32, (height, LANES), 1)
    return lane >= NZ, lane % NZ == 0, lane % NZ == NZ - 1


def shift_lanes(here, d, masks):
    first, last = masks[1:]
    dy, dz = d[1:]
    if dz == 0:
        return here if dy == 0 else pltpu.roll(here, NZ, 1)
    if dz == 1:
        one, other, edge = 1, NZ + 1, first
    else:
        one, other, edge = LANES - 1, NZ - 1, last
    inner, wrapped = (one, other) if dy == 0 else (other, one)
    return jnp.where(edge, pltpu.roll(here, wrapped, 1), pltpu.roll(here, inner, 1))


def pull(load, d, masks):
    high = masks[0]
    here = load(0)
    if d[1] == 1:
        here = jnp.where(high, load(-1), here)
    elif d[1] == -1:
        here = jnp.where(high, here, load(1))
    return shift_lanes(here, d, masks)


def stacked(parts):
    return parts[0] if len(parts) == 1 else jnp.concatenate(parts, 0)


def read_rows(ref, base, pieces):
    return stacked([ref[pl.ds(base + r, n), :] for r, n in pieces])


def write_rows(ref, base, pieces, value):
    done = 0
    for r, n in pieces:
        ref[pl.ds(base + r, n), :] = value[done : done + n]
        done += n


def pull_block(g, buf, sign, k, pieces, masks, fields=27):
    base = pl.multiple_of(k * g.panel, 8)
    after = pl.multiple_of(jnp.where(k == g.halo, g.panel, base + g.panel), 8)
    out = []
    for i in range(fields):
        d = velocity(i, sign)

        def load(n, i=i, d=d):
            start = {-1: base - g.panel, 0: base, 1: after}[n]
            return read_rows(buf, start + (g.field(i) - d[0]), pieces)

        out.append(pull(load, d, masks))
    return out


def pull_edge(g, buf, sign, side, masks, fields=27):
    out = []
    for i in range(fields):
        d = velocity(i, sign)
        if side == 1:
            row = g.rows - d[0]
        else:
            row = {1: g.rows, 0: g.rows + 1, -1: 0}[d[0]]

        def load(n, i=i, row=row):
            return buf[pl.ds(g.at(i, 1 + n, row), g.cols, stride=g.panel), :]

        out.append(pull(load, d, masks))
    return out


def moments(f):
    flat = {}
    along_z = None
    for a in (-1, 0, 1):
        for b in (-1, 0, 1):
            lo, mid, hi = (f[INDEX[(a, b, c)]] for c in (-1, 0, 1))
            flat[a, b] = lo + mid + hi
            diff = hi - lo
            along_z = diff if along_z is None else along_z + diff
    line = {}
    along_y = None
    for a in (-1, 0, 1):
        line[a] = flat[a, -1] + flat[a, 0] + flat[a, 1]
        diff = flat[a, 1] - flat[a, -1]
        along_y = diff if along_y is None else along_y + diff
    return line[-1] + line[0] + line[1], line[1] - line[-1], along_y, along_z


def combos(x, y, z):
    plane = {}
    for a in (-1, 0, 1):
        for b in (-1, 0, 1):
            if (a, b) > (0, 0):
                continue
            if a == 0:
                plane[a, b] = -y if b else None
            else:
                plane[a, b] = -x if b == 0 else (-x - y if b < 0 else y - x)
    out = []
    for a, b, c in VELOCITY[:13]:
        base = plane[a, b]
        if base is None:
            out.append(-z)
        else:
            out.append(base if c == 0 else (base - z if c < 0 else base + z))
    return out


def relax(f, rho, wx, wy, wz, damp, push, solid):
    ux, uy, uz = (wx + push) * damp, wy * damp, wz * damp
    base = 1.0 - 1.5 * (ux * ux + uy * uy + uz * uz)
    keep = 1.0 - 1.0 / RELAX
    gain = rho * (1.0 / RELAX)
    level = [gain * w for w in (8.0 / 27, 2.0 / 27, 1.0 / 54, 1.0 / 216)]
    along = combos(3.0 * ux, 3.0 * uy, 3.0 * uz)
    out = [None] * 27
    for i in range(13):
        j = 26 - i
        even = base + 0.5 * (along[i] * along[i])
        lift = level[NORM[i]]
        out[i] = jnp.where(solid, f[j], keep * f[i] + lift * (even + along[i]))
        out[j] = jnp.where(solid, f[i], keep * f[j] + lift * (even - along[i]))
    out[13] = jnp.where(solid, f[13], keep * f[13] + level[0] * base)
    return out


def pulled_moments(p):
    first = {}
    for a in (-1, 0, 1):
        for b in (-1, 0, 1):
            lo, mid, hi = (p[INDEX[(a, b, c)]] for c in (-1, 0, 1))
            both = lo + hi
            first[a, b] = (4.0 * mid + both, hi - lo, both)
    second = {}
    for a in (-1, 0, 1):
        lo, mid, hi = (first[a, b] for b in (-1, 0, 1))
        b0 = lo[0] + hi[0]
        b1 = lo[1] + hi[1]
        second[a] = dict(
            one=4.0 * mid[0] + b0,
            y=hi[0] - lo[0],
            yy=b0,
            z=4.0 * mid[1] + b1,
            yz=hi[1] - lo[1],
            zz=4.0 * mid[2] + lo[2] + hi[2],
        )
    lo, mid, hi = (second[a] for a in (-1, 0, 1))

    def full(key):
        return 4.0 * mid[key] + lo[key] + hi[key]

    xx = lo["one"] + hi["one"]
    return dict(
        one=4.0 * mid["one"] + xx,
        x=hi["one"] - lo["one"],
        xx=xx,
        y=full("y"),
        xy=hi["y"] - lo["y"],
        yy=full("yy"),
        z=full("z"),
        xz=hi["z"] - lo["z"],
        yz=full("yz"),
        zz=full("zz"),
    )


def adjoint_scalars(p, rho, wx, wy, wz, damp, push, solid):
    ux, uy, uz = (wx + push) * damp, wy * damp, wz * damp
    s = pulled_moments(p)
    scale = 1.0 / (216.0 * RELAX)
    one = s["one"] * scale
    b = [s[k] * (3.0 * scale) for k in ("x", "y", "z")]
    d = {k: s[k] * (9.0 * scale) for k in ("xx", "xy", "yy", "xz", "yz", "zz")}
    qx = d["xx"] * ux + d["xy"] * uy + d["xz"] * uz
    qy = d["xy"] * ux + d["yy"] * uy + d["yz"] * uz
    qz = d["xz"] * ux + d["yz"] * uy + d["zz"] * uz
    linear = b[0] * ux + b[1] * uy + b[2] * uz
    square = ux * ux + uy * uy + uz * uz
    even = one + linear + 0.5 * (qx * ux + qy * uy + qz * uz) - 1.5 * one * square
    three = 3.0 * one
    gx = (b[0] + qx - three * ux) * damp
    gy = (b[1] + qy - three * uy) * damp
    gz = (b[2] + qz - three * uz) * damp
    even = even - (gx * wx + gy * wy + gz * wz)
    porous = jnp.where(solid, 0.0, -rho * (gx * ux + gy * uy + gz * uz))
    return even, gx, gy, gz, porous


def adjoint_spread(p, even, gx, gy, gz, solid):
    keep = 1.0 - 1.0 / RELAX
    along = combos(gx, gy, gz)
    out = [None] * 27
    for i in range(13):
        j = 26 - i
        out[i] = jnp.where(solid, p[j], keep * p[i] + (even + along[i]))
        out[j] = jnp.where(solid, p[i], keep * p[j] + (even - along[i]))
    out[13] = jnp.where(solid, p[13], keep * p[13] + even)
    return out


def x_lines(g, sign, fields, side):
    lines = []
    for i in moving(fields, sign, 0, side):
        if side == 1:
            lines.append((i, g.rows - 1, (-1, g.rows + 1)))
            lines.append((i, g.rows - 2, (g.rows,)))
        else:
            lines += [(i, 0, (g.rows,)), (i, 1, (g.rows + 1,))]
    edge, target = (g.rows - 1, g.rows + 1) if side == 1 else (0, g.rows)
    return lines + [(i, edge, (target,)) for i in moving(fields, sign, 0, 0)]


def pack_x(g, buf, sign, fields, up, down):
    for side, ref in ((1, up), (-1, down)):
        for n, (i, r, _) in enumerate(x_lines(g, sign, fields, side)):
            ref[n * g.cols : (n + 1) * g.cols, :] = buf[
                pl.ds(g.at(i, 1, r), g.cols, stride=g.panel), :
            ]


def unpack_x(g, buf, sign, fields, up, down):
    for side, ref in ((1, up), (-1, down)):
        for n, (i, _, targets) in enumerate(x_lines(g, sign, fields, side)):
            value = ref[n * g.cols : (n + 1) * g.cols, :]
            for r in targets:
                buf[pl.ds(g.at(i, 1, r), g.cols, stride=g.panel), :] = value
    for i in moving(fields, sign, 0, -1):
        buf[pl.ds(g.at(i, 1, g.rows + 2), g.cols, stride=g.panel), :] = buf[
            pl.ds(g.at(i, 1, 0), g.cols, stride=g.panel), :
        ]


def halo_panels(g, i, sign):
    return (0, g.halo) if velocity(i, sign)[1] == 1 else (g.halo,)


def pack_corners(g, buf, sign, fields, up, down):
    for side, ref in ((1, up), (-1, down)):
        for n, (i, r, _) in enumerate(x_lines(g, sign, fields, side)):
            ref[n : n + 1, :] = buf[pl.ds(g.at(i, g.halo, r), 1), :]


def unpack_corners(g, buf, sign, fields, up, down):
    for side, ref in ((1, up), (-1, down)):
        for n, (i, _, targets) in enumerate(x_lines(g, sign, fields, side)):
            value = ref[n : n + 1, :]
            for r in targets:
                for k in halo_panels(g, i, sign):
                    buf[pl.ds(g.at(i, k, r), 1), :] = value
    for i in moving(fields, sign, 0, -1):
        for k in halo_panels(g, i, sign):
            buf[pl.ds(g.at(i, k, g.rows + 2), 1), :] = buf[pl.ds(g.at(i, k, 0), 1), :]


def still_pairs(fields, sign):
    still = moving(fields, sign, 1, 0)
    half = (len(still) + 1) // 2
    return [(still[n], still[n + half] if n + half < len(still) else None) for n in range(half)]


def y_slots(fields, sign):
    return 9 + len(still_pairs(fields, sign))


def pack_y(g, buf, sign, fields, high, up, down):
    for side, ref in ((1, up), (-1, down)):
        k = g.cols if side == 1 else 1
        for n, i in enumerate(moving(fields, sign, 1, side)):
            ref[n * g.rows : (n + 1) * g.rows, :] = buf[pl.ds(g.at(i, k, 0), g.rows), :]
        for n, (i, j) in enumerate(still_pairs(fields, sign)):
            value = buf[pl.ds(g.at(i, k, 0), g.rows), :]
            if j is not None:
                other = pltpu.roll(buf[pl.ds(g.at(j, k, 0), g.rows), :], NZ, 1)
                pair = (value, other) if side == 1 else (other, value)
                value = jnp.where(high, *pair)
            ref[(9 + n) * g.rows : (10 + n) * g.rows, :] = value


def unpack_y(g, buf, sign, fields, high, up, down):
    for side, ref in ((1, up), (-1, down)):
        for n, i in enumerate(moving(fields, sign, 1, side)):
            value = ref[n * g.rows : (n + 1) * g.rows, :]
            for k in halo_panels(g, i, sign):
                buf[pl.ds(g.at(i, k, 0), g.rows), :] = value
    for n, (i, j) in enumerate(still_pairs(fields, sign)):
        spot = slice((9 + n) * g.rows, (10 + n) * g.rows)
        before, after = up[spot, :], down[spot, :]
        buf[pl.ds(g.at(i, g.halo, 0), g.rows), :] = jnp.where(high, before, after)
        if j is not None:
            value = pltpu.roll(jnp.where(high, after, before), NZ, 1)
            buf[pl.ds(g.at(j, g.halo, 0), g.rows), :] = value


def by_parity(axis, first, second, act):
    even = lax.rem(lax.axis_index(axis), 2) == 0

    @pl.when(even)
    def _():
        act(first, second)

    @pl.when(jnp.logical_not(even))
    def _():
        act(second, first)


def load_fields(ref, rows, base, pieces, count):
    return [read_rows(ref, base + n * rows, pieces) for n in range(count)]


def save_fields(ref, rows, base, pieces, values):
    for n, value in enumerate(values):
        write_rows(ref, base + n * rows, pieces, value)


def save_populations(g, out, k, pieces, values):
    base = pl.multiple_of(k * g.panel, 8)
    for i, value in enumerate(values):
        write_rows(out, base + g.field(i), pieces, value)


def spot_of(g, k):
    return pl.multiple_of((k - 1) * g.rows, 8)


def lanes_of(k):
    return pl.ds(pl.multiple_of((k - 1) * LANES, LANES), LANES)


def every(first, last, act):
    def step(k, carry):
        act(k)
        return carry

    count = last + 1 - first
    unroll = max(n for n in (1, 2, 3, 4) if count % n == 0)
    lax.fori_loop(first, last + 1, step, 0, unroll=unroll)


def side_panels(g, act, count):
    def step(n, carry):
        act(jnp.where(n == 0, 1, g.cols - 1 + n))
        return carry

    lax.fori_loop(0, count, step, 0, unroll=count)


def interior_tiles(g, act):
    for pieces in g.inner:
        every(2, g.cols - 1, functools.partial(act, pieces=pieces))


def middle_tiles(g, act):
    for pieces in g.inner:
        side_panels(g, functools.partial(act, pieces=pieces), 3)
    every(2, g.cols - 1, functools.partial(act, pieces=g.outer))


def core_tiles(g, act):
    for pieces in g.inner:
        every(3, g.cols - 2, functools.partial(act, pieces=pieces))


def near_core_tiles(g, act):
    def step(n, carry):
        for pieces in g.inner:
            act(jnp.where(n == 0, 2, g.cols - 1), pieces=pieces)
        return carry

    lax.fori_loop(0, 2, step, 0, unroll=2)


def rim_tiles(g, act):
    every(1, g.cols, functools.partial(act, pieces=g.outer))
    for pieces in g.inner:
        side_panels(g, functools.partial(act, pieces=pieces), 2)


def step_tile(g, buf, out, sign, fields, masks, compute):
    def act(k, pieces):
        values = compute(
            pull_block(g, buf, sign, k, pieces, masks, fields), spot_of(g, k), pieces
        )
        save_populations(g, out, k, pieces, values)

    return act


def corner_tiles(g, buf, out, sign, fields, masks, compute):
    small = tuple(mask[:8] for mask in masks)
    act = step_tile(g, buf, out, sign, fields, masks, compute)
    side_panels(g, functools.partial(act, pieces=g.outer), 3)
    spot = g.halo * g.rows
    pieces = ((g.rows, 8),)
    values = compute(pull_block(g, buf, sign, g.halo, pieces, small, fields), spot, ((0, 8),))
    for i in range(27):
        dx = velocity(i, sign)[0]
        if dx == -1:
            out[pl.ds(g.at(i, g.halo, g.rows), 1), :] = values[i][0:1]
        elif dx == 1:
            out[pl.ds(g.at(i, g.halo, -1), 1), :] = values[i][1:2]
    edges = [pull_edge(g, buf, sign, side, small, fields) for side in (1, -1)]
    both = [stacked(pair) for pair in zip(*edges)]
    values = compute(both, spot, ((8, 16),))
    for i in moving(27, sign, 0, -1):
        out[pl.ds(g.at(i, 1, g.rows), g.cols, stride=g.panel), :] = values[i][:8]
    for i in moving(27, sign, 0, 1):
        out[pl.ds(g.at(i, 1, -1), g.cols, stride=g.panel), :] = values[i][8:]
    for i in moving(27, sign, 1, 1):
        out[pl.ds(g.at(i, 0, 0), g.rows), :] = out[pl.ds(g.at(i, g.halo, 0), g.rows), :]
        for r in (-1, g.rows):
            out[pl.ds(g.at(i, 0, r), 1), :] = out[pl.ds(g.at(i, g.halo, r), 1), :]


def flow_of(f):
    rho, mx, my, mz = moments(f)
    inverse = 1.0 / rho
    return inverse, rho, mx * inverse, my * inverse, mz * inverse


def collide_first(g, state, out):
    def act(k, pieces, f):
        base = pl.multiple_of(k * g.panel, 8)
        damp, push, wall = (read_rows(out, base + g.field(i), pieces) for i in (27, 28, 29))
        flow = flow_of(f)[1:] + (damp, push)
        save_fields(state, g.local, spot_of(g, k), pieces, flow + (wall,))
        save_populations(g, out, k, pieces, relax(f, *flow, wall > 0.5))

    return act


def collide_second(g, state):
    def compute(values, spot, pieces):
        f, (damp, push, wall) = values[:27], values[27:]
        flow = flow_of(f)[1:] + (damp, push)
        save_fields(state, g.extended, spot, pieces, flow + (wall,))
        return relax(f, *flow, wall > 0.5)

    return compute


def adjoint_second(g, state, total):
    def compute(p, spot, pieces):
        *flow, wall = load_fields(state, g.extended, spot, pieces, 7)
        *spread, porous = adjoint_scalars(p, *flow, wall > 0.5)
        save_fields(total, g.extended, spot, pieces, [porous])
        return adjoint_spread(p, *spread, wall > 0.5)

    return compute


def seed_tile(g, buf, adjoint, stage, out, masks):
    def act(k, pieces):
        f = pull_block(g, buf, 1, k, pieces, masks)
        for i in range(27):
            write_rows(stage.at[k - 1, i], 0, pieces, f[i])
        inverse, _, wx, wy, wz = flow_of(f)
        even = -(wx * wx + wy * wy + wz * wz) * inverse
        along = combos(wx * inverse, wy * inverse, wz * inverse)
        lanes = lanes_of(k)
        seeded = [
            stacked([adjoint[i, pl.ds(r, n), lanes] for r, n in pieces]) + even for i in range(27)
        ]
        for i in range(13):
            seeded[i] = seeded[i] + along[i]
            seeded[26 - i] = seeded[26 - i] - along[i]
        save_populations(g, out, k, pieces, seeded)

    return act


def block_of(ref, k):
    return ref.at[:, :, lanes_of(k)]


def pack_faces(g, buf, sign, fields, x_first, x_second, y_first, y_second):
    high = lane_masks(g.rows)[0]
    by_parity("gx", x_first, x_second, functools.partial(pack_x, g, buf, sign, fields))
    by_parity("gy", y_first, y_second, functools.partial(pack_y, g, buf, sign, fields, high))


def rim_first_kernel(g, pops, *refs):
    flat, (out, state, stage, *faces), near, (sems, flat_sems) = (
        refs[:3],
        refs[3:10],
        refs[10:13],
        refs[13:],
    )
    porosity, solid, labels = near

    def copy(k, r, n):
        rows = pl.ds(r, n)
        source = pops.at[:, rows, lanes_of(k)]
        part = 0 if r == 0 else 2 if r + n == g.rows else 1
        return pltpu.make_async_copy(source, stage.at[k - 1, :, rows], sems.at[k - 1, part])

    middle = (8, g.rows - 16)
    flat_copies = [
        pltpu.make_async_copy(source, target, flat_sems.at[n])
        for n, (source, target) in enumerate(zip(flat, near))
    ]
    for each in flat_copies:
        each.start()
    for k in range(1, g.cols + 1):
        for piece in g.outer:
            copy(k, *piece).start()
    for k in (1, g.cols, *range(2, g.cols)):
        copy(k, *middle).start()
    for each in flat_copies:
        each.wait()

    def fields_of(k):
        lanes = lanes_of(k)
        label = labels[:, lanes]
        damp = 1.0 / (1.0 + porosity[:, lanes])
        push = jnp.where(label == 1, PUSH, jnp.where(label == 2, -PUSH, 0.0))
        base = pl.multiple_of(k * g.panel, 8)
        for i, value in ((27, damp), (28, push), (29, solid[:, lanes].astype(F32))):
            out[pl.ds(base + g.field(i), g.rows), :] = value

    every(1, g.cols, fields_of)
    collide = collide_first(g, state, out)

    def act(k, pieces):
        collide(k, pieces, [read_rows(stage.at[k - 1, i], 0, pieces) for i in range(27)])

    def column(k):
        for piece in g.outer:
            copy(k, *piece).wait()
        act(k, g.outer)

    every(1, g.cols, column)
    for k in (1, g.cols):
        copy(k, *middle).wait()
    for pieces in g.inner:
        side_panels(g, functools.partial(act, pieces=pieces), 2)
    pack_faces(g, out, 1, 30, *faces)
    for k in range(2, g.cols):
        copy(k, *middle).wait()


def inner_first_kernel(g, _, _state, stage, post, state0, out, state1):
    masks = lane_masks(16)
    collide = collide_first(g, state0, post)

    def act(k, pieces):
        collide(k, pieces, [read_rows(stage.at[k - 1, i], 0, pieces) for i in range(27)])

    interior_tiles(g, act)
    interior_tiles(g, step_tile(g, post, out, 1, 30, masks, collide_second(g, state1)))


def relay_kernel(g, sign, fields, _, y_second, y_first, buf, first, second):
    high = lane_masks(g.rows)[0]
    by_parity("gy", y_second, y_first, functools.partial(unpack_y, g, buf, sign, fields, high))
    by_parity("gx", first, second, functools.partial(pack_corners, g, buf, sign, fields))


def middle_second_kernel(g, adjoint, post, out, state1, stage, field, x_second, x_first):
    masks = lane_masks(16)
    by_parity("gx", x_second, x_first, functools.partial(unpack_x, g, post, 1, 30))
    middle_tiles(g, step_tile(g, post, out, 1, 30, masks, collide_second(g, state1)))
    core_tiles(g, seed_tile(g, out, adjoint, stage, field, masks))


def rim_seed_kernel(g, _post, _out, _state, _stage, _field, first, second, adjoint, *refs):
    post, out, state1, stage, field, *faces = refs
    masks = lane_masks(16)
    by_parity("gx", second, first, functools.partial(unpack_corners, g, post, 1, 30))
    corner_tiles(g, post, out, 1, 30, masks, collide_second(g, state1))
    rim_tiles(g, seed_tile(g, out, adjoint, stage, field, masks))
    pack_faces(g, field, -1, 27, *faces)


def inner_seed_kernel(
    g, post, _stage, _field, state1, adjoint, stage, field, out, total, final, sems
):
    masks = lane_masks(16)

    def copy(k):
        return pltpu.make_async_copy(stage.at[k - 1], block_of(final, k), sems.at[k - 1])

    copy(1).start()
    copy(g.cols).start()
    seed = seed_tile(g, post, adjoint, stage, field, masks)

    near_core_tiles(g, seed)
    every(2, g.cols - 1, lambda k: copy(k).start())
    interior_tiles(g, step_tile(g, field, out, -1, 27, masks, adjoint_second(g, state1, total)))
    every(1, g.cols, lambda k: copy(k).wait())


def total_tile(g, out, before, state0, total, parts, masks):
    def act(k, pieces):
        p = pull_block(g, out, -1, k, pieces, masks)
        spot = spot_of(g, k)
        *flow, wall = load_fields(state0, g.local, spot, pieces, 7)
        *spread, porous = adjoint_scalars(p, *flow, wall > 0.5)
        here = load_fields(before, g.extended, spot, pieces, 1)[0] + porous
        save_fields(total, g.local, spot, pieces, [here])
        save_fields(parts, g.local, spot, pieces, spread + [wall])

    return act


def middle_adjoint_kernel(g, field, out, before, total, parts, state1, state0, x_second, x_first):
    masks = lane_masks(16)
    by_parity("gx", x_second, x_first, functools.partial(unpack_x, g, field, -1, 27))
    middle_tiles(g, step_tile(g, field, out, -1, 27, masks, adjoint_second(g, state1, before)))
    core_tiles(g, total_tile(g, out, before, state0, total, parts, masks))


def total_kernel(g, *refs):
    state1, state0, first, second, field, out, before, total, parts, peak = refs[5:]
    masks = lane_masks(16)
    by_parity("gx", second, first, functools.partial(unpack_corners, g, field, -1, 27))
    corner_tiles(g, field, out, -1, 27, masks, adjoint_second(g, state1, before))
    act = total_tile(g, out, before, state0, total, parts, masks)
    near_core_tiles(g, act)
    rim_tiles(g, act)
    size = 8 * (g.local // 64)
    largest = jnp.zeros((8, LANES), F32)
    for start in range(0, g.local, size):
        value = jnp.abs(total[start : start + size, :]).reshape(-1, 8, LANES)
        largest = jnp.maximum(largest, jnp.max(value, 0))
    peak[...] = largest


def adjoint_kernel(g, first, last, buf, parts, result, stage, sems):
    masks = lane_masks(16)

    def copy(k):
        return pltpu.make_async_copy(stage.at[k - first], block_of(result, k), sems.at[k - first])

    def column(k):
        for pieces in (g.outer,) + g.inner:
            p = pull_block(g, buf, -1, k, pieces, masks)
            *spread, wall = load_fields(parts, g.local, spot_of(g, k), pieces, 5)
            for i, value in enumerate(adjoint_spread(p, *spread, wall > 0.5)):
                write_rows(stage.at[k - first, i], 0, pieces, value)
        copy(k).start()

    every(first, last, column)
    every(first, last, lambda k: copy(k).wait())


def scale_kernel(g, total, peak, out):
    largest = jnp.max(peak[...])
    factor = 1.0 / (jnp.full((g.rows, LANES), largest, F32) + EPS)
    for c in range(g.cols):
        value = total[c * g.rows : (c + 1) * g.rows, :] * factor
        out[:, c * LANES : (c + 1) * LANES] = value


def swap_pairs(count, start):
    pairs = []
    for i in range(start, count, 2):
        j = (i + 1) % count
        pairs += [(i, j), (j, i)]
    return pairs


def swap(axis, count, first, second):
    return (
        lax.ppermute(first, axis, swap_pairs(count, 0)),
        lax.ppermute(second, axis, swap_pairs(count, 1)),
    )


def largest_of_all(peak, sizes, beside):
    nx, ny = sizes
    peak = jnp.maximum(peak, lax.ppermute(peak, "gy", [(i, i ^ 1) for i in range(ny)]))
    groups = 0
    for axis, count, first, widths in (("gy", ny, 2, (4, 4)), ("gx", nx, 1, (4, 2))):
        step = first
        for width in widths:
            width = min(width, count // step)
            parts = []
            for n in range(1, width):
                if axis == "gy":
                    pairs = [(i, i ^ (n * step) ^ 1) for i in range(ny)]
                    parts.append(lax.ppermute(peak, "gy", pairs))
                else:
                    pairs = [
                        (i * ny + y, (i ^ (n * step)) * ny + (y ^ 1))
                        for i in range(nx)
                        for y in range(ny)
                    ]
                    parts.append(lax.ppermute(peak, ("gx", "gy"), pairs))
            groups += 1
            if groups == 1:
                peak = beside(peak)
            peak = functools.reduce(jnp.maximum, parts, peak)
            step *= width
    return peak


def on_device(sizes, populations, adjoint_in, porosity, solid, labels):
    rows, width = porosity.shape
    g = Grid(rows, width)
    in_vmem = pl.BlockSpec(memory_space=pltpu.VMEM)
    in_hbm = pl.BlockSpec(memory_space=pltpu.HBM)
    nx, ny = sizes

    def vmem(*shape):
        return pltpu.VMEM(shape, F32)

    def fields(count, size):
        return vmem(count * size, LANES)

    def padded(count):
        return vmem(*g.padded(count))

    def faces(count, sign):
        along_x = vmem(count * g.cols, LANES)
        along_y = vmem(y_slots(count, sign) * rows, LANES)
        return [along_x, along_x, along_y, along_y]

    def corners(count):
        return [vmem(-(-count // 8) * 8, LANES)] * 2

    whole = pltpu.HBM(populations.shape, F32)
    stage = vmem(g.cols, 27, rows, LANES)
    sems = pltpu.SemaphoreType.DMA((g.cols,))

    def call(name, kernel, operands, out_shape, scratch=(), kept=0, load=0, result=None):
        out_shape = [pltpu.VMEM(x.shape, x.dtype) for x in operands[:kept]] + out_shape
        aliases = {n: n for n in range(kept)}
        space = pltpu.HBM if name == "rim_first" else pltpu.VMEM
        pinned = [pltpu.with_memory_space_constraint(x, space) for x in operands]
        in_specs = [pl.BlockSpec(memory_space=space)] * len(operands)
        if result is not None:
            aliases[len(operands)] = len(out_shape) - 1
            pinned.append(pltpu.with_memory_space_constraint(result, pltpu.HBM))
            in_specs.append(in_hbm)
        return pl.pallas_call(
            functools.partial(kernel, g),
            in_specs=in_specs,
            out_shape=out_shape,
            out_specs=[in_hbm if x is whole else in_vmem for x in out_shape],
            scratch_shapes=list(scratch),
            input_output_aliases=aliases,
            compiler_params=pltpu.CompilerParams(vmem_limit_bytes=VMEM_LIMIT),
            cost_estimate=pl.CostEstimate(flops=0, bytes_accessed=load, transcendentals=0)
            if load
            else None,
            name=name,
        )(*pinned)

    def swap_faces(parcels):
        x_first, x_second = swap("gx", nx, *parcels[:2])
        y_first, y_second = swap("gy", ny, *parcels[2:])
        return [x_second, x_first], [y_second, y_first]

    def relay(buf, parcels, sign, count):
        def kernel(grid, *refs):
            relay_kernel(grid, sign, count, *refs)

        buf, *parcels = call("relay", kernel, [buf, *parcels], corners(count), kept=1)
        return buf, swap("gx", nx, *parcels)

    post, state0, staged, *parcels = call(
        "rim_first",
        rim_first_kernel,
        [populations, porosity, solid, labels],
        [padded(30), fields(7, g.local), stage] + faces(30, 1),
        [vmem(*porosity.shape)]
        + [pltpu.VMEM(porosity.shape, jnp.int32)] * 2
        + [pltpu.SemaphoreType.DMA((g.cols, 3)), pltpu.SemaphoreType.DMA((3,))],
    )
    along_x, along_y = swap_faces(parcels)
    post, state0, second, state1 = call(
        "inner_first",
        inner_first_kernel,
        [post, state0, staged],
        [padded(27), fields(7, g.extended)],
        kept=2,
        load=FLIGHT,
    )
    post, parcels = relay(post, along_y, 1, 30)
    post, second, state1, staged, field = call(
        "middle_second",
        lambda grid, _post, _out, _state, b, a, source, *refs: middle_second_kernel(
            grid, source, *refs, b, a
        ),
        [post, second, state1, *along_x, adjoint_in],
        [stage, padded(27)],
        kept=3,
        load=FLIGHT,
    )
    _, second, state1, staged, field, *parcels = call(
        "rim_seed",
        rim_seed_kernel,
        [post, second, state1, staged, field, *parcels, adjoint_in],
        faces(27, -1),
        kept=5,
    )
    along_x, along_y = swap_faces(parcels)
    _, field, pulled, before, final = call(
        "inner_seed",
        lambda grid, kept, into, buf, *refs: inner_seed_kernel(grid, buf, kept, into, *refs),
        [staged, field, second, state1, adjoint_in],
        [padded(27), fields(1, g.extended), whole],
        [sems],
        kept=2,
        load=FLIGHT,
    )
    field, parcels = relay(field, along_y, -1, 27)
    field, pulled, before, total, parts = call(
        "middle_adjoint",
        lambda grid, _field, _out, _before, near, far, b, a, *refs: middle_adjoint_kernel(
            grid, *refs, near, far, b, a
        ),
        [field, pulled, before, state1, state0, *along_x],
        [fields(1, g.local), fields(5, g.local)],
        kept=3,
        load=FLIGHT,
    )
    _, pulled, _, total, parts, peak = call(
        "total",
        total_kernel,
        [field, pulled, before, total, parts, state1, state0, *parcels],
        [vmem(8, LANES)],
        kept=5,
    )
    half = g.cols // 2
    scratch = [vmem(half, 27, rows, LANES), pltpu.SemaphoreType.DMA((half,))]
    halves = []

    def first_half(peak):
        def kernel(grid, buf, fields, near, echo, *refs):
            echo[...] = near[...]
            adjoint_kernel(grid, 1, half, buf, fields, *refs)

        echo, result = call(
            "adjoint_low",
            kernel,
            [pulled, parts, peak],
            [vmem(8, LANES), whole],
            scratch,
            load=FLIGHT // 2,
        )
        halves.append(result)
        return echo

    largest = largest_of_all(peak, sizes, first_half)
    (adjoint_out,) = call(
        "adjoint_high",
        lambda grid, buf, fields, _, *refs: adjoint_kernel(
            grid, 1 + half, g.cols, buf, fields, *refs
        ),
        [pulled, parts],
        [whole],
        scratch,
        load=FLIGHT // 2,
        result=halves[0],
    )
    (sensitivity,) = call(
        "normalize",
        scale_kernel,
        [total, largest],
        [jax.ShapeDtypeStruct(porosity.shape, F32)],
    )
    return final, adjoint_out, sensitivity


def solution(mesh):
    sizes = (mesh.shape["gx"], mesh.shape["gy"])
    whole, flat = P(None, "gx", "gy"), P("gx", "gy")
    return jax.shard_map(
        functools.partial(on_device, sizes),
        mesh=mesh,
        in_specs=(whole, whole, flat, flat, flat),
        out_specs=(whole, whole, flat),
        check_vma=False,
    )
```

```python
import functools

import jax
import jax.numpy as jnp
from jax import lax
from jax.experimental import pallas as pl
from jax.experimental.pallas import tpu as pltpu
from jax.sharding import PartitionSpec as P

NZ = 64
RELAX = 0.8
PUSH = 0.2
EPS = 1e-06
LANES = 128
VELOCITY = [(a, b, c) for a in (-1, 0, 1) for b in (-1, 0, 1) for c in (-1, 0, 1)]
INDEX = {v: i for i, v in enumerate(VELOCITY)}
WEIGHT = [
    [8.0 / 27, 2.0 / 27, 1.0 / 54, 1.0 / 216][abs(v[0]) + abs(v[1]) + abs(v[2])]
    for v in VELOCITY
]
NORM = [abs(v[0]) + abs(v[1]) + abs(v[2]) for v in VELOCITY]
F32 = jnp.float32
VMEM_LIMIT = 6 * 1024 * 1024
FLIGHT = 12 * 1024 * 1024


class Grid:
    def __init__(self, rows, width):
        self.rows = rows
        self.cols = width // LANES
        self.panel = rows + 16
        self.halo = self.cols + 1
        self.local = self.cols * rows
        self.extended = self.halo * rows + 24
        self.outer = ((0, 8), (rows - 8, 8))
        self.inner = tuple(((r, 16),) for r in range(8, rows - 8, 16))

    def at(self, i, k, r):
        return self.field(i) + k * self.panel + r

    def field(self, i):
        return i * (self.cols + 2) * self.panel + 8

    def padded(self, fields):
        return (fields * (self.cols + 2) * self.panel + 8, LANES)


def velocity(i, sign):
    return tuple(sign * n for n in VELOCITY[i]) if i < 27 else (0, 0, 0)


def moving(fields, sign, axis, side):
    return [i for i in range(fields) if velocity(i, sign)[axis] == side]


def lane_masks(height):
    lane = lax.broadcasted_iota(jnp.int32, (height, LANES), 1)
    return lane >= NZ, lane % NZ == 0, lane % NZ == NZ - 1


def shift_lanes(here, d, masks):
    first, last = masks[1:]
    dy, dz = d[1:]
    if dz == 0:
        return here if dy == 0 else pltpu.roll(here, NZ, 1)
    if dz == 1:
        one, other, edge = 1, NZ + 1, first
    else:
        one, other, edge = LANES - 1, NZ - 1, last
    inner, wrapped = (one, other) if dy == 0 else (other, one)
    return jnp.where(edge, pltpu.roll(here, wrapped, 1), pltpu.roll(here, inner, 1))


def pull(load, d, masks):
    high = masks[0]
    here = load(0)
    if d[1] == 1:
        here = jnp.where(high, load(-1), here)
    elif d[1] == -1:
        here = jnp.where(high, here, load(1))
    return shift_lanes(here, d, masks)


def stacked(parts):
    return parts[0] if len(parts) == 1 else jnp.concatenate(parts, 0)


def read_rows(ref, base, pieces):
    return stacked([ref[pl.ds(base + r, n), :] for r, n in pieces])


def write_rows(ref, base, pieces, value):
    done = 0
    for r, n in pieces:
        ref[pl.ds(base + r, n), :] = value[done : done + n]
        done += n


def pull_block(g, buf, sign, k, pieces, masks, fields=27):
    base = pl.multiple_of(k * g.panel, 8)
    after = pl.multiple_of(jnp.where(k == g.halo, g.panel, base + g.panel), 8)
    out = []
    for i in range(fields):
        d = velocity(i, sign)

        def load(n, i=i, d=d):
            start = {-1: base - g.panel, 0: base, 1: after}[n]
            return read_rows(buf, start + (g.field(i) - d[0]), pieces)

        out.append(pull(load, d, masks))
    return out


def pull_edge(g, buf, sign, side, masks, fields=27):
    out = []
    for i in range(fields):
        d = velocity(i, sign)
        if side == 1:
            row = g.rows - d[0]
        else:
            row = {1: g.rows, 0: g.rows + 1, -1: 0}[d[0]]

        def load(n, i=i, row=row):
            return buf[pl.ds(g.at(i, 1 + n, row), g.cols, stride=g.panel), :]

        out.append(pull(load, d, masks))
    return out


def moments(f):
    flat = {}
    along_z = None
    for a in (-1, 0, 1):
        for b in (-1, 0, 1):
            lo, mid, hi = (f[INDEX[(a, b, c)]] for c in (-1, 0, 1))
            flat[a, b] = lo + mid + hi
            diff = hi - lo
            along_z = diff if along_z is None else along_z + diff
    line = {}
    along_y = None
    for a in (-1, 0, 1):
        line[a] = flat[a, -1] + flat[a, 0] + flat[a, 1]
        diff = flat[a, 1] - flat[a, -1]
        along_y = diff if along_y is None else along_y + diff
    return line[-1] + line[0] + line[1], line[1] - line[-1], along_y, along_z


def combos(x, y, z):
    plane = {}
    for a in (-1, 0, 1):
        for b in (-1, 0, 1):
            if (a, b) > (0, 0):
                continue
            if a == 0:
                plane[a, b] = -y if b else None
            else:
                plane[a, b] = -x if b == 0 else (-x - y if b < 0 else y - x)
    out = []
    for a, b, c in VELOCITY[:13]:
        base = plane[a, b]
        if base is None:
            out.append(-z)
        else:
            out.append(base if c == 0 else (base - z if c < 0 else base + z))
    return out


def relax(f, rho, wx, wy, wz, damp, push, solid):
    ux, uy, uz = (wx + push) * damp, wy * damp, wz * damp
    base = 1.0 - 1.5 * (ux * ux + uy * uy + uz * uz)
    keep = 1.0 - 1.0 / RELAX
    gain = rho * (1.0 / RELAX)
    level = [gain * w for w in (8.0 / 27, 2.0 / 27, 1.0 / 54, 1.0 / 216)]
    along = combos(3.0 * ux, 3.0 * uy, 3.0 * uz)
    out = [None] * 27
    for i in range(13):
        j = 26 - i
        even = base + 0.5 * (along[i] * along[i])
        lift = level[NORM[i]]
        out[i] = jnp.where(solid, f[j], keep * f[i] + lift * (even + along[i]))
        out[j] = jnp.where(solid, f[i], keep * f[j] + lift * (even - along[i]))
    out[13] = jnp.where(solid, f[13], keep * f[13] + level[0] * base)
    return out


def pulled_moments(p):
    first = {}
    for a in (-1, 0, 1):
        for b in (-1, 0, 1):
            lo, mid, hi = (p[INDEX[(a, b, c)]] for c in (-1, 0, 1))
            both = lo + hi
            first[a, b] = (4.0 * mid + both, hi - lo, both)
    second = {}
    for a in (-1, 0, 1):
        lo, mid, hi = (first[a, b] for b in (-1, 0, 1))
        b0 = lo[0] + hi[0]
        b1 = lo[1] + hi[1]
        second[a] = dict(
            one=4.0 * mid[0] + b0,
            y=hi[0] - lo[0],
            yy=b0,
            z=4.0 * mid[1] + b1,
            yz=hi[1] - lo[1],
            zz=4.0 * mid[2] + lo[2] + hi[2],
        )
    lo, mid, hi = (second[a] for a in (-1, 0, 1))

    def full(key):
        return 4.0 * mid[key] + lo[key] + hi[key]

    xx = lo["one"] + hi["one"]
    return dict(
        one=4.0 * mid["one"] + xx,
        x=hi["one"] - lo["one"],
        xx=xx,
        y=full("y"),
        xy=hi["y"] - lo["y"],
        yy=full("yy"),
        z=full("z"),
        xz=hi["z"] - lo["z"],
        yz=full("yz"),
        zz=full("zz"),
    )


def adjoint_scalars(p, rho, wx, wy, wz, damp, push, solid):
    ux, uy, uz = (wx + push) * damp, wy * damp, wz * damp
    s = pulled_moments(p)
    scale = 1.0 / (216.0 * RELAX)
    one = s["one"] * scale
    b = [s[k] * (3.0 * scale) for k in ("x", "y", "z")]
    d = {k: s[k] * (9.0 * scale) for k in ("xx", "xy", "yy", "xz", "yz", "zz")}
    qx = d["xx"] * ux + d["xy"] * uy + d["xz"] * uz
    qy = d["xy"] * ux + d["yy"] * uy + d["yz"] * uz
    qz = d["xz"] * ux + d["yz"] * uy + d["zz"] * uz
    linear = b[0] * ux + b[1] * uy + b[2] * uz
    square = ux * ux + uy * uy + uz * uz
    even = one + linear + 0.5 * (qx * ux + qy * uy + qz * uz) - 1.5 * one * square
    three = 3.0 * one
    gx = (b[0] + qx - three * ux) * damp
    gy = (b[1] + qy - three * uy) * damp
    gz = (b[2] + qz - three * uz) * damp
    even = even - (gx * wx + gy * wy + gz * wz)
    porous = jnp.where(solid, 0.0, -rho * (gx * ux + gy * uy + gz * uz))
    return even, gx, gy, gz, porous


def adjoint_spread(p, even, gx, gy, gz, solid):
    keep = 1.0 - 1.0 / RELAX
    along = combos(gx, gy, gz)
    out = [None] * 27
    for i in range(13):
        j = 26 - i
        out[i] = jnp.where(solid, p[j], keep * p[i] + (even + along[i]))
        out[j] = jnp.where(solid, p[i], keep * p[j] + (even - along[i]))
    out[13] = jnp.where(solid, p[13], keep * p[13] + even)
    return out


def x_lines(g, sign, fields, side):
    lines = []
    for i in moving(fields, sign, 0, side):
        if side == 1:
            lines.append((i, g.rows - 1, (-1, g.rows + 1)))
            lines.append((i, g.rows - 2, (g.rows,)))
        else:
            lines += [(i, 0, (g.rows,)), (i, 1, (g.rows + 1,))]
    edge, target = (g.rows - 1, g.rows + 1) if side == 1 else (0, g.rows)
    return lines + [(i, edge, (target,)) for i in moving(fields, sign, 0, 0)]


def pack_x(g, buf, sign, fields, up, down):
    for side, ref in ((1, up), (-1, down)):
        for n, (i, r, _) in enumerate(x_lines(g, sign, fields, side)):
            ref[n * g.cols : (n + 1) * g.cols, :] = buf[
                pl.ds(g.at(i, 1, r), g.cols, stride=g.panel), :
            ]


def unpack_x(g, buf, sign, fields, up, down):
    for side, ref in ((1, up), (-1, down)):
        for n, (i, _, targets) in enumerate(x_lines(g, sign, fields, side)):
            value = ref[n * g.cols : (n + 1) * g.cols, :]
            for r in targets:
                buf[pl.ds(g.at(i, 1, r), g.cols, stride=g.panel), :] = value
    for i in moving(fields, sign, 0, -1):
        buf[pl.ds(g.at(i, 1, g.rows + 2), g.cols, stride=g.panel), :] = buf[
            pl.ds(g.at(i, 1, 0), g.cols, stride=g.panel), :
        ]


def halo_panels(g, i, sign):
    return (0, g.halo) if velocity(i, sign)[1] == 1 else (g.halo,)


def pack_corners(g, buf, sign, fields, up, down):
    for side, ref in ((1, up), (-1, down)):
        for n, (i, r, _) in enumerate(x_lines(g, sign, fields, side)):
            ref[n : n + 1, :] = buf[pl.ds(g.at(i, g.halo, r), 1), :]


def unpack_corners(g, buf, sign, fields, up, down):
    for side, ref in ((1, up), (-1, down)):
        for n, (i, _, targets) in enumerate(x_lines(g, sign, fields, side)):
            value = ref[n : n + 1, :]
            for r in targets:
                for k in halo_panels(g, i, sign):
                    buf[pl.ds(g.at(i, k, r), 1), :] = value
    for i in moving(fields, sign, 0, -1):
        for k in halo_panels(g, i, sign):
            buf[pl.ds(g.at(i, k, g.rows + 2), 1), :] = buf[pl.ds(g.at(i, k, 0), 1), :]


def still_pairs(fields, sign):
    still = moving(fields, sign, 1, 0)
    half = (len(still) + 1) // 2
    return [(still[n], still[n + half] if n + half < len(still) else None) for n in range(half)]


def y_slots(fields, sign):
    return 9 + len(still_pairs(fields, sign))


def pack_y(g, buf, sign, fields, up, down):
    high = lane_masks(g.rows)[0]
    for side, ref in ((1, up), (-1, down)):
        k = g.cols if side == 1 else 1
        for n, i in enumerate(moving(fields, sign, 1, side)):
            ref[n * g.rows : (n + 1) * g.rows, :] = buf[pl.ds(g.at(i, k, 0), g.rows), :]
        for n, (i, j) in enumerate(still_pairs(fields, sign)):
            value = buf[pl.ds(g.at(i, k, 0), g.rows), :]
            if j is not None:
                other = pltpu.roll(buf[pl.ds(g.at(j, k, 0), g.rows), :], NZ, 1)
                pair = (value, other) if side == 1 else (other, value)
                value = jnp.where(high, *pair)
            ref[(9 + n) * g.rows : (10 + n) * g.rows, :] = value


def unpack_y(g, buf, sign, fields, high, up, down):
    for side, ref in ((1, up), (-1, down)):
        for n, i in enumerate(moving(fields, sign, 1, side)):
            value = ref[n * g.rows : (n + 1) * g.rows, :]
            for k in halo_panels(g, i, sign):
                buf[pl.ds(g.at(i, k, 0), g.rows), :] = value
    for n, (i, j) in enumerate(still_pairs(fields, sign)):
        spot = slice((9 + n) * g.rows, (10 + n) * g.rows)
        before, after = up[spot, :], down[spot, :]
        buf[pl.ds(g.at(i, g.halo, 0), g.rows), :] = jnp.where(high, before, after)
        if j is not None:
            value = pltpu.roll(jnp.where(high, after, before), NZ, 1)
            buf[pl.ds(g.at(j, g.halo, 0), g.rows), :] = value


def by_parity(axis, first, second, act):
    even = lax.rem(lax.axis_index(axis), 2) == 0

    @pl.when(even)
    def _():
        act(first, second)

    @pl.when(jnp.logical_not(even))
    def _():
        act(second, first)


def load_fields(ref, rows, base, pieces, count):
    return [read_rows(ref, base + n * rows, pieces) for n in range(count)]


def save_fields(ref, rows, base, pieces, values):
    for n, value in enumerate(values):
        write_rows(ref, base + n * rows, pieces, value)


def save_populations(g, out, k, pieces, values):
    base = pl.multiple_of(k * g.panel, 8)
    for i, value in enumerate(values):
        write_rows(out, base + g.field(i), pieces, value)


def spot_of(g, k):
    return pl.multiple_of((k - 1) * g.rows, 8)


def lanes_of(k):
    return pl.ds(pl.multiple_of((k - 1) * LANES, LANES), LANES)


def every(first, last, act):
    def step(k, carry):
        act(k)
        return carry

    count = last + 1 - first
    unroll = max(n for n in (1, 2, 3, 4) if count % n == 0)
    lax.fori_loop(first, last + 1, step, 0, unroll=unroll)


def side_panels(g, act, count):
    def step(n, carry):
        act(jnp.where(n == 0, 1, g.cols - 1 + n))
        return carry

    lax.fori_loop(0, count, step, 0, unroll=count)


def interior_tiles(g, act):
    for pieces in g.inner:
        every(2, g.cols - 1, functools.partial(act, pieces=pieces))


def middle_tiles(g, act):
    for pieces in g.inner:
        side_panels(g, functools.partial(act, pieces=pieces), 3)
    every(2, g.cols - 1, functools.partial(act, pieces=g.outer))


def core_tiles(g, act):
    for pieces in g.inner:
        every(3, g.cols - 2, functools.partial(act, pieces=pieces))


def near_core_tiles(g, act):
    def step(n, carry):
        for pieces in g.inner:
            act(jnp.where(n == 0, 2, g.cols - 1), pieces=pieces)
        return carry

    lax.fori_loop(0, 2, step, 0, unroll=2)


def rim_tiles(g, act):
    every(1, g.cols, functools.partial(act, pieces=g.outer))
    for pieces in g.inner:
        side_panels(g, functools.partial(act, pieces=pieces), 2)


def step_tile(g, buf, out, sign, fields, masks, compute):
    def act(k, pieces):
        values = compute(
            pull_block(g, buf, sign, k, pieces, masks, fields), spot_of(g, k), pieces
        )
        save_populations(g, out, k, pieces, values)

    return act


def corner_tiles(g, buf, out, sign, fields, masks, compute):
    small = tuple(mask[:8] for mask in masks)
    act = step_tile(g, buf, out, sign, fields, masks, compute)
    side_panels(g, functools.partial(act, pieces=g.outer), 3)
    spot = g.halo * g.rows
    pieces = ((g.rows, 8),)
    values = compute(pull_block(g, buf, sign, g.halo, pieces, small, fields), spot, ((0, 8),))
    for i in range(27):
        dx = velocity(i, sign)[0]
        if dx == -1:
            out[pl.ds(g.at(i, g.halo, g.rows), 1), :] = values[i][0:1]
        elif dx == 1:
            out[pl.ds(g.at(i, g.halo, -1), 1), :] = values[i][1:2]
    edges = [pull_edge(g, buf, sign, side, small, fields) for side in (1, -1)]
    both = [stacked(pair) for pair in zip(*edges)]
    values = compute(both, spot, ((8, 16),))
    for i in moving(27, sign, 0, -1):
        out[pl.ds(g.at(i, 1, g.rows), g.cols, stride=g.panel), :] = values[i][:8]
    for i in moving(27, sign, 0, 1):
        out[pl.ds(g.at(i, 1, -1), g.cols, stride=g.panel), :] = values[i][8:]
    for i in moving(27, sign, 1, 1):
        out[pl.ds(g.at(i, 0, 0), g.rows), :] = out[pl.ds(g.at(i, g.halo, 0), g.rows), :]
        for r in (-1, g.rows):
            out[pl.ds(g.at(i, 0, r), 1), :] = out[pl.ds(g.at(i, g.halo, r), 1), :]


def flow_of(f):
    rho, mx, my, mz = moments(f)
    inverse = 1.0 / rho
    return inverse, rho, mx * inverse, my * inverse, mz * inverse


def collide_first(g, state, out):
    def act(k, pieces, f):
        base = pl.multiple_of(k * g.panel, 8)
        damp, push, wall = (read_rows(out, base + g.field(i), pieces) for i in (27, 28, 29))
        flow = flow_of(f)[1:] + (damp, push)
        save_fields(state, g.local, spot_of(g, k), pieces, flow + (wall,))
        save_populations(g, out, k, pieces, relax(f, *flow, wall > 0.5))

    return act


def collide_second(g, state):
    def compute(values, spot, pieces):
        f, (damp, push, wall) = values[:27], values[27:]
        flow = flow_of(f)[1:] + (damp, push)
        save_fields(state, g.extended, spot, pieces, flow + (wall,))
        return relax(f, *flow, wall > 0.5)

    return compute


def adjoint_second(g, state, total):
    def compute(p, spot, pieces):
        *flow, wall = load_fields(state, g.extended, spot, pieces, 7)
        *spread, porous = adjoint_scalars(p, *flow, wall > 0.5)
        save_fields(total, g.extended, spot, pieces, [porous])
        return adjoint_spread(p, *spread, wall > 0.5)

    return compute


def seed_tile(g, buf, adjoint, stage, out, masks):
    def act(k, pieces):
        f = pull_block(g, buf, 1, k, pieces, masks)
        for i in range(27):
            write_rows(stage.at[k - 1, i], 0, pieces, f[i])
        inverse, _, wx, wy, wz = flow_of(f)
        even = -(wx * wx + wy * wy + wz * wz) * inverse
        along = combos(wx * inverse, wy * inverse, wz * inverse)
        lanes = lanes_of(k)
        seeded = [
            stacked([adjoint[i, pl.ds(r, n), lanes] for r, n in pieces]) + even for i in range(27)
        ]
        for i in range(13):
            seeded[i] = seeded[i] + along[i]
            seeded[26 - i] = seeded[26 - i] - along[i]
        save_populations(g, out, k, pieces, seeded)

    return act


def block_of(ref, k):
    return ref.at[:, :, lanes_of(k)]


def flat_fields(g, out, near, k):
    porosity, solid, labels = near
    lanes = lanes_of(k)
    label = labels[:, lanes]
    damp = 1.0 / (1.0 + porosity[:, lanes])
    push = jnp.where(label == 1, PUSH, jnp.where(label == 2, -PUSH, 0.0))
    base = pl.multiple_of(k * g.panel, 8)
    for i, value in ((27, damp), (28, push), (29, solid[:, lanes].astype(F32))):
        out[pl.ds(base + g.field(i), g.rows), :] = value


def staged_tile(g, collide, stage):
    def act(k, pieces):
        collide(k, pieces, [read_rows(stage.at[k - 1, i], 0, pieces) for i in range(27)])

    return act


def side_tiles(g, act):
    for pieces in (g.outer,) + g.inner:
        side_panels(g, functools.partial(act, pieces=pieces), 2)


def side_first_kernel(g, pops, *refs):
    flat, (out, state, stage), near, faces, (sems, flat_sems) = (
        refs[:3],
        refs[3:6],
        refs[6:9],
        refs[9:11],
        refs[11:],
    )

    def copy(k):
        return pltpu.make_async_copy(block_of(pops, k), stage.at[k - 1], sems.at[k - 1])

    flat_copies = [
        pltpu.make_async_copy(source, target, flat_sems.at[n])
        for n, (source, target) in enumerate(zip(flat, near))
    ]
    for each in flat_copies:
        each.start()
    for k in (1, g.cols, *range(2, g.cols)):
        copy(k).start()
    for each in flat_copies:
        each.wait()
    for k in (1, g.cols):
        flat_fields(g, out, near, k)
    copy(1).wait()
    copy(g.cols).wait()
    side_tiles(g, staged_tile(g, collide_first(g, state, out), stage))
    by_parity("gy", *faces, functools.partial(pack_y, g, out, 1, 30))
    for k in range(2, g.cols):
        copy(k).wait()


def rim_first_kernel(g, _out, _state, stage, *refs):
    near, (out, state), faces = refs[:3], refs[3:5], refs[5:]
    every(2, g.cols - 1, functools.partial(flat_fields, g, out, near))
    act = staged_tile(g, collide_first(g, state, out), stage)
    every(2, g.cols - 1, functools.partial(act, pieces=g.outer))
    by_parity("gx", *faces, functools.partial(pack_x, g, out, 1, 30))


def inner_first_kernel(g, _, _state, stage, post, state0, out, state1):
    masks = lane_masks(16)
    interior_tiles(g, staged_tile(g, collide_first(g, state0, post), stage))
    interior_tiles(g, step_tile(g, post, out, 1, 30, masks, collide_second(g, state1)))


def relay_kernel(g, sign, fields, _, y_second, y_first, buf, first, second):
    high = lane_masks(g.rows)[0]
    by_parity("gy", y_second, y_first, functools.partial(unpack_y, g, buf, sign, fields, high))
    by_parity("gx", first, second, functools.partial(pack_corners, g, buf, sign, fields))


def middle_second_kernel(g, adjoint, post, out, state1, stage, field, x_second, x_first):
    masks = lane_masks(16)
    by_parity("gx", x_second, x_first, functools.partial(unpack_x, g, post, 1, 30))
    middle_tiles(g, step_tile(g, post, out, 1, 30, masks, collide_second(g, state1)))
    core_tiles(g, seed_tile(g, out, adjoint, stage, field, masks))


def side_seed_kernel(g, _post, _out, _state, _stage, _field, first, second, adjoint, *refs):
    post, out, state1, stage, field, *faces = refs
    masks = lane_masks(16)
    by_parity("gx", second, first, functools.partial(unpack_corners, g, post, 1, 30))
    corner_tiles(g, post, out, 1, 30, masks, collide_second(g, state1))
    side_tiles(g, seed_tile(g, out, adjoint, stage, field, masks))
    by_parity("gy", *faces, functools.partial(pack_y, g, field, -1, 27))


def rim_seed_kernel(g, _stage, _field, out, adjoint, stage, field, *faces):
    seed = seed_tile(g, out, adjoint, stage, field, lane_masks(16))
    every(2, g.cols - 1, functools.partial(seed, pieces=g.outer))
    by_parity("gx", *faces, functools.partial(pack_x, g, field, -1, 27))


def inner_seed_kernel(
    g, post, _stage, _field, state1, adjoint, stage, field, out, total, final, sems
):
    masks = lane_masks(16)

    def copy(k):
        return pltpu.make_async_copy(stage.at[k - 1], block_of(final, k), sems.at[k - 1])

    copy(1).start()
    copy(g.cols).start()
    seed = seed_tile(g, post, adjoint, stage, field, masks)

    near_core_tiles(g, seed)
    every(2, g.cols - 1, lambda k: copy(k).start())
    interior_tiles(g, step_tile(g, field, out, -1, 27, masks, adjoint_second(g, state1, total)))
    every(1, g.cols, lambda k: copy(k).wait())


def total_tile(g, out, before, state0, total, parts, masks):
    def act(k, pieces):
        p = pull_block(g, out, -1, k, pieces, masks)
        spot = spot_of(g, k)
        *flow, wall = load_fields(state0, g.local, spot, pieces, 7)
        *spread, porous = adjoint_scalars(p, *flow, wall > 0.5)
        here = load_fields(before, g.extended, spot, pieces, 1)[0] + porous
        save_fields(total, g.local, spot, pieces, [here])
        save_fields(parts, g.local, spot, pieces, spread + [wall])

    return act


def middle_adjoint_kernel(g, field, out, before, total, parts, state1, state0, x_second, x_first):
    masks = lane_masks(16)
    by_parity("gx", x_second, x_first, functools.partial(unpack_x, g, field, -1, 27))
    middle_tiles(g, step_tile(g, field, out, -1, 27, masks, adjoint_second(g, state1, before)))
    core_tiles(g, total_tile(g, out, before, state0, total, parts, masks))


def total_kernel(g, *refs):
    state1, state0, first, second, field, out, before, total, parts, peak = refs[5:]
    masks = lane_masks(16)
    by_parity("gx", second, first, functools.partial(unpack_corners, g, field, -1, 27))
    corner_tiles(g, field, out, -1, 27, masks, adjoint_second(g, state1, before))
    act = total_tile(g, out, before, state0, total, parts, masks)
    near_core_tiles(g, act)
    rim_tiles(g, act)
    size = 8 * (g.local // 64)
    largest = jnp.zeros((8, LANES), F32)
    for start in range(0, g.local, size):
        value = jnp.abs(total[start : start + size, :]).reshape(-1, 8, LANES)
        largest = jnp.maximum(largest, jnp.max(value, 0))
    peak[...] = largest


def adjoint_kernel(g, first, last, buf, parts, result, stage, sems):
    masks = lane_masks(16)

    def copy(k):
        return pltpu.make_async_copy(stage.at[k - first], block_of(result, k), sems.at[k - first])

    def column(k):
        for pieces in (g.outer,) + g.inner:
            p = pull_block(g, buf, -1, k, pieces, masks)
            *spread, wall = load_fields(parts, g.local, spot_of(g, k), pieces, 5)
            for i, value in enumerate(adjoint_spread(p, *spread, wall > 0.5)):
                write_rows(stage.at[k - first, i], 0, pieces, value)
        copy(k).start()

    every(first, last, column)
    every(first, last, lambda k: copy(k).wait())


def scale_kernel(g, total, peak, out):
    largest = jnp.max(peak[...])
    factor = 1.0 / (jnp.full((g.rows, LANES), largest, F32) + EPS)
    for c in range(g.cols):
        value = total[c * g.rows : (c + 1) * g.rows, :] * factor
        out[:, c * LANES : (c + 1) * LANES] = value


def swap_pairs(count, start):
    pairs = []
    for i in range(start, count, 2):
        j = (i + 1) % count
        pairs += [(i, j), (j, i)]
    return pairs


def swap(axis, count, first, second):
    return (
        lax.ppermute(first, axis, swap_pairs(count, 0)),
        lax.ppermute(second, axis, swap_pairs(count, 1)),
    )


def largest_of_all(peak, sizes, beside):
    nx, ny = sizes
    peak = jnp.maximum(peak, lax.ppermute(peak, "gy", [(i, i ^ 1) for i in range(ny)]))
    groups = 0
    for axis, count, first, widths in (("gy", ny, 2, (4, 4)), ("gx", nx, 1, (4, 2))):
        step = first
        for width in widths:
            width = min(width, count // step)
            parts = []
            for n in range(1, width):
                if axis == "gy":
                    pairs = [(i, i ^ (n * step) ^ 1) for i in range(ny)]
                    parts.append(lax.ppermute(peak, "gy", pairs))
                else:
                    pairs = [
                        (i * ny + y, (i ^ (n * step)) * ny + (y ^ 1))
                        for i in range(nx)
                        for y in range(ny)
                    ]
                    parts.append(lax.ppermute(peak, ("gx", "gy"), pairs))
            groups += 1
            if groups == 1:
                peak = beside(peak)
            peak = functools.reduce(jnp.maximum, parts, peak)
            step *= width
    return peak


def on_device(sizes, populations, adjoint_in, porosity, solid, labels):
    rows, width = porosity.shape
    g = Grid(rows, width)
    in_vmem = pl.BlockSpec(memory_space=pltpu.VMEM)
    in_hbm = pl.BlockSpec(memory_space=pltpu.HBM)
    nx, ny = sizes

    def vmem(*shape):
        return pltpu.VMEM(shape, F32)

    def fields(count, size):
        return vmem(count * size, LANES)

    def padded(count):
        return vmem(*g.padded(count))

    def x_faces(count):
        return [vmem(count * g.cols, LANES)] * 2

    def y_faces(count, sign):
        return [vmem(y_slots(count, sign) * rows, LANES)] * 2

    def corners(count):
        return [vmem(-(-count // 8) * 8, LANES)] * 2

    whole = pltpu.HBM(populations.shape, F32)
    stage = vmem(g.cols, 27, rows, LANES)
    sems = pltpu.SemaphoreType.DMA((g.cols,))

    def call(name, kernel, operands, out_shape, scratch=(), kept=0, load=0, result=None):
        out_shape = [pltpu.VMEM(x.shape, x.dtype) for x in operands[:kept]] + out_shape
        aliases = {n: n for n in range(kept)}
        space = pltpu.HBM if name == "side_first" else pltpu.VMEM
        pinned = [pltpu.with_memory_space_constraint(x, space) for x in operands]
        in_specs = [pl.BlockSpec(memory_space=space)] * len(operands)
        if result is not None:
            aliases[len(operands)] = len(out_shape) - 1
            pinned.append(pltpu.with_memory_space_constraint(result, pltpu.HBM))
            in_specs.append(in_hbm)
        return pl.pallas_call(
            functools.partial(kernel, g),
            in_specs=in_specs,
            out_shape=out_shape,
            out_specs=[in_hbm if x is whole else in_vmem for x in out_shape],
            scratch_shapes=list(scratch),
            input_output_aliases=aliases,
            compiler_params=pltpu.CompilerParams(vmem_limit_bytes=VMEM_LIMIT),
            cost_estimate=pl.CostEstimate(flops=0, bytes_accessed=load, transcendentals=0)
            if load
            else None,
            name=name,
        )(*pinned)

    def swap_faces(axis, count, parcels):
        return swap(axis, count, *parcels)[::-1]

    def relay(buf, parcels, sign, count):
        def kernel(grid, *refs):
            relay_kernel(grid, sign, count, *refs)

        buf, *parcels = call("relay", kernel, [buf, *parcels], corners(count), kept=1)
        return buf, swap("gx", nx, *parcels)

    flat_space = [vmem(*porosity.shape)] + [pltpu.VMEM(porosity.shape, jnp.int32)] * 2
    post, state0, staged, *rest = call(
        "side_first",
        side_first_kernel,
        [populations, porosity, solid, labels],
        [padded(30), fields(7, g.local), stage] + flat_space + y_faces(30, 1),
        [sems, pltpu.SemaphoreType.DMA((3,))],
    )
    along_y = swap_faces("gy", ny, rest[3:])
    post, state0, *parcels = call(
        "rim_first",
        rim_first_kernel,
        [post, state0, staged, *rest[:3]],
        x_faces(30),
        kept=2,
        load=FLIGHT,
    )
    along_x = swap_faces("gx", nx, parcels)
    post, state0, second, state1 = call(
        "inner_first",
        inner_first_kernel,
        [post, state0, staged],
        [padded(27), fields(7, g.extended)],
        kept=2,
        load=FLIGHT,
    )
    post, parcels = relay(post, along_y, 1, 30)
    post, second, state1, staged, field = call(
        "middle_second",
        lambda grid, _post, _out, _state, b, a, source, *refs: middle_second_kernel(
            grid, source, *refs, b, a
        ),
        [post, second, state1, *along_x, adjoint_in],
        [stage, padded(27)],
        kept=3,
        load=FLIGHT,
    )
    _, second, state1, staged, field, *parcels = call(
        "side_seed",
        side_seed_kernel,
        [post, second, state1, staged, field, *parcels, adjoint_in],
        y_faces(27, -1),
        kept=5,
    )
    along_y = swap_faces("gy", ny, parcels)
    staged, field, *parcels = call(
        "rim_seed",
        rim_seed_kernel,
        [staged, field, second, adjoint_in],
        x_faces(27),
        kept=2,
        load=FLIGHT,
    )
    along_x = swap_faces("gx", nx, parcels)
    _, field, pulled, before, final = call(
        "inner_seed",
        lambda grid, kept, into, buf, *refs: inner_seed_kernel(grid, buf, kept, into, *refs),
        [staged, field, second, state1, adjoint_in],
        [padded(27), fields(1, g.extended), whole],
        [sems],
        kept=2,
        load=FLIGHT,
    )
    field, parcels = relay(field, along_y, -1, 27)
    field, pulled, before, total, parts = call(
        "middle_adjoint",
        lambda grid, _field, _out, _before, near, far, b, a, *refs: middle_adjoint_kernel(
            grid, *refs, near, far, b, a
        ),
        [field, pulled, before, state1, state0, *along_x],
        [fields(1, g.local), fields(5, g.local)],
        kept=3,
        load=FLIGHT,
    )
    _, pulled, _, total, parts, peak = call(
        "total",
        total_kernel,
        [field, pulled, before, total, parts, state1, state0, *parcels],
        [vmem(8, LANES)],
        kept=5,
    )
    half = g.cols // 2
    scratch = [vmem(half, 27, rows, LANES), pltpu.SemaphoreType.DMA((half,))]
    halves = []

    def first_half(peak):
        def kernel(grid, buf, fields, near, echo, *refs):
            echo[...] = near[...]
            adjoint_kernel(grid, 1, half, buf, fields, *refs)

        echo, result = call(
            "adjoint_low",
            kernel,
            [pulled, parts, peak],
            [vmem(8, LANES), whole],
            scratch,
            load=FLIGHT // 2,
        )
        halves.append(result)
        return echo

    largest = largest_of_all(peak, sizes, first_half)
    (adjoint_out,) = call(
        "adjoint_high",
        lambda grid, buf, fields, _, *refs: adjoint_kernel(
            grid, 1 + half, g.cols, buf, fields, *refs
        ),
        [pulled, parts],
        [whole],
        scratch,
        load=FLIGHT // 2,
        result=halves[0],
    )
    (sensitivity,) = call(
        "normalize",
        scale_kernel,
        [total, largest],
        [jax.ShapeDtypeStruct(porosity.shape, F32)],
    )
    return final, adjoint_out, sensitivity


def solution(mesh):
    sizes = (mesh.shape["gx"], mesh.shape["gy"])
    whole, flat = P(None, "gx", "gy"), P("gx", "gy")
    return jax.shard_map(
        functools.partial(on_device, sizes),
        mesh=mesh,
        in_specs=(whole, whole, flat, flat, flat),
        out_specs=(whole, whole, flat),
        check_vma=False,
    )
```

```python
import functools

import jax
import jax.numpy as jnp
from jax import lax
from jax.experimental import pallas as pl
from jax.experimental.pallas import tpu as pltpu
from jax.sharding import PartitionSpec as P

NZ = 64
RELAX = 0.8
PUSH = 0.2
EPS = 1e-06
LANES = 128
VELOCITY = [(a, b, c) for a in (-1, 0, 1) for b in (-1, 0, 1) for c in (-1, 0, 1)]
INDEX = {v: i for i, v in enumerate(VELOCITY)}
WEIGHT = [
    [8.0 / 27, 2.0 / 27, 1.0 / 54, 1.0 / 216][abs(v[0]) + abs(v[1]) + abs(v[2])]
    for v in VELOCITY
]
NORM = [abs(v[0]) + abs(v[1]) + abs(v[2]) for v in VELOCITY]
F32 = jnp.float32
VMEM_LIMIT = 6 * 1024 * 1024
FLIGHT = 12 * 1024 * 1024


class Grid:
    def __init__(self, rows, width):
        self.rows = rows
        self.cols = width // LANES
        self.panel = rows + 16
        self.halo = self.cols + 1
        self.local = self.cols * rows
        self.extended = self.halo * rows + 24
        self.outer = ((0, 8), (rows - 8, 8))
        self.inner = tuple(((r, 16),) for r in range(8, rows - 8, 16))

    def at(self, i, k, r):
        return self.field(i) + k * self.panel + r

    def field(self, i):
        return i * (self.cols + 2) * self.panel + 8

    def padded(self, fields):
        return (fields * (self.cols + 2) * self.panel + 8, LANES)


def velocity(i, sign):
    return tuple(sign * n for n in VELOCITY[i]) if i < 27 else (0, 0, 0)


def moving(fields, sign, axis, side):
    return [i for i in range(fields) if velocity(i, sign)[axis] == side]


def lane_masks(height):
    lane = lax.broadcasted_iota(jnp.int32, (height, LANES), 1)
    return lane >= NZ, lane % NZ == 0, lane % NZ == NZ - 1


def shift_lanes(here, d, masks):
    first, last = masks[1:]
    dy, dz = d[1:]
    if dz == 0:
        return here if dy == 0 else pltpu.roll(here, NZ, 1)
    if dz == 1:
        one, other, edge = 1, NZ + 1, first
    else:
        one, other, edge = LANES - 1, NZ - 1, last
    inner, wrapped = (one, other) if dy == 0 else (other, one)
    return jnp.where(edge, pltpu.roll(here, wrapped, 1), pltpu.roll(here, inner, 1))


def pull(load, d, masks):
    high = masks[0]
    here = load(0)
    if d[1] == 1:
        here = jnp.where(high, load(-1), here)
    elif d[1] == -1:
        here = jnp.where(high, here, load(1))
    return shift_lanes(here, d, masks)


def stacked(parts):
    return parts[0] if len(parts) == 1 else jnp.concatenate(parts, 0)


def read_rows(ref, base, pieces):
    return stacked([ref[pl.ds(base + r, n), :] for r, n in pieces])


def write_rows(ref, base, pieces, value):
    done = 0
    for r, n in pieces:
        ref[pl.ds(base + r, n), :] = value[done : done + n]
        done += n


def pull_block(g, buf, sign, k, pieces, masks, fields=27):
    base = pl.multiple_of(k * g.panel, 8)
    after = pl.multiple_of(jnp.where(k == g.halo, g.panel, base + g.panel), 8)
    out = []
    for i in range(fields):
        d = velocity(i, sign)

        def load(n, i=i, d=d):
            start = {-1: base - g.panel, 0: base, 1: after}[n]
            return read_rows(buf, start + (g.field(i) - d[0]), pieces)

        out.append(pull(load, d, masks))
    return out


def pull_edge(g, buf, sign, side, masks, fields=27):
    out = []
    for i in range(fields):
        d = velocity(i, sign)
        if side == 1:
            row = g.rows - d[0]
        else:
            row = {1: g.rows, 0: g.rows + 1, -1: 0}[d[0]]

        def load(n, i=i, row=row):
            return buf[pl.ds(g.at(i, 1 + n, row), g.cols, stride=g.panel), :]

        out.append(pull(load, d, masks))
    return out


def moments(f):
    flat = {}
    along_z = None
    for a in (-1, 0, 1):
        for b in (-1, 0, 1):
            lo, mid, hi = (f[INDEX[(a, b, c)]] for c in (-1, 0, 1))
            flat[a, b] = lo + mid + hi
            diff = hi - lo
            along_z = diff if along_z is None else along_z + diff
    line = {}
    along_y = None
    for a in (-1, 0, 1):
        line[a] = flat[a, -1] + flat[a, 0] + flat[a, 1]
        diff = flat[a, 1] - flat[a, -1]
        along_y = diff if along_y is None else along_y + diff
    return line[-1] + line[0] + line[1], line[1] - line[-1], along_y, along_z


def combos(x, y, z):
    plane = {}
    for a in (-1, 0, 1):
        for b in (-1, 0, 1):
            if (a, b) > (0, 0):
                continue
            if a == 0:
                plane[a, b] = -y if b else None
            else:
                plane[a, b] = -x if b == 0 else (-x - y if b < 0 else y - x)
    out = []
    for a, b, c in VELOCITY[:13]:
        base = plane[a, b]
        if base is None:
            out.append(-z)
        else:
            out.append(base if c == 0 else (base - z if c < 0 else base + z))
    return out


def relax(f, rho, wx, wy, wz, damp, push, solid):
    ux, uy, uz = (wx + push) * damp, wy * damp, wz * damp
    base = 1.0 - 1.5 * (ux * ux + uy * uy + uz * uz)
    keep = 1.0 - 1.0 / RELAX
    gain = rho * (1.0 / RELAX)
    level = [gain * w for w in (8.0 / 27, 2.0 / 27, 1.0 / 54, 1.0 / 216)]
    along = combos(3.0 * ux, 3.0 * uy, 3.0 * uz)
    out = [None] * 27
    for i in range(13):
        j = 26 - i
        even = base + 0.5 * (along[i] * along[i])
        lift = level[NORM[i]]
        out[i] = jnp.where(solid, f[j], keep * f[i] + lift * (even + along[i]))
        out[j] = jnp.where(solid, f[i], keep * f[j] + lift * (even - along[i]))
    out[13] = jnp.where(solid, f[13], keep * f[13] + level[0] * base)
    return out


def pulled_moments(p):
    first = {}
    for a in (-1, 0, 1):
        for b in (-1, 0, 1):
            lo, mid, hi = (p[INDEX[(a, b, c)]] for c in (-1, 0, 1))
            both = lo + hi
            first[a, b] = (4.0 * mid + both, hi - lo, both)
    second = {}
    for a in (-1, 0, 1):
        lo, mid, hi = (first[a, b] for b in (-1, 0, 1))
        b0 = lo[0] + hi[0]
        b1 = lo[1] + hi[1]
        second[a] = dict(
            one=4.0 * mid[0] + b0,
            y=hi[0] - lo[0],
            yy=b0,
            z=4.0 * mid[1] + b1,
            yz=hi[1] - lo[1],
            zz=4.0 * mid[2] + lo[2] + hi[2],
        )
    lo, mid, hi = (second[a] for a in (-1, 0, 1))

    def full(key):
        return 4.0 * mid[key] + lo[key] + hi[key]

    xx = lo["one"] + hi["one"]
    return dict(
        one=4.0 * mid["one"] + xx,
        x=hi["one"] - lo["one"],
        xx=xx,
        y=full("y"),
        xy=hi["y"] - lo["y"],
        yy=full("yy"),
        z=full("z"),
        xz=hi["z"] - lo["z"],
        yz=full("yz"),
        zz=full("zz"),
    )


def adjoint_scalars(p, rho, wx, wy, wz, damp, push, solid):
    ux, uy, uz = (wx + push) * damp, wy * damp, wz * damp
    s = pulled_moments(p)
    scale = 1.0 / (216.0 * RELAX)
    one = s["one"] * scale
    b = [s[k] * (3.0 * scale) for k in ("x", "y", "z")]
    d = {k: s[k] * (9.0 * scale) for k in ("xx", "xy", "yy", "xz", "yz", "zz")}
    qx = d["xx"] * ux + d["xy"] * uy + d["xz"] * uz
    qy = d["xy"] * ux + d["yy"] * uy + d["yz"] * uz
    qz = d["xz"] * ux + d["yz"] * uy + d["zz"] * uz
    linear = b[0] * ux + b[1] * uy + b[2] * uz
    square = ux * ux + uy * uy + uz * uz
    even = one + linear + 0.5 * (qx * ux + qy * uy + qz * uz) - 1.5 * one * square
    three = 3.0 * one
    gx = (b[0] + qx - three * ux) * damp
    gy = (b[1] + qy - three * uy) * damp
    gz = (b[2] + qz - three * uz) * damp
    even = even - (gx * wx + gy * wy + gz * wz)
    porous = jnp.where(solid, 0.0, -rho * (gx * ux + gy * uy + gz * uz))
    return even, gx, gy, gz, porous


def adjoint_spread(p, even, gx, gy, gz, solid):
    keep = 1.0 - 1.0 / RELAX
    along = combos(gx, gy, gz)
    out = [None] * 27
    for i in range(13):
        j = 26 - i
        out[i] = jnp.where(solid, p[j], keep * p[i] + (even + along[i]))
        out[j] = jnp.where(solid, p[i], keep * p[j] + (even - along[i]))
    out[13] = jnp.where(solid, p[13], keep * p[13] + even)
    return out


def x_lines(g, sign, fields, side):
    lines = []
    for i in moving(fields, sign, 0, side):
        if side == 1:
            lines.append((i, g.rows - 1, (-1, g.rows + 1)))
            lines.append((i, g.rows - 2, (g.rows,)))
        else:
            lines += [(i, 0, (g.rows,)), (i, 1, (g.rows + 1,))]
    edge, target = (g.rows - 1, g.rows + 1) if side == 1 else (0, g.rows)
    return lines + [(i, edge, (target,)) for i in moving(fields, sign, 0, 0)]


def pack_x(g, buf, sign, fields, up, down):
    for side, ref in ((1, up), (-1, down)):
        for n, (i, r, _) in enumerate(x_lines(g, sign, fields, side)):
            ref[n * g.cols : (n + 1) * g.cols, :] = buf[
                pl.ds(g.at(i, 1, r), g.cols, stride=g.panel), :
            ]


def unpack_x(g, buf, sign, fields, up, down):
    for side, ref in ((1, up), (-1, down)):
        for n, (i, _, targets) in enumerate(x_lines(g, sign, fields, side)):
            value = ref[n * g.cols : (n + 1) * g.cols, :]
            for r in targets:
                buf[pl.ds(g.at(i, 1, r), g.cols, stride=g.panel), :] = value
    for i in moving(fields, sign, 0, -1):
        buf[pl.ds(g.at(i, 1, g.rows + 2), g.cols, stride=g.panel), :] = buf[
            pl.ds(g.at(i, 1, 0), g.cols, stride=g.panel), :
        ]


def halo_panels(g, i, sign):
    return (0, g.halo) if velocity(i, sign)[1] == 1 else (g.halo,)


def pack_corners(g, buf, sign, fields, up, down):
    for side, ref in ((1, up), (-1, down)):
        for n, (i, r, _) in enumerate(x_lines(g, sign, fields, side)):
            ref[n : n + 1, :] = buf[pl.ds(g.at(i, g.halo, r), 1), :]


def unpack_corners(g, buf, sign, fields, up, down):
    for side, ref in ((1, up), (-1, down)):
        for n, (i, _, targets) in enumerate(x_lines(g, sign, fields, side)):
            value = ref[n : n + 1, :]
            for r in targets:
                for k in halo_panels(g, i, sign):
                    buf[pl.ds(g.at(i, k, r), 1), :] = value
    for i in moving(fields, sign, 0, -1):
        for k in halo_panels(g, i, sign):
            buf[pl.ds(g.at(i, k, g.rows + 2), 1), :] = buf[pl.ds(g.at(i, k, 0), 1), :]


def still_pairs(fields, sign):
    still = moving(fields, sign, 1, 0)
    half = (len(still) + 1) // 2
    return [(still[n], still[n + half] if n + half < len(still) else None) for n in range(half)]


def y_slots(fields, sign):
    return 9 + len(still_pairs(fields, sign))


def pack_y(g, buf, sign, fields, up, down):
    high = lane_masks(g.rows)[0]
    for side, ref in ((1, up), (-1, down)):
        k = g.cols if side == 1 else 1
        for n, i in enumerate(moving(fields, sign, 1, side)):
            ref[n * g.rows : (n + 1) * g.rows, :] = buf[pl.ds(g.at(i, k, 0), g.rows), :]
        for n, (i, j) in enumerate(still_pairs(fields, sign)):
            value = buf[pl.ds(g.at(i, k, 0), g.rows), :]
            if j is not None:
                other = pltpu.roll(buf[pl.ds(g.at(j, k, 0), g.rows), :], NZ, 1)
                pair = (value, other) if side == 1 else (other, value)
                value = jnp.where(high, *pair)
            ref[(9 + n) * g.rows : (10 + n) * g.rows, :] = value


def unpack_y(g, buf, sign, fields, high, up, down):
    for side, ref in ((1, up), (-1, down)):
        for n, i in enumerate(moving(fields, sign, 1, side)):
            value = ref[n * g.rows : (n + 1) * g.rows, :]
            for k in halo_panels(g, i, sign):
                buf[pl.ds(g.at(i, k, 0), g.rows), :] = value
    for n, (i, j) in enumerate(still_pairs(fields, sign)):
        spot = slice((9 + n) * g.rows, (10 + n) * g.rows)
        before, after = up[spot, :], down[spot, :]
        buf[pl.ds(g.at(i, g.halo, 0), g.rows), :] = jnp.where(high, before, after)
        if j is not None:
            value = pltpu.roll(jnp.where(high, after, before), NZ, 1)
            buf[pl.ds(g.at(j, g.halo, 0), g.rows), :] = value


def by_parity(axis, first, second, act):
    even = lax.rem(lax.axis_index(axis), 2) == 0

    @pl.when(even)
    def _():
        act(first, second)

    @pl.when(jnp.logical_not(even))
    def _():
        act(second, first)


def load_fields(ref, rows, base, pieces, count):
    return [read_rows(ref, base + n * rows, pieces) for n in range(count)]


def save_fields(ref, rows, base, pieces, values):
    for n, value in enumerate(values):
        write_rows(ref, base + n * rows, pieces, value)


def save_populations(g, out, k, pieces, values):
    base = pl.multiple_of(k * g.panel, 8)
    for i, value in enumerate(values):
        write_rows(out, base + g.field(i), pieces, value)


def spot_of(g, k):
    return pl.multiple_of((k - 1) * g.rows, 8)


def lanes_of(k):
    return pl.ds(pl.multiple_of((k - 1) * LANES, LANES), LANES)


def every(first, last, act):
    def step(k, carry):
        act(k)
        return carry

    count = last + 1 - first
    unroll = max(n for n in (1, 2, 3, 4) if count % n == 0)
    lax.fori_loop(first, last + 1, step, 0, unroll=unroll)


def side_panels(g, act, count):
    def step(n, carry):
        act(jnp.where(n == 0, 1, g.cols - 1 + n))
        return carry

    lax.fori_loop(0, count, step, 0, unroll=count)


def interior_tiles(g, act):
    for pieces in g.inner:
        every(2, g.cols - 1, functools.partial(act, pieces=pieces))


def middle_tiles(g, act):
    for pieces in g.inner:
        side_panels(g, functools.partial(act, pieces=pieces), 3)
    every(2, g.cols - 1, functools.partial(act, pieces=g.outer))


def core_tiles(g, act):
    for pieces in g.inner:
        every(3, g.cols - 2, functools.partial(act, pieces=pieces))


def near_core_tiles(g, act):
    def step(n, carry):
        for pieces in g.inner:
            act(jnp.where(n == 0, 2, g.cols - 1), pieces=pieces)
        return carry

    lax.fori_loop(0, 2, step, 0, unroll=2)


def rim_tiles(g, act):
    every(1, g.cols, functools.partial(act, pieces=g.outer))
    for pieces in g.inner:
        side_panels(g, functools.partial(act, pieces=pieces), 2)


def step_tile(g, buf, out, sign, fields, masks, compute):
    def act(k, pieces):
        values = compute(
            pull_block(g, buf, sign, k, pieces, masks, fields), spot_of(g, k), pieces
        )
        save_populations(g, out, k, pieces, values)

    return act


def corner_tiles(g, buf, out, sign, fields, masks, compute):
    small = tuple(mask[:8] for mask in masks)
    act = step_tile(g, buf, out, sign, fields, masks, compute)
    side_panels(g, functools.partial(act, pieces=g.outer), 3)
    spot = g.halo * g.rows
    pieces = ((g.rows, 8),)
    values = compute(pull_block(g, buf, sign, g.halo, pieces, small, fields), spot, ((0, 8),))
    for i in range(27):
        dx = velocity(i, sign)[0]
        if dx == -1:
            out[pl.ds(g.at(i, g.halo, g.rows), 1), :] = values[i][0:1]
        elif dx == 1:
            out[pl.ds(g.at(i, g.halo, -1), 1), :] = values[i][1:2]
    edges = [pull_edge(g, buf, sign, side, small, fields) for side in (1, -1)]
    both = [stacked(pair) for pair in zip(*edges)]
    values = compute(both, spot, ((8, 16),))
    for i in moving(27, sign, 0, -1):
        out[pl.ds(g.at(i, 1, g.rows), g.cols, stride=g.panel), :] = values[i][:8]
    for i in moving(27, sign, 0, 1):
        out[pl.ds(g.at(i, 1, -1), g.cols, stride=g.panel), :] = values[i][8:]
    for i in moving(27, sign, 1, 1):
        out[pl.ds(g.at(i, 0, 0), g.rows), :] = out[pl.ds(g.at(i, g.halo, 0), g.rows), :]
        for r in (-1, g.rows):
            out[pl.ds(g.at(i, 0, r), 1), :] = out[pl.ds(g.at(i, g.halo, r), 1), :]


def flow_of(f):
    rho, mx, my, mz = moments(f)
    inverse = 1.0 / rho
    return inverse, rho, mx * inverse, my * inverse, mz * inverse


def collide_first(g, state, out):
    def act(k, pieces, f):
        base = pl.multiple_of(k * g.panel, 8)
        damp, push, wall = (read_rows(out, base + g.field(i), pieces) for i in (27, 28, 29))
        flow = flow_of(f)[1:] + (damp, push)
        save_fields(state, g.local, spot_of(g, k), pieces, flow + (wall,))
        save_populations(g, out, k, pieces, relax(f, *flow, wall > 0.5))

    return act


def collide_second(g, state):
    def compute(values, spot, pieces):
        f, (damp, push, wall) = values[:27], values[27:]
        flow = flow_of(f)[1:] + (damp, push)
        save_fields(state, g.extended, spot, pieces, flow + (wall,))
        return relax(f, *flow, wall > 0.5)

    return compute


def adjoint_second(g, state, total):
    def compute(p, spot, pieces):
        *flow, wall = load_fields(state, g.extended, spot, pieces, 7)
        *spread, porous = adjoint_scalars(p, *flow, wall > 0.5)
        save_fields(total, g.extended, spot, pieces, [porous])
        return adjoint_spread(p, *spread, wall > 0.5)

    return compute


def seed_tile(g, buf, adjoint, stage, out, masks):
    def act(k, pieces):
        f = pull_block(g, buf, 1, k, pieces, masks)
        for i in range(27):
            write_rows(stage.at[k - 1, i], 0, pieces, f[i])
        inverse, _, wx, wy, wz = flow_of(f)
        even = -(wx * wx + wy * wy + wz * wz) * inverse
        along = combos(wx * inverse, wy * inverse, wz * inverse)
        lanes = lanes_of(k)
        seeded = [
            stacked([adjoint[i, pl.ds(r, n), lanes] for r, n in pieces]) + even for i in range(27)
        ]
        for i in range(13):
            seeded[i] = seeded[i] + along[i]
            seeded[26 - i] = seeded[26 - i] - along[i]
        save_populations(g, out, k, pieces, seeded)

    return act


def block_of(ref, k):
    return ref.at[:, :, lanes_of(k)]


def flat_fields(g, out, near, k):
    porosity, solid, labels = near
    lanes = lanes_of(k)
    label = labels[:, lanes]
    damp = 1.0 / (1.0 + porosity[:, lanes])
    push = jnp.where(label == 1, PUSH, jnp.where(label == 2, -PUSH, 0.0))
    base = pl.multiple_of(k * g.panel, 8)
    for i, value in ((27, damp), (28, push), (29, solid[:, lanes].astype(F32))):
        out[pl.ds(base + g.field(i), g.rows), :] = value


def staged_tile(g, collide, stage):
    def act(k, pieces):
        collide(k, pieces, [read_rows(stage.at[k - 1, i], 0, pieces) for i in range(27)])

    return act


def side_tiles(g, act):
    for pieces in (g.outer,) + g.inner:
        side_panels(g, functools.partial(act, pieces=pieces), 2)


def side_first_kernel(g, pops, *refs):
    flat, (out, state, stage), near, faces, (sems, flat_sems) = (
        refs[:3],
        refs[3:6],
        refs[6:9],
        refs[9:11],
        refs[11:],
    )

    def copy(k, r, n):
        rows = pl.ds(r, n)
        source = pops.at[:, rows, lanes_of(k)]
        part = 1 if r else 0
        return pltpu.make_async_copy(source, stage.at[k - 1, :, rows], sems.at[k - 1, part])

    flat_copies = [
        pltpu.make_async_copy(source, target, flat_sems.at[n])
        for n, (source, target) in enumerate(zip(flat, near))
    ]
    for each in flat_copies:
        each.start()
    for k in (1, g.cols):
        copy(k, 0, g.rows).start()
    for k in range(2, g.cols):
        for piece in g.outer:
            copy(k, *piece).start()
    for each in flat_copies:
        each.wait()
    for k in (1, g.cols):
        flat_fields(g, out, near, k)
    for k in (1, g.cols):
        copy(k, 0, g.rows).wait()
    side_tiles(g, staged_tile(g, collide_first(g, state, out), stage))
    by_parity("gy", *faces, functools.partial(pack_y, g, out, 1, 30))
    for k in range(2, g.cols):
        for piece in g.outer:
            copy(k, *piece).wait()


def rim_first_kernel(g, _out, _state, stage, *refs):
    near, (out, state), faces = refs[:3], refs[3:5], refs[5:]
    every(2, g.cols - 1, functools.partial(flat_fields, g, out, near))
    act = staged_tile(g, collide_first(g, state, out), stage)
    every(2, g.cols - 1, functools.partial(act, pieces=g.outer))
    by_parity("gx", *faces, functools.partial(pack_x, g, out, 1, 30))


def inner_first_kernel(g, _, _state, pops, post, state0, out, state1, stage, sems):
    masks = lane_masks(16)
    middle = pl.ds(8, g.rows - 16)

    def copy(k):
        source = pops.at[:, middle, lanes_of(k)]
        return pltpu.make_async_copy(source, stage.at[k - 1, :, middle], sems.at[k - 1])

    for k in range(2, g.cols):
        copy(k).start()
    for k in range(2, g.cols):
        copy(k).wait()
    interior_tiles(g, staged_tile(g, collide_first(g, state0, post), stage))
    interior_tiles(g, step_tile(g, post, out, 1, 30, masks, collide_second(g, state1)))


def relay_kernel(g, sign, fields, _, y_second, y_first, buf, first, second):
    high = lane_masks(g.rows)[0]
    by_parity("gy", y_second, y_first, functools.partial(unpack_y, g, buf, sign, fields, high))
    by_parity("gx", first, second, functools.partial(pack_corners, g, buf, sign, fields))


def middle_second_kernel(g, adjoint, post, out, state1, stage, field, x_second, x_first):
    masks = lane_masks(16)
    by_parity("gx", x_second, x_first, functools.partial(unpack_x, g, post, 1, 30))
    middle_tiles(g, step_tile(g, post, out, 1, 30, masks, collide_second(g, state1)))
    core_tiles(g, seed_tile(g, out, adjoint, stage, field, masks))


def side_seed_kernel(g, _post, _out, _state, _stage, _field, first, second, adjoint, *refs):
    post, out, state1, stage, field, *faces = refs
    masks = lane_masks(16)
    by_parity("gx", second, first, functools.partial(unpack_corners, g, post, 1, 30))
    corner_tiles(g, post, out, 1, 30, masks, collide_second(g, state1))
    side_tiles(g, seed_tile(g, out, adjoint, stage, field, masks))
    by_parity("gy", *faces, functools.partial(pack_y, g, field, -1, 27))


def rim_seed_kernel(g, _stage, _field, out, adjoint, stage, field, *faces):
    seed = seed_tile(g, out, adjoint, stage, field, lane_masks(16))
    every(2, g.cols - 1, functools.partial(seed, pieces=g.outer))
    by_parity("gx", *faces, functools.partial(pack_x, g, field, -1, 27))


def inner_seed_kernel(
    g, post, _stage, _field, state1, adjoint, stage, field, out, total, final, sems
):
    masks = lane_masks(16)

    def copy(k):
        return pltpu.make_async_copy(stage.at[k - 1], block_of(final, k), sems.at[k - 1])

    copy(1).start()
    copy(g.cols).start()
    seed = seed_tile(g, post, adjoint, stage, field, masks)

    near_core_tiles(g, seed)
    every(2, g.cols - 1, lambda k: copy(k).start())
    interior_tiles(g, step_tile(g, field, out, -1, 27, masks, adjoint_second(g, state1, total)))
    every(1, g.cols, lambda k: copy(k).wait())


def total_tile(g, out, before, state0, total, parts, masks):
    def act(k, pieces):
        p = pull_block(g, out, -1, k, pieces, masks)
        spot = spot_of(g, k)
        *flow, wall = load_fields(state0, g.local, spot, pieces, 7)
        *spread, porous = adjoint_scalars(p, *flow, wall > 0.5)
        here = load_fields(before, g.extended, spot, pieces, 1)[0] + porous
        save_fields(total, g.local, spot, pieces, [here])
        save_fields(parts, g.local, spot, pieces, spread + [wall])

    return act


def middle_adjoint_kernel(g, field, out, before, total, parts, state1, state0, x_second, x_first):
    masks = lane_masks(16)
    by_parity("gx", x_second, x_first, functools.partial(unpack_x, g, field, -1, 27))
    middle_tiles(g, step_tile(g, field, out, -1, 27, masks, adjoint_second(g, state1, before)))
    core_tiles(g, total_tile(g, out, before, state0, total, parts, masks))


def total_kernel(g, *refs):
    state1, state0, first, second, field, out, before, total, parts, peak = refs[5:]
    masks = lane_masks(16)
    by_parity("gx", second, first, functools.partial(unpack_corners, g, field, -1, 27))
    corner_tiles(g, field, out, -1, 27, masks, adjoint_second(g, state1, before))
    act = total_tile(g, out, before, state0, total, parts, masks)
    near_core_tiles(g, act)
    rim_tiles(g, act)
    size = 8 * (g.local // 64)
    largest = jnp.zeros((8, LANES), F32)
    for start in range(0, g.local, size):
        value = jnp.abs(total[start : start + size, :]).reshape(-1, 8, LANES)
        largest = jnp.maximum(largest, jnp.max(value, 0))
    peak[...] = largest


def adjoint_kernel(g, first, last, buf, parts, result, stage, sems):
    masks = lane_masks(16)

    def copy(k):
        return pltpu.make_async_copy(stage.at[k - first], block_of(result, k), sems.at[k - first])

    def column(k):
        for pieces in (g.outer,) + g.inner:
            p = pull_block(g, buf, -1, k, pieces, masks)
            *spread, wall = load_fields(parts, g.local, spot_of(g, k), pieces, 5)
            for i, value in enumerate(adjoint_spread(p, *spread, wall > 0.5)):
                write_rows(stage.at[k - first, i], 0, pieces, value)
        copy(k).start()

    every(first, last, column)
    every(first, last, lambda k: copy(k).wait())


def scale_kernel(g, total, peak, out):
    largest = jnp.max(peak[...])
    factor = 1.0 / (jnp.full((g.rows, LANES), largest, F32) + EPS)
    for c in range(g.cols):
        value = total[c * g.rows : (c + 1) * g.rows, :] * factor
        out[:, c * LANES : (c + 1) * LANES] = value


def swap_pairs(count, start):
    pairs = []
    for i in range(start, count, 2):
        j = (i + 1) % count
        pairs += [(i, j), (j, i)]
    return pairs


def swap(axis, count, first, second):
    return (
        lax.ppermute(first, axis, swap_pairs(count, 0)),
        lax.ppermute(second, axis, swap_pairs(count, 1)),
    )


def largest_of_all(peak, sizes, beside):
    nx, ny = sizes
    peak = jnp.maximum(peak, lax.ppermute(peak, "gy", [(i, i ^ 1) for i in range(ny)]))
    groups = 0
    for axis, count, first, widths in (("gy", ny, 2, (4, 4)), ("gx", nx, 1, (4, 2))):
        step = first
        for width in widths:
            width = min(width, count // step)
            parts = []
            for n in range(1, width):
                if axis == "gy":
                    pairs = [(i, i ^ (n * step) ^ 1) for i in range(ny)]
                    parts.append(lax.ppermute(peak, "gy", pairs))
                else:
                    pairs = [
                        (i * ny + y, (i ^ (n * step)) * ny + (y ^ 1))
                        for i in range(nx)
                        for y in range(ny)
                    ]
                    parts.append(lax.ppermute(peak, ("gx", "gy"), pairs))
            groups += 1
            if groups == 1:
                peak = beside(peak)
            peak = functools.reduce(jnp.maximum, parts, peak)
            step *= width
    return peak


def on_device(sizes, populations, adjoint_in, porosity, solid, labels):
    rows, width = porosity.shape
    g = Grid(rows, width)
    in_vmem = pl.BlockSpec(memory_space=pltpu.VMEM)
    in_hbm = pl.BlockSpec(memory_space=pltpu.HBM)
    nx, ny = sizes

    def vmem(*shape):
        return pltpu.VMEM(shape, F32)

    def fields(count, size):
        return vmem(count * size, LANES)

    def padded(count):
        return vmem(*g.padded(count))

    def x_faces(count):
        return [vmem(count * g.cols, LANES)] * 2

    def y_faces(count, sign):
        return [vmem(y_slots(count, sign) * rows, LANES)] * 2

    def corners(count):
        return [vmem(-(-count // 8) * 8, LANES)] * 2

    whole = pltpu.HBM(populations.shape, F32)
    stage = vmem(g.cols, 27, rows, LANES)
    sems = pltpu.SemaphoreType.DMA((g.cols,))

    def call(name, kernel, operands, out_shape, scratch=(), kept=0, load=0, result=None, far=()):
        out_shape = [pltpu.VMEM(x.shape, x.dtype) for x in operands[:kept]] + out_shape
        aliases = {n: n for n in range(kept)}
        spaces = [pltpu.HBM if n in far else pltpu.VMEM for n in range(len(operands))]
        pinned = [
            pltpu.with_memory_space_constraint(x, space) for x, space in zip(operands, spaces)
        ]
        in_specs = [pl.BlockSpec(memory_space=space) for space in spaces]
        if result is not None:
            aliases[len(operands)] = len(out_shape) - 1
            pinned.append(pltpu.with_memory_space_constraint(result, pltpu.HBM))
            in_specs.append(in_hbm)
        return pl.pallas_call(
            functools.partial(kernel, g),
            in_specs=in_specs,
            out_shape=out_shape,
            out_specs=[in_hbm if x is whole else in_vmem for x in out_shape],
            scratch_shapes=list(scratch),
            input_output_aliases=aliases,
            compiler_params=pltpu.CompilerParams(vmem_limit_bytes=VMEM_LIMIT),
            cost_estimate=pl.CostEstimate(flops=0, bytes_accessed=load, transcendentals=0)
            if load
            else None,
            name=name,
        )(*pinned)

    def swap_faces(axis, count, parcels):
        return swap(axis, count, *parcels)[::-1]

    def relay(buf, parcels, sign, count):
        def kernel(grid, *refs):
            relay_kernel(grid, sign, count, *refs)

        buf, *parcels = call("relay", kernel, [buf, *parcels], corners(count), kept=1)
        return buf, swap("gx", nx, *parcels)

    flat_space = [vmem(*porosity.shape)] + [pltpu.VMEM(porosity.shape, jnp.int32)] * 2
    post, state0, staged, *rest = call(
        "side_first",
        side_first_kernel,
        [populations, porosity, solid, labels],
        [padded(30), fields(7, g.local), stage] + flat_space + y_faces(30, 1),
        [pltpu.SemaphoreType.DMA((g.cols, 2)), pltpu.SemaphoreType.DMA((3,))],
        far=range(4),
    )
    along_y = swap_faces("gy", ny, rest[3:])
    post, state0, *parcels = call(
        "rim_first",
        rim_first_kernel,
        [post, state0, staged, *rest[:3]],
        x_faces(30),
        kept=2,
        load=FLIGHT,
    )
    along_x = swap_faces("gx", nx, parcels)
    post, state0, second, state1 = call(
        "inner_first",
        inner_first_kernel,
        [post, state0, populations],
        [padded(27), fields(7, g.extended)],
        [stage, sems],
        kept=2,
        load=FLIGHT,
        far=(2,),
    )
    post, parcels = relay(post, along_y, 1, 30)
    post, second, state1, staged, field = call(
        "middle_second",
        lambda grid, _post, _out, _state, b, a, source, *refs: middle_second_kernel(
            grid, source, *refs, b, a
        ),
        [post, second, state1, *along_x, adjoint_in],
        [stage, padded(27)],
        kept=3,
        load=FLIGHT,
    )
    _, second, state1, staged, field, *parcels = call(
        "side_seed",
        side_seed_kernel,
        [post, second, state1, staged, field, *parcels, adjoint_in],
        y_faces(27, -1),
        kept=5,
    )
    along_y = swap_faces("gy", ny, parcels)
    staged, field, *parcels = call(
        "rim_seed",
        rim_seed_kernel,
        [staged, field, second, adjoint_in],
        x_faces(27),
        kept=2,
        load=FLIGHT,
    )
    along_x = swap_faces("gx", nx, parcels)
    _, field, pulled, before, final = call(
        "inner_seed",
        lambda grid, kept, into, buf, *refs: inner_seed_kernel(grid, buf, kept, into, *refs),
        [staged, field, second, state1, adjoint_in],
        [padded(27), fields(1, g.extended), whole],
        [sems],
        kept=2,
        load=FLIGHT,
    )
    field, parcels = relay(field, along_y, -1, 27)
    field, pulled, before, total, parts = call(
        "middle_adjoint",
        lambda grid, _field, _out, _before, near, far, b, a, *refs: middle_adjoint_kernel(
            grid, *refs, near, far, b, a
        ),
        [field, pulled, before, state1, state0, *along_x],
        [fields(1, g.local), fields(5, g.local)],
        kept=3,
        load=FLIGHT,
    )
    _, pulled, _, total, parts, peak = call(
        "total",
        total_kernel,
        [field, pulled, before, total, parts, state1, state0, *parcels],
        [vmem(8, LANES)],
        kept=5,
    )
    half = g.cols // 2
    scratch = [vmem(half, 27, rows, LANES), pltpu.SemaphoreType.DMA((half,))]
    halves = []

    def first_half(peak):
        def kernel(grid, buf, fields, near, echo, *refs):
            echo[...] = near[...]
            adjoint_kernel(grid, 1, half, buf, fields, *refs)

        echo, result = call(
            "adjoint_low",
            kernel,
            [pulled, parts, peak],
            [vmem(8, LANES), whole],
            scratch,
            load=FLIGHT // 2,
        )
        halves.append(result)
        return echo

    largest = largest_of_all(peak, sizes, first_half)
    (adjoint_out,) = call(
        "adjoint_high",
        lambda grid, buf, fields, _, *refs: adjoint_kernel(
            grid, 1 + half, g.cols, buf, fields, *refs
        ),
        [pulled, parts],
        [whole],
        scratch,
        load=FLIGHT // 2,
        result=halves[0],
    )
    (sensitivity,) = call(
        "normalize",
        scale_kernel,
        [total, largest],
        [jax.ShapeDtypeStruct(porosity.shape, F32)],
    )
    return final, adjoint_out, sensitivity


def solution(mesh):
    sizes = (mesh.shape["gx"], mesh.shape["gy"])
    whole, flat = P(None, "gx", "gy"), P("gx", "gy")
    return jax.shard_map(
        functools.partial(on_device, sizes),
        mesh=mesh,
        in_specs=(whole, whole, flat, flat, flat),
        out_specs=(whole, whole, flat),
        check_vma=False,
    )
```

```python
import functools

import jax
import jax.numpy as jnp
from jax import lax
from jax.experimental import pallas as pl
from jax.experimental.pallas import tpu as pltpu
from jax.sharding import PartitionSpec as P

NZ = 64
RELAX = 0.8
PUSH = 0.2
EPS = 1e-06
LANES = 128
VELOCITY = [(a, b, c) for a in (-1, 0, 1) for b in (-1, 0, 1) for c in (-1, 0, 1)]
INDEX = {v: i for i, v in enumerate(VELOCITY)}
WEIGHT = [
    [8.0 / 27, 2.0 / 27, 1.0 / 54, 1.0 / 216][abs(v[0]) + abs(v[1]) + abs(v[2])]
    for v in VELOCITY
]
NORM = [abs(v[0]) + abs(v[1]) + abs(v[2]) for v in VELOCITY]
F32 = jnp.float32
VMEM_LIMIT = 6 * 1024 * 1024
FLIGHT = 12 * 1024 * 1024


class Grid:
    def __init__(self, rows, width):
        self.rows = rows
        self.cols = width // LANES
        self.panel = rows + 16
        self.halo = self.cols + 1
        self.local = self.cols * rows
        self.extended = self.halo * rows + 24
        self.outer = ((0, 8), (rows - 8, 8))
        self.inner = tuple(((r, 16),) for r in range(8, rows - 8, 16))

    def at(self, i, k, r):
        return self.field(i) + k * self.panel + r

    def field(self, i):
        return i * (self.cols + 2) * self.panel + 8

    def padded(self, fields):
        return (fields * (self.cols + 2) * self.panel + 8, LANES)


def velocity(i, sign):
    return tuple(sign * n for n in VELOCITY[i]) if i < 27 else (0, 0, 0)


def moving(fields, sign, axis, side):
    return [i for i in range(fields) if velocity(i, sign)[axis] == side]


def lane_masks(height):
    lane = lax.broadcasted_iota(jnp.int32, (height, LANES), 1)
    return lane >= NZ, lane % NZ == 0, lane % NZ == NZ - 1


def shift_lanes(here, d, masks):
    first, last = masks[1:]
    dy, dz = d[1:]
    if dz == 0:
        return here if dy == 0 else pltpu.roll(here, NZ, 1)
    if dz == 1:
        one, other, edge = 1, NZ + 1, first
    else:
        one, other, edge = LANES - 1, NZ - 1, last
    inner, wrapped = (one, other) if dy == 0 else (other, one)
    return jnp.where(edge, pltpu.roll(here, wrapped, 1), pltpu.roll(here, inner, 1))


def pull(load, d, masks):
    high = masks[0]
    here = load(0)
    if d[1] == 1:
        here = jnp.where(high, load(-1), here)
    elif d[1] == -1:
        here = jnp.where(high, here, load(1))
    return shift_lanes(here, d, masks)


def stacked(parts):
    return parts[0] if len(parts) == 1 else jnp.concatenate(parts, 0)


def read_rows(ref, base, pieces):
    return stacked([ref[pl.ds(base + r, n), :] for r, n in pieces])


def write_rows(ref, base, pieces, value):
    done = 0
    for r, n in pieces:
        ref[pl.ds(base + r, n), :] = value[done : done + n]
        done += n


def pull_block(g, buf, sign, k, pieces, masks, fields=27):
    base = pl.multiple_of(k * g.panel, 8)
    after = pl.multiple_of(jnp.where(k == g.halo, g.panel, base + g.panel), 8)
    out = []
    for i in range(fields):
        d = velocity(i, sign)

        def load(n, i=i, d=d):
            start = {-1: base - g.panel, 0: base, 1: after}[n]
            return read_rows(buf, start + (g.field(i) - d[0]), pieces)

        out.append(pull(load, d, masks))
    return out


def pull_edge(g, buf, sign, side, masks, fields=27):
    out = []
    for i in range(fields):
        d = velocity(i, sign)
        if side == 1:
            row = g.rows - d[0]
        else:
            row = {1: g.rows, 0: g.rows + 1, -1: 0}[d[0]]

        def load(n, i=i, row=row):
            return buf[pl.ds(g.at(i, 1 + n, row), g.cols, stride=g.panel), :]

        out.append(pull(load, d, masks))
    return out


def moments(f):
    flat = {}
    along_z = None
    for a in (-1, 0, 1):
        for b in (-1, 0, 1):
            lo, mid, hi = (f[INDEX[(a, b, c)]] for c in (-1, 0, 1))
            flat[a, b] = lo + mid + hi
            diff = hi - lo
            along_z = diff if along_z is None else along_z + diff
    line = {}
    along_y = None
    for a in (-1, 0, 1):
        line[a] = flat[a, -1] + flat[a, 0] + flat[a, 1]
        diff = flat[a, 1] - flat[a, -1]
        along_y = diff if along_y is None else along_y + diff
    return line[-1] + line[0] + line[1], line[1] - line[-1], along_y, along_z


def combos(x, y, z):
    plane = {}
    for a in (-1, 0, 1):
        for b in (-1, 0, 1):
            if (a, b) > (0, 0):
                continue
            if a == 0:
                plane[a, b] = -y if b else None
            else:
                plane[a, b] = -x if b == 0 else (-x - y if b < 0 else y - x)
    out = []
    for a, b, c in VELOCITY[:13]:
        base = plane[a, b]
        if base is None:
            out.append(-z)
        else:
            out.append(base if c == 0 else (base - z if c < 0 else base + z))
    return out


def relax(f, rho, wx, wy, wz, damp, push, solid):
    ux, uy, uz = (wx + push) * damp, wy * damp, wz * damp
    base = 1.0 - 1.5 * (ux * ux + uy * uy + uz * uz)
    keep = 1.0 - 1.0 / RELAX
    gain = rho * (1.0 / RELAX)
    level = [gain * w for w in (8.0 / 27, 2.0 / 27, 1.0 / 54, 1.0 / 216)]
    along = combos(3.0 * ux, 3.0 * uy, 3.0 * uz)
    out = [None] * 27
    for i in range(13):
        j = 26 - i
        even = base + 0.5 * (along[i] * along[i])
        lift = level[NORM[i]]
        out[i] = jnp.where(solid, f[j], keep * f[i] + lift * (even + along[i]))
        out[j] = jnp.where(solid, f[i], keep * f[j] + lift * (even - along[i]))
    out[13] = jnp.where(solid, f[13], keep * f[13] + level[0] * base)
    return out


def pulled_moments(p):
    first = {}
    for a in (-1, 0, 1):
        for b in (-1, 0, 1):
            lo, mid, hi = (p[INDEX[(a, b, c)]] for c in (-1, 0, 1))
            both = lo + hi
            first[a, b] = (4.0 * mid + both, hi - lo, both)
    second = {}
    for a in (-1, 0, 1):
        lo, mid, hi = (first[a, b] for b in (-1, 0, 1))
        b0 = lo[0] + hi[0]
        b1 = lo[1] + hi[1]
        second[a] = dict(
            one=4.0 * mid[0] + b0,
            y=hi[0] - lo[0],
            yy=b0,
            z=4.0 * mid[1] + b1,
            yz=hi[1] - lo[1],
            zz=4.0 * mid[2] + lo[2] + hi[2],
        )
    lo, mid, hi = (second[a] for a in (-1, 0, 1))

    def full(key):
        return 4.0 * mid[key] + lo[key] + hi[key]

    xx = lo["one"] + hi["one"]
    return dict(
        one=4.0 * mid["one"] + xx,
        x=hi["one"] - lo["one"],
        xx=xx,
        y=full("y"),
        xy=hi["y"] - lo["y"],
        yy=full("yy"),
        z=full("z"),
        xz=hi["z"] - lo["z"],
        yz=full("yz"),
        zz=full("zz"),
    )


def adjoint_scalars(p, rho, wx, wy, wz, damp, push, solid):
    ux, uy, uz = (wx + push) * damp, wy * damp, wz * damp
    s = pulled_moments(p)
    scale = 1.0 / (216.0 * RELAX)
    one = s["one"] * scale
    b = [s[k] * (3.0 * scale) for k in ("x", "y", "z")]
    d = {k: s[k] * (9.0 * scale) for k in ("xx", "xy", "yy", "xz", "yz", "zz")}
    qx = d["xx"] * ux + d["xy"] * uy + d["xz"] * uz
    qy = d["xy"] * ux + d["yy"] * uy + d["yz"] * uz
    qz = d["xz"] * ux + d["yz"] * uy + d["zz"] * uz
    linear = b[0] * ux + b[1] * uy + b[2] * uz
    square = ux * ux + uy * uy + uz * uz
    even = one + linear + 0.5 * (qx * ux + qy * uy + qz * uz) - 1.5 * one * square
    three = 3.0 * one
    gx = (b[0] + qx - three * ux) * damp
    gy = (b[1] + qy - three * uy) * damp
    gz = (b[2] + qz - three * uz) * damp
    even = even - (gx * wx + gy * wy + gz * wz)
    porous = jnp.where(solid, 0.0, -rho * (gx * ux + gy * uy + gz * uz))
    return even, gx, gy, gz, porous


def adjoint_spread(p, even, gx, gy, gz, solid):
    keep = 1.0 - 1.0 / RELAX
    along = combos(gx, gy, gz)
    out = [None] * 27
    for i in range(13):
        j = 26 - i
        out[i] = jnp.where(solid, p[j], keep * p[i] + (even + along[i]))
        out[j] = jnp.where(solid, p[i], keep * p[j] + (even - along[i]))
    out[13] = jnp.where(solid, p[13], keep * p[13] + even)
    return out


def x_lines(g, sign, fields, side):
    lines = []
    for i in moving(fields, sign, 0, side):
        if side == 1:
            lines.append((i, g.rows - 1, (-1, g.rows + 1)))
            lines.append((i, g.rows - 2, (g.rows,)))
        else:
            lines += [(i, 0, (g.rows,)), (i, 1, (g.rows + 1,))]
    edge, target = (g.rows - 1, g.rows + 1) if side == 1 else (0, g.rows)
    return lines + [(i, edge, (target,)) for i in moving(fields, sign, 0, 0)]


def pack_x(g, buf, sign, fields, up, down):
    for side, ref in ((1, up), (-1, down)):
        for n, (i, r, _) in enumerate(x_lines(g, sign, fields, side)):
            ref[n * g.cols : (n + 1) * g.cols, :] = buf[
                pl.ds(g.at(i, 1, r), g.cols, stride=g.panel), :
            ]


def unpack_x(g, buf, sign, fields, up, down):
    for side, ref in ((1, up), (-1, down)):
        for n, (i, _, targets) in enumerate(x_lines(g, sign, fields, side)):
            value = ref[n * g.cols : (n + 1) * g.cols, :]
            for r in targets:
                buf[pl.ds(g.at(i, 1, r), g.cols, stride=g.panel), :] = value
    for i in moving(fields, sign, 0, -1):
        buf[pl.ds(g.at(i, 1, g.rows + 2), g.cols, stride=g.panel), :] = buf[
            pl.ds(g.at(i, 1, 0), g.cols, stride=g.panel), :
        ]


def halo_panels(g, i, sign):
    return (0, g.halo) if velocity(i, sign)[1] == 1 else (g.halo,)


def pack_corners(g, buf, sign, fields, up, down):
    for side, ref in ((1, up), (-1, down)):
        for n, (i, r, _) in enumerate(x_lines(g, sign, fields, side)):
            ref[n : n + 1, :] = buf[pl.ds(g.at(i, g.halo, r), 1), :]


def unpack_corners(g, buf, sign, fields, up, down):
    for side, ref in ((1, up), (-1, down)):
        for n, (i, _, targets) in enumerate(x_lines(g, sign, fields, side)):
            value = ref[n : n + 1, :]
            for r in targets:
                for k in halo_panels(g, i, sign):
                    buf[pl.ds(g.at(i, k, r), 1), :] = value
    for i in moving(fields, sign, 0, -1):
        for k in halo_panels(g, i, sign):
            buf[pl.ds(g.at(i, k, g.rows + 2), 1), :] = buf[pl.ds(g.at(i, k, 0), 1), :]


def still_pairs(fields, sign):
    still = moving(fields, sign, 1, 0)
    half = (len(still) + 1) // 2
    return [(still[n], still[n + half] if n + half < len(still) else None) for n in range(half)]


def y_slots(fields, sign):
    return 9 + len(still_pairs(fields, sign))


def pack_y(g, buf, sign, fields, up, down):
    high = lane_masks(g.rows)[0]
    for side, ref in ((1, up), (-1, down)):
        k = g.cols if side == 1 else 1
        for n, i in enumerate(moving(fields, sign, 1, side)):
            ref[n * g.rows : (n + 1) * g.rows, :] = buf[pl.ds(g.at(i, k, 0), g.rows), :]
        for n, (i, j) in enumerate(still_pairs(fields, sign)):
            value = buf[pl.ds(g.at(i, k, 0), g.rows), :]
            if j is not None:
                other = pltpu.roll(buf[pl.ds(g.at(j, k, 0), g.rows), :], NZ, 1)
                pair = (value, other) if side == 1 else (other, value)
                value = jnp.where(high, *pair)
            ref[(9 + n) * g.rows : (10 + n) * g.rows, :] = value


def unpack_y(g, buf, sign, fields, high, up, down):
    for side, ref in ((1, up), (-1, down)):
        for n, i in enumerate(moving(fields, sign, 1, side)):
            value = ref[n * g.rows : (n + 1) * g.rows, :]
            for k in halo_panels(g, i, sign):
                buf[pl.ds(g.at(i, k, 0), g.rows), :] = value
    for n, (i, j) in enumerate(still_pairs(fields, sign)):
        spot = slice((9 + n) * g.rows, (10 + n) * g.rows)
        before, after = up[spot, :], down[spot, :]
        buf[pl.ds(g.at(i, g.halo, 0), g.rows), :] = jnp.where(high, before, after)
        if j is not None:
            value = pltpu.roll(jnp.where(high, after, before), NZ, 1)
            buf[pl.ds(g.at(j, g.halo, 0), g.rows), :] = value


def by_parity(axis, first, second, act):
    even = lax.rem(lax.axis_index(axis), 2) == 0

    @pl.when(even)
    def _():
        act(first, second)

    @pl.when(jnp.logical_not(even))
    def _():
        act(second, first)


def load_fields(ref, rows, base, pieces, count):
    return [read_rows(ref, base + n * rows, pieces) for n in range(count)]


def save_fields(ref, rows, base, pieces, values):
    for n, value in enumerate(values):
        write_rows(ref, base + n * rows, pieces, value)


def save_populations(g, out, k, pieces, values):
    base = pl.multiple_of(k * g.panel, 8)
    for i, value in enumerate(values):
        write_rows(out, base + g.field(i), pieces, value)


def spot_of(g, k):
    return pl.multiple_of((k - 1) * g.rows, 8)


def lanes_of(k):
    return pl.ds(pl.multiple_of((k - 1) * LANES, LANES), LANES)


def every(first, last, act):
    def step(k, carry):
        act(k)
        return carry

    count = last + 1 - first
    unroll = max(n for n in (1, 2, 3, 4, 6, 8) if count % n == 0)
    lax.fori_loop(first, last + 1, step, 0, unroll=unroll)


def side_panels(g, act, count):
    def step(n, carry):
        act(jnp.where(n == 0, 1, g.cols - 1 + n))
        return carry

    lax.fori_loop(0, count, step, 0, unroll=count)


def interior_tiles(g, act):
    for pieces in g.inner:
        every(2, g.cols - 1, functools.partial(act, pieces=pieces))


def middle_tiles(g, act):
    for pieces in g.inner:
        side_panels(g, functools.partial(act, pieces=pieces), 3)
    every(2, g.cols - 1, functools.partial(act, pieces=g.outer))


def core_tiles(g, act):
    for pieces in g.inner:
        every(3, g.cols - 2, functools.partial(act, pieces=pieces))


def near_core_tiles(g, act):
    def step(n, carry):
        for pieces in g.inner:
            act(jnp.where(n == 0, 2, g.cols - 1), pieces=pieces)
        return carry

    lax.fori_loop(0, 2, step, 0, unroll=2)


def rim_tiles(g, act):
    every(1, g.cols, functools.partial(act, pieces=g.outer))
    for pieces in g.inner:
        side_panels(g, functools.partial(act, pieces=pieces), 2)


def step_tile(g, buf, out, sign, fields, masks, compute):
    def act(k, pieces):
        values = compute(
            pull_block(g, buf, sign, k, pieces, masks, fields), spot_of(g, k), pieces
        )
        save_populations(g, out, k, pieces, values)

    return act


def corner_tiles(g, buf, out, sign, fields, masks, compute):
    small = tuple(mask[:8] for mask in masks)
    act = step_tile(g, buf, out, sign, fields, masks, compute)
    side_panels(g, functools.partial(act, pieces=g.outer), 3)
    spot = g.halo * g.rows
    pieces = ((g.rows, 8),)
    values = compute(pull_block(g, buf, sign, g.halo, pieces, small, fields), spot, ((0, 8),))
    for i in range(27):
        dx = velocity(i, sign)[0]
        if dx == -1:
            out[pl.ds(g.at(i, g.halo, g.rows), 1), :] = values[i][0:1]
        elif dx == 1:
            out[pl.ds(g.at(i, g.halo, -1), 1), :] = values[i][1:2]
    edges = [pull_edge(g, buf, sign, side, small, fields) for side in (1, -1)]
    both = [stacked(pair) for pair in zip(*edges)]
    values = compute(both, spot, ((8, 16),))
    for i in moving(27, sign, 0, -1):
        out[pl.ds(g.at(i, 1, g.rows), g.cols, stride=g.panel), :] = values[i][:8]
    for i in moving(27, sign, 0, 1):
        out[pl.ds(g.at(i, 1, -1), g.cols, stride=g.panel), :] = values[i][8:]
    for i in moving(27, sign, 1, 1):
        out[pl.ds(g.at(i, 0, 0), g.rows), :] = out[pl.ds(g.at(i, g.halo, 0), g.rows), :]
        for r in (-1, g.rows):
            out[pl.ds(g.at(i, 0, r), 1), :] = out[pl.ds(g.at(i, g.halo, r), 1), :]


def flow_of(f):
    rho, mx, my, mz = moments(f)
    inverse = 1.0 / rho
    return inverse, rho, mx * inverse, my * inverse, mz * inverse


def collide_first(g, state, out):
    def act(k, pieces, f):
        base = pl.multiple_of(k * g.panel, 8)
        damp, push, wall = (read_rows(out, base + g.field(i), pieces) for i in (27, 28, 29))
        flow = flow_of(f)[1:] + (damp, push)
        save_fields(state, g.local, spot_of(g, k), pieces, flow + (wall,))
        save_populations(g, out, k, pieces, relax(f, *flow, wall > 0.5))

    return act


def collide_second(g, state):
    def compute(values, spot, pieces):
        f, (damp, push, wall) = values[:27], values[27:]
        flow = flow_of(f)[1:] + (damp, push)
        save_fields(state, g.extended, spot, pieces, flow + (wall,))
        return relax(f, *flow, wall > 0.5)

    return compute


def adjoint_second(g, state, total):
    def compute(p, spot, pieces):
        *flow, wall = load_fields(state, g.extended, spot, pieces, 7)
        *spread, porous = adjoint_scalars(p, *flow, wall > 0.5)
        save_fields(total, g.extended, spot, pieces, [porous])
        return adjoint_spread(p, *spread, wall > 0.5)

    return compute


def seed_tile(g, buf, adjoint, stage, out, masks):
    def act(k, pieces):
        f = pull_block(g, buf, 1, k, pieces, masks)
        for i in range(27):
            write_rows(stage.at[k - 1, i], 0, pieces, f[i])
        inverse, _, wx, wy, wz = flow_of(f)
        even = -(wx * wx + wy * wy + wz * wz) * inverse
        along = combos(wx * inverse, wy * inverse, wz * inverse)
        lanes = lanes_of(k)
        seeded = [
            stacked([adjoint[i, pl.ds(r, n), lanes] for r, n in pieces]) + even for i in range(27)
        ]
        for i in range(13):
            seeded[i] = seeded[i] + along[i]
            seeded[26 - i] = seeded[26 - i] - along[i]
        save_populations(g, out, k, pieces, seeded)

    return act


def block_of(ref, k):
    return ref.at[:, :, lanes_of(k)]


def flat_fields(g, out, near, k):
    porosity, solid, labels = near
    lanes = lanes_of(k)
    label = labels[:, lanes]
    damp = 1.0 / (1.0 + porosity[:, lanes])
    push = jnp.where(label == 1, PUSH, jnp.where(label == 2, -PUSH, 0.0))
    base = pl.multiple_of(k * g.panel, 8)
    for i, value in ((27, damp), (28, push), (29, solid[:, lanes].astype(F32))):
        out[pl.ds(base + g.field(i), g.rows), :] = value


def staged_tile(g, collide, stage):
    def act(k, pieces):
        collide(k, pieces, [read_rows(stage.at[k - 1, i], 0, pieces) for i in range(27)])

    return act


def side_tiles(g, act):
    for pieces in (g.outer,) + g.inner:
        side_panels(g, functools.partial(act, pieces=pieces), 2)


def side_first_kernel(g, pops, *refs):
    flat, (out, state, stage), near, faces, (sems, flat_sems) = (
        refs[:3],
        refs[3:6],
        refs[6:9],
        refs[9:11],
        refs[11:],
    )

    def copy(k):
        return pltpu.make_async_copy(block_of(pops, k), stage.at[k - 1], sems.at[k - 1])

    flat_copies = [
        pltpu.make_async_copy(source, target, flat_sems.at[n])
        for n, (source, target) in enumerate(zip(flat, near))
    ]
    for each in flat_copies:
        each.start()
    for k in (1, g.cols, *range(2, g.cols)):
        copy(k).start()
    for each in flat_copies:
        each.wait()
    for k in (1, g.cols):
        flat_fields(g, out, near, k)
    copy(1).wait()
    copy(g.cols).wait()
    side_tiles(g, staged_tile(g, collide_first(g, state, out), stage))
    by_parity("gy", *faces, functools.partial(pack_y, g, out, 1, 30))
    for k in range(2, g.cols):
        copy(k).wait()


def rim_first_kernel(g, _out, _state, stage, *refs):
    near, (out, state), faces = refs[:3], refs[3:5], refs[5:]
    every(2, g.cols - 1, functools.partial(flat_fields, g, out, near))
    act = staged_tile(g, collide_first(g, state, out), stage)
    every(2, g.cols - 1, functools.partial(act, pieces=g.outer))
    by_parity("gx", *faces, functools.partial(pack_x, g, out, 1, 30))


def inner_first_kernel(g, _, _state, stage, post, state0, out, state1):
    masks = lane_masks(16)
    interior_tiles(g, staged_tile(g, collide_first(g, state0, post), stage))
    interior_tiles(g, step_tile(g, post, out, 1, 30, masks, collide_second(g, state1)))


def relay_kernel(g, sign, fields, _, y_second, y_first, buf, first, second):
    high = lane_masks(g.rows)[0]
    by_parity("gy", y_second, y_first, functools.partial(unpack_y, g, buf, sign, fields, high))
    by_parity("gx", first, second, functools.partial(pack_corners, g, buf, sign, fields))


def middle_second_kernel(g, adjoint, post, out, state1, stage, field, x_second, x_first):
    masks = lane_masks(16)
    by_parity("gx", x_second, x_first, functools.partial(unpack_x, g, post, 1, 30))
    middle_tiles(g, step_tile(g, post, out, 1, 30, masks, collide_second(g, state1)))
    core_tiles(g, seed_tile(g, out, adjoint, stage, field, masks))


def side_seed_kernel(g, _post, _out, _state, _stage, _field, second, first, adjoint, *refs):
    post, out, state1, stage, field, *faces = refs
    masks = lane_masks(16)
    by_parity("gx", second, first, functools.partial(unpack_corners, g, post, 1, 30))
    corner_tiles(g, post, out, 1, 30, masks, collide_second(g, state1))
    side_tiles(g, seed_tile(g, out, adjoint, stage, field, masks))
    by_parity("gy", *faces, functools.partial(pack_y, g, field, -1, 27))


def rim_seed_kernel(g, _stage, _field, out, adjoint, stage, field, *faces):
    seed = seed_tile(g, out, adjoint, stage, field, lane_masks(16))
    every(2, g.cols - 1, functools.partial(seed, pieces=g.outer))
    by_parity("gx", *faces, functools.partial(pack_x, g, field, -1, 27))


def inner_seed_kernel(
    g, post, _stage, _field, state1, adjoint, stage, field, out, total, final, sems
):
    masks = lane_masks(16)

    def copy(k):
        return pltpu.make_async_copy(stage.at[k - 1], block_of(final, k), sems.at[k - 1])

    copy(1).start()
    copy(g.cols).start()
    seed = seed_tile(g, post, adjoint, stage, field, masks)

    near_core_tiles(g, seed)
    every(2, g.cols - 1, lambda k: copy(k).start())
    interior_tiles(g, step_tile(g, field, out, -1, 27, masks, adjoint_second(g, state1, total)))
    every(1, g.cols, lambda k: copy(k).wait())


def total_tile(g, out, before, state0, total, parts, masks):
    def act(k, pieces):
        p = pull_block(g, out, -1, k, pieces, masks)
        spot = spot_of(g, k)
        *flow, wall = load_fields(state0, g.local, spot, pieces, 7)
        *spread, porous = adjoint_scalars(p, *flow, wall > 0.5)
        here = load_fields(before, g.extended, spot, pieces, 1)[0] + porous
        save_fields(total, g.local, spot, pieces, [here])
        save_fields(parts, g.local, spot, pieces, spread + [wall])

    return act


def middle_adjoint_kernel(g, field, out, before, total, parts, state1, state0, x_second, x_first):
    masks = lane_masks(16)
    by_parity("gx", x_second, x_first, functools.partial(unpack_x, g, field, -1, 27))
    middle_tiles(g, step_tile(g, field, out, -1, 27, masks, adjoint_second(g, state1, before)))
    core_tiles(g, total_tile(g, out, before, state0, total, parts, masks))


def total_kernel(g, *refs):
    state1, state0, second, first, field, out, before, total, parts, peak = refs[5:]
    masks = lane_masks(16)
    by_parity("gx", second, first, functools.partial(unpack_corners, g, field, -1, 27))
    corner_tiles(g, field, out, -1, 27, masks, adjoint_second(g, state1, before))
    act = total_tile(g, out, before, state0, total, parts, masks)
    near_core_tiles(g, act)
    rim_tiles(g, act)
    size = 8 * (g.local // 64)
    largest = jnp.zeros((8, LANES), F32)
    for start in range(0, g.local, size):
        value = jnp.abs(total[start : start + size, :]).reshape(-1, 8, LANES)
        largest = jnp.maximum(largest, jnp.max(value, 0))
    peak[...] = largest


def adjoint_kernel(g, first, last, buf, parts, result, stage, sems):
    masks = lane_masks(16)

    def copy(k):
        return pltpu.make_async_copy(stage.at[k - first], block_of(result, k), sems.at[k - first])

    def column(k):
        for pieces in (g.outer,) + g.inner:
            p = pull_block(g, buf, -1, k, pieces, masks)
            *spread, wall = load_fields(parts, g.local, spot_of(g, k), pieces, 5)
            for i, value in enumerate(adjoint_spread(p, *spread, wall > 0.5)):
                write_rows(stage.at[k - first, i], 0, pieces, value)
        copy(k).start()

    every(first, last, column)
    every(first, last, lambda k: copy(k).wait())


def scale_kernel(g, total, peak, out):
    largest = jnp.max(peak[...])
    factor = 1.0 / (jnp.full((g.rows, LANES), largest, F32) + EPS)
    for c in range(g.cols):
        value = total[c * g.rows : (c + 1) * g.rows, :] * factor
        out[:, c * LANES : (c + 1) * LANES] = value


def swap_pairs(count, start):
    pairs = []
    for i in range(start, count, 2):
        j = (i + 1) % count
        pairs += [(i, j), (j, i)]
    return pairs


def swap(axis, count, first, second):
    return (
        lax.ppermute(first, axis, swap_pairs(count, 0)),
        lax.ppermute(second, axis, swap_pairs(count, 1)),
    )


def largest_of_all(peak, sizes, beside):
    nx, ny = sizes
    peak = jnp.maximum(peak, lax.ppermute(peak, "gy", [(i, i ^ 1) for i in range(ny)]))
    groups = 0
    for axis, count, first, widths in (("gy", ny, 2, (4, 4)), ("gx", nx, 1, (4, 2))):
        step = first
        for width in widths:
            width = min(width, count // step)
            parts = []
            for n in range(1, width):
                if axis == "gy":
                    pairs = [(i, i ^ (n * step) ^ 1) for i in range(ny)]
                    parts.append(lax.ppermute(peak, "gy", pairs))
                else:
                    pairs = [
                        (i * ny + y, (i ^ (n * step)) * ny + (y ^ 1))
                        for i in range(nx)
                        for y in range(ny)
                    ]
                    parts.append(lax.ppermute(peak, ("gx", "gy"), pairs))
            groups += 1
            if groups == 1:
                peak = beside(peak)
            peak = functools.reduce(jnp.maximum, parts, peak)
            step *= width
    return peak


def on_device(sizes, populations, adjoint_in, porosity, solid, labels):
    rows, width = porosity.shape
    g = Grid(rows, width)
    in_vmem = pl.BlockSpec(memory_space=pltpu.VMEM)
    in_hbm = pl.BlockSpec(memory_space=pltpu.HBM)
    nx, ny = sizes

    def vmem(*shape):
        return pltpu.VMEM(shape, F32)

    def fields(count, size):
        return vmem(count * size, LANES)

    def padded(count):
        return vmem(*g.padded(count))

    def x_faces(count):
        return [vmem(count * g.cols, LANES)] * 2

    def y_faces(count, sign):
        return [vmem(y_slots(count, sign) * rows, LANES)] * 2

    def corners(count):
        return [vmem(-(-count // 8) * 8, LANES)] * 2

    whole = pltpu.HBM(populations.shape, F32)
    stage = vmem(g.cols, 27, rows, LANES)
    sems = pltpu.SemaphoreType.DMA((g.cols,))

    def call(name, kernel, operands, out_shape, scratch=(), kept=0, load=0, result=None):
        out_shape = [pltpu.VMEM(x.shape, x.dtype) for x in operands[:kept]] + out_shape
        aliases = {n: n for n in range(kept)}
        space = pltpu.HBM if name == "side_first" else pltpu.VMEM
        pinned = [pltpu.with_memory_space_constraint(x, space) for x in operands]
        in_specs = [pl.BlockSpec(memory_space=space)] * len(operands)
        if result is not None:
            aliases[len(operands)] = len(out_shape) - 1
            pinned.append(pltpu.with_memory_space_constraint(result, pltpu.HBM))
            in_specs.append(in_hbm)
        return pl.pallas_call(
            functools.partial(kernel, g),
            in_specs=in_specs,
            out_shape=out_shape,
            out_specs=[in_hbm if x is whole else in_vmem for x in out_shape],
            scratch_shapes=list(scratch),
            input_output_aliases=aliases,
            compiler_params=pltpu.CompilerParams(vmem_limit_bytes=VMEM_LIMIT),
            cost_estimate=pl.CostEstimate(flops=0, bytes_accessed=load, transcendentals=0)
            if load
            else None,
            name=name,
        )(*pinned)

    def swap_faces(axis, count, parcels):
        return swap(axis, count, *parcels)[::-1]

    def relay(buf, parcels, sign, count):
        def kernel(grid, *refs):
            relay_kernel(grid, sign, count, *refs)

        buf, *parcels = call("relay", kernel, [buf, *parcels], corners(count), kept=1)
        return buf, swap("gx", nx, *parcels)[::-1]

    flat_space = [vmem(*porosity.shape)] + [pltpu.VMEM(porosity.shape, jnp.int32)] * 2
    post, state0, staged, *rest = call(
        "side_first",
        side_first_kernel,
        [populations, porosity, solid, labels],
        [padded(30), fields(7, g.local), stage] + flat_space + y_faces(30, 1),
        [sems, pltpu.SemaphoreType.DMA((3,))],
    )
    along_y = swap_faces("gy", ny, rest[3:])
    post, state0, *parcels = call(
        "rim_first",
        rim_first_kernel,
        [post, state0, staged, *rest[:3]],
        x_faces(30),
        kept=2,
        load=FLIGHT,
    )
    along_x = swap_faces("gx", nx, parcels)
    post, state0, second, state1 = call(
        "inner_first",
        inner_first_kernel,
        [post, state0, staged],
        [padded(27), fields(7, g.extended)],
        kept=2,
        load=FLIGHT,
    )
    post, parcels = relay(post, along_y, 1, 30)
    post, second, state1, staged, field = call(
        "middle_second",
        lambda grid, _post, _out, _state, b, a, source, *refs: middle_second_kernel(
            grid, source, *refs, b, a
        ),
        [post, second, state1, *along_x, adjoint_in],
        [stage, padded(27)],
        kept=3,
        load=FLIGHT,
    )
    _, second, state1, staged, field, *parcels = call(
        "side_seed",
        side_seed_kernel,
        [post, second, state1, staged, field, *parcels, adjoint_in],
        y_faces(27, -1),
        kept=5,
    )
    along_y = swap_faces("gy", ny, parcels)
    staged, field, *parcels = call(
        "rim_seed",
        rim_seed_kernel,
        [staged, field, second, adjoint_in],
        x_faces(27),
        kept=2,
        load=FLIGHT,
    )
    along_x = swap_faces("gx", nx, parcels)
    _, field, pulled, before, final = call(
        "inner_seed",
        lambda grid, kept, into, buf, *refs: inner_seed_kernel(grid, buf, kept, into, *refs),
        [staged, field, second, state1, adjoint_in],
        [padded(27), fields(1, g.extended), whole],
        [sems],
        kept=2,
        load=FLIGHT,
    )
    field, parcels = relay(field, along_y, -1, 27)
    field, pulled, before, total, parts = call(
        "middle_adjoint",
        lambda grid, _field, _out, _before, near, far, b, a, *refs: middle_adjoint_kernel(
            grid, *refs, near, far, b, a
        ),
        [field, pulled, before, state1, state0, *along_x],
        [fields(1, g.local), fields(5, g.local)],
        kept=3,
        load=FLIGHT,
    )
    _, pulled, _, total, parts, peak = call(
        "total",
        total_kernel,
        [field, pulled, before, total, parts, state1, state0, *parcels],
        [vmem(8, LANES)],
        kept=5,
    )
    half = g.cols // 2
    scratch = [vmem(half, 27, rows, LANES), pltpu.SemaphoreType.DMA((half,))]
    halves = []

    def first_half(peak):
        def kernel(grid, buf, fields, near, echo, *refs):
            echo[...] = near[...]
            adjoint_kernel(grid, 1, half, buf, fields, *refs)

        echo, result = call(
            "adjoint_low",
            kernel,
            [pulled, parts, peak],
            [vmem(8, LANES), whole],
            scratch,
            load=FLIGHT // 2,
        )
        halves.append(result)
        return echo

    largest = largest_of_all(peak, sizes, first_half)
    (adjoint_out,) = call(
        "adjoint_high",
        lambda grid, buf, fields, _, *refs: adjoint_kernel(
            grid, 1 + half, g.cols, buf, fields, *refs
        ),
        [pulled, parts],
        [whole],
        scratch,
        load=FLIGHT // 2,
        result=halves[0],
    )
    (sensitivity,) = call(
        "normalize",
        scale_kernel,
        [total, largest],
        [jax.ShapeDtypeStruct(porosity.shape, F32)],
    )
    return final, adjoint_out, sensitivity


def solution(mesh):
    sizes = (mesh.shape["gx"], mesh.shape["gy"])
    whole, flat = P(None, "gx", "gy"), P("gx", "gy")
    return jax.shard_map(
        functools.partial(on_device, sizes),
        mesh=mesh,
        in_specs=(whole, whole, flat, flat, flat),
        out_specs=(whole, whole, flat),
        check_vma=False,
    )
```

```python
import functools

import jax
import jax.numpy as jnp
from jax import lax
from jax.experimental import pallas as pl
from jax.experimental.pallas import tpu as pltpu
from jax.sharding import PartitionSpec as P

NZ = 64
RELAX = 0.8
PUSH = 0.2
EPS = 1e-06
LANES = 128
VELOCITY = [(a, b, c) for a in (-1, 0, 1) for b in (-1, 0, 1) for c in (-1, 0, 1)]
INDEX = {v: i for i, v in enumerate(VELOCITY)}
WEIGHT = [
    [8.0 / 27, 2.0 / 27, 1.0 / 54, 1.0 / 216][abs(v[0]) + abs(v[1]) + abs(v[2])]
    for v in VELOCITY
]
NORM = [abs(v[0]) + abs(v[1]) + abs(v[2]) for v in VELOCITY]
F32 = jnp.float32
VMEM_LIMIT = 6 * 1024 * 1024
FLIGHT = 12 * 1024 * 1024


class Grid:
    def __init__(self, rows, width):
        self.rows = rows
        self.cols = width // LANES
        self.panel = rows + 16
        self.halo = self.cols + 1
        self.local = self.cols * rows
        self.extended = self.halo * rows + 24
        self.outer = ((0, 8), (rows - 8, 8))
        self.inner = tuple(((r, 16),) for r in range(8, rows - 8, 16))

    def at(self, i, k, r):
        return self.field(i) + k * self.panel + r

    def field(self, i):
        return i * (self.cols + 2) * self.panel + 8

    def padded(self, fields):
        return (fields * (self.cols + 2) * self.panel + 8, LANES)


def velocity(i, sign):
    return tuple(sign * n for n in VELOCITY[i]) if i < 27 else (0, 0, 0)


def moving(fields, sign, axis, side):
    return [i for i in range(fields) if velocity(i, sign)[axis] == side]


def lane_masks(height):
    lane = lax.broadcasted_iota(jnp.int32, (height, LANES), 1)
    return lane >= NZ, lane % NZ == 0, lane % NZ == NZ - 1


def shift_lanes(here, d, masks):
    first, last = masks[1:]
    dy, dz = d[1:]
    if dz == 0:
        return here if dy == 0 else pltpu.roll(here, NZ, 1)
    if dz == 1:
        one, other, edge = 1, NZ + 1, first
    else:
        one, other, edge = LANES - 1, NZ - 1, last
    inner, wrapped = (one, other) if dy == 0 else (other, one)
    return jnp.where(edge, pltpu.roll(here, wrapped, 1), pltpu.roll(here, inner, 1))


def pull(load, d, masks):
    high = masks[0]
    here = load(0)
    if d[1] == 1:
        here = jnp.where(high, load(-1), here)
    elif d[1] == -1:
        here = jnp.where(high, here, load(1))
    return shift_lanes(here, d, masks)


def stacked(parts):
    return parts[0] if len(parts) == 1 else jnp.concatenate(parts, 0)


def read_rows(ref, base, pieces):
    return stacked([ref[pl.ds(base + r, n), :] for r, n in pieces])


def write_rows(ref, base, pieces, value):
    done = 0
    for r, n in pieces:
        ref[pl.ds(base + r, n), :] = value[done : done + n]
        done += n


def pull_block(g, buf, sign, k, pieces, masks, fields=27):
    base = pl.multiple_of(k * g.panel, 8)
    after = pl.multiple_of(jnp.where(k == g.halo, g.panel, base + g.panel), 8)
    out = []
    for i in range(fields):
        d = velocity(i, sign)

        def load(n, i=i, d=d):
            start = {-1: base - g.panel, 0: base, 1: after}[n]
            return read_rows(buf, start + (g.field(i) - d[0]), pieces)

        out.append(pull(load, d, masks))
    return out


def pull_edge(g, buf, sign, side, masks, fields=27):
    out = []
    for i in range(fields):
        d = velocity(i, sign)
        if side == 1:
            row = g.rows - d[0]
        else:
            row = {1: g.rows, 0: g.rows + 1, -1: 0}[d[0]]

        def load(n, i=i, row=row):
            return buf[pl.ds(g.at(i, 1 + n, row), g.cols, stride=g.panel), :]

        out.append(pull(load, d, masks))
    return out


def moments(f):
    flat = {}
    along_z = None
    for a in (-1, 0, 1):
        for b in (-1, 0, 1):
            lo, mid, hi = (f[INDEX[(a, b, c)]] for c in (-1, 0, 1))
            flat[a, b] = lo + mid + hi
            diff = hi - lo
            along_z = diff if along_z is None else along_z + diff
    line = {}
    along_y = None
    for a in (-1, 0, 1):
        line[a] = flat[a, -1] + flat[a, 0] + flat[a, 1]
        diff = flat[a, 1] - flat[a, -1]
        along_y = diff if along_y is None else along_y + diff
    return line[-1] + line[0] + line[1], line[1] - line[-1], along_y, along_z


def combos(x, y, z):
    plane = {}
    for a in (-1, 0, 1):
        for b in (-1, 0, 1):
            if (a, b) > (0, 0):
                continue
            if a == 0:
                plane[a, b] = -y if b else None
            else:
                plane[a, b] = -x if b == 0 else (-x - y if b < 0 else y - x)
    out = []
    for a, b, c in VELOCITY[:13]:
        base = plane[a, b]
        if base is None:
            out.append(-z)
        else:
            out.append(base if c == 0 else (base - z if c < 0 else base + z))
    return out


def relax(f, rho, wx, wy, wz, damp, push, solid):
    ux, uy, uz = (wx + push) * damp, wy * damp, wz * damp
    base = 1.0 - 1.5 * (ux * ux + uy * uy + uz * uz)
    keep = 1.0 - 1.0 / RELAX
    gain = rho * (1.0 / RELAX)
    level = [gain * w for w in (8.0 / 27, 2.0 / 27, 1.0 / 54, 1.0 / 216)]
    along = combos(3.0 * ux, 3.0 * uy, 3.0 * uz)
    out = [None] * 27
    for i in range(13):
        j = 26 - i
        even = base + 0.5 * (along[i] * along[i])
        lift = level[NORM[i]]
        out[i] = jnp.where(solid, f[j], keep * f[i] + lift * (even + along[i]))
        out[j] = jnp.where(solid, f[i], keep * f[j] + lift * (even - along[i]))
    out[13] = jnp.where(solid, f[13], keep * f[13] + level[0] * base)
    return out


def pulled_moments(p):
    first = {}
    for a in (-1, 0, 1):
        for b in (-1, 0, 1):
            lo, mid, hi = (p[INDEX[(a, b, c)]] for c in (-1, 0, 1))
            both = lo + hi
            first[a, b] = (4.0 * mid + both, hi - lo, both)
    second = {}
    for a in (-1, 0, 1):
        lo, mid, hi = (first[a, b] for b in (-1, 0, 1))
        b0 = lo[0] + hi[0]
        b1 = lo[1] + hi[1]
        second[a] = dict(
            one=4.0 * mid[0] + b0,
            y=hi[0] - lo[0],
            yy=b0,
            z=4.0 * mid[1] + b1,
            yz=hi[1] - lo[1],
            zz=4.0 * mid[2] + lo[2] + hi[2],
        )
    lo, mid, hi = (second[a] for a in (-1, 0, 1))

    def full(key):
        return 4.0 * mid[key] + lo[key] + hi[key]

    xx = lo["one"] + hi["one"]
    return dict(
        one=4.0 * mid["one"] + xx,
        x=hi["one"] - lo["one"],
        xx=xx,
        y=full("y"),
        xy=hi["y"] - lo["y"],
        yy=full("yy"),
        z=full("z"),
        xz=hi["z"] - lo["z"],
        yz=full("yz"),
        zz=full("zz"),
    )


def adjoint_scalars(p, rho, wx, wy, wz, damp, push, solid):
    ux, uy, uz = (wx + push) * damp, wy * damp, wz * damp
    s = pulled_moments(p)
    scale = 1.0 / (216.0 * RELAX)
    one = s["one"] * scale
    b = [s[k] * (3.0 * scale) for k in ("x", "y", "z")]
    d = {k: s[k] * (9.0 * scale) for k in ("xx", "xy", "yy", "xz", "yz", "zz")}
    qx = d["xx"] * ux + d["xy"] * uy + d["xz"] * uz
    qy = d["xy"] * ux + d["yy"] * uy + d["yz"] * uz
    qz = d["xz"] * ux + d["yz"] * uy + d["zz"] * uz
    linear = b[0] * ux + b[1] * uy + b[2] * uz
    square = ux * ux + uy * uy + uz * uz
    even = one + linear + 0.5 * (qx * ux + qy * uy + qz * uz) - 1.5 * one * square
    three = 3.0 * one
    gx = (b[0] + qx - three * ux) * damp
    gy = (b[1] + qy - three * uy) * damp
    gz = (b[2] + qz - three * uz) * damp
    even = even - (gx * wx + gy * wy + gz * wz)
    porous = jnp.where(solid, 0.0, -rho * (gx * ux + gy * uy + gz * uz))
    return even, gx, gy, gz, porous


def adjoint_spread(p, even, gx, gy, gz, solid):
    keep = 1.0 - 1.0 / RELAX
    along = combos(gx, gy, gz)
    out = [None] * 27
    for i in range(13):
        j = 26 - i
        out[i] = jnp.where(solid, p[j], keep * p[i] + (even + along[i]))
        out[j] = jnp.where(solid, p[i], keep * p[j] + (even - along[i]))
    out[13] = jnp.where(solid, p[13], keep * p[13] + even)
    return out


def x_lines(g, sign, fields, side):
    lines = []
    for i in moving(fields, sign, 0, side):
        if side == 1:
            lines.append((i, g.rows - 1, (-1, g.rows + 1)))
            lines.append((i, g.rows - 2, (g.rows,)))
        else:
            lines += [(i, 0, (g.rows,)), (i, 1, (g.rows + 1,))]
    edge, target = (g.rows - 1, g.rows + 1) if side == 1 else (0, g.rows)
    return lines + [(i, edge, (target,)) for i in moving(fields, sign, 0, 0)]


def pack_x(g, buf, sign, fields, up, down):
    for side, ref in ((1, up), (-1, down)):
        for n, (i, r, _) in enumerate(x_lines(g, sign, fields, side)):
            ref[n * g.cols : (n + 1) * g.cols, :] = buf[
                pl.ds(g.at(i, 1, r), g.cols, stride=g.panel), :
            ]


def unpack_x(g, buf, sign, fields, up, down):
    for side, ref in ((1, up), (-1, down)):
        for n, (i, _, targets) in enumerate(x_lines(g, sign, fields, side)):
            value = ref[n * g.cols : (n + 1) * g.cols, :]
            for r in targets:
                buf[pl.ds(g.at(i, 1, r), g.cols, stride=g.panel), :] = value
    for i in moving(fields, sign, 0, -1):
        buf[pl.ds(g.at(i, 1, g.rows + 2), g.cols, stride=g.panel), :] = buf[
            pl.ds(g.at(i, 1, 0), g.cols, stride=g.panel), :
        ]


def halo_panels(g, i, sign):
    return (0, g.halo) if velocity(i, sign)[1] == 1 else (g.halo,)


def pack_corners(g, buf, sign, fields, up, down):
    for side, ref in ((1, up), (-1, down)):
        for n, (i, r, _) in enumerate(x_lines(g, sign, fields, side)):
            ref[n : n + 1, :] = buf[pl.ds(g.at(i, g.halo, r), 1), :]


def unpack_corners(g, buf, sign, fields, up, down):
    for side, ref in ((1, up), (-1, down)):
        for n, (i, _, targets) in enumerate(x_lines(g, sign, fields, side)):
            value = ref[n : n + 1, :]
            for r in targets:
                for k in halo_panels(g, i, sign):
                    buf[pl.ds(g.at(i, k, r), 1), :] = value
    for i in moving(fields, sign, 0, -1):
        for k in halo_panels(g, i, sign):
            buf[pl.ds(g.at(i, k, g.rows + 2), 1), :] = buf[pl.ds(g.at(i, k, 0), 1), :]


def still_pairs(fields, sign):
    still = moving(fields, sign, 1, 0)
    half = (len(still) + 1) // 2
    return [(still[n], still[n + half] if n + half < len(still) else None) for n in range(half)]


def y_slots(fields, sign):
    return 9 + len(still_pairs(fields, sign))


def pack_y(g, buf, sign, fields, up, down):
    high = lane_masks(g.rows)[0]
    for side, ref in ((1, up), (-1, down)):
        k = g.cols if side == 1 else 1
        for n, i in enumerate(moving(fields, sign, 1, side)):
            ref[n * g.rows : (n + 1) * g.rows, :] = buf[pl.ds(g.at(i, k, 0), g.rows), :]
        for n, (i, j) in enumerate(still_pairs(fields, sign)):
            value = buf[pl.ds(g.at(i, k, 0), g.rows), :]
            if j is not None:
                other = pltpu.roll(buf[pl.ds(g.at(j, k, 0), g.rows), :], NZ, 1)
                pair = (value, other) if side == 1 else (other, value)
                value = jnp.where(high, *pair)
            ref[(9 + n) * g.rows : (10 + n) * g.rows, :] = value


def unpack_y(g, buf, sign, fields, high, up, down):
    for side, ref in ((1, up), (-1, down)):
        for n, i in enumerate(moving(fields, sign, 1, side)):
            value = ref[n * g.rows : (n + 1) * g.rows, :]
            for k in halo_panels(g, i, sign):
                buf[pl.ds(g.at(i, k, 0), g.rows), :] = value
    for n, (i, j) in enumerate(still_pairs(fields, sign)):
        spot = slice((9 + n) * g.rows, (10 + n) * g.rows)
        before, after = up[spot, :], down[spot, :]
        buf[pl.ds(g.at(i, g.halo, 0), g.rows), :] = jnp.where(high, before, after)
        if j is not None:
            value = pltpu.roll(jnp.where(high, after, before), NZ, 1)
            buf[pl.ds(g.at(j, g.halo, 0), g.rows), :] = value


def by_parity(axis, first, second, act):
    even = lax.rem(lax.axis_index(axis), 2) == 0

    @pl.when(even)
    def _():
        act(first, second)

    @pl.when(jnp.logical_not(even))
    def _():
        act(second, first)


def load_fields(ref, rows, base, pieces, count):
    return [read_rows(ref, base + n * rows, pieces) for n in range(count)]


def save_fields(ref, rows, base, pieces, values):
    for n, value in enumerate(values):
        write_rows(ref, base + n * rows, pieces, value)


def save_populations(g, out, k, pieces, values):
    base = pl.multiple_of(k * g.panel, 8)
    for i, value in enumerate(values):
        write_rows(out, base + g.field(i), pieces, value)


def spot_of(g, k):
    return pl.multiple_of((k - 1) * g.rows, 8)


def lanes_of(k):
    return pl.ds(pl.multiple_of((k - 1) * LANES, LANES), LANES)


def every(first, last, act):
    def step(k, carry):
        act(k)
        return carry

    count = last + 1 - first
    unroll = max(n for n in (1, 2, 3, 4, 6, 8) if count % n == 0)
    lax.fori_loop(first, last + 1, step, 0, unroll=unroll)


def side_panels(g, act, count):
    def step(n, carry):
        act(jnp.where(n == 0, 1, g.cols - 1 + n))
        return carry

    lax.fori_loop(0, count, step, 0, unroll=count)


def interior_tiles(g, act):
    for pieces in g.inner:
        every(2, g.cols - 1, functools.partial(act, pieces=pieces))


def middle_tiles(g, act):
    for pieces in g.inner:
        side_panels(g, functools.partial(act, pieces=pieces), 3)
    every(2, g.cols - 1, functools.partial(act, pieces=g.outer))


def core_tiles(g, act):
    for pieces in g.inner:
        every(3, g.cols - 2, functools.partial(act, pieces=pieces))


def near_core_tiles(g, act):
    def step(n, carry):
        for pieces in g.inner:
            act(jnp.where(n == 0, 2, g.cols - 1), pieces=pieces)
        return carry

    lax.fori_loop(0, 2, step, 0, unroll=2)


def rim_tiles(g, act):
    every(1, g.cols, functools.partial(act, pieces=g.outer))
    for pieces in g.inner:
        side_panels(g, functools.partial(act, pieces=pieces), 2)


def step_tile(g, buf, out, sign, fields, masks, compute):
    def act(k, pieces):
        values = compute(
            pull_block(g, buf, sign, k, pieces, masks, fields), spot_of(g, k), pieces
        )
        save_populations(g, out, k, pieces, values)

    return act


def corner_tiles(g, buf, out, sign, fields, masks, compute):
    small = tuple(mask[:8] for mask in masks)
    act = step_tile(g, buf, out, sign, fields, masks, compute)
    side_panels(g, functools.partial(act, pieces=g.outer), 3)
    spot = g.halo * g.rows
    pieces = ((g.rows, 8),)
    values = compute(pull_block(g, buf, sign, g.halo, pieces, small, fields), spot, ((0, 8),))
    for i in range(27):
        dx = velocity(i, sign)[0]
        if dx == -1:
            out[pl.ds(g.at(i, g.halo, g.rows), 1), :] = values[i][0:1]
        elif dx == 1:
            out[pl.ds(g.at(i, g.halo, -1), 1), :] = values[i][1:2]
    edges = [pull_edge(g, buf, sign, side, small, fields) for side in (1, -1)]
    both = [stacked(pair) for pair in zip(*edges)]
    values = compute(both, spot, ((8, 16),))
    for i in moving(27, sign, 0, -1):
        out[pl.ds(g.at(i, 1, g.rows), g.cols, stride=g.panel), :] = values[i][:8]
    for i in moving(27, sign, 0, 1):
        out[pl.ds(g.at(i, 1, -1), g.cols, stride=g.panel), :] = values[i][8:]
    for i in moving(27, sign, 1, 1):
        out[pl.ds(g.at(i, 0, 0), g.rows), :] = out[pl.ds(g.at(i, g.halo, 0), g.rows), :]
        for r in (-1, g.rows):
            out[pl.ds(g.at(i, 0, r), 1), :] = out[pl.ds(g.at(i, g.halo, r), 1), :]


def flow_of(f):
    rho, mx, my, mz = moments(f)
    inverse = 1.0 / rho
    return inverse, rho, mx * inverse, my * inverse, mz * inverse


def collide_first(g, state, out):
    def act(k, pieces, f):
        base = pl.multiple_of(k * g.panel, 8)
        damp, push, wall = (read_rows(out, base + g.field(i), pieces) for i in (27, 28, 29))
        flow = flow_of(f)[1:] + (damp, push)
        save_fields(state, g.local, spot_of(g, k), pieces, flow + (wall,))
        save_populations(g, out, k, pieces, relax(f, *flow, wall > 0.5))

    return act


def collide_second(g, state):
    def compute(values, spot, pieces):
        f, (damp, push, wall) = values[:27], values[27:]
        flow = flow_of(f)[1:] + (damp, push)
        save_fields(state, g.extended, spot, pieces, flow + (wall,))
        return relax(f, *flow, wall > 0.5)

    return compute


def adjoint_second(g, state, total):
    def compute(p, spot, pieces):
        *flow, wall = load_fields(state, g.extended, spot, pieces, 7)
        *spread, porous = adjoint_scalars(p, *flow, wall > 0.5)
        save_fields(total, g.extended, spot, pieces, [porous])
        return adjoint_spread(p, *spread, wall > 0.5)

    return compute


def seed_tile(g, buf, adjoint, stage, out, masks):
    def act(k, pieces):
        f = pull_block(g, buf, 1, k, pieces, masks)
        for i in range(27):
            write_rows(stage.at[k - 1, i], 0, pieces, f[i])
        inverse, _, wx, wy, wz = flow_of(f)
        even = -(wx * wx + wy * wy + wz * wz) * inverse
        along = combos(wx * inverse, wy * inverse, wz * inverse)
        lanes = lanes_of(k)
        seeded = [
            stacked([adjoint[i, pl.ds(r, n), lanes] for r, n in pieces]) + even for i in range(27)
        ]
        for i in range(13):
            seeded[i] = seeded[i] + along[i]
            seeded[26 - i] = seeded[26 - i] - along[i]
        save_populations(g, out, k, pieces, seeded)

    return act


def block_of(ref, k):
    return ref.at[:, :, lanes_of(k)]


def flat_fields(g, out, near, k):
    porosity, solid, labels = near
    lanes = lanes_of(k)
    label = labels[:, lanes]
    damp = 1.0 / (1.0 + porosity[:, lanes])
    push = jnp.where(label == 1, PUSH, jnp.where(label == 2, -PUSH, 0.0))
    base = pl.multiple_of(k * g.panel, 8)
    for i, value in ((27, damp), (28, push), (29, solid[:, lanes].astype(F32))):
        out[pl.ds(base + g.field(i), g.rows), :] = value


def staged_tile(g, collide, stage):
    def act(k, pieces):
        collide(k, pieces, [read_rows(stage.at[k - 1, i], 0, pieces) for i in range(27)])

    return act


def side_tiles(g, act):
    for pieces in (g.outer,) + g.inner:
        side_panels(g, functools.partial(act, pieces=pieces), 2)


def side_first_kernel(g, pops, *refs):
    flat, (out, state, stage), near, faces, (sems, flat_sems) = (
        refs[:3],
        refs[3:6],
        refs[6:9],
        refs[9:11],
        refs[11:],
    )

    def copy(k):
        return pltpu.make_async_copy(block_of(pops, k), stage.at[k - 1], sems.at[k - 1])

    flat_copies = [
        pltpu.make_async_copy(source, target, flat_sems.at[n])
        for n, (source, target) in enumerate(zip(flat, near))
    ]
    for each in flat_copies:
        each.start()
    for k in (1, g.cols, *range(2, g.cols)):
        copy(k).start()
    for each in flat_copies:
        each.wait()
    for k in (1, g.cols):
        flat_fields(g, out, near, k)
    copy(1).wait()
    copy(g.cols).wait()
    side_tiles(g, staged_tile(g, collide_first(g, state, out), stage))
    by_parity("gy", *faces, functools.partial(pack_y, g, out, 1, 30))
    for k in range(2, g.cols):
        copy(k).wait()


def rim_first_kernel(g, _out, _state, stage, *refs):
    near, (out, state), faces = refs[:3], refs[3:5], refs[5:]
    every(2, g.cols - 1, functools.partial(flat_fields, g, out, near))
    act = staged_tile(g, collide_first(g, state, out), stage)
    every(2, g.cols - 1, functools.partial(act, pieces=g.outer))
    by_parity("gx", *faces, functools.partial(pack_x, g, out, 1, 30))


def inner_first_kernel(g, _, _state, stage, post, state0, out, state1):
    masks = lane_masks(16)
    interior_tiles(g, staged_tile(g, collide_first(g, state0, post), stage))
    interior_tiles(g, step_tile(g, post, out, 1, 30, masks, collide_second(g, state1)))


def relay_kernel(g, sign, fields, _, y_second, y_first, buf, first, second):
    high = lane_masks(g.rows)[0]
    by_parity("gy", y_second, y_first, functools.partial(unpack_y, g, buf, sign, fields, high))
    by_parity("gx", first, second, functools.partial(pack_corners, g, buf, sign, fields))


def middle_second_kernel(g, adjoint, post, out, state1, stage, field, x_second, x_first):
    masks = lane_masks(16)
    by_parity("gx", x_second, x_first, functools.partial(unpack_x, g, post, 1, 30))
    middle_tiles(g, step_tile(g, post, out, 1, 30, masks, collide_second(g, state1)))
    core_tiles(g, seed_tile(g, out, adjoint, stage, field, masks))


def side_seed_kernel(g, _post, _out, _state, _stage, _field, second, first, adjoint, *refs):
    post, out, state1, stage, field, *faces = refs
    masks = lane_masks(16)
    by_parity("gx", second, first, functools.partial(unpack_corners, g, post, 1, 30))
    corner_tiles(g, post, out, 1, 30, masks, collide_second(g, state1))
    side_tiles(g, seed_tile(g, out, adjoint, stage, field, masks))
    by_parity("gy", *faces, functools.partial(pack_y, g, field, -1, 27))


def rim_seed_kernel(g, _stage, _field, out, adjoint, stage, field, *faces):
    seed = seed_tile(g, out, adjoint, stage, field, lane_masks(16))
    every(2, g.cols - 1, functools.partial(seed, pieces=g.outer))
    by_parity("gx", *faces, functools.partial(pack_x, g, field, -1, 27))


def inner_seed_kernel(
    g, post, _stage, _field, state1, adjoint, stage, field, out, total, final, sems
):
    masks = lane_masks(16)

    def copy(k):
        return pltpu.make_async_copy(stage.at[k - 1], block_of(final, k), sems.at[k - 1])

    for k in (1, g.cols, *range(3, g.cols - 1)):
        copy(k).start()
    seed = seed_tile(g, post, adjoint, stage, field, masks)

    near_core_tiles(g, seed)
    for k in (2, g.cols - 1):
        copy(k).start()
    interior_tiles(g, step_tile(g, field, out, -1, 27, masks, adjoint_second(g, state1, total)))
    every(1, g.cols, lambda k: copy(k).wait())


def total_tile(g, out, before, state0, total, parts, masks):
    def act(k, pieces):
        p = pull_block(g, out, -1, k, pieces, masks)
        spot = spot_of(g, k)
        *flow, wall = load_fields(state0, g.local, spot, pieces, 7)
        *spread, porous = adjoint_scalars(p, *flow, wall > 0.5)
        here = load_fields(before, g.extended, spot, pieces, 1)[0] + porous
        save_fields(total, g.local, spot, pieces, [here])
        save_fields(parts, g.local, spot, pieces, spread + [wall])

    return act


def middle_adjoint_kernel(g, field, out, before, total, parts, state1, state0, x_second, x_first):
    masks = lane_masks(16)
    by_parity("gx", x_second, x_first, functools.partial(unpack_x, g, field, -1, 27))
    middle_tiles(g, step_tile(g, field, out, -1, 27, masks, adjoint_second(g, state1, before)))
    core_tiles(g, total_tile(g, out, before, state0, total, parts, masks))


def total_kernel(g, *refs):
    state1, state0, second, first, field, out, before, total, parts, peak = refs[5:]
    masks = lane_masks(16)
    by_parity("gx", second, first, functools.partial(unpack_corners, g, field, -1, 27))
    corner_tiles(g, field, out, -1, 27, masks, adjoint_second(g, state1, before))
    act = total_tile(g, out, before, state0, total, parts, masks)
    near_core_tiles(g, act)
    rim_tiles(g, act)
    size = 8 * (g.local // 64)
    largest = jnp.zeros((8, LANES), F32)
    for start in range(0, g.local, size):
        value = jnp.abs(total[start : start + size, :]).reshape(-1, 8, LANES)
        largest = jnp.maximum(largest, jnp.max(value, 0))
    for n in range(0, peak.shape[0], 8):
        peak[n : n + 8, :] = largest


def adjoint_kernel(g, first, last, buf, parts, result, stage, sems):
    masks = lane_masks(16)

    def copy(k):
        return pltpu.make_async_copy(stage.at[k - first], block_of(result, k), sems.at[k - first])

    def column(k):
        for pieces in (g.outer,) + g.inner:
            p = pull_block(g, buf, -1, k, pieces, masks)
            *spread, wall = load_fields(parts, g.local, spot_of(g, k), pieces, 5)
            for i, value in enumerate(adjoint_spread(p, *spread, wall > 0.5)):
                write_rows(stage.at[k - first, i], 0, pieces, value)
        copy(k).start()

    every(first, last, column)
    every(first, last, lambda k: copy(k).wait())


def scale_kernel(g, total, peak, out):
    largest = jnp.max(peak[...])
    factor = 1.0 / (jnp.full((g.rows, LANES), largest, F32) + EPS)
    for c in range(g.cols):
        value = total[c * g.rows : (c + 1) * g.rows, :] * factor
        out[:, c * LANES : (c + 1) * LANES] = value


def swap_pairs(count, start):
    pairs = []
    for i in range(start, count, 2):
        j = (i + 1) % count
        pairs += [(i, j), (j, i)]
    return pairs


def swap(axis, count, first, second):
    return (
        lax.ppermute(first, axis, swap_pairs(count, 0)),
        lax.ppermute(second, axis, swap_pairs(count, 1)),
    )


def on_device(sizes, populations, adjoint_in, porosity, solid, labels):
    rows, width = porosity.shape
    g = Grid(rows, width)
    in_vmem = pl.BlockSpec(memory_space=pltpu.VMEM)
    in_hbm = pl.BlockSpec(memory_space=pltpu.HBM)
    nx, ny = sizes

    def vmem(*shape):
        return pltpu.VMEM(shape, F32)

    def fields(count, size):
        return vmem(count * size, LANES)

    def padded(count):
        return vmem(*g.padded(count))

    def x_faces(count):
        return [vmem(count * g.cols, LANES)] * 2

    def y_faces(count, sign):
        return [vmem(y_slots(count, sign) * rows, LANES)] * 2

    def corners(count):
        return [vmem(-(-count // 8) * 8, LANES)] * 2

    whole = pltpu.HBM(populations.shape, F32)
    stage = vmem(g.cols, 27, rows, LANES)
    sems = pltpu.SemaphoreType.DMA((g.cols,))

    def call(name, kernel, operands, out_shape, scratch=(), kept=0, load=0, result=None):
        out_shape = [pltpu.VMEM(x.shape, x.dtype) for x in operands[:kept]] + out_shape
        aliases = {n: n for n in range(kept)}
        space = pltpu.HBM if name == "side_first" else pltpu.VMEM
        pinned = [pltpu.with_memory_space_constraint(x, space) for x in operands]
        in_specs = [pl.BlockSpec(memory_space=space)] * len(operands)
        if result is not None:
            aliases[len(operands)] = len(out_shape) - 1
            pinned.append(pltpu.with_memory_space_constraint(result, pltpu.HBM))
            in_specs.append(in_hbm)
        return pl.pallas_call(
            functools.partial(kernel, g),
            in_specs=in_specs,
            out_shape=out_shape,
            out_specs=[in_hbm if x is whole else in_vmem for x in out_shape],
            scratch_shapes=list(scratch),
            input_output_aliases=aliases,
            compiler_params=pltpu.CompilerParams(vmem_limit_bytes=VMEM_LIMIT),
            cost_estimate=pl.CostEstimate(flops=0, bytes_accessed=load, transcendentals=0)
            if load
            else None,
            name=name,
        )(*pinned)

    def swap_faces(axis, count, parcels):
        return swap(axis, count, *parcels)[::-1]

    def relay(buf, parcels, sign, count):
        def kernel(grid, *refs):
            relay_kernel(grid, sign, count, *refs)

        buf, *parcels = call("relay", kernel, [buf, *parcels], corners(count), kept=1)
        return buf, swap("gx", nx, *parcels)[::-1]

    flat_space = [vmem(*porosity.shape)] + [pltpu.VMEM(porosity.shape, jnp.int32)] * 2
    post, state0, staged, *rest = call(
        "side_first",
        side_first_kernel,
        [populations, porosity, solid, labels],
        [padded(30), fields(7, g.local), stage] + flat_space + y_faces(30, 1),
        [sems, pltpu.SemaphoreType.DMA((3,))],
    )
    along_y = swap_faces("gy", ny, rest[3:])
    post, state0, *parcels = call(
        "rim_first",
        rim_first_kernel,
        [post, state0, staged, *rest[:3]],
        x_faces(30),
        kept=2,
        load=FLIGHT,
    )
    along_x = swap_faces("gx", nx, parcels)
    post, state0, second, state1 = call(
        "inner_first",
        inner_first_kernel,
        [post, state0, staged],
        [padded(27), fields(7, g.extended)],
        kept=2,
        load=FLIGHT,
    )
    post, parcels = relay(post, along_y, 1, 30)
    post, second, state1, staged, field = call(
        "middle_second",
        lambda grid, _post, _out, _state, b, a, source, *refs: middle_second_kernel(
            grid, source, *refs, b, a
        ),
        [post, second, state1, *along_x, adjoint_in],
        [stage, padded(27)],
        kept=3,
        load=FLIGHT,
    )
    _, second, state1, staged, field, *parcels = call(
        "side_seed",
        side_seed_kernel,
        [post, second, state1, staged, field, *parcels, adjoint_in],
        y_faces(27, -1),
        kept=5,
    )
    along_y = swap_faces("gy", ny, parcels)
    staged, field, *parcels = call(
        "rim_seed",
        rim_seed_kernel,
        [staged, field, second, adjoint_in],
        x_faces(27),
        kept=2,
        load=FLIGHT,
    )
    along_x = swap_faces("gx", nx, parcels)
    _, field, pulled, before, final = call(
        "inner_seed",
        lambda grid, kept, into, buf, *refs: inner_seed_kernel(grid, buf, kept, into, *refs),
        [staged, field, second, state1, adjoint_in],
        [padded(27), fields(1, g.extended), whole],
        [sems],
        kept=2,
        load=FLIGHT,
    )
    field, parcels = relay(field, along_y, -1, 27)
    field, pulled, before, total, parts = call(
        "middle_adjoint",
        lambda grid, _field, _out, _before, near, far, b, a, *refs: middle_adjoint_kernel(
            grid, *refs, near, far, b, a
        ),
        [field, pulled, before, state1, state0, *along_x],
        [fields(1, g.local), fields(5, g.local)],
        kept=3,
        load=FLIGHT,
    )
    _, pulled, _, total, parts, peak = call(
        "total",
        total_kernel,
        [field, pulled, before, total, parts, state1, state0, *parcels],
        [vmem(8 * nx * ny, LANES)],
        kept=5,
    )
    largest = lax.all_to_all(peak, ("gx", "gy"), 0, 0, tiled=True)
    (adjoint_out,) = call(
        "adjoint_first",
        lambda grid, buf, fields, *refs: adjoint_kernel(grid, 1, g.cols, buf, fields, *refs),
        [pulled, parts],
        [whole],
        [stage, sems],
        load=FLIGHT,
    )
    (sensitivity,) = call(
        "normalize",
        scale_kernel,
        [total, largest],
        [jax.ShapeDtypeStruct(porosity.shape, F32)],
    )
    return final, adjoint_out, sensitivity


def solution(mesh):
    sizes = (mesh.shape["gx"], mesh.shape["gy"])
    whole, flat = P(None, "gx", "gy"), P("gx", "gy")
    return jax.shard_map(
        functools.partial(on_device, sizes),
        mesh=mesh,
        in_specs=(whole, whole, flat, flat, flat),
        out_specs=(whole, whole, flat),
        check_vma=False,
    )
```

```python
import functools

import jax
import jax.numpy as jnp
from jax import lax
from jax.experimental import pallas as pl
from jax.experimental.pallas import tpu as pltpu
from jax.sharding import PartitionSpec as P

NZ = 64
RELAX = 0.8
PUSH = 0.2
EPS = 1e-06
LANES = 128
VELOCITY = [(a, b, c) for a in (-1, 0, 1) for b in (-1, 0, 1) for c in (-1, 0, 1)]
INDEX = {v: i for i, v in enumerate(VELOCITY)}
WEIGHT = [
    [8.0 / 27, 2.0 / 27, 1.0 / 54, 1.0 / 216][abs(v[0]) + abs(v[1]) + abs(v[2])]
    for v in VELOCITY
]
NORM = [abs(v[0]) + abs(v[1]) + abs(v[2]) for v in VELOCITY]
F32 = jnp.float32
VMEM_LIMIT = 6 * 1024 * 1024
FLIGHT = 12 * 1024 * 1024


class Grid:
    def __init__(self, rows, width):
        self.rows = rows
        self.cols = width // LANES
        self.panel = rows + 16
        self.halo = self.cols + 1
        self.local = self.cols * rows
        self.extended = self.halo * rows + 24
        self.outer = ((0, 8), (rows - 8, 8))
        self.inner = tuple(((r, 16),) for r in range(8, rows - 8, 16))

    def at(self, i, k, r):
        return self.field(i) + k * self.panel + r

    def field(self, i):
        return i * (self.cols + 2) * self.panel + 8

    def padded(self, fields):
        return (fields * (self.cols + 2) * self.panel + 8, LANES)


def velocity(i, sign):
    return tuple(sign * n for n in VELOCITY[i]) if i < 27 else (0, 0, 0)


def moving(fields, sign, axis, side):
    return [i for i in range(fields) if velocity(i, sign)[axis] == side]


def lane_masks(height):
    lane = lax.broadcasted_iota(jnp.int32, (height, LANES), 1)
    return lane >= NZ, lane % NZ == 0, lane % NZ == NZ - 1


def shift_lanes(here, d, masks):
    first, last = masks[1:]
    dy, dz = d[1:]
    if dz == 0:
        return here if dy == 0 else pltpu.roll(here, NZ, 1)
    if dz == 1:
        one, other, edge = 1, NZ + 1, first
    else:
        one, other, edge = LANES - 1, NZ - 1, last
    inner, wrapped = (one, other) if dy == 0 else (other, one)
    return jnp.where(edge, pltpu.roll(here, wrapped, 1), pltpu.roll(here, inner, 1))


def pull(load, d, masks):
    high = masks[0]
    here = load(0)
    if d[1] == 1:
        here = jnp.where(high, load(-1), here)
    elif d[1] == -1:
        here = jnp.where(high, here, load(1))
    return shift_lanes(here, d, masks)


def stacked(parts):
    return parts[0] if len(parts) == 1 else jnp.concatenate(parts, 0)


def read_rows(ref, base, pieces):
    return stacked([ref[pl.ds(base + r, n), :] for r, n in pieces])


def write_rows(ref, base, pieces, value):
    done = 0
    for r, n in pieces:
        ref[pl.ds(base + r, n), :] = value[done : done + n]
        done += n


def pull_block(g, buf, sign, k, pieces, masks, fields=27):
    base = pl.multiple_of(k * g.panel, 8)
    after = pl.multiple_of(jnp.where(k == g.halo, g.panel, base + g.panel), 8)
    out = []
    for i in range(fields):
        d = velocity(i, sign)

        def load(n, i=i, d=d):
            start = {-1: base - g.panel, 0: base, 1: after}[n]
            return read_rows(buf, start + (g.field(i) - d[0]), pieces)

        out.append(pull(load, d, masks))
    return out


def pull_edge(g, buf, sign, side, masks, fields=27):
    out = []
    for i in range(fields):
        d = velocity(i, sign)
        if side == 1:
            row = g.rows - d[0]
        else:
            row = {1: g.rows, 0: g.rows + 1, -1: 0}[d[0]]

        def load(n, i=i, row=row):
            return buf[pl.ds(g.at(i, 1 + n, row), g.cols, stride=g.panel), :]

        out.append(pull(load, d, masks))
    return out


def moments(f):
    flat = {}
    along_z = None
    for a in (-1, 0, 1):
        for b in (-1, 0, 1):
            lo, mid, hi = (f[INDEX[(a, b, c)]] for c in (-1, 0, 1))
            flat[a, b] = lo + mid + hi
            diff = hi - lo
            along_z = diff if along_z is None else along_z + diff
    line = {}
    along_y = None
    for a in (-1, 0, 1):
        line[a] = flat[a, -1] + flat[a, 0] + flat[a, 1]
        diff = flat[a, 1] - flat[a, -1]
        along_y = diff if along_y is None else along_y + diff
    return line[-1] + line[0] + line[1], line[1] - line[-1], along_y, along_z


def combos(x, y, z):
    plane = {}
    for a in (-1, 0, 1):
        for b in (-1, 0, 1):
            if (a, b) > (0, 0):
                continue
            if a == 0:
                plane[a, b] = -y if b else None
            else:
                plane[a, b] = -x if b == 0 else (-x - y if b < 0 else y - x)
    out = []
    for a, b, c in VELOCITY[:13]:
        base = plane[a, b]
        if base is None:
            out.append(-z)
        else:
            out.append(base if c == 0 else (base - z if c < 0 else base + z))
    return out


def relax(f, rho, wx, wy, wz, damp, push, solid):
    ux, uy, uz = (wx + push) * damp, wy * damp, wz * damp
    base = 1.0 - 1.5 * (ux * ux + uy * uy + uz * uz)
    keep = 1.0 - 1.0 / RELAX
    gain = rho * (1.0 / RELAX)
    level = [gain * w for w in (8.0 / 27, 2.0 / 27, 1.0 / 54, 1.0 / 216)]
    along = combos(3.0 * ux, 3.0 * uy, 3.0 * uz)
    out = [None] * 27
    for i in range(13):
        j = 26 - i
        even = base + 0.5 * (along[i] * along[i])
        lift = level[NORM[i]]
        out[i] = jnp.where(solid, f[j], keep * f[i] + lift * (even + along[i]))
        out[j] = jnp.where(solid, f[i], keep * f[j] + lift * (even - along[i]))
    out[13] = jnp.where(solid, f[13], keep * f[13] + level[0] * base)
    return out


def pulled_moments(p):
    first = {}
    for a in (-1, 0, 1):
        for b in (-1, 0, 1):
            lo, mid, hi = (p[INDEX[(a, b, c)]] for c in (-1, 0, 1))
            both = lo + hi
            first[a, b] = (4.0 * mid + both, hi - lo, both)
    second = {}
    for a in (-1, 0, 1):
        lo, mid, hi = (first[a, b] for b in (-1, 0, 1))
        b0 = lo[0] + hi[0]
        b1 = lo[1] + hi[1]
        second[a] = dict(
            one=4.0 * mid[0] + b0,
            y=hi[0] - lo[0],
            yy=b0,
            z=4.0 * mid[1] + b1,
            yz=hi[1] - lo[1],
            zz=4.0 * mid[2] + lo[2] + hi[2],
        )
    lo, mid, hi = (second[a] for a in (-1, 0, 1))

    def full(key):
        return 4.0 * mid[key] + lo[key] + hi[key]

    xx = lo["one"] + hi["one"]
    return dict(
        one=4.0 * mid["one"] + xx,
        x=hi["one"] - lo["one"],
        xx=xx,
        y=full("y"),
        xy=hi["y"] - lo["y"],
        yy=full("yy"),
        z=full("z"),
        xz=hi["z"] - lo["z"],
        yz=full("yz"),
        zz=full("zz"),
    )


def adjoint_scalars(p, rho, wx, wy, wz, damp, push, solid):
    ux, uy, uz = (wx + push) * damp, wy * damp, wz * damp
    s = pulled_moments(p)
    scale = 1.0 / (216.0 * RELAX)
    one = s["one"] * scale
    b = [s[k] * (3.0 * scale) for k in ("x", "y", "z")]
    d = {k: s[k] * (9.0 * scale) for k in ("xx", "xy", "yy", "xz", "yz", "zz")}
    qx = d["xx"] * ux + d["xy"] * uy + d["xz"] * uz
    qy = d["xy"] * ux + d["yy"] * uy + d["yz"] * uz
    qz = d["xz"] * ux + d["yz"] * uy + d["zz"] * uz
    linear = b[0] * ux + b[1] * uy + b[2] * uz
    square = ux * ux + uy * uy + uz * uz
    even = one + linear + 0.5 * (qx * ux + qy * uy + qz * uz) - 1.5 * one * square
    three = 3.0 * one
    gx = (b[0] + qx - three * ux) * damp
    gy = (b[1] + qy - three * uy) * damp
    gz = (b[2] + qz - three * uz) * damp
    even = even - (gx * wx + gy * wy + gz * wz)
    porous = jnp.where(solid, 0.0, -rho * (gx * ux + gy * uy + gz * uz))
    return even, gx, gy, gz, porous


def adjoint_spread(p, even, gx, gy, gz, solid):
    keep = 1.0 - 1.0 / RELAX
    along = combos(gx, gy, gz)
    out = [None] * 27
    for i in range(13):
        j = 26 - i
        out[i] = jnp.where(solid, p[j], keep * p[i] + (even + along[i]))
        out[j] = jnp.where(solid, p[i], keep * p[j] + (even - along[i]))
    out[13] = jnp.where(solid, p[13], keep * p[13] + even)
    return out


def x_lines(g, sign, fields, side):
    lines = []
    for i in moving(fields, sign, 0, side):
        if side == 1:
            lines.append((i, g.rows - 1, (-1, g.rows + 1)))
            lines.append((i, g.rows - 2, (g.rows,)))
        else:
            lines += [(i, 0, (g.rows,)), (i, 1, (g.rows + 1,))]
    edge, target = (g.rows - 1, g.rows + 1) if side == 1 else (0, g.rows)
    return lines + [(i, edge, (target,)) for i in moving(fields, sign, 0, 0)]


def pack_x(g, buf, sign, fields, up, down):
    for side, ref in ((1, up), (-1, down)):
        for n, (i, r, _) in enumerate(x_lines(g, sign, fields, side)):
            ref[n * g.cols : (n + 1) * g.cols, :] = buf[
                pl.ds(g.at(i, 1, r), g.cols, stride=g.panel), :
            ]


def unpack_x(g, buf, sign, fields, up, down):
    for side, ref in ((1, up), (-1, down)):
        for n, (i, _, targets) in enumerate(x_lines(g, sign, fields, side)):
            value = ref[n * g.cols : (n + 1) * g.cols, :]
            for r in targets:
                buf[pl.ds(g.at(i, 1, r), g.cols, stride=g.panel), :] = value
    for i in moving(fields, sign, 0, -1):
        buf[pl.ds(g.at(i, 1, g.rows + 2), g.cols, stride=g.panel), :] = buf[
            pl.ds(g.at(i, 1, 0), g.cols, stride=g.panel), :
        ]


def halo_panels(g, i, sign):
    return (0, g.halo) if velocity(i, sign)[1] == 1 else (g.halo,)


def pack_corners(g, buf, sign, fields, up, down):
    for side, ref in ((1, up), (-1, down)):
        for n, (i, r, _) in enumerate(x_lines(g, sign, fields, side)):
            ref[n : n + 1, :] = buf[pl.ds(g.at(i, g.halo, r), 1), :]


def unpack_corners(g, buf, sign, fields, up, down):
    for side, ref in ((1, up), (-1, down)):
        for n, (i, _, targets) in enumerate(x_lines(g, sign, fields, side)):
            value = ref[n : n + 1, :]
            for r in targets:
                for k in halo_panels(g, i, sign):
                    buf[pl.ds(g.at(i, k, r), 1), :] = value
    for i in moving(fields, sign, 0, -1):
        for k in halo_panels(g, i, sign):
            buf[pl.ds(g.at(i, k, g.rows + 2), 1), :] = buf[pl.ds(g.at(i, k, 0), 1), :]


def still_pairs(fields, sign):
    still = moving(fields, sign, 1, 0)
    half = (len(still) + 1) // 2
    return [(still[n], still[n + half] if n + half < len(still) else None) for n in range(half)]


def y_slots(fields, sign):
    return 9 + len(still_pairs(fields, sign))


def pack_y(g, buf, sign, fields, up, down):
    high = lane_masks(g.rows)[0]
    for side, ref in ((1, up), (-1, down)):
        k = g.cols if side == 1 else 1
        for n, i in enumerate(moving(fields, sign, 1, side)):
            ref[n * g.rows : (n + 1) * g.rows, :] = buf[pl.ds(g.at(i, k, 0), g.rows), :]
        for n, (i, j) in enumerate(still_pairs(fields, sign)):
            value = buf[pl.ds(g.at(i, k, 0), g.rows), :]
            if j is not None:
                other = pltpu.roll(buf[pl.ds(g.at(j, k, 0), g.rows), :], NZ, 1)
                pair = (value, other) if side == 1 else (other, value)
                value = jnp.where(high, *pair)
            ref[(9 + n) * g.rows : (10 + n) * g.rows, :] = value


def unpack_y(g, buf, sign, fields, high, up, down):
    for side, ref in ((1, up), (-1, down)):
        for n, i in enumerate(moving(fields, sign, 1, side)):
            value = ref[n * g.rows : (n + 1) * g.rows, :]
            for k in halo_panels(g, i, sign):
                buf[pl.ds(g.at(i, k, 0), g.rows), :] = value
    for n, (i, j) in enumerate(still_pairs(fields, sign)):
        spot = slice((9 + n) * g.rows, (10 + n) * g.rows)
        before, after = up[spot, :], down[spot, :]
        buf[pl.ds(g.at(i, g.halo, 0), g.rows), :] = jnp.where(high, before, after)
        if j is not None:
            value = pltpu.roll(jnp.where(high, after, before), NZ, 1)
            buf[pl.ds(g.at(j, g.halo, 0), g.rows), :] = value


def by_parity(axis, first, second, act):
    even = lax.rem(lax.axis_index(axis), 2) == 0

    @pl.when(even)
    def _():
        act(first, second)

    @pl.when(jnp.logical_not(even))
    def _():
        act(second, first)


def load_fields(ref, rows, base, pieces, count):
    return [read_rows(ref, base + n * rows, pieces) for n in range(count)]


def save_fields(ref, rows, base, pieces, values):
    for n, value in enumerate(values):
        write_rows(ref, base + n * rows, pieces, value)


def save_populations(g, out, k, pieces, values):
    base = pl.multiple_of(k * g.panel, 8)
    for i, value in enumerate(values):
        write_rows(out, base + g.field(i), pieces, value)


def spot_of(g, k):
    return pl.multiple_of((k - 1) * g.rows, 8)


def lanes_of(k):
    return pl.ds(pl.multiple_of((k - 1) * LANES, LANES), LANES)


def every(first, last, act):
    def step(k, carry):
        act(k)
        return carry

    count = last + 1 - first
    unroll = max(n for n in (1, 2, 3, 4, 6, 8) if count % n == 0)
    lax.fori_loop(first, last + 1, step, 0, unroll=unroll)


def side_panels(g, act, count):
    def step(n, carry):
        act(jnp.where(n == 0, 1, g.cols - 1 + n))
        return carry

    lax.fori_loop(0, count, step, 0, unroll=count)


def interior_tiles(g, act):
    for pieces in g.inner:
        every(2, g.cols - 1, functools.partial(act, pieces=pieces))


def middle_tiles(g, act):
    for pieces in g.inner:
        side_panels(g, functools.partial(act, pieces=pieces), 3)
    every(2, g.cols - 1, functools.partial(act, pieces=g.outer))


def core_tiles(g, act):
    for pieces in g.inner:
        every(3, g.cols - 2, functools.partial(act, pieces=pieces))


def near_core_tiles(g, act):
    def step(n, carry):
        for pieces in g.inner:
            act(jnp.where(n == 0, 2, g.cols - 1), pieces=pieces)
        return carry

    lax.fori_loop(0, 2, step, 0, unroll=2)


def step_tile(g, buf, out, sign, fields, masks, compute):
    def act(k, pieces):
        values = compute(
            pull_block(g, buf, sign, k, pieces, masks, fields), spot_of(g, k), pieces
        )
        save_populations(g, out, k, pieces, values)

    return act


def corner_tiles(g, buf, out, sign, fields, masks, compute):
    small = tuple(mask[:8] for mask in masks)
    act = step_tile(g, buf, out, sign, fields, masks, compute)
    side_panels(g, functools.partial(act, pieces=g.outer), 3)
    spot = g.halo * g.rows
    pieces = ((g.rows, 8),)
    values = compute(pull_block(g, buf, sign, g.halo, pieces, small, fields), spot, ((0, 8),))
    for i in range(27):
        dx = velocity(i, sign)[0]
        if dx == -1:
            out[pl.ds(g.at(i, g.halo, g.rows), 1), :] = values[i][0:1]
        elif dx == 1:
            out[pl.ds(g.at(i, g.halo, -1), 1), :] = values[i][1:2]
    edges = [pull_edge(g, buf, sign, side, small, fields) for side in (1, -1)]
    both = [stacked(pair) for pair in zip(*edges)]
    values = compute(both, spot, ((8, 16),))
    for i in moving(27, sign, 0, -1):
        out[pl.ds(g.at(i, 1, g.rows), g.cols, stride=g.panel), :] = values[i][:8]
    for i in moving(27, sign, 0, 1):
        out[pl.ds(g.at(i, 1, -1), g.cols, stride=g.panel), :] = values[i][8:]
    for i in moving(27, sign, 1, 1):
        out[pl.ds(g.at(i, 0, 0), g.rows), :] = out[pl.ds(g.at(i, g.halo, 0), g.rows), :]
        for r in (-1, g.rows):
            out[pl.ds(g.at(i, 0, r), 1), :] = out[pl.ds(g.at(i, g.halo, r), 1), :]


def flow_of(f):
    rho, mx, my, mz = moments(f)
    inverse = 1.0 / rho
    return inverse, rho, mx * inverse, my * inverse, mz * inverse


def collide_first(g, state, out):
    def act(k, pieces, f):
        base = pl.multiple_of(k * g.panel, 8)
        damp, push, wall = (read_rows(out, base + g.field(i), pieces) for i in (27, 28, 29))
        flow = flow_of(f)[1:] + (damp, push)
        save_fields(state, g.local, spot_of(g, k), pieces, flow + (wall,))
        save_populations(g, out, k, pieces, relax(f, *flow, wall > 0.5))

    return act


def collide_second(g, state):
    def compute(values, spot, pieces):
        f, (damp, push, wall) = values[:27], values[27:]
        flow = flow_of(f)[1:] + (damp, push)
        save_fields(state, g.extended, spot, pieces, flow + (wall,))
        return relax(f, *flow, wall > 0.5)

    return compute


def adjoint_second(g, state, total):
    def compute(p, spot, pieces):
        *flow, wall = load_fields(state, g.extended, spot, pieces, 7)
        *spread, porous = adjoint_scalars(p, *flow, wall > 0.5)
        save_fields(total, g.extended, spot, pieces, [porous])
        return adjoint_spread(p, *spread, wall > 0.5)

    return compute


def seed_tile(g, buf, adjoint, stage, out, masks):
    def act(k, pieces):
        f = pull_block(g, buf, 1, k, pieces, masks)
        for i in range(27):
            write_rows(stage.at[k - 1, i], 0, pieces, f[i])
        inverse, _, wx, wy, wz = flow_of(f)
        even = -(wx * wx + wy * wy + wz * wz) * inverse
        along = combos(wx * inverse, wy * inverse, wz * inverse)
        lanes = lanes_of(k)
        seeded = [
            stacked([adjoint[i, pl.ds(r, n), lanes] for r, n in pieces]) + even for i in range(27)
        ]
        for i in range(13):
            seeded[i] = seeded[i] + along[i]
            seeded[26 - i] = seeded[26 - i] - along[i]
        save_populations(g, out, k, pieces, seeded)

    return act


def block_of(ref, k):
    return ref.at[:, :, lanes_of(k)]


def flat_fields(g, out, near, k):
    porosity, solid, labels = near
    lanes = lanes_of(k)
    label = labels[:, lanes]
    damp = 1.0 / (1.0 + porosity[:, lanes])
    push = jnp.where(label == 1, PUSH, jnp.where(label == 2, -PUSH, 0.0))
    base = pl.multiple_of(k * g.panel, 8)
    for i, value in ((27, damp), (28, push), (29, solid[:, lanes].astype(F32))):
        out[pl.ds(base + g.field(i), g.rows), :] = value


def staged_tile(g, collide, stage):
    def act(k, pieces):
        collide(k, pieces, [read_rows(stage.at[k - 1, i], 0, pieces) for i in range(27)])

    return act


def side_tiles(g, act):
    for pieces in (g.outer,) + g.inner:
        side_panels(g, functools.partial(act, pieces=pieces), 2)


def side_first_kernel(g, pops, *refs):
    flat, (out, state, stage), near, faces, (sems, flat_sems) = (
        refs[:3],
        refs[3:6],
        refs[6:9],
        refs[9:11],
        refs[11:],
    )

    def copy(k):
        return pltpu.make_async_copy(block_of(pops, k), stage.at[k - 1], sems.at[k - 1])

    flat_copies = [
        pltpu.make_async_copy(source, target, flat_sems.at[n])
        for n, (source, target) in enumerate(zip(flat, near))
    ]
    for each in flat_copies:
        each.start()
    for k in (1, g.cols, *range(2, g.cols)):
        copy(k).start()
    for each in flat_copies:
        each.wait()
    for k in (1, g.cols):
        flat_fields(g, out, near, k)
    copy(1).wait()
    copy(g.cols).wait()
    side_tiles(g, staged_tile(g, collide_first(g, state, out), stage))
    by_parity("gy", *faces, functools.partial(pack_y, g, out, 1, 30))
    for k in range(2, g.cols):
        copy(k).wait()


def rim_first_kernel(g, _out, _state, stage, *refs):
    near, (out, state), faces = refs[:3], refs[3:5], refs[5:]
    every(2, g.cols - 1, functools.partial(flat_fields, g, out, near))
    act = staged_tile(g, collide_first(g, state, out), stage)
    every(2, g.cols - 1, functools.partial(act, pieces=g.outer))
    by_parity("gx", *faces, functools.partial(pack_x, g, out, 1, 30))


def inner_first_kernel(g, _, _state, stage, post, state0, out, state1):
    masks = lane_masks(16)
    interior_tiles(g, staged_tile(g, collide_first(g, state0, post), stage))
    interior_tiles(g, step_tile(g, post, out, 1, 30, masks, collide_second(g, state1)))


def relay_kernel(g, sign, fields, _, y_second, y_first, buf, first, second):
    high = lane_masks(g.rows)[0]
    by_parity("gy", y_second, y_first, functools.partial(unpack_y, g, buf, sign, fields, high))
    by_parity("gx", first, second, functools.partial(pack_corners, g, buf, sign, fields))


def middle_second_kernel(g, adjoint, post, out, state1, stage, field, x_second, x_first):
    masks = lane_masks(16)
    by_parity("gx", x_second, x_first, functools.partial(unpack_x, g, post, 1, 30))
    middle_tiles(g, step_tile(g, post, out, 1, 30, masks, collide_second(g, state1)))
    core_tiles(g, seed_tile(g, out, adjoint, stage, field, masks))


def side_seed_kernel(g, _post, _out, _state, _stage, _field, second, first, adjoint, *refs):
    post, out, state1, stage, field, *faces = refs
    masks = lane_masks(16)
    by_parity("gx", second, first, functools.partial(unpack_corners, g, post, 1, 30))
    corner_tiles(g, post, out, 1, 30, masks, collide_second(g, state1))
    side_tiles(g, seed_tile(g, out, adjoint, stage, field, masks))
    by_parity("gy", *faces, functools.partial(pack_y, g, field, -1, 27))


def rim_seed_kernel(g, _stage, _field, out, adjoint, stage, field, *faces):
    seed = seed_tile(g, out, adjoint, stage, field, lane_masks(16))
    every(2, g.cols - 1, functools.partial(seed, pieces=g.outer))
    by_parity("gx", *faces, functools.partial(pack_x, g, field, -1, 27))


def inner_seed_kernel(
    g, post, _stage, _field, state1, adjoint, stage, field, out, total, final, sems
):
    masks = lane_masks(16)

    def copy(k):
        return pltpu.make_async_copy(stage.at[k - 1], block_of(final, k), sems.at[k - 1])

    for k in (1, g.cols, *range(3, g.cols - 1)):
        copy(k).start()
    seed = seed_tile(g, post, adjoint, stage, field, masks)

    near_core_tiles(g, seed)
    for k in (2, g.cols - 1):
        copy(k).start()
    interior_tiles(g, step_tile(g, field, out, -1, 27, masks, adjoint_second(g, state1, total)))
    every(1, g.cols, lambda k: copy(k).wait())


def total_tile(g, out, before, state0, total, stage, masks):
    def act(k, pieces):
        p = pull_block(g, out, -1, k, pieces, masks)
        spot = spot_of(g, k)
        *flow, wall = load_fields(state0, g.local, spot, pieces, 7)
        solid = wall > 0.5
        *spread, porous = adjoint_scalars(p, *flow, solid)
        here = load_fields(before, g.extended, spot, pieces, 1)[0] + porous
        save_fields(total, g.local, spot, pieces, [here])
        for i, value in enumerate(adjoint_spread(p, *spread, solid)):
            write_rows(stage.at[k - 1, i], 0, pieces, value)

    return act


def middle_adjoint_kernel(g, field, out, before, total, stage, state1, state0, x_second, x_first):
    masks = lane_masks(16)
    by_parity("gx", x_second, x_first, functools.partial(unpack_x, g, field, -1, 27))
    middle_tiles(g, step_tile(g, field, out, -1, 27, masks, adjoint_second(g, state1, before)))
    core_tiles(g, total_tile(g, out, before, state0, total, stage, masks))


def total_kernel(g, *refs):
    state1, state0, second, first, field, out, before, total, stage, peak, result, sems = refs[5:]
    masks = lane_masks(16)

    def copy(k):
        return pltpu.make_async_copy(stage.at[k - 1], block_of(result, k), sems.at[k - 1])

    by_parity("gx", second, first, functools.partial(unpack_corners, g, field, -1, 27))
    corner_tiles(g, field, out, -1, 27, masks, adjoint_second(g, state1, before))
    act = total_tile(g, out, before, state0, total, stage, masks)
    near_core_tiles(g, act)
    for pieces in g.inner:
        side_panels(g, functools.partial(act, pieces=pieces), 2)

    def column(k):
        act(k, g.outer)
        copy(k).start()

    every(1, g.cols, column)
    size = 8 * (g.local // 64)
    largest = jnp.zeros((8, LANES), F32)
    for start in range(0, g.local, size):
        value = jnp.abs(total[start : start + size, :]).reshape(-1, 8, LANES)
        largest = jnp.maximum(largest, jnp.max(value, 0))
    for n in range(0, peak.shape[0], 8):
        peak[n : n + 8, :] = largest
    every(1, g.cols, lambda k: copy(k).wait())


def scale_kernel(g, total, peak, out):
    largest = jnp.max(peak[...])
    factor = 1.0 / (jnp.full((g.rows, LANES), largest, F32) + EPS)
    for c in range(g.cols):
        value = total[c * g.rows : (c + 1) * g.rows, :] * factor
        out[:, c * LANES : (c + 1) * LANES] = value


def swap_pairs(count, start):
    pairs = []
    for i in range(start, count, 2):
        j = (i + 1) % count
        pairs += [(i, j), (j, i)]
    return pairs


def swap(axis, count, first, second):
    return (
        lax.ppermute(first, axis, swap_pairs(count, 0)),
        lax.ppermute(second, axis, swap_pairs(count, 1)),
    )


def on_device(sizes, populations, adjoint_in, porosity, solid, labels):
    rows, width = porosity.shape
    g = Grid(rows, width)
    in_vmem = pl.BlockSpec(memory_space=pltpu.VMEM)
    in_hbm = pl.BlockSpec(memory_space=pltpu.HBM)
    nx, ny = sizes

    def vmem(*shape):
        return pltpu.VMEM(shape, F32)

    def fields(count, size):
        return vmem(count * size, LANES)

    def padded(count):
        return vmem(*g.padded(count))

    def x_faces(count):
        return [vmem(count * g.cols, LANES)] * 2

    def y_faces(count, sign):
        return [vmem(y_slots(count, sign) * rows, LANES)] * 2

    def corners(count):
        return [vmem(-(-count // 8) * 8, LANES)] * 2

    whole = pltpu.HBM(populations.shape, F32)
    stage = vmem(g.cols, 27, rows, LANES)
    sems = pltpu.SemaphoreType.DMA((g.cols,))

    def call(name, kernel, operands, out_shape, scratch=(), kept=0, load=0, result=None):
        out_shape = [pltpu.VMEM(x.shape, x.dtype) for x in operands[:kept]] + out_shape
        aliases = {n: n for n in range(kept)}
        space = pltpu.HBM if name == "side_first" else pltpu.VMEM
        pinned = [pltpu.with_memory_space_constraint(x, space) for x in operands]
        in_specs = [pl.BlockSpec(memory_space=space)] * len(operands)
        return pl.pallas_call(
            functools.partial(kernel, g),
            in_specs=in_specs,
            out_shape=out_shape,
            out_specs=[in_hbm if x is whole else in_vmem for x in out_shape],
            scratch_shapes=list(scratch),
            input_output_aliases=aliases,
            compiler_params=pltpu.CompilerParams(vmem_limit_bytes=VMEM_LIMIT),
            cost_estimate=pl.CostEstimate(flops=0, bytes_accessed=load, transcendentals=0)
            if load
            else None,
            name=name,
        )(*pinned)

    def swap_faces(axis, count, parcels):
        return swap(axis, count, *parcels)[::-1]

    def relay(buf, parcels, sign, count):
        def kernel(grid, *refs):
            relay_kernel(grid, sign, count, *refs)

        buf, *parcels = call("relay", kernel, [buf, *parcels], corners(count), kept=1)
        return buf, swap("gx", nx, *parcels)[::-1]

    flat_space = [vmem(*porosity.shape)] + [pltpu.VMEM(porosity.shape, jnp.int32)] * 2
    post, state0, staged, *rest = call(
        "side_first",
        side_first_kernel,
        [populations, porosity, solid, labels],
        [padded(30), fields(7, g.local), stage] + flat_space + y_faces(30, 1),
        [sems, pltpu.SemaphoreType.DMA((3,))],
    )
    along_y = swap_faces("gy", ny, rest[3:])
    post, state0, *parcels = call(
        "rim_first",
        rim_first_kernel,
        [post, state0, staged, *rest[:3]],
        x_faces(30),
        kept=2,
        load=FLIGHT,
    )
    along_x = swap_faces("gx", nx, parcels)
    post, state0, second, state1 = call(
        "inner_first",
        inner_first_kernel,
        [post, state0, staged],
        [padded(27), fields(7, g.extended)],
        kept=2,
        load=FLIGHT,
    )
    post, parcels = relay(post, along_y, 1, 30)
    post, second, state1, staged, field = call(
        "middle_second",
        lambda grid, _post, _out, _state, b, a, source, *refs: middle_second_kernel(
            grid, source, *refs, b, a
        ),
        [post, second, state1, *along_x, adjoint_in],
        [stage, padded(27)],
        kept=3,
        load=FLIGHT,
    )
    _, second, state1, staged, field, *parcels = call(
        "side_seed",
        side_seed_kernel,
        [post, second, state1, staged, field, *parcels, adjoint_in],
        y_faces(27, -1),
        kept=5,
    )
    along_y = swap_faces("gy", ny, parcels)
    staged, field, *parcels = call(
        "rim_seed",
        rim_seed_kernel,
        [staged, field, second, adjoint_in],
        x_faces(27),
        kept=2,
        load=FLIGHT,
    )
    along_x = swap_faces("gx", nx, parcels)
    _, field, pulled, before, final = call(
        "inner_seed",
        lambda grid, kept, into, buf, *refs: inner_seed_kernel(grid, buf, kept, into, *refs),
        [staged, field, second, state1, adjoint_in],
        [padded(27), fields(1, g.extended), whole],
        [sems],
        kept=2,
        load=FLIGHT,
    )
    field, parcels = relay(field, along_y, -1, 27)
    field, pulled, before, total, staged = call(
        "middle_adjoint",
        lambda grid, _field, _out, _before, near, far, b, a, *refs: middle_adjoint_kernel(
            grid, *refs, near, far, b, a
        ),
        [field, pulled, before, state1, state0, *along_x],
        [fields(1, g.local), stage],
        kept=3,
        load=FLIGHT,
    )
    _, _, _, total, _, peak, adjoint_out = call(
        "total",
        total_kernel,
        [field, pulled, before, total, staged, state1, state0, *parcels],
        [vmem(8 * nx * ny, LANES), whole],
        [sems],
        kept=5,
    )
    largest = lax.all_to_all(peak, ("gx", "gy"), 0, 0, tiled=True)
    (sensitivity,) = call(
        "normalize",
        scale_kernel,
        [total, largest],
        [jax.ShapeDtypeStruct(porosity.shape, F32)],
    )
    return final, adjoint_out, sensitivity


def solution(mesh):
    sizes = (mesh.shape["gx"], mesh.shape["gy"])
    whole, flat = P(None, "gx", "gy"), P("gx", "gy")
    return jax.shard_map(
        functools.partial(on_device, sizes),
        mesh=mesh,
        in_specs=(whole, whole, flat, flat, flat),
        out_specs=(whole, whole, flat),
        check_vma=False,
    )
```

```python
import functools

import jax
import jax.numpy as jnp
from jax import lax
from jax.experimental import pallas as pl
from jax.experimental.pallas import tpu as pltpu
from jax.sharding import PartitionSpec as P

NZ = 64
RELAX = 0.8
PUSH = 0.2
EPS = 1e-06
LANES = 128
VELOCITY = [(a, b, c) for a in (-1, 0, 1) for b in (-1, 0, 1) for c in (-1, 0, 1)]
INDEX = {v: i for i, v in enumerate(VELOCITY)}
WEIGHT = [
    [8.0 / 27, 2.0 / 27, 1.0 / 54, 1.0 / 216][abs(v[0]) + abs(v[1]) + abs(v[2])]
    for v in VELOCITY
]
NORM = [abs(v[0]) + abs(v[1]) + abs(v[2]) for v in VELOCITY]
F32 = jnp.float32
VMEM_LIMIT = 6 * 1024 * 1024
FLIGHT = 12 * 1024 * 1024


class Grid:
    def __init__(self, rows, width):
        self.rows = rows
        self.cols = width // LANES
        self.panel = rows + 16
        self.halo = self.cols + 1
        self.local = self.cols * rows
        self.extended = self.halo * rows + 24
        self.outer = ((0, 8), (rows - 8, 8))
        self.inner = tuple(((r, 16),) for r in range(8, rows - 8, 16))

    def at(self, i, k, r):
        return self.field(i) + k * self.panel + r

    def field(self, i):
        return i * (self.cols + 2) * self.panel + 8

    def padded(self, fields):
        return (fields * (self.cols + 2) * self.panel + 8, LANES)


def velocity(i, sign):
    return tuple(sign * n for n in VELOCITY[i]) if i < 27 else (0, 0, 0)


def moving(fields, sign, axis, side):
    return [i for i in range(fields) if velocity(i, sign)[axis] == side]


def lane_masks(height):
    lane = lax.broadcasted_iota(jnp.int32, (height, LANES), 1)
    level = lane % NZ
    below = jnp.where(level == 0, lane + (NZ - 1), lane - 1)
    above = jnp.where(level == NZ - 1, lane - (NZ - 1), lane + 1)
    return lane >= NZ, below, above, below ^ NZ, above ^ NZ


def shift_lanes(here, d, masks):
    dy, dz = d[1:]
    if dz == 0:
        return here if dy == 0 else pltpu.roll(here, NZ, 1)
    source = masks[(1 if dz == 1 else 2) + (0 if dy == 0 else 2)]
    return jnp.take_along_axis(here, source, axis=1, mode="promise_in_bounds")


def pull(load, d, masks):
    high = masks[0]
    here = load(0)
    if d[1] == 1:
        here = jnp.where(high, load(-1), here)
    elif d[1] == -1:
        here = jnp.where(high, here, load(1))
    return shift_lanes(here, d, masks)


def stacked(parts):
    return parts[0] if len(parts) == 1 else jnp.concatenate(parts, 0)


def read_rows(ref, base, pieces):
    return stacked([ref[pl.ds(base + r, n), :] for r, n in pieces])


def write_rows(ref, base, pieces, value):
    done = 0
    for r, n in pieces:
        ref[pl.ds(base + r, n), :] = value[done : done + n]
        done += n


def pull_block(g, buf, sign, k, pieces, masks, fields=27):
    base = pl.multiple_of(k * g.panel, 8)
    after = pl.multiple_of(jnp.where(k == g.halo, g.panel, base + g.panel), 8)
    out = []
    for i in range(fields):
        d = velocity(i, sign)

        def load(n, i=i, d=d):
            start = {-1: base - g.panel, 0: base, 1: after}[n]
            return read_rows(buf, start + (g.field(i) - d[0]), pieces)

        out.append(pull(load, d, masks))
    return out


def pull_edge(g, buf, sign, side, masks, fields=27):
    out = []
    for i in range(fields):
        d = velocity(i, sign)
        if side == 1:
            row = g.rows - d[0]
        else:
            row = {1: g.rows, 0: g.rows + 1, -1: 0}[d[0]]

        def load(n, i=i, row=row):
            return buf[pl.ds(g.at(i, 1 + n, row), g.cols, stride=g.panel), :]

        out.append(pull(load, d, masks))
    return out


def moments(f):
    flat = {}
    along_z = None
    for a in (-1, 0, 1):
        for b in (-1, 0, 1):
            lo, mid, hi = (f[INDEX[(a, b, c)]] for c in (-1, 0, 1))
            flat[a, b] = lo + mid + hi
            diff = hi - lo
            along_z = diff if along_z is None else along_z + diff
    line = {}
    along_y = None
    for a in (-1, 0, 1):
        line[a] = flat[a, -1] + flat[a, 0] + flat[a, 1]
        diff = flat[a, 1] - flat[a, -1]
        along_y = diff if along_y is None else along_y + diff
    return line[-1] + line[0] + line[1], line[1] - line[-1], along_y, along_z


def combos(x, y, z):
    plane = {}
    for a in (-1, 0, 1):
        for b in (-1, 0, 1):
            if (a, b) > (0, 0):
                continue
            if a == 0:
                plane[a, b] = -y if b else None
            else:
                plane[a, b] = -x if b == 0 else (-x - y if b < 0 else y - x)
    out = []
    for a, b, c in VELOCITY[:13]:
        base = plane[a, b]
        if base is None:
            out.append(-z)
        else:
            out.append(base if c == 0 else (base - z if c < 0 else base + z))
    return out


def relax(f, rho, wx, wy, wz, damp, push, solid):
    ux, uy, uz = (wx + push) * damp, wy * damp, wz * damp
    base = 1.0 - 1.5 * (ux * ux + uy * uy + uz * uz)
    keep = 1.0 - 1.0 / RELAX
    gain = rho * (1.0 / RELAX)
    level = [gain * w for w in (8.0 / 27, 2.0 / 27, 1.0 / 54, 1.0 / 216)]
    along = combos(3.0 * ux, 3.0 * uy, 3.0 * uz)
    out = [None] * 27
    for i in range(13):
        j = 26 - i
        even = base + 0.5 * (along[i] * along[i])
        lift = level[NORM[i]]
        out[i] = jnp.where(solid, f[j], keep * f[i] + lift * (even + along[i]))
        out[j] = jnp.where(solid, f[i], keep * f[j] + lift * (even - along[i]))
    out[13] = jnp.where(solid, f[13], keep * f[13] + level[0] * base)
    return out


def pulled_moments(p):
    first = {}
    for a in (-1, 0, 1):
        for b in (-1, 0, 1):
            lo, mid, hi = (p[INDEX[(a, b, c)]] for c in (-1, 0, 1))
            both = lo + hi
            first[a, b] = (4.0 * mid + both, hi - lo, both)
    second = {}
    for a in (-1, 0, 1):
        lo, mid, hi = (first[a, b] for b in (-1, 0, 1))
        b0 = lo[0] + hi[0]
        b1 = lo[1] + hi[1]
        second[a] = dict(
            one=4.0 * mid[0] + b0,
            y=hi[0] - lo[0],
            yy=b0,
            z=4.0 * mid[1] + b1,
            yz=hi[1] - lo[1],
            zz=4.0 * mid[2] + lo[2] + hi[2],
        )
    lo, mid, hi = (second[a] for a in (-1, 0, 1))

    def full(key):
        return 4.0 * mid[key] + lo[key] + hi[key]

    xx = lo["one"] + hi["one"]
    return dict(
        one=4.0 * mid["one"] + xx,
        x=hi["one"] - lo["one"],
        xx=xx,
        y=full("y"),
        xy=hi["y"] - lo["y"],
        yy=full("yy"),
        z=full("z"),
        xz=hi["z"] - lo["z"],
        yz=full("yz"),
        zz=full("zz"),
    )


def adjoint_scalars(p, rho, wx, wy, wz, damp, push, solid):
    ux, uy, uz = (wx + push) * damp, wy * damp, wz * damp
    s = pulled_moments(p)
    scale = 1.0 / (216.0 * RELAX)
    one = s["one"] * scale
    b = [s[k] * (3.0 * scale) for k in ("x", "y", "z")]
    d = {k: s[k] * (9.0 * scale) for k in ("xx", "xy", "yy", "xz", "yz", "zz")}
    qx = d["xx"] * ux + d["xy"] * uy + d["xz"] * uz
    qy = d["xy"] * ux + d["yy"] * uy + d["yz"] * uz
    qz = d["xz"] * ux + d["yz"] * uy + d["zz"] * uz
    linear = b[0] * ux + b[1] * uy + b[2] * uz
    square = ux * ux + uy * uy + uz * uz
    even = one + linear + 0.5 * (qx * ux + qy * uy + qz * uz) - 1.5 * one * square
    three = 3.0 * one
    gx = (b[0] + qx - three * ux) * damp
    gy = (b[1] + qy - three * uy) * damp
    gz = (b[2] + qz - three * uz) * damp
    even = even - (gx * wx + gy * wy + gz * wz)
    porous = jnp.where(solid, 0.0, -rho * (gx * ux + gy * uy + gz * uz))
    return even, gx, gy, gz, porous


def adjoint_spread(p, even, gx, gy, gz, solid):
    keep = 1.0 - 1.0 / RELAX
    along = combos(gx, gy, gz)
    out = [None] * 27
    for i in range(13):
        j = 26 - i
        out[i] = jnp.where(solid, p[j], keep * p[i] + (even + along[i]))
        out[j] = jnp.where(solid, p[i], keep * p[j] + (even - along[i]))
    out[13] = jnp.where(solid, p[13], keep * p[13] + even)
    return out


def x_lines(g, sign, fields, side):
    lines = []
    for i in moving(fields, sign, 0, side):
        if side == 1:
            lines.append((i, g.rows - 1, (-1, g.rows + 1)))
            lines.append((i, g.rows - 2, (g.rows,)))
        else:
            lines += [(i, 0, (g.rows,)), (i, 1, (g.rows + 1,))]
    edge, target = (g.rows - 1, g.rows + 1) if side == 1 else (0, g.rows)
    return lines + [(i, edge, (target,)) for i in moving(fields, sign, 0, 0)]


def pack_x(g, buf, sign, fields, up, down):
    for side, ref in ((1, up), (-1, down)):
        for n, (i, r, _) in enumerate(x_lines(g, sign, fields, side)):
            ref[n * g.cols : (n + 1) * g.cols, :] = buf[
                pl.ds(g.at(i, 1, r), g.cols, stride=g.panel), :
            ]


def unpack_x(g, buf, sign, fields, up, down):
    for side, ref in ((1, up), (-1, down)):
        for n, (i, _, targets) in enumerate(x_lines(g, sign, fields, side)):
            value = ref[n * g.cols : (n + 1) * g.cols, :]
            for r in targets:
                buf[pl.ds(g.at(i, 1, r), g.cols, stride=g.panel), :] = value
    for i in moving(fields, sign, 0, -1):
        buf[pl.ds(g.at(i, 1, g.rows + 2), g.cols, stride=g.panel), :] = buf[
            pl.ds(g.at(i, 1, 0), g.cols, stride=g.panel), :
        ]


def halo_panels(g, i, sign):
    return (0, g.halo) if velocity(i, sign)[1] == 1 else (g.halo,)


def pack_corners(g, buf, sign, fields, up, down):
    for side, ref in ((1, up), (-1, down)):
        for n, (i, r, _) in enumerate(x_lines(g, sign, fields, side)):
            ref[n : n + 1, :] = buf[pl.ds(g.at(i, g.halo, r), 1), :]


def unpack_corners(g, buf, sign, fields, up, down):
    for side, ref in ((1, up), (-1, down)):
        for n, (i, _, targets) in enumerate(x_lines(g, sign, fields, side)):
            value = ref[n : n + 1, :]
            for r in targets:
                for k in halo_panels(g, i, sign):
                    buf[pl.ds(g.at(i, k, r), 1), :] = value
    for i in moving(fields, sign, 0, -1):
        for k in halo_panels(g, i, sign):
            buf[pl.ds(g.at(i, k, g.rows + 2), 1), :] = buf[pl.ds(g.at(i, k, 0), 1), :]


def still_pairs(fields, sign):
    still = moving(fields, sign, 1, 0)
    half = (len(still) + 1) // 2
    return [(still[n], still[n + half] if n + half < len(still) else None) for n in range(half)]


def y_slots(fields, sign):
    return 9 + len(still_pairs(fields, sign))


def pack_y(g, buf, sign, fields, up, down):
    high = lane_masks(g.rows)[0]
    for side, ref in ((1, up), (-1, down)):
        k = g.cols if side == 1 else 1
        for n, i in enumerate(moving(fields, sign, 1, side)):
            ref[n * g.rows : (n + 1) * g.rows, :] = buf[pl.ds(g.at(i, k, 0), g.rows), :]
        for n, (i, j) in enumerate(still_pairs(fields, sign)):
            value = buf[pl.ds(g.at(i, k, 0), g.rows), :]
            if j is not None:
                other = pltpu.roll(buf[pl.ds(g.at(j, k, 0), g.rows), :], NZ, 1)
                pair = (value, other) if side == 1 else (other, value)
                value = jnp.where(high, *pair)
            ref[(9 + n) * g.rows : (10 + n) * g.rows, :] = value


def unpack_y(g, buf, sign, fields, high, up, down):
    for side, ref in ((1, up), (-1, down)):
        for n, i in enumerate(moving(fields, sign, 1, side)):
            value = ref[n * g.rows : (n + 1) * g.rows, :]
            for k in halo_panels(g, i, sign):
                buf[pl.ds(g.at(i, k, 0), g.rows), :] = value
    for n, (i, j) in enumerate(still_pairs(fields, sign)):
        spot = slice((9 + n) * g.rows, (10 + n) * g.rows)
        before, after = up[spot, :], down[spot, :]
        buf[pl.ds(g.at(i, g.halo, 0), g.rows), :] = jnp.where(high, before, after)
        if j is not None:
            value = pltpu.roll(jnp.where(high, after, before), NZ, 1)
            buf[pl.ds(g.at(j, g.halo, 0), g.rows), :] = value


def by_parity(axis, first, second, act):
    even = lax.rem(lax.axis_index(axis), 2) == 0

    @pl.when(even)
    def _():
        act(first, second)

    @pl.when(jnp.logical_not(even))
    def _():
        act(second, first)


def load_fields(ref, rows, base, pieces, count):
    return [read_rows(ref, base + n * rows, pieces) for n in range(count)]


def save_fields(ref, rows, base, pieces, values):
    for n, value in enumerate(values):
        write_rows(ref, base + n * rows, pieces, value)


def save_populations(g, out, k, pieces, values):
    base = pl.multiple_of(k * g.panel, 8)
    for i, value in enumerate(values):
        write_rows(out, base + g.field(i), pieces, value)


def spot_of(g, k):
    return pl.multiple_of((k - 1) * g.rows, 8)


def lanes_of(k):
    return pl.ds(pl.multiple_of((k - 1) * LANES, LANES), LANES)


def every(first, last, act):
    def step(k, carry):
        act(k)
        return carry

    count = last + 1 - first
    unroll = max(n for n in (1, 2, 3, 4, 6, 8) if count % n == 0)
    lax.fori_loop(first, last + 1, step, 0, unroll=unroll)


def side_panels(g, act, count):
    def step(n, carry):
        act(jnp.where(n == 0, 1, g.cols - 1 + n))
        return carry

    lax.fori_loop(0, count, step, 0, unroll=count)


def interior_tiles(g, act):
    for pieces in g.inner:
        every(2, g.cols - 1, functools.partial(act, pieces=pieces))


def middle_tiles(g, act):
    for pieces in g.inner:
        side_panels(g, functools.partial(act, pieces=pieces), 3)
    every(2, g.cols - 1, functools.partial(act, pieces=g.outer))


def core_tiles(g, act):
    for pieces in g.inner:
        every(3, g.cols - 2, functools.partial(act, pieces=pieces))


def near_core_tiles(g, act):
    def step(n, carry):
        for pieces in g.inner:
            act(jnp.where(n == 0, 2, g.cols - 1), pieces=pieces)
        return carry

    lax.fori_loop(0, 2, step, 0, unroll=2)


def rim_tiles(g, act):
    every(1, g.cols, functools.partial(act, pieces=g.outer))
    for pieces in g.inner:
        side_panels(g, functools.partial(act, pieces=pieces), 2)


def step_tile(g, buf, out, sign, fields, masks, compute):
    def act(k, pieces):
        values = compute(
            pull_block(g, buf, sign, k, pieces, masks, fields), spot_of(g, k), pieces
        )
        save_populations(g, out, k, pieces, values)

    return act


def corner_tiles(g, buf, out, sign, fields, masks, compute):
    small = tuple(mask[:8] for mask in masks)
    act = step_tile(g, buf, out, sign, fields, masks, compute)
    side_panels(g, functools.partial(act, pieces=g.outer), 3)
    spot = g.halo * g.rows
    pieces = ((g.rows, 8),)
    values = compute(pull_block(g, buf, sign, g.halo, pieces, small, fields), spot, ((0, 8),))
    for i in range(27):
        dx = velocity(i, sign)[0]
        if dx == -1:
            out[pl.ds(g.at(i, g.halo, g.rows), 1), :] = values[i][0:1]
        elif dx == 1:
            out[pl.ds(g.at(i, g.halo, -1), 1), :] = values[i][1:2]
    edges = [pull_edge(g, buf, sign, side, small, fields) for side in (1, -1)]
    both = [stacked(pair) for pair in zip(*edges)]
    values = compute(both, spot, ((8, 16),))
    for i in moving(27, sign, 0, -1):
        out[pl.ds(g.at(i, 1, g.rows), g.cols, stride=g.panel), :] = values[i][:8]
    for i in moving(27, sign, 0, 1):
        out[pl.ds(g.at(i, 1, -1), g.cols, stride=g.panel), :] = values[i][8:]
    for i in moving(27, sign, 1, 1):
        out[pl.ds(g.at(i, 0, 0), g.rows), :] = out[pl.ds(g.at(i, g.halo, 0), g.rows), :]
        for r in (-1, g.rows):
            out[pl.ds(g.at(i, 0, r), 1), :] = out[pl.ds(g.at(i, g.halo, r), 1), :]


def flow_of(f):
    rho, mx, my, mz = moments(f)
    inverse = 1.0 / rho
    return inverse, rho, mx * inverse, my * inverse, mz * inverse


def collide_first(g, state, out):
    def act(k, pieces, f):
        base = pl.multiple_of(k * g.panel, 8)
        damp, push, wall = (read_rows(out, base + g.field(i), pieces) for i in (27, 28, 29))
        flow = flow_of(f)[1:] + (damp, push)
        save_fields(state, g.local, spot_of(g, k), pieces, flow + (wall,))
        save_populations(g, out, k, pieces, relax(f, *flow, wall > 0.5))

    return act


def collide_second(g, state):
    def compute(values, spot, pieces):
        f, (damp, push, wall) = values[:27], values[27:]
        flow = flow_of(f)[1:] + (damp, push)
        save_fields(state, g.extended, spot, pieces, flow + (wall,))
        return relax(f, *flow, wall > 0.5)

    return compute


def adjoint_second(g, state, total):
    def compute(p, spot, pieces):
        *flow, wall = load_fields(state, g.extended, spot, pieces, 7)
        *spread, porous = adjoint_scalars(p, *flow, wall > 0.5)
        save_fields(total, g.extended, spot, pieces, [porous])
        return adjoint_spread(p, *spread, wall > 0.5)

    return compute


def seed_tile(g, buf, adjoint, stage, out, masks):
    def act(k, pieces):
        f = pull_block(g, buf, 1, k, pieces, masks)
        for i in range(27):
            write_rows(stage.at[k - 1, i], 0, pieces, f[i])
        inverse, _, wx, wy, wz = flow_of(f)
        even = -(wx * wx + wy * wy + wz * wz) * inverse
        along = combos(wx * inverse, wy * inverse, wz * inverse)
        lanes = lanes_of(k)
        seeded = [
            stacked([adjoint[i, pl.ds(r, n), lanes] for r, n in pieces]) + even for i in range(27)
        ]
        for i in range(13):
            seeded[i] = seeded[i] + along[i]
            seeded[26 - i] = seeded[26 - i] - along[i]
        save_populations(g, out, k, pieces, seeded)

    return act


def block_of(ref, k):
    return ref.at[:, :, lanes_of(k)]


def flat_fields(g, out, near, k):
    porosity, solid, labels = near
    lanes = lanes_of(k)
    label = labels[:, lanes]
    damp = 1.0 / (1.0 + porosity[:, lanes])
    push = jnp.where(label == 1, PUSH, jnp.where(label == 2, -PUSH, 0.0))
    base = pl.multiple_of(k * g.panel, 8)
    for i, value in ((27, damp), (28, push), (29, solid[:, lanes].astype(F32))):
        out[pl.ds(base + g.field(i), g.rows), :] = value


def staged_tile(g, collide, stage):
    def act(k, pieces):
        collide(k, pieces, [read_rows(stage.at[k - 1, i], 0, pieces) for i in range(27)])

    return act


def side_tiles(g, act):
    for pieces in (g.outer,) + g.inner:
        side_panels(g, functools.partial(act, pieces=pieces), 2)


def side_first_kernel(g, pops, *refs):
    flat, (out, state, stage), near, faces, (sems, flat_sems) = (
        refs[:3],
        refs[3:6],
        refs[6:9],
        refs[9:11],
        refs[11:],
    )

    def copy(k):
        return pltpu.make_async_copy(block_of(pops, k), stage.at[k - 1], sems.at[k - 1])

    flat_copies = [
        pltpu.make_async_copy(source, target, flat_sems.at[n])
        for n, (source, target) in enumerate(zip(flat, near))
    ]
    for each in flat_copies:
        each.start()
    for k in (1, g.cols, *range(2, g.cols)):
        copy(k).start()
    for each in flat_copies:
        each.wait()
    for k in (1, g.cols):
        flat_fields(g, out, near, k)
    copy(1).wait()
    copy(g.cols).wait()
    side_tiles(g, staged_tile(g, collide_first(g, state, out), stage))
    by_parity("gy", *faces, functools.partial(pack_y, g, out, 1, 30))
    for k in range(2, g.cols):
        copy(k).wait()


def rim_first_kernel(g, _out, _state, stage, *refs):
    near, (out, state), faces = refs[:3], refs[3:5], refs[5:]
    every(2, g.cols - 1, functools.partial(flat_fields, g, out, near))
    act = staged_tile(g, collide_first(g, state, out), stage)
    every(2, g.cols - 1, functools.partial(act, pieces=g.outer))
    by_parity("gx", *faces, functools.partial(pack_x, g, out, 1, 30))


def inner_first_kernel(g, _, _state, stage, post, state0, out, state1):
    masks = lane_masks(16)
    interior_tiles(g, staged_tile(g, collide_first(g, state0, post), stage))
    interior_tiles(g, step_tile(g, post, out, 1, 30, masks, collide_second(g, state1)))


def relay_kernel(g, sign, fields, _, y_second, y_first, buf, first, second):
    high = lane_masks(g.rows)[0]
    by_parity("gy", y_second, y_first, functools.partial(unpack_y, g, buf, sign, fields, high))
    by_parity("gx", first, second, functools.partial(pack_corners, g, buf, sign, fields))


def middle_second_kernel(g, adjoint, post, out, state1, stage, field, x_second, x_first):
    masks = lane_masks(16)
    by_parity("gx", x_second, x_first, functools.partial(unpack_x, g, post, 1, 30))
    middle_tiles(g, step_tile(g, post, out, 1, 30, masks, collide_second(g, state1)))
    core_tiles(g, seed_tile(g, out, adjoint, stage, field, masks))


def side_seed_kernel(g, _post, _out, _state, _stage, _field, second, first, adjoint, *refs):
    post, out, state1, stage, field, *faces = refs
    masks = lane_masks(16)
    by_parity("gx", second, first, functools.partial(unpack_corners, g, post, 1, 30))
    corner_tiles(g, post, out, 1, 30, masks, collide_second(g, state1))
    side_tiles(g, seed_tile(g, out, adjoint, stage, field, masks))
    by_parity("gy", *faces, functools.partial(pack_y, g, field, -1, 27))


def rim_seed_kernel(g, _stage, _field, out, adjoint, stage, field, *faces):
    seed = seed_tile(g, out, adjoint, stage, field, lane_masks(16))
    every(2, g.cols - 1, functools.partial(seed, pieces=g.outer))
    by_parity("gx", *faces, functools.partial(pack_x, g, field, -1, 27))


def inner_seed_kernel(
    g, post, _stage, _field, state1, adjoint, stage, field, out, total, final, sems
):
    masks = lane_masks(16)

    def copy(k):
        return pltpu.make_async_copy(stage.at[k - 1], block_of(final, k), sems.at[k - 1])

    for k in (1, g.cols, *range(3, g.cols - 1)):
        copy(k).start()
    seed = seed_tile(g, post, adjoint, stage, field, masks)

    near_core_tiles(g, seed)
    for k in (2, g.cols - 1):
        copy(k).start()
    interior_tiles(g, step_tile(g, field, out, -1, 27, masks, adjoint_second(g, state1, total)))
    every(1, g.cols, lambda k: copy(k).wait())


def total_tile(g, out, before, state0, total, parts, masks):
    def act(k, pieces):
        p = pull_block(g, out, -1, k, pieces, masks)
        spot = spot_of(g, k)
        *flow, wall = load_fields(state0, g.local, spot, pieces, 7)
        *spread, porous = adjoint_scalars(p, *flow, wall > 0.5)
        here = load_fields(before, g.extended, spot, pieces, 1)[0] + porous
        save_fields(total, g.local, spot, pieces, [here])
        save_fields(parts, g.local, spot, pieces, spread + [wall])

    return act


def middle_adjoint_kernel(g, field, out, before, total, parts, state1, state0, x_second, x_first):
    masks = lane_masks(16)
    by_parity("gx", x_second, x_first, functools.partial(unpack_x, g, field, -1, 27))
    middle_tiles(g, step_tile(g, field, out, -1, 27, masks, adjoint_second(g, state1, before)))
    core_tiles(g, total_tile(g, out, before, state0, total, parts, masks))


def total_kernel(g, *refs):
    state1, state0, second, first, field, out, before, total, parts, peak = refs[5:]
    masks = lane_masks(16)
    by_parity("gx", second, first, functools.partial(unpack_corners, g, field, -1, 27))
    corner_tiles(g, field, out, -1, 27, masks, adjoint_second(g, state1, before))
    act = total_tile(g, out, before, state0, total, parts, masks)
    near_core_tiles(g, act)
    rim_tiles(g, act)
    size = 8 * (g.local // 64)
    largest = jnp.zeros((8, LANES), F32)
    for start in range(0, g.local, size):
        value = jnp.abs(total[start : start + size, :]).reshape(-1, 8, LANES)
        largest = jnp.maximum(largest, jnp.max(value, 0))
    peak[...] = largest


def adjoint_kernel(g, first, last, buf, parts, result, stage, sems):
    masks = lane_masks(16)

    def copy(k):
        return pltpu.make_async_copy(stage.at[k - first], block_of(result, k), sems.at[k - first])

    def column(k):
        for pieces in (g.outer,) + g.inner:
            p = pull_block(g, buf, -1, k, pieces, masks)
            *spread, wall = load_fields(parts, g.local, spot_of(g, k), pieces, 5)
            for i, value in enumerate(adjoint_spread(p, *spread, wall > 0.5)):
                write_rows(stage.at[k - first, i], 0, pieces, value)
        copy(k).start()

    every(first, last, column)
    every(first, last, lambda k: copy(k).wait())


def scale_kernel(g, total, peak, out):
    largest = jnp.max(peak[...])
    factor = 1.0 / (jnp.full((g.rows, LANES), largest, F32) + EPS)
    for c in range(g.cols):
        value = total[c * g.rows : (c + 1) * g.rows, :] * factor
        out[:, c * LANES : (c + 1) * LANES] = value


def swap_pairs(count, start):
    pairs = []
    for i in range(start, count, 2):
        j = (i + 1) % count
        pairs += [(i, j), (j, i)]
    return pairs


def swap(axis, count, first, second):
    return (
        lax.ppermute(first, axis, swap_pairs(count, 0)),
        lax.ppermute(second, axis, swap_pairs(count, 1)),
    )


def largest_of_all(peak, sizes, beside):
    nx, ny = sizes
    peak = jnp.maximum(peak, lax.ppermute(peak, "gy", [(i, i ^ 1) for i in range(ny)]))
    groups = 0
    for axis, count, first, widths in (("gy", ny, 2, (4, 4)), ("gx", nx, 1, (4, 2))):
        step = first
        for width in widths:
            width = min(width, count // step)
            parts = []
            for n in range(1, width):
                if axis == "gy":
                    pairs = [(i, i ^ (n * step) ^ 1) for i in range(ny)]
                    parts.append(lax.ppermute(peak, "gy", pairs))
                else:
                    pairs = [
                        (i * ny + y, (i ^ (n * step)) * ny + (y ^ 1))
                        for i in range(nx)
                        for y in range(ny)
                    ]
                    parts.append(lax.ppermute(peak, ("gx", "gy"), pairs))
            groups += 1
            if groups == 1:
                peak = beside(peak)
            peak = functools.reduce(jnp.maximum, parts, peak)
            step *= width
    return peak


def on_device(sizes, populations, adjoint_in, porosity, solid, labels):
    rows, width = porosity.shape
    g = Grid(rows, width)
    in_vmem = pl.BlockSpec(memory_space=pltpu.VMEM)
    in_hbm = pl.BlockSpec(memory_space=pltpu.HBM)
    nx, ny = sizes

    def vmem(*shape):
        return pltpu.VMEM(shape, F32)

    def fields(count, size):
        return vmem(count * size, LANES)

    def padded(count):
        return vmem(*g.padded(count))

    def x_faces(count):
        return [vmem(count * g.cols, LANES)] * 2

    def y_faces(count, sign):
        return [vmem(y_slots(count, sign) * rows, LANES)] * 2

    def corners(count):
        return [vmem(-(-count // 8) * 8, LANES)] * 2

    whole = pltpu.HBM(populations.shape, F32)
    stage = vmem(g.cols, 27, rows, LANES)
    sems = pltpu.SemaphoreType.DMA((g.cols,))

    def call(name, kernel, operands, out_shape, scratch=(), kept=0, load=0, result=None):
        out_shape = [pltpu.VMEM(x.shape, x.dtype) for x in operands[:kept]] + out_shape
        aliases = {n: n for n in range(kept)}
        space = pltpu.HBM if name == "side_first" else pltpu.VMEM
        pinned = [pltpu.with_memory_space_constraint(x, space) for x in operands]
        in_specs = [pl.BlockSpec(memory_space=space)] * len(operands)
        if result is not None:
            aliases[len(operands)] = len(out_shape) - 1
            pinned.append(pltpu.with_memory_space_constraint(result, pltpu.HBM))
            in_specs.append(in_hbm)
        return pl.pallas_call(
            functools.partial(kernel, g),
            in_specs=in_specs,
            out_shape=out_shape,
            out_specs=[in_hbm if x is whole else in_vmem for x in out_shape],
            scratch_shapes=list(scratch),
            input_output_aliases=aliases,
            compiler_params=pltpu.CompilerParams(vmem_limit_bytes=VMEM_LIMIT),
            cost_estimate=pl.CostEstimate(flops=0, bytes_accessed=load, transcendentals=0)
            if load
            else None,
            name=name,
        )(*pinned)

    def swap_faces(axis, count, parcels):
        return swap(axis, count, *parcels)[::-1]

    def relay(buf, parcels, sign, count):
        def kernel(grid, *refs):
            relay_kernel(grid, sign, count, *refs)

        buf, *parcels = call("relay", kernel, [buf, *parcels], corners(count), kept=1)
        return buf, swap("gx", nx, *parcels)[::-1]

    flat_space = [vmem(*porosity.shape)] + [pltpu.VMEM(porosity.shape, jnp.int32)] * 2
    post, state0, staged, *rest = call(
        "side_first",
        side_first_kernel,
        [populations, porosity, solid, labels],
        [padded(30), fields(7, g.local), stage] + flat_space + y_faces(30, 1),
        [sems, pltpu.SemaphoreType.DMA((3,))],
    )
    along_y = swap_faces("gy", ny, rest[3:])
    post, state0, *parcels = call(
        "rim_first",
        rim_first_kernel,
        [post, state0, staged, *rest[:3]],
        x_faces(30),
        kept=2,
        load=FLIGHT,
    )
    along_x = swap_faces("gx", nx, parcels)
    post, state0, second, state1 = call(
        "inner_first",
        inner_first_kernel,
        [post, state0, staged],
        [padded(27), fields(7, g.extended)],
        kept=2,
        load=FLIGHT,
    )
    post, parcels = relay(post, along_y, 1, 30)
    post, second, state1, staged, field = call(
        "middle_second",
        lambda grid, _post, _out, _state, b, a, source, *refs: middle_second_kernel(
            grid, source, *refs, b, a
        ),
        [post, second, state1, *along_x, adjoint_in],
        [stage, padded(27)],
        kept=3,
        load=FLIGHT,
    )
    _, second, state1, staged, field, *parcels = call(
        "side_seed",
        side_seed_kernel,
        [post, second, state1, staged, field, *parcels, adjoint_in],
        y_faces(27, -1),
        kept=5,
    )
    along_y = swap_faces("gy", ny, parcels)
    staged, field, *parcels = call(
        "rim_seed",
        rim_seed_kernel,
        [staged, field, second, adjoint_in],
        x_faces(27),
        kept=2,
        load=FLIGHT,
    )
    along_x = swap_faces("gx", nx, parcels)
    _, field, pulled, before, final = call(
        "inner_seed",
        lambda grid, kept, into, buf, *refs: inner_seed_kernel(grid, buf, kept, into, *refs),
        [staged, field, second, state1, adjoint_in],
        [padded(27), fields(1, g.extended), whole],
        [sems],
        kept=2,
        load=FLIGHT,
    )
    field, parcels = relay(field, along_y, -1, 27)
    field, pulled, before, total, parts = call(
        "middle_adjoint",
        lambda grid, _field, _out, _before, near, far, b, a, *refs: middle_adjoint_kernel(
            grid, *refs, near, far, b, a
        ),
        [field, pulled, before, state1, state0, *along_x],
        [fields(1, g.local), fields(5, g.local)],
        kept=3,
        load=FLIGHT,
    )
    _, pulled, _, total, parts, peak = call(
        "total",
        total_kernel,
        [field, pulled, before, total, parts, state1, state0, *parcels],
        [vmem(8, LANES)],
        kept=5,
    )
    half = g.cols // 2
    scratch = [vmem(half, 27, rows, LANES), pltpu.SemaphoreType.DMA((half,))]
    halves = []

    def first_half(peak):
        def kernel(grid, buf, fields, near, echo, *refs):
            echo[...] = near[...]
            adjoint_kernel(grid, 1, half, buf, fields, *refs)

        echo, result = call(
            "adjoint_low",
            kernel,
            [pulled, parts, peak],
            [vmem(8, LANES), whole],
            scratch,
            load=FLIGHT // 2,
        )
        halves.append(result)
        return echo

    largest = largest_of_all(peak, sizes, first_half)
    (adjoint_out,) = call(
        "adjoint_high",
        lambda grid, buf, fields, _, *refs: adjoint_kernel(
            grid, 1 + half, g.cols, buf, fields, *refs
        ),
        [pulled, parts],
        [whole],
        scratch,
        load=FLIGHT // 2,
        result=halves[0],
    )
    (sensitivity,) = call(
        "normalize",
        scale_kernel,
        [total, largest],
        [jax.ShapeDtypeStruct(porosity.shape, F32)],
    )
    return final, adjoint_out, sensitivity


def solution(mesh):
    sizes = (mesh.shape["gx"], mesh.shape["gy"])
    whole, flat = P(None, "gx", "gy"), P("gx", "gy")
    return jax.shard_map(
        functools.partial(on_device, sizes),
        mesh=mesh,
        in_specs=(whole, whole, flat, flat, flat),
        out_specs=(whole, whole, flat),
        check_vma=False,
    )
```

```python
import functools

import jax
import jax.numpy as jnp
from jax import lax
from jax.experimental import pallas as pl
from jax.experimental.pallas import tpu as pltpu
from jax.sharding import PartitionSpec as P

NZ = 64
RELAX = 0.8
PUSH = 0.2
EPS = 1e-06
LANES = 128
VELOCITY = [(a, b, c) for a in (-1, 0, 1) for b in (-1, 0, 1) for c in (-1, 0, 1)]
INDEX = {v: i for i, v in enumerate(VELOCITY)}
WEIGHT = [
    [8.0 / 27, 2.0 / 27, 1.0 / 54, 1.0 / 216][abs(v[0]) + abs(v[1]) + abs(v[2])]
    for v in VELOCITY
]
NORM = [abs(v[0]) + abs(v[1]) + abs(v[2]) for v in VELOCITY]
F32 = jnp.float32
VMEM_LIMIT = 6 * 1024 * 1024
FLIGHT = 12 * 1024 * 1024


class Grid:
    def __init__(self, rows, width):
        self.rows = rows
        self.cols = width // LANES
        self.panel = rows + 16
        self.halo = self.cols + 1
        self.local = self.cols * rows
        self.extended = self.halo * rows + 24
        self.outer = ((0, 8), (rows - 8, 8))
        self.inner = tuple(((r, 16),) for r in range(8, rows - 8, 16))

    def at(self, i, k, r):
        return self.field(i) + k * self.panel + r

    def field(self, i):
        return i * (self.cols + 2) * self.panel + 8

    def padded(self, fields):
        return (fields * (self.cols + 2) * self.panel + 8, LANES)


def velocity(i, sign):
    return tuple(sign * n for n in VELOCITY[i]) if i < 27 else (0, 0, 0)


def moving(fields, sign, axis, side):
    return [i for i in range(fields) if velocity(i, sign)[axis] == side]


def lane_masks(height):
    lane = lax.broadcasted_iota(jnp.int32, (height, LANES), 1)
    return lane >= NZ, lane % NZ == 0, lane % NZ == NZ - 1


def halves(load, d, masks):
    high = masks[0]
    if d[1] == 1:
        return jnp.where(high, load(-1), load(0))
    if d[1] == -1:
        return jnp.where(high, load(0), load(1))
    return load(0)


def turns(dz):
    return (1, NZ + 1) if dz == 1 else (LANES - 1, NZ - 1)


def shift_pair(flat, steep, dz, masks):
    edge, source = (masks[1], masks[2]) if dz == 1 else (masks[2], masks[1])
    near, far = turns(dz)
    one = pltpu.roll(jnp.where(source, steep, flat), near, 1)
    two = pltpu.roll(jnp.where(source, flat, steep), far, 1)
    return jnp.where(edge, two, one), jnp.where(edge, one, two)


def shift_steep(tile, dz, masks):
    if dz == 0:
        return pltpu.roll(tile, NZ, 1)
    near, far = turns(dz)
    edge = masks[1] if dz == 1 else masks[2]
    return jnp.where(edge, pltpu.roll(tile, near, 1), pltpu.roll(tile, far, 1))


def shift_lanes(tiles, sign, masks):
    out = list(tiles)
    place = {velocity(i, sign): i for i in range(27)}
    for dx in (-1, 0, 1):
        for dy in (-1, 1):
            i = place[dx, dy, 0]
            out[i] = shift_steep(tiles[i], 0, masks)
        for dz in (-1, 1):
            i, j, k = (place[dx, dy, dz] for dy in (0, 1, -1))
            out[i], out[j] = shift_pair(tiles[i], tiles[j], dz, masks)
            out[k] = shift_steep(tiles[k], dz, masks)
    return out


def stacked(parts):
    return parts[0] if len(parts) == 1 else jnp.concatenate(parts, 0)


def read_rows(ref, base, pieces):
    return stacked([ref[pl.ds(base + r, n), :] for r, n in pieces])


def write_rows(ref, base, pieces, value):
    done = 0
    for r, n in pieces:
        ref[pl.ds(base + r, n), :] = value[done : done + n]
        done += n


def pull_block(g, buf, sign, k, pieces, masks, fields=27):
    base = pl.multiple_of(k * g.panel, 8)
    after = pl.multiple_of(jnp.where(k == g.halo, g.panel, base + g.panel), 8)
    out = []
    for i in range(fields):
        d = velocity(i, sign)

        def load(n, i=i, d=d):
            start = {-1: base - g.panel, 0: base, 1: after}[n]
            return read_rows(buf, start + (g.field(i) - d[0]), pieces)

        out.append(halves(load, d, masks))
    return shift_lanes(out, sign, masks)


def pull_edge(g, buf, sign, side, masks, fields=27):
    out = []
    for i in range(fields):
        d = velocity(i, sign)
        if side == 1:
            row = g.rows - d[0]
        else:
            row = {1: g.rows, 0: g.rows + 1, -1: 0}[d[0]]

        def load(n, i=i, row=row):
            return buf[pl.ds(g.at(i, 1 + n, row), g.cols, stride=g.panel), :]

        out.append(halves(load, d, masks))
    return shift_lanes(out, sign, masks)


def moments(f):
    flat = {}
    along_z = None
    for a in (-1, 0, 1):
        for b in (-1, 0, 1):
            lo, mid, hi = (f[INDEX[(a, b, c)]] for c in (-1, 0, 1))
            flat[a, b] = lo + mid + hi
            diff = hi - lo
            along_z = diff if along_z is None else along_z + diff
    line = {}
    along_y = None
    for a in (-1, 0, 1):
        line[a] = flat[a, -1] + flat[a, 0] + flat[a, 1]
        diff = flat[a, 1] - flat[a, -1]
        along_y = diff if along_y is None else along_y + diff
    return line[-1] + line[0] + line[1], line[1] - line[-1], along_y, along_z


def combos(x, y, z):
    plane = {}
    for a in (-1, 0, 1):
        for b in (-1, 0, 1):
            if (a, b) > (0, 0):
                continue
            if a == 0:
                plane[a, b] = -y if b else None
            else:
                plane[a, b] = -x if b == 0 else (-x - y if b < 0 else y - x)
    out = []
    for a, b, c in VELOCITY[:13]:
        base = plane[a, b]
        if base is None:
            out.append(-z)
        else:
            out.append(base if c == 0 else (base - z if c < 0 else base + z))
    return out


def relax(f, rho, wx, wy, wz, damp, push, solid):
    ux, uy, uz = (wx + push) * damp, wy * damp, wz * damp
    base = 1.0 - 1.5 * (ux * ux + uy * uy + uz * uz)
    keep = 1.0 - 1.0 / RELAX
    gain = rho * (1.0 / RELAX)
    level = [gain * w for w in (8.0 / 27, 2.0 / 27, 1.0 / 54, 1.0 / 216)]
    along = combos(3.0 * ux, 3.0 * uy, 3.0 * uz)
    out = [None] * 27
    for i in range(13):
        j = 26 - i
        even = base + 0.5 * (along[i] * along[i])
        lift = level[NORM[i]]
        out[i] = jnp.where(solid, f[j], keep * f[i] + lift * (even + along[i]))
        out[j] = jnp.where(solid, f[i], keep * f[j] + lift * (even - along[i]))
    out[13] = jnp.where(solid, f[13], keep * f[13] + level[0] * base)
    return out


def pulled_moments(p):
    first = {}
    for a in (-1, 0, 1):
        for b in (-1, 0, 1):
            lo, mid, hi = (p[INDEX[(a, b, c)]] for c in (-1, 0, 1))
            both = lo + hi
            first[a, b] = (4.0 * mid + both, hi - lo, both)
    second = {}
    for a in (-1, 0, 1):
        lo, mid, hi = (first[a, b] for b in (-1, 0, 1))
        b0 = lo[0] + hi[0]
        b1 = lo[1] + hi[1]
        second[a] = dict(
            one=4.0 * mid[0] + b0,
            y=hi[0] - lo[0],
            yy=b0,
            z=4.0 * mid[1] + b1,
            yz=hi[1] - lo[1],
            zz=4.0 * mid[2] + lo[2] + hi[2],
        )
    lo, mid, hi = (second[a] for a in (-1, 0, 1))

    def full(key):
        return 4.0 * mid[key] + lo[key] + hi[key]

    xx = lo["one"] + hi["one"]
    return dict(
        one=4.0 * mid["one"] + xx,
        x=hi["one"] - lo["one"],
        xx=xx,
        y=full("y"),
        xy=hi["y"] - lo["y"],
        yy=full("yy"),
        z=full("z"),
        xz=hi["z"] - lo["z"],
        yz=full("yz"),
        zz=full("zz"),
    )


def adjoint_scalars(p, rho, wx, wy, wz, damp, push, solid):
    ux, uy, uz = (wx + push) * damp, wy * damp, wz * damp
    s = pulled_moments(p)
    scale = 1.0 / (216.0 * RELAX)
    one = s["one"] * scale
    b = [s[k] * (3.0 * scale) for k in ("x", "y", "z")]
    d = {k: s[k] * (9.0 * scale) for k in ("xx", "xy", "yy", "xz", "yz", "zz")}
    qx = d["xx"] * ux + d["xy"] * uy + d["xz"] * uz
    qy = d["xy"] * ux + d["yy"] * uy + d["yz"] * uz
    qz = d["xz"] * ux + d["yz"] * uy + d["zz"] * uz
    linear = b[0] * ux + b[1] * uy + b[2] * uz
    square = ux * ux + uy * uy + uz * uz
    even = one + linear + 0.5 * (qx * ux + qy * uy + qz * uz) - 1.5 * one * square
    three = 3.0 * one
    gx = (b[0] + qx - three * ux) * damp
    gy = (b[1] + qy - three * uy) * damp
    gz = (b[2] + qz - three * uz) * damp
    even = even - (gx * wx + gy * wy + gz * wz)
    porous = jnp.where(solid, 0.0, -rho * (gx * ux + gy * uy + gz * uz))
    return even, gx, gy, gz, porous


def adjoint_spread(p, even, gx, gy, gz, solid):
    keep = 1.0 - 1.0 / RELAX
    along = combos(gx, gy, gz)
    out = [None] * 27
    for i in range(13):
        j = 26 - i
        out[i] = jnp.where(solid, p[j], keep * p[i] + (even + along[i]))
        out[j] = jnp.where(solid, p[i], keep * p[j] + (even - along[i]))
    out[13] = jnp.where(solid, p[13], keep * p[13] + even)
    return out


def x_lines(g, sign, fields, side):
    lines = []
    for i in moving(fields, sign, 0, side):
        if side == 1:
            lines.append((i, g.rows - 1, (-1, g.rows + 1)))
            lines.append((i, g.rows - 2, (g.rows,)))
        else:
            lines += [(i, 0, (g.rows,)), (i, 1, (g.rows + 1,))]
    edge, target = (g.rows - 1, g.rows + 1) if side == 1 else (0, g.rows)
    return lines + [(i, edge, (target,)) for i in moving(fields, sign, 0, 0)]


def pack_x(g, buf, sign, fields, up, down):
    for side, ref in ((1, up), (-1, down)):
        for n, (i, r, _) in enumerate(x_lines(g, sign, fields, side)):
            ref[n * g.cols : (n + 1) * g.cols, :] = buf[
                pl.ds(g.at(i, 1, r), g.cols, stride=g.panel), :
            ]


def unpack_x(g, buf, sign, fields, up, down):
    for side, ref in ((1, up), (-1, down)):
        for n, (i, _, targets) in enumerate(x_lines(g, sign, fields, side)):
            value = ref[n * g.cols : (n + 1) * g.cols, :]
            for r in targets:
                buf[pl.ds(g.at(i, 1, r), g.cols, stride=g.panel), :] = value
    for i in moving(fields, sign, 0, -1):
        buf[pl.ds(g.at(i, 1, g.rows + 2), g.cols, stride=g.panel), :] = buf[
            pl.ds(g.at(i, 1, 0), g.cols, stride=g.panel), :
        ]


def halo_panels(g, i, sign):
    return (0, g.halo) if velocity(i, sign)[1] == 1 else (g.halo,)


def pack_corners(g, buf, sign, fields, up, down):
    for side, ref in ((1, up), (-1, down)):
        for n, (i, r, _) in enumerate(x_lines(g, sign, fields, side)):
            ref[n : n + 1, :] = buf[pl.ds(g.at(i, g.halo, r), 1), :]


def unpack_corners(g, buf, sign, fields, up, down):
    for side, ref in ((1, up), (-1, down)):
        for n, (i, _, targets) in enumerate(x_lines(g, sign, fields, side)):
            value = ref[n : n + 1, :]
            for r in targets:
                for k in halo_panels(g, i, sign):
                    buf[pl.ds(g.at(i, k, r), 1), :] = value
    for i in moving(fields, sign, 0, -1):
        for k in halo_panels(g, i, sign):
            buf[pl.ds(g.at(i, k, g.rows + 2), 1), :] = buf[pl.ds(g.at(i, k, 0), 1), :]


def still_pairs(fields, sign):
    still = moving(fields, sign, 1, 0)
    half = (len(still) + 1) // 2
    return [(still[n], still[n + half] if n + half < len(still) else None) for n in range(half)]


def y_slots(fields, sign):
    return 9 + len(still_pairs(fields, sign))


def pack_y(g, buf, sign, fields, up, down):
    high = lane_masks(g.rows)[0]
    for side, ref in ((1, up), (-1, down)):
        k = g.cols if side == 1 else 1
        for n, i in enumerate(moving(fields, sign, 1, side)):
            ref[n * g.rows : (n + 1) * g.rows, :] = buf[pl.ds(g.at(i, k, 0), g.rows), :]
        for n, (i, j) in enumerate(still_pairs(fields, sign)):
            value = buf[pl.ds(g.at(i, k, 0), g.rows), :]
            if j is not None:
                other = pltpu.roll(buf[pl.ds(g.at(j, k, 0), g.rows), :], NZ, 1)
                pair = (value, other) if side == 1 else (other, value)
                value = jnp.where(high, *pair)
            ref[(9 + n) * g.rows : (10 + n) * g.rows, :] = value


def unpack_y(g, buf, sign, fields, high, up, down):
    for side, ref in ((1, up), (-1, down)):
        for n, i in enumerate(moving(fields, sign, 1, side)):
            value = ref[n * g.rows : (n + 1) * g.rows, :]
            for k in halo_panels(g, i, sign):
                buf[pl.ds(g.at(i, k, 0), g.rows), :] = value
    for n, (i, j) in enumerate(still_pairs(fields, sign)):
        spot = slice((9 + n) * g.rows, (10 + n) * g.rows)
        before, after = up[spot, :], down[spot, :]
        buf[pl.ds(g.at(i, g.halo, 0), g.rows), :] = jnp.where(high, before, after)
        if j is not None:
            value = pltpu.roll(jnp.where(high, after, before), NZ, 1)
            buf[pl.ds(g.at(j, g.halo, 0), g.rows), :] = value


def by_parity(axis, first, second, act):
    even = lax.rem(lax.axis_index(axis), 2) == 0

    @pl.when(even)
    def _():
        act(first, second)

    @pl.when(jnp.logical_not(even))
    def _():
        act(second, first)


def load_fields(ref, rows, base, pieces, count):
    return [read_rows(ref, base + n * rows, pieces) for n in range(count)]


def save_fields(ref, rows, base, pieces, values):
    for n, value in enumerate(values):
        write_rows(ref, base + n * rows, pieces, value)


def save_populations(g, out, k, pieces, values):
    base = pl.multiple_of(k * g.panel, 8)
    for i, value in enumerate(values):
        write_rows(out, base + g.field(i), pieces, value)


def spot_of(g, k):
    return pl.multiple_of((k - 1) * g.rows, 8)


def lanes_of(k):
    return pl.ds(pl.multiple_of((k - 1) * LANES, LANES), LANES)


def every(first, last, act):
    def step(k, carry):
        act(k)
        return carry

    count = last + 1 - first
    unroll = max(n for n in (1, 2, 3, 4, 6, 8) if count % n == 0)
    lax.fori_loop(first, last + 1, step, 0, unroll=unroll)


def side_panels(g, act, count):
    def step(n, carry):
        act(jnp.where(n == 0, 1, g.cols - 1 + n))
        return carry

    lax.fori_loop(0, count, step, 0, unroll=count)


def interior_tiles(g, act):
    for pieces in g.inner:
        every(2, g.cols - 1, functools.partial(act, pieces=pieces))


def middle_tiles(g, act):
    for pieces in g.inner:
        side_panels(g, functools.partial(act, pieces=pieces), 3)
    every(2, g.cols - 1, functools.partial(act, pieces=g.outer))


def core_tiles(g, act):
    for pieces in g.inner:
        every(3, g.cols - 2, functools.partial(act, pieces=pieces))


def near_core_tiles(g, act):
    def step(n, carry):
        for pieces in g.inner:
            act(jnp.where(n == 0, 2, g.cols - 1), pieces=pieces)
        return carry

    lax.fori_loop(0, 2, step, 0, unroll=2)


def rim_tiles(g, act):
    every(1, g.cols, functools.partial(act, pieces=g.outer))
    for pieces in g.inner:
        side_panels(g, functools.partial(act, pieces=pieces), 2)


def step_tile(g, buf, out, sign, fields, masks, compute):
    def act(k, pieces):
        values = compute(
            pull_block(g, buf, sign, k, pieces, masks, fields), spot_of(g, k), pieces
        )
        save_populations(g, out, k, pieces, values)

    return act


def corner_tiles(g, buf, out, sign, fields, masks, compute):
    small = tuple(mask[:8] for mask in masks)
    act = step_tile(g, buf, out, sign, fields, masks, compute)
    side_panels(g, functools.partial(act, pieces=g.outer), 3)
    spot = g.halo * g.rows
    pieces = ((g.rows, 8),)
    values = compute(pull_block(g, buf, sign, g.halo, pieces, small, fields), spot, ((0, 8),))
    for i in range(27):
        dx = velocity(i, sign)[0]
        if dx == -1:
            out[pl.ds(g.at(i, g.halo, g.rows), 1), :] = values[i][0:1]
        elif dx == 1:
            out[pl.ds(g.at(i, g.halo, -1), 1), :] = values[i][1:2]
    edges = [pull_edge(g, buf, sign, side, small, fields) for side in (1, -1)]
    both = [stacked(pair) for pair in zip(*edges)]
    values = compute(both, spot, ((8, 16),))
    for i in moving(27, sign, 0, -1):
        out[pl.ds(g.at(i, 1, g.rows), g.cols, stride=g.panel), :] = values[i][:8]
    for i in moving(27, sign, 0, 1):
        out[pl.ds(g.at(i, 1, -1), g.cols, stride=g.panel), :] = values[i][8:]
    for i in moving(27, sign, 1, 1):
        out[pl.ds(g.at(i, 0, 0), g.rows), :] = out[pl.ds(g.at(i, g.halo, 0), g.rows), :]
        for r in (-1, g.rows):
            out[pl.ds(g.at(i, 0, r), 1), :] = out[pl.ds(g.at(i, g.halo, r), 1), :]


def flow_of(f):
    rho, mx, my, mz = moments(f)
    inverse = 1.0 / rho
    return inverse, rho, mx * inverse, my * inverse, mz * inverse


def collide_first(g, state, out):
    def act(k, pieces, f):
        base = pl.multiple_of(k * g.panel, 8)
        damp, push, wall = (read_rows(out, base + g.field(i), pieces) for i in (27, 28, 29))
        flow = flow_of(f)[1:] + (damp, push)
        save_fields(state, g.local, spot_of(g, k), pieces, flow + (wall,))
        save_populations(g, out, k, pieces, relax(f, *flow, wall > 0.5))

    return act


def collide_second(g, state):
    def compute(values, spot, pieces):
        f, (damp, push, wall) = values[:27], values[27:]
        flow = flow_of(f)[1:] + (damp, push)
        save_fields(state, g.extended, spot, pieces, flow + (wall,))
        return relax(f, *flow, wall > 0.5)

    return compute


def adjoint_second(g, state, total):
    def compute(p, spot, pieces):
        *flow, wall = load_fields(state, g.extended, spot, pieces, 7)
        *spread, porous = adjoint_scalars(p, *flow, wall > 0.5)
        save_fields(total, g.extended, spot, pieces, [porous])
        return adjoint_spread(p, *spread, wall > 0.5)

    return compute


def seed_tile(g, buf, adjoint, stage, out, masks):
    def act(k, pieces):
        f = pull_block(g, buf, 1, k, pieces, masks)
        for i in range(27):
            write_rows(stage.at[k - 1, i], 0, pieces, f[i])
        inverse, _, wx, wy, wz = flow_of(f)
        even = -(wx * wx + wy * wy + wz * wz) * inverse
        along = combos(wx * inverse, wy * inverse, wz * inverse)
        lanes = lanes_of(k)
        seeded = [
            stacked([adjoint[i, pl.ds(r, n), lanes] for r, n in pieces]) + even for i in range(27)
        ]
        for i in range(13):
            seeded[i] = seeded[i] + along[i]
            seeded[26 - i] = seeded[26 - i] - along[i]
        save_populations(g, out, k, pieces, seeded)

    return act


def block_of(ref, k):
    return ref.at[:, :, lanes_of(k)]


def flat_fields(g, out, near, k):
    porosity, solid, labels = near
    lanes = lanes_of(k)
    label = labels[:, lanes]
    damp = 1.0 / (1.0 + porosity[:, lanes])
    push = jnp.where(label == 1, PUSH, jnp.where(label == 2, -PUSH, 0.0))
    base = pl.multiple_of(k * g.panel, 8)
    for i, value in ((27, damp), (28, push), (29, solid[:, lanes].astype(F32))):
        out[pl.ds(base + g.field(i), g.rows), :] = value


def staged_tile(g, collide, stage):
    def act(k, pieces):
        collide(k, pieces, [read_rows(stage.at[k - 1, i], 0, pieces) for i in range(27)])

    return act


def side_tiles(g, act):
    for pieces in (g.outer,) + g.inner:
        side_panels(g, functools.partial(act, pieces=pieces), 2)


def side_first_kernel(g, pops, *refs):
    flat, (out, state, stage), near, faces, (sems, flat_sems) = (
        refs[:3],
        refs[3:6],
        refs[6:9],
        refs[9:11],
        refs[11:],
    )

    def copy(k):
        return pltpu.make_async_copy(block_of(pops, k), stage.at[k - 1], sems.at[k - 1])

    flat_copies = [
        pltpu.make_async_copy(source, target, flat_sems.at[n])
        for n, (source, target) in enumerate(zip(flat, near))
    ]
    for each in flat_copies:
        each.start()
    for k in (1, g.cols, *range(2, g.cols)):
        copy(k).start()
    for each in flat_copies:
        each.wait()
    for k in (1, g.cols):
        flat_fields(g, out, near, k)
    copy(1).wait()
    copy(g.cols).wait()
    side_tiles(g, staged_tile(g, collide_first(g, state, out), stage))
    by_parity("gy", *faces, functools.partial(pack_y, g, out, 1, 30))
    for k in range(2, g.cols):
        copy(k).wait()


def rim_first_kernel(g, _out, _state, stage, *refs):
    near, (out, state), faces = refs[:3], refs[3:5], refs[5:]
    every(2, g.cols - 1, functools.partial(flat_fields, g, out, near))
    act = staged_tile(g, collide_first(g, state, out), stage)
    every(2, g.cols - 1, functools.partial(act, pieces=g.outer))
    by_parity("gx", *faces, functools.partial(pack_x, g, out, 1, 30))


def inner_first_kernel(g, _, _state, stage, post, state0, out, state1):
    masks = lane_masks(16)
    interior_tiles(g, staged_tile(g, collide_first(g, state0, post), stage))
    interior_tiles(g, step_tile(g, post, out, 1, 30, masks, collide_second(g, state1)))


def relay_kernel(g, sign, fields, _, y_second, y_first, buf, first, second):
    high = lane_masks(g.rows)[0]
    by_parity("gy", y_second, y_first, functools.partial(unpack_y, g, buf, sign, fields, high))
    by_parity("gx", first, second, functools.partial(pack_corners, g, buf, sign, fields))


def middle_second_kernel(g, adjoint, post, out, state1, stage, field, x_second, x_first):
    masks = lane_masks(16)
    by_parity("gx", x_second, x_first, functools.partial(unpack_x, g, post, 1, 30))
    middle_tiles(g, step_tile(g, post, out, 1, 30, masks, collide_second(g, state1)))
    core_tiles(g, seed_tile(g, out, adjoint, stage, field, masks))


def side_seed_kernel(g, _post, _out, _state, _stage, _field, second, first, adjoint, *refs):
    post, out, state1, stage, field, *faces = refs
    masks = lane_masks(16)
    by_parity("gx", second, first, functools.partial(unpack_corners, g, post, 1, 30))
    corner_tiles(g, post, out, 1, 30, masks, collide_second(g, state1))
    side_tiles(g, seed_tile(g, out, adjoint, stage, field, masks))
    by_parity("gy", *faces, functools.partial(pack_y, g, field, -1, 27))


def rim_seed_kernel(g, _stage, _field, out, adjoint, stage, field, *faces):
    seed = seed_tile(g, out, adjoint, stage, field, lane_masks(16))
    every(2, g.cols - 1, functools.partial(seed, pieces=g.outer))
    by_parity("gx", *faces, functools.partial(pack_x, g, field, -1, 27))


def inner_seed_kernel(
    g, post, _stage, _field, state1, adjoint, stage, field, out, total, final, sems
):
    masks = lane_masks(16)

    def copy(k):
        return pltpu.make_async_copy(stage.at[k - 1], block_of(final, k), sems.at[k - 1])

    for k in (1, g.cols, *range(3, g.cols - 1)):
        copy(k).start()
    seed = seed_tile(g, post, adjoint, stage, field, masks)

    near_core_tiles(g, seed)
    for k in (2, g.cols - 1):
        copy(k).start()
    interior_tiles(g, step_tile(g, field, out, -1, 27, masks, adjoint_second(g, state1, total)))
    every(1, g.cols, lambda k: copy(k).wait())


def total_tile(g, out, before, state0, total, parts, masks):
    def act(k, pieces):
        p = pull_block(g, out, -1, k, pieces, masks)
        spot = spot_of(g, k)
        *flow, wall = load_fields(state0, g.local, spot, pieces, 7)
        *spread, porous = adjoint_scalars(p, *flow, wall > 0.5)
        here = load_fields(before, g.extended, spot, pieces, 1)[0] + porous
        save_fields(total, g.local, spot, pieces, [here])
        save_fields(parts, g.local, spot, pieces, spread + [wall])

    return act


def middle_adjoint_kernel(g, field, out, before, total, parts, state1, state0, x_second, x_first):
    masks = lane_masks(16)
    by_parity("gx", x_second, x_first, functools.partial(unpack_x, g, field, -1, 27))
    middle_tiles(g, step_tile(g, field, out, -1, 27, masks, adjoint_second(g, state1, before)))
    core_tiles(g, total_tile(g, out, before, state0, total, parts, masks))


def total_kernel(g, *refs):
    state1, state0, second, first, field, out, before, total, parts, peak = refs[5:]
    masks = lane_masks(16)
    by_parity("gx", second, first, functools.partial(unpack_corners, g, field, -1, 27))
    corner_tiles(g, field, out, -1, 27, masks, adjoint_second(g, state1, before))
    act = total_tile(g, out, before, state0, total, parts, masks)
    near_core_tiles(g, act)
    rim_tiles(g, act)
    size = 8 * (g.local // 64)
    largest = jnp.zeros((8, LANES), F32)
    for start in range(0, g.local, size):
        value = jnp.abs(total[start : start + size, :]).reshape(-1, 8, LANES)
        largest = jnp.maximum(largest, jnp.max(value, 0))
    peak[...] = largest


def adjoint_kernel(g, first, last, buf, parts, result, stage, sems):
    masks = lane_masks(16)

    def copy(k):
        return pltpu.make_async_copy(stage.at[k - first], block_of(result, k), sems.at[k - first])

    def column(k):
        for pieces in (g.outer,) + g.inner:
            p = pull_block(g, buf, -1, k, pieces, masks)
            *spread, wall = load_fields(parts, g.local, spot_of(g, k), pieces, 5)
            for i, value in enumerate(adjoint_spread(p, *spread, wall > 0.5)):
                write_rows(stage.at[k - first, i], 0, pieces, value)
        copy(k).start()

    every(first, last, column)
    every(first, last, lambda k: copy(k).wait())


def scale_kernel(g, total, peak, out):
    largest = jnp.max(peak[...])
    factor = 1.0 / (jnp.full((g.rows, LANES), largest, F32) + EPS)
    for c in range(g.cols):
        value = total[c * g.rows : (c + 1) * g.rows, :] * factor
        out[:, c * LANES : (c + 1) * LANES] = value


def swap_pairs(count, start):
    pairs = []
    for i in range(start, count, 2):
        j = (i + 1) % count
        pairs += [(i, j), (j, i)]
    return pairs


def swap(axis, count, first, second):
    return (
        lax.ppermute(first, axis, swap_pairs(count, 0)),
        lax.ppermute(second, axis, swap_pairs(count, 1)),
    )


def largest_of_all(peak, sizes, beside):
    nx, ny = sizes
    peak = jnp.maximum(peak, lax.ppermute(peak, "gy", [(i, i ^ 1) for i in range(ny)]))
    groups = 0
    for axis, count, first, widths in (("gy", ny, 2, (4, 4)), ("gx", nx, 1, (4, 2))):
        step = first
        for width in widths:
            width = min(width, count // step)
            parts = []
            for n in range(1, width):
                if axis == "gy":
                    pairs = [(i, i ^ (n * step) ^ 1) for i in range(ny)]
                    parts.append(lax.ppermute(peak, "gy", pairs))
                else:
                    pairs = [
                        (i * ny + y, (i ^ (n * step)) * ny + (y ^ 1))
                        for i in range(nx)
                        for y in range(ny)
                    ]
                    parts.append(lax.ppermute(peak, ("gx", "gy"), pairs))
            groups += 1
            if groups == 1:
                peak = beside(peak)
            peak = functools.reduce(jnp.maximum, parts, peak)
            step *= width
    return peak


def on_device(sizes, populations, adjoint_in, porosity, solid, labels):
    rows, width = porosity.shape
    g = Grid(rows, width)
    in_vmem = pl.BlockSpec(memory_space=pltpu.VMEM)
    in_hbm = pl.BlockSpec(memory_space=pltpu.HBM)
    nx, ny = sizes

    def vmem(*shape):
        return pltpu.VMEM(shape, F32)

    def fields(count, size):
        return vmem(count * size, LANES)

    def padded(count):
        return vmem(*g.padded(count))

    def x_faces(count):
        return [vmem(count * g.cols, LANES)] * 2

    def y_faces(count, sign):
        return [vmem(y_slots(count, sign) * rows, LANES)] * 2

    def corners(count):
        return [vmem(-(-count // 8) * 8, LANES)] * 2

    whole = pltpu.HBM(populations.shape, F32)
    stage = vmem(g.cols, 27, rows, LANES)
    sems = pltpu.SemaphoreType.DMA((g.cols,))

    def call(name, kernel, operands, out_shape, scratch=(), kept=0, load=0, result=None):
        out_shape = [pltpu.VMEM(x.shape, x.dtype) for x in operands[:kept]] + out_shape
        aliases = {n: n for n in range(kept)}
        space = pltpu.HBM if name == "side_first" else pltpu.VMEM
        pinned = [pltpu.with_memory_space_constraint(x, space) for x in operands]
        in_specs = [pl.BlockSpec(memory_space=space)] * len(operands)
        if result is not None:
            aliases[len(operands)] = len(out_shape) - 1
            pinned.append(pltpu.with_memory_space_constraint(result, pltpu.HBM))
            in_specs.append(in_hbm)
        return pl.pallas_call(
            functools.partial(kernel, g),
            in_specs=in_specs,
            out_shape=out_shape,
            out_specs=[in_hbm if x is whole else in_vmem for x in out_shape],
            scratch_shapes=list(scratch),
            input_output_aliases=aliases,
            compiler_params=pltpu.CompilerParams(vmem_limit_bytes=VMEM_LIMIT),
            cost_estimate=pl.CostEstimate(flops=0, bytes_accessed=load, transcendentals=0)
            if load
            else None,
            name=name,
        )(*pinned)

    def swap_faces(axis, count, parcels):
        return swap(axis, count, *parcels)[::-1]

    def relay(buf, parcels, sign, count):
        def kernel(grid, *refs):
            relay_kernel(grid, sign, count, *refs)

        buf, *parcels = call("relay", kernel, [buf, *parcels], corners(count), kept=1)
        return buf, swap("gx", nx, *parcels)[::-1]

    flat_space = [vmem(*porosity.shape)] + [pltpu.VMEM(porosity.shape, jnp.int32)] * 2
    post, state0, staged, *rest = call(
        "side_first",
        side_first_kernel,
        [populations, porosity, solid, labels],
        [padded(30), fields(7, g.local), stage] + flat_space + y_faces(30, 1),
        [sems, pltpu.SemaphoreType.DMA((3,))],
    )
    along_y = swap_faces("gy", ny, rest[3:])
    post, state0, *parcels = call(
        "rim_first",
        rim_first_kernel,
        [post, state0, staged, *rest[:3]],
        x_faces(30),
        kept=2,
        load=FLIGHT,
    )
    along_x = swap_faces("gx", nx, parcels)
    post, state0, second, state1 = call(
        "inner_first",
        inner_first_kernel,
        [post, state0, staged],
        [padded(27), fields(7, g.extended)],
        kept=2,
        load=FLIGHT,
    )
    post, parcels = relay(post, along_y, 1, 30)
    post, second, state1, staged, field = call(
        "middle_second",
        lambda grid, _post, _out, _state, b, a, source, *refs: middle_second_kernel(
            grid, source, *refs, b, a
        ),
        [post, second, state1, *along_x, adjoint_in],
        [stage, padded(27)],
        kept=3,
        load=FLIGHT,
    )
    _, second, state1, staged, field, *parcels = call(
        "side_seed",
        side_seed_kernel,
        [post, second, state1, staged, field, *parcels, adjoint_in],
        y_faces(27, -1),
        kept=5,
    )
    along_y = swap_faces("gy", ny, parcels)
    staged, field, *parcels = call(
        "rim_seed",
        rim_seed_kernel,
        [staged, field, second, adjoint_in],
        x_faces(27),
        kept=2,
        load=FLIGHT,
    )
    along_x = swap_faces("gx", nx, parcels)
    _, field, pulled, before, final = call(
        "inner_seed",
        lambda grid, kept, into, buf, *refs: inner_seed_kernel(grid, buf, kept, into, *refs),
        [staged, field, second, state1, adjoint_in],
        [padded(27), fields(1, g.extended), whole],
        [sems],
        kept=2,
        load=FLIGHT,
    )
    field, parcels = relay(field, along_y, -1, 27)
    field, pulled, before, total, parts = call(
        "middle_adjoint",
        lambda grid, _field, _out, _before, near, far, b, a, *refs: middle_adjoint_kernel(
            grid, *refs, near, far, b, a
        ),
        [field, pulled, before, state1, state0, *along_x],
        [fields(1, g.local), fields(5, g.local)],
        kept=3,
        load=FLIGHT,
    )
    _, pulled, _, total, parts, peak = call(
        "total",
        total_kernel,
        [field, pulled, before, total, parts, state1, state0, *parcels],
        [vmem(8, LANES)],
        kept=5,
    )
    half = g.cols // 2
    scratch = [vmem(half, 27, rows, LANES), pltpu.SemaphoreType.DMA((half,))]
    halves = []

    def first_half(peak):
        def kernel(grid, buf, fields, near, echo, *refs):
            echo[...] = near[...]
            adjoint_kernel(grid, 1, half, buf, fields, *refs)

        echo, result = call(
            "adjoint_low",
            kernel,
            [pulled, parts, peak],
            [vmem(8, LANES), whole],
            scratch,
            load=FLIGHT // 2,
        )
        halves.append(result)
        return echo

    largest = largest_of_all(peak, sizes, first_half)
    (adjoint_out,) = call(
        "adjoint_high",
        lambda grid, buf, fields, _, *refs: adjoint_kernel(
            grid, 1 + half, g.cols, buf, fields, *refs
        ),
        [pulled, parts],
        [whole],
        scratch,
        load=FLIGHT // 2,
        result=halves[0],
    )
    (sensitivity,) = call(
        "normalize",
        scale_kernel,
        [total, largest],
        [jax.ShapeDtypeStruct(porosity.shape, F32)],
    )
    return final, adjoint_out, sensitivity


def solution(mesh):
    sizes = (mesh.shape["gx"], mesh.shape["gy"])
    whole, flat = P(None, "gx", "gy"), P("gx", "gy")
    return jax.shard_map(
        functools.partial(on_device, sizes),
        mesh=mesh,
        in_specs=(whole, whole, flat, flat, flat),
        out_specs=(whole, whole, flat),
        check_vma=False,
    )
```

```python
import functools

import jax
import jax.numpy as jnp
from jax import lax
from jax.experimental import pallas as pl
from jax.experimental.pallas import tpu as pltpu
from jax.sharding import PartitionSpec as P

NZ = 64
RELAX = 0.8
PUSH = 0.2
EPS = 1e-06
LANES = 128
VELOCITY = [(a, b, c) for a in (-1, 0, 1) for b in (-1, 0, 1) for c in (-1, 0, 1)]
INDEX = {v: i for i, v in enumerate(VELOCITY)}
WEIGHT = [
    [8.0 / 27, 2.0 / 27, 1.0 / 54, 1.0 / 216][abs(v[0]) + abs(v[1]) + abs(v[2])]
    for v in VELOCITY
]
NORM = [abs(v[0]) + abs(v[1]) + abs(v[2]) for v in VELOCITY]
F32 = jnp.float32
VMEM_LIMIT = 6 * 1024 * 1024
FLIGHT = 12 * 1024 * 1024


class Grid:
    def __init__(self, rows, width):
        self.rows = rows
        self.cols = width // LANES
        self.panel = rows + 16
        self.halo = self.cols + 1
        self.local = self.cols * rows
        self.extended = self.halo * rows + 24
        self.outer = ((0, 8), (rows - 8, 8))
        self.inner = tuple(((r, 16),) for r in range(8, rows - 8, 16))

    def at(self, i, k, r):
        return self.field(i) + k * self.panel + r

    def field(self, i):
        return i * (self.cols + 2) * self.panel + 8

    def padded(self, fields):
        return (fields * (self.cols + 2) * self.panel + 8, LANES)


def velocity(i, sign):
    return tuple(sign * n for n in VELOCITY[i]) if i < 27 else (0, 0, 0)


def moving(fields, sign, axis, side):
    return [i for i in range(fields) if velocity(i, sign)[axis] == side]


def lane_masks(height):
    lane = lax.broadcasted_iota(jnp.int32, (height, LANES), 1)
    return lane >= NZ, lane % NZ == 0, lane % NZ == NZ - 1


def halves(load, d, masks):
    high = masks[0]
    if d[1] == 1:
        return jnp.where(high, load(-1), load(0))
    if d[1] == -1:
        return jnp.where(high, load(0), load(1))
    return load(0)


def turns(dz):
    return (1, NZ + 1) if dz == 1 else (LANES - 1, NZ - 1)


def shift_pair(flat, steep, dz, masks):
    edge, source = (masks[1], masks[2]) if dz == 1 else (masks[2], masks[1])
    near, far = turns(dz)
    one = pltpu.roll(jnp.where(source, steep, flat), near, 1)
    two = pltpu.roll(jnp.where(source, flat, steep), far, 1)
    return jnp.where(edge, two, one), jnp.where(edge, one, two)


def shift_steep(tile, dz, masks):
    if dz == 0:
        return pltpu.roll(tile, NZ, 1)
    near, far = turns(dz)
    edge = masks[1] if dz == 1 else masks[2]
    return jnp.where(edge, pltpu.roll(tile, near, 1), pltpu.roll(tile, far, 1))


def shift_lanes(tiles, sign, masks):
    out = list(tiles)
    place = {velocity(i, sign): i for i in range(27)}
    for dx in (-1, 0, 1):
        for dy in (-1, 1):
            i = place[dx, dy, 0]
            out[i] = shift_steep(tiles[i], 0, masks)
        for dz in (-1, 1):
            i, j, k = (place[dx, dy, dz] for dy in (0, 1, -1))
            out[i], out[j] = shift_pair(tiles[i], tiles[j], dz, masks)
            out[k] = shift_steep(tiles[k], dz, masks)
    return out


def stacked(parts):
    return parts[0] if len(parts) == 1 else jnp.concatenate(parts, 0)


def read_rows(ref, base, pieces):
    return stacked([ref[pl.ds(base + r, n), :] for r, n in pieces])


def write_rows(ref, base, pieces, value):
    done = 0
    for r, n in pieces:
        ref[pl.ds(base + r, n), :] = value[done : done + n]
        done += n


def pull_block(g, buf, sign, k, pieces, masks, fields=27):
    base = pl.multiple_of(k * g.panel, 8)
    after = pl.multiple_of(jnp.where(k == g.halo, g.panel, base + g.panel), 8)
    out = []
    for i in range(fields):
        d = velocity(i, sign)

        def load(n, i=i, d=d):
            start = {-1: base - g.panel, 0: base, 1: after}[n]
            return read_rows(buf, start + (g.field(i) - d[0]), pieces)

        out.append(halves(load, d, masks))
    return shift_lanes(out, sign, masks)


def pull_edge(g, buf, sign, side, masks, fields=27):
    out = []
    for i in range(fields):
        d = velocity(i, sign)
        if side == 1:
            row = g.rows - d[0]
        else:
            row = {1: g.rows, 0: g.rows + 1, -1: 0}[d[0]]

        def load(n, i=i, row=row):
            return buf[pl.ds(g.at(i, 1 + n, row), g.cols, stride=g.panel), :]

        out.append(halves(load, d, masks))
    return shift_lanes(out, sign, masks)


def moments(f):
    flat = {}
    along_z = None
    for a in (-1, 0, 1):
        for b in (-1, 0, 1):
            lo, mid, hi = (f[INDEX[(a, b, c)]] for c in (-1, 0, 1))
            flat[a, b] = lo + mid + hi
            diff = hi - lo
            along_z = diff if along_z is None else along_z + diff
    line = {}
    along_y = None
    for a in (-1, 0, 1):
        line[a] = flat[a, -1] + flat[a, 0] + flat[a, 1]
        diff = flat[a, 1] - flat[a, -1]
        along_y = diff if along_y is None else along_y + diff
    return line[-1] + line[0] + line[1], line[1] - line[-1], along_y, along_z


def combos(x, y, z):
    plane = {}
    for a in (-1, 0, 1):
        for b in (-1, 0, 1):
            if (a, b) > (0, 0):
                continue
            if a == 0:
                plane[a, b] = -y if b else None
            else:
                plane[a, b] = -x if b == 0 else (-x - y if b < 0 else y - x)
    out = []
    for a, b, c in VELOCITY[:13]:
        base = plane[a, b]
        if base is None:
            out.append(-z)
        else:
            out.append(base if c == 0 else (base - z if c < 0 else base + z))
    return out


def relax(f, rho, wx, wy, wz, damp, push, solid):
    ux, uy, uz = (wx + push) * damp, wy * damp, wz * damp
    base = 1.0 - 1.5 * (ux * ux + uy * uy + uz * uz)
    keep = 1.0 - 1.0 / RELAX
    gain = rho * (1.0 / RELAX)
    level = [gain * w for w in (8.0 / 27, 2.0 / 27, 1.0 / 54, 1.0 / 216)]
    along = combos(3.0 * ux, 3.0 * uy, 3.0 * uz)
    out = [None] * 27
    for i in range(13):
        j = 26 - i
        even = base + 0.5 * (along[i] * along[i])
        lift = level[NORM[i]]
        out[i] = jnp.where(solid, f[j], keep * f[i] + lift * (even + along[i]))
        out[j] = jnp.where(solid, f[i], keep * f[j] + lift * (even - along[i]))
    out[13] = jnp.where(solid, f[13], keep * f[13] + level[0] * base)
    return out


def pulled_moments(p):
    first = {}
    for a in (-1, 0, 1):
        for b in (-1, 0, 1):
            lo, mid, hi = (p[INDEX[(a, b, c)]] for c in (-1, 0, 1))
            both = lo + hi
            first[a, b] = (4.0 * mid + both, hi - lo, both)
    second = {}
    for a in (-1, 0, 1):
        lo, mid, hi = (first[a, b] for b in (-1, 0, 1))
        b0 = lo[0] + hi[0]
        b1 = lo[1] + hi[1]
        second[a] = dict(
            one=4.0 * mid[0] + b0,
            y=hi[0] - lo[0],
            yy=b0,
            z=4.0 * mid[1] + b1,
            yz=hi[1] - lo[1],
            zz=4.0 * mid[2] + lo[2] + hi[2],
        )
    lo, mid, hi = (second[a] for a in (-1, 0, 1))

    def full(key):
        return 4.0 * mid[key] + lo[key] + hi[key]

    xx = lo["one"] + hi["one"]
    return dict(
        one=4.0 * mid["one"] + xx,
        x=hi["one"] - lo["one"],
        xx=xx,
        y=full("y"),
        xy=hi["y"] - lo["y"],
        yy=full("yy"),
        z=full("z"),
        xz=hi["z"] - lo["z"],
        yz=full("yz"),
        zz=full("zz"),
    )


def adjoint_scalars(p, rho, wx, wy, wz, damp, push, solid):
    ux, uy, uz = (wx + push) * damp, wy * damp, wz * damp
    s = pulled_moments(p)
    scale = 1.0 / (216.0 * RELAX)
    one = s["one"] * scale
    b = [s[k] * (3.0 * scale) for k in ("x", "y", "z")]
    d = {k: s[k] * (9.0 * scale) for k in ("xx", "xy", "yy", "xz", "yz", "zz")}
    qx = d["xx"] * ux + d["xy"] * uy + d["xz"] * uz
    qy = d["xy"] * ux + d["yy"] * uy + d["yz"] * uz
    qz = d["xz"] * ux + d["yz"] * uy + d["zz"] * uz
    linear = b[0] * ux + b[1] * uy + b[2] * uz
    square = ux * ux + uy * uy + uz * uz
    even = one + linear + 0.5 * (qx * ux + qy * uy + qz * uz) - 1.5 * one * square
    three = 3.0 * one
    gx = (b[0] + qx - three * ux) * damp
    gy = (b[1] + qy - three * uy) * damp
    gz = (b[2] + qz - three * uz) * damp
    even = even - (gx * wx + gy * wy + gz * wz)
    porous = jnp.where(solid, 0.0, -rho * (gx * ux + gy * uy + gz * uz))
    return even, gx, gy, gz, porous


def adjoint_spread(p, even, gx, gy, gz, solid):
    keep = 1.0 - 1.0 / RELAX
    along = combos(gx, gy, gz)
    out = [None] * 27
    for i in range(13):
        j = 26 - i
        out[i] = jnp.where(solid, p[j], keep * p[i] + (even + along[i]))
        out[j] = jnp.where(solid, p[i], keep * p[j] + (even - along[i]))
    out[13] = jnp.where(solid, p[13], keep * p[13] + even)
    return out


def x_lines(g, sign, fields, side):
    lines = []
    for i in moving(fields, sign, 0, side):
        if side == 1:
            lines.append((i, g.rows - 1, (-1, g.rows + 1)))
            lines.append((i, g.rows - 2, (g.rows,)))
        else:
            lines += [(i, 0, (g.rows,)), (i, 1, (g.rows + 1,))]
    edge, target = (g.rows - 1, g.rows + 1) if side == 1 else (0, g.rows)
    return lines + [(i, edge, (target,)) for i in moving(fields, sign, 0, 0)]


def pack_x(g, buf, sign, fields, up, down):
    for side, ref in ((1, up), (-1, down)):
        for n, (i, r, _) in enumerate(x_lines(g, sign, fields, side)):
            ref[n * g.cols : (n + 1) * g.cols, :] = buf[
                pl.ds(g.at(i, 1, r), g.cols, stride=g.panel), :
            ]


def unpack_x(g, buf, sign, fields, up, down):
    for side, ref in ((1, up), (-1, down)):
        for n, (i, _, targets) in enumerate(x_lines(g, sign, fields, side)):
            value = ref[n * g.cols : (n + 1) * g.cols, :]
            for r in targets:
                buf[pl.ds(g.at(i, 1, r), g.cols, stride=g.panel), :] = value
    for i in moving(fields, sign, 0, -1):
        buf[pl.ds(g.at(i, 1, g.rows + 2), g.cols, stride=g.panel), :] = buf[
            pl.ds(g.at(i, 1, 0), g.cols, stride=g.panel), :
        ]


def halo_panels(g, i, sign):
    return (0, g.halo) if velocity(i, sign)[1] == 1 else (g.halo,)


def pack_corners(g, buf, sign, fields, up, down):
    for side, ref in ((1, up), (-1, down)):
        for n, (i, r, _) in enumerate(x_lines(g, sign, fields, side)):
            ref[n : n + 1, :] = buf[pl.ds(g.at(i, g.halo, r), 1), :]


def unpack_corners(g, buf, sign, fields, up, down):
    for side, ref in ((1, up), (-1, down)):
        for n, (i, _, targets) in enumerate(x_lines(g, sign, fields, side)):
            value = ref[n : n + 1, :]
            for r in targets:
                for k in halo_panels(g, i, sign):
                    buf[pl.ds(g.at(i, k, r), 1), :] = value
    for i in moving(fields, sign, 0, -1):
        for k in halo_panels(g, i, sign):
            buf[pl.ds(g.at(i, k, g.rows + 2), 1), :] = buf[pl.ds(g.at(i, k, 0), 1), :]


def still_pairs(fields, sign):
    still = moving(fields, sign, 1, 0)
    half = (len(still) + 1) // 2
    return [(still[n], still[n + half] if n + half < len(still) else None) for n in range(half)]


def y_slots(fields, sign):
    return 9 + len(still_pairs(fields, sign))


def pack_y(g, buf, sign, fields, up, down):
    high = lane_masks(g.rows)[0]
    for side, ref in ((1, up), (-1, down)):
        k = g.cols if side == 1 else 1
        for n, i in enumerate(moving(fields, sign, 1, side)):
            ref[n * g.rows : (n + 1) * g.rows, :] = buf[pl.ds(g.at(i, k, 0), g.rows), :]
        for n, (i, j) in enumerate(still_pairs(fields, sign)):
            value = buf[pl.ds(g.at(i, k, 0), g.rows), :]
            if j is not None:
                other = pltpu.roll(buf[pl.ds(g.at(j, k, 0), g.rows), :], NZ, 1)
                pair = (value, other) if side == 1 else (other, value)
                value = jnp.where(high, *pair)
            ref[(9 + n) * g.rows : (10 + n) * g.rows, :] = value


def unpack_y(g, buf, sign, fields, high, up, down):
    for side, ref in ((1, up), (-1, down)):
        for n, i in enumerate(moving(fields, sign, 1, side)):
            value = ref[n * g.rows : (n + 1) * g.rows, :]
            for k in halo_panels(g, i, sign):
                buf[pl.ds(g.at(i, k, 0), g.rows), :] = value
    for n, (i, j) in enumerate(still_pairs(fields, sign)):
        spot = slice((9 + n) * g.rows, (10 + n) * g.rows)
        before, after = up[spot, :], down[spot, :]
        buf[pl.ds(g.at(i, g.halo, 0), g.rows), :] = jnp.where(high, before, after)
        if j is not None:
            value = pltpu.roll(jnp.where(high, after, before), NZ, 1)
            buf[pl.ds(g.at(j, g.halo, 0), g.rows), :] = value


def by_parity(axis, first, second, act):
    even = lax.rem(lax.axis_index(axis), 2) == 0

    @pl.when(even)
    def _():
        act(first, second)

    @pl.when(jnp.logical_not(even))
    def _():
        act(second, first)


def load_fields(ref, rows, base, pieces, count):
    return [read_rows(ref, base + n * rows, pieces) for n in range(count)]


def save_fields(ref, rows, base, pieces, values):
    for n, value in enumerate(values):
        write_rows(ref, base + n * rows, pieces, value)


def save_populations(g, out, k, pieces, values):
    base = pl.multiple_of(k * g.panel, 8)
    for i, value in enumerate(values):
        write_rows(out, base + g.field(i), pieces, value)


def spot_of(g, k):
    return pl.multiple_of((k - 1) * g.rows, 8)


def lanes_of(k):
    return pl.ds(pl.multiple_of((k - 1) * LANES, LANES), LANES)


def every(first, last, act):
    def step(k, carry):
        act(k)
        return carry

    count = last + 1 - first
    unroll = max(n for n in (1, 2, 3, 4, 6, 8) if count % n == 0)
    lax.fori_loop(first, last + 1, step, 0, unroll=unroll)


def side_panels(g, act, count):
    def step(n, carry):
        act(jnp.where(n == 0, 1, g.cols - 1 + n))
        return carry

    lax.fori_loop(0, count, step, 0, unroll=count)


def interior_tiles(g, act):
    for pieces in g.inner:
        every(2, g.cols - 1, functools.partial(act, pieces=pieces))


def middle_tiles(g, act):
    for pieces in g.inner:
        side_panels(g, functools.partial(act, pieces=pieces), 3)
    every(2, g.cols - 1, functools.partial(act, pieces=g.outer))


def core_tiles(g, act):
    for pieces in g.inner:
        every(3, g.cols - 2, functools.partial(act, pieces=pieces))


def near_core_tiles(g, act):
    def step(n, carry):
        for pieces in g.inner:
            act(jnp.where(n == 0, 2, g.cols - 1), pieces=pieces)
        return carry

    lax.fori_loop(0, 2, step, 0, unroll=2)


def rim_tiles(g, act):
    every(1, g.cols, functools.partial(act, pieces=g.outer))
    for pieces in g.inner:
        side_panels(g, functools.partial(act, pieces=pieces), 2)


def step_tile(g, buf, out, sign, fields, masks, compute):
    def act(k, pieces):
        values = compute(
            pull_block(g, buf, sign, k, pieces, masks, fields), spot_of(g, k), pieces
        )
        save_populations(g, out, k, pieces, values)

    return act


def corner_tiles(g, buf, out, sign, fields, masks, compute):
    small = tuple(mask[:8] for mask in masks)
    act = step_tile(g, buf, out, sign, fields, masks, compute)
    side_panels(g, functools.partial(act, pieces=g.outer), 3)
    spot = g.halo * g.rows
    pieces = ((g.rows, 8),)
    values = compute(pull_block(g, buf, sign, g.halo, pieces, small, fields), spot, ((0, 8),))
    for i in range(27):
        dx = velocity(i, sign)[0]
        if dx == -1:
            out[pl.ds(g.at(i, g.halo, g.rows), 1), :] = values[i][0:1]
        elif dx == 1:
            out[pl.ds(g.at(i, g.halo, -1), 1), :] = values[i][1:2]
    edges = [pull_edge(g, buf, sign, side, small, fields) for side in (1, -1)]
    both = [stacked(pair) for pair in zip(*edges)]
    values = compute(both, spot, ((8, 16),))
    for i in moving(27, sign, 0, -1):
        out[pl.ds(g.at(i, 1, g.rows), g.cols, stride=g.panel), :] = values[i][:8]
    for i in moving(27, sign, 0, 1):
        out[pl.ds(g.at(i, 1, -1), g.cols, stride=g.panel), :] = values[i][8:]
    for i in moving(27, sign, 1, 1):
        out[pl.ds(g.at(i, 0, 0), g.rows), :] = out[pl.ds(g.at(i, g.halo, 0), g.rows), :]
        for r in (-1, g.rows):
            out[pl.ds(g.at(i, 0, r), 1), :] = out[pl.ds(g.at(i, g.halo, r), 1), :]


def flow_of(f):
    rho, mx, my, mz = moments(f)
    inverse = 1.0 / rho
    return inverse, rho, mx * inverse, my * inverse, mz * inverse


def collide_first(g, state, out):
    def act(k, pieces, f):
        base = pl.multiple_of(k * g.panel, 8)
        damp, push, wall = (read_rows(out, base + g.field(i), pieces) for i in (27, 28, 29))
        flow = flow_of(f)[1:] + (damp, push)
        save_fields(state, g.local, spot_of(g, k), pieces, flow + (wall,))
        save_populations(g, out, k, pieces, relax(f, *flow, wall > 0.5))

    return act


def collide_second(g, state):
    def compute(values, spot, pieces):
        f, (damp, push, wall) = values[:27], values[27:]
        flow = flow_of(f)[1:] + (damp, push)
        save_fields(state, g.extended, spot, pieces, flow + (wall,))
        return relax(f, *flow, wall > 0.5)

    return compute


def adjoint_second(g, state, total):
    def compute(p, spot, pieces):
        *flow, wall = load_fields(state, g.extended, spot, pieces, 7)
        *spread, porous = adjoint_scalars(p, *flow, wall > 0.5)
        save_fields(total, g.extended, spot, pieces, [porous])
        return adjoint_spread(p, *spread, wall > 0.5)

    return compute


def seed_tile(g, buf, adjoint, stage, out, masks):
    def act(k, pieces):
        f = pull_block(g, buf, 1, k, pieces, masks)
        for i in range(27):
            write_rows(stage.at[k - 1, i], 0, pieces, f[i])
        inverse, _, wx, wy, wz = flow_of(f)
        even = -(wx * wx + wy * wy + wz * wz) * inverse
        along = combos(wx * inverse, wy * inverse, wz * inverse)
        lanes = lanes_of(k)
        seeded = [
            stacked([adjoint[i, pl.ds(r, n), lanes] for r, n in pieces]) + even for i in range(27)
        ]
        for i in range(13):
            seeded[i] = seeded[i] + along[i]
            seeded[26 - i] = seeded[26 - i] - along[i]
        save_populations(g, out, k, pieces, seeded)

    return act


def block_of(ref, k):
    return ref.at[:, :, lanes_of(k)]


def flat_fields(g, out, near, k):
    porosity, solid, labels = near
    lanes = lanes_of(k)
    label = labels[:, lanes]
    damp = 1.0 / (1.0 + porosity[:, lanes])
    push = jnp.where(label == 1, PUSH, jnp.where(label == 2, -PUSH, 0.0))
    base = pl.multiple_of(k * g.panel, 8)
    for i, value in ((27, damp), (28, push), (29, solid[:, lanes].astype(F32))):
        out[pl.ds(base + g.field(i), g.rows), :] = value


def staged_tile(g, collide, stage):
    def act(k, pieces):
        collide(k, pieces, [read_rows(stage.at[k - 1, i], 0, pieces) for i in range(27)])

    return act


def side_tiles(g, act):
    for pieces in (g.outer,) + g.inner:
        side_panels(g, functools.partial(act, pieces=pieces), 2)


def side_first_kernel(g, pops, *refs):
    flat, (out, state, stage), near, faces, (sems, flat_sems) = (
        refs[:3],
        refs[3:6],
        refs[6:9],
        refs[9:11],
        refs[11:],
    )

    def copy(k):
        return pltpu.make_async_copy(block_of(pops, k), stage.at[k - 1], sems.at[k - 1])

    flat_copies = [
        pltpu.make_async_copy(source, target, flat_sems.at[n])
        for n, (source, target) in enumerate(zip(flat, near))
    ]
    for each in flat_copies:
        each.start()
    for k in (1, g.cols, *range(2, g.cols)):
        copy(k).start()
    for each in flat_copies:
        each.wait()
    for k in (1, g.cols):
        flat_fields(g, out, near, k)
    copy(1).wait()
    copy(g.cols).wait()
    side_tiles(g, staged_tile(g, collide_first(g, state, out), stage))
    by_parity("gy", *faces, functools.partial(pack_y, g, out, 1, 30))
    for k in range(2, g.cols):
        copy(k).wait()


def rim_first_kernel(g, _out, _state, stage, *refs):
    near, (out, state), faces = refs[:3], refs[3:5], refs[5:]
    every(2, g.cols - 1, functools.partial(flat_fields, g, out, near))
    act = staged_tile(g, collide_first(g, state, out), stage)
    every(2, g.cols - 1, functools.partial(act, pieces=g.outer))
    by_parity("gx", *faces, functools.partial(pack_x, g, out, 1, 30))


def inner_first_kernel(g, _, _state, stage, post, state0, out, state1):
    masks = lane_masks(16)
    interior_tiles(g, staged_tile(g, collide_first(g, state0, post), stage))
    interior_tiles(g, step_tile(g, post, out, 1, 30, masks, collide_second(g, state1)))


def relay_kernel(g, sign, fields, _, y_second, y_first, buf, first, second):
    high = lane_masks(g.rows)[0]
    by_parity("gy", y_second, y_first, functools.partial(unpack_y, g, buf, sign, fields, high))
    by_parity("gx", first, second, functools.partial(pack_corners, g, buf, sign, fields))


def middle_second_kernel(g, adjoint, post, out, state1, stage, field, x_second, x_first):
    masks = lane_masks(16)
    by_parity("gx", x_second, x_first, functools.partial(unpack_x, g, post, 1, 30))
    middle_tiles(g, step_tile(g, post, out, 1, 30, masks, collide_second(g, state1)))
    core_tiles(g, seed_tile(g, out, adjoint, stage, field, masks))


def side_seed_kernel(g, _post, _out, _state, _stage, _field, second, first, adjoint, *refs):
    post, out, state1, stage, field, *faces = refs
    masks = lane_masks(16)
    by_parity("gx", second, first, functools.partial(unpack_corners, g, post, 1, 30))
    corner_tiles(g, post, out, 1, 30, masks, collide_second(g, state1))
    side_tiles(g, seed_tile(g, out, adjoint, stage, field, masks))
    by_parity("gy", *faces, functools.partial(pack_y, g, field, -1, 27))


def rim_seed_kernel(g, _stage, _field, out, adjoint, stage, field, *faces):
    seed = seed_tile(g, out, adjoint, stage, field, lane_masks(16))
    every(2, g.cols - 1, functools.partial(seed, pieces=g.outer))
    by_parity("gx", *faces, functools.partial(pack_x, g, field, -1, 27))


def early_panels(g):
    return (1, g.cols, *range(3, g.cols // 2 + 1))


def inner_seed_kernel(
    g, post, _stage, _field, state1, adjoint, stage, field, out, total, final, sems
):
    masks = lane_masks(16)

    def copy(k):
        return pltpu.make_async_copy(stage.at[k - 1], block_of(final, k), sems.at[k - 1])

    for k in early_panels(g):
        copy(k).start()
    seed = seed_tile(g, post, adjoint, stage, field, masks)

    near_core_tiles(g, seed)
    interior_tiles(g, step_tile(g, field, out, -1, 27, masks, adjoint_second(g, state1, total)))
    for k in early_panels(g):
        copy(k).wait()


def total_tile(g, out, before, state0, total, parts, masks):
    def act(k, pieces):
        p = pull_block(g, out, -1, k, pieces, masks)
        spot = spot_of(g, k)
        *flow, wall = load_fields(state0, g.local, spot, pieces, 7)
        *spread, porous = adjoint_scalars(p, *flow, wall > 0.5)
        here = load_fields(before, g.extended, spot, pieces, 1)[0] + porous
        save_fields(total, g.local, spot, pieces, [here])
        save_fields(parts, g.local, spot, pieces, spread + [wall])

    return act


def middle_adjoint_kernel(
    g, state1, state0, x_second, x_first, stage, _, field, out, before, total, parts, final, sems
):
    masks = lane_masks(16)
    copies = [
        pltpu.make_async_copy(stage.at[k - 1], block_of(final, k), sems.at[k - 1])
        for k in range(1, g.cols + 1)
        if k not in early_panels(g)
    ]
    for each in copies:
        each.start()
    by_parity("gx", x_second, x_first, functools.partial(unpack_x, g, field, -1, 27))
    middle_tiles(g, step_tile(g, field, out, -1, 27, masks, adjoint_second(g, state1, before)))
    core_tiles(g, total_tile(g, out, before, state0, total, parts, masks))
    for each in copies:
        each.wait()


def total_kernel(g, *refs):
    state1, state0, second, first, field, out, before, total, parts, peak = refs[5:]
    masks = lane_masks(16)
    by_parity("gx", second, first, functools.partial(unpack_corners, g, field, -1, 27))
    corner_tiles(g, field, out, -1, 27, masks, adjoint_second(g, state1, before))
    act = total_tile(g, out, before, state0, total, parts, masks)
    near_core_tiles(g, act)
    rim_tiles(g, act)
    size = 8 * (g.local // 64)
    largest = jnp.zeros((8, LANES), F32)
    for start in range(0, g.local, size):
        value = jnp.abs(total[start : start + size, :]).reshape(-1, 8, LANES)
        largest = jnp.maximum(largest, jnp.max(value, 0))
    peak[...] = largest


def adjoint_kernel(g, first, last, buf, parts, result, stage, sems):
    masks = lane_masks(16)

    def copy(k):
        return pltpu.make_async_copy(stage.at[k - first], block_of(result, k), sems.at[k - first])

    def column(k):
        for pieces in (g.outer,) + g.inner:
            p = pull_block(g, buf, -1, k, pieces, masks)
            *spread, wall = load_fields(parts, g.local, spot_of(g, k), pieces, 5)
            for i, value in enumerate(adjoint_spread(p, *spread, wall > 0.5)):
                write_rows(stage.at[k - first, i], 0, pieces, value)
        copy(k).start()

    every(first, last, column)
    every(first, last, lambda k: copy(k).wait())


def scale_kernel(g, total, peak, out):
    largest = jnp.max(peak[...])
    factor = 1.0 / (jnp.full((g.rows, LANES), largest, F32) + EPS)
    for c in range(g.cols):
        value = total[c * g.rows : (c + 1) * g.rows, :] * factor
        out[:, c * LANES : (c + 1) * LANES] = value


def swap_pairs(count, start):
    pairs = []
    for i in range(start, count, 2):
        j = (i + 1) % count
        pairs += [(i, j), (j, i)]
    return pairs


def swap(axis, count, first, second):
    return (
        lax.ppermute(first, axis, swap_pairs(count, 0)),
        lax.ppermute(second, axis, swap_pairs(count, 1)),
    )


def largest_of_all(peak, sizes, beside):
    nx, ny = sizes
    peak = jnp.maximum(peak, lax.ppermute(peak, "gy", [(i, i ^ 1) for i in range(ny)]))
    groups = 0
    for axis, count, first, widths in (("gy", ny, 2, (4, 4)), ("gx", nx, 1, (4, 2))):
        step = first
        for width in widths:
            width = min(width, count // step)
            parts = []
            for n in range(1, width):
                if axis == "gy":
                    pairs = [(i, i ^ (n * step) ^ 1) for i in range(ny)]
                    parts.append(lax.ppermute(peak, "gy", pairs))
                else:
                    pairs = [
                        (i * ny + y, (i ^ (n * step)) * ny + (y ^ 1))
                        for i in range(nx)
                        for y in range(ny)
                    ]
                    parts.append(lax.ppermute(peak, ("gx", "gy"), pairs))
            groups += 1
            if groups == 1:
                peak = beside(peak)
            peak = functools.reduce(jnp.maximum, parts, peak)
            step *= width
    return peak


def on_device(sizes, populations, adjoint_in, porosity, solid, labels):
    rows, width = porosity.shape
    g = Grid(rows, width)
    in_vmem = pl.BlockSpec(memory_space=pltpu.VMEM)
    in_hbm = pl.BlockSpec(memory_space=pltpu.HBM)
    nx, ny = sizes

    def vmem(*shape):
        return pltpu.VMEM(shape, F32)

    def fields(count, size):
        return vmem(count * size, LANES)

    def padded(count):
        return vmem(*g.padded(count))

    def x_faces(count):
        return [vmem(count * g.cols, LANES)] * 2

    def y_faces(count, sign):
        return [vmem(y_slots(count, sign) * rows, LANES)] * 2

    def corners(count):
        return [vmem(-(-count // 8) * 8, LANES)] * 2

    whole = pltpu.HBM(populations.shape, F32)
    stage = vmem(g.cols, 27, rows, LANES)
    sems = pltpu.SemaphoreType.DMA((g.cols,))

    def call(name, kernel, operands, out_shape, scratch=(), kept=0, load=0, result=None):
        out_shape = [pltpu.VMEM(x.shape, x.dtype) for x in operands[:kept]] + out_shape
        aliases = {n: n for n in range(kept)}
        space = pltpu.HBM if name == "side_first" else pltpu.VMEM
        pinned = [pltpu.with_memory_space_constraint(x, space) for x in operands]
        in_specs = [pl.BlockSpec(memory_space=space)] * len(operands)
        if result is not None:
            aliases[len(operands)] = len(out_shape) - 1
            pinned.append(pltpu.with_memory_space_constraint(result, pltpu.HBM))
            in_specs.append(in_hbm)
        return pl.pallas_call(
            functools.partial(kernel, g),
            in_specs=in_specs,
            out_shape=out_shape,
            out_specs=[in_hbm if x is whole else in_vmem for x in out_shape],
            scratch_shapes=list(scratch),
            input_output_aliases=aliases,
            compiler_params=pltpu.CompilerParams(vmem_limit_bytes=VMEM_LIMIT),
            cost_estimate=pl.CostEstimate(flops=0, bytes_accessed=load, transcendentals=0)
            if load
            else None,
            name=name,
        )(*pinned)

    def swap_faces(axis, count, parcels):
        return swap(axis, count, *parcels)[::-1]

    def relay(buf, parcels, sign, count):
        def kernel(grid, *refs):
            relay_kernel(grid, sign, count, *refs)

        buf, *parcels = call("relay", kernel, [buf, *parcels], corners(count), kept=1)
        return buf, swap("gx", nx, *parcels)[::-1]

    flat_space = [vmem(*porosity.shape)] + [pltpu.VMEM(porosity.shape, jnp.int32)] * 2
    post, state0, staged, *rest = call(
        "side_first",
        side_first_kernel,
        [populations, porosity, solid, labels],
        [padded(30), fields(7, g.local), stage] + flat_space + y_faces(30, 1),
        [sems, pltpu.SemaphoreType.DMA((3,))],
    )
    along_y = swap_faces("gy", ny, rest[3:])
    post, state0, *parcels = call(
        "rim_first",
        rim_first_kernel,
        [post, state0, staged, *rest[:3]],
        x_faces(30),
        kept=2,
        load=FLIGHT,
    )
    along_x = swap_faces("gx", nx, parcels)
    post, state0, second, state1 = call(
        "inner_first",
        inner_first_kernel,
        [post, state0, staged],
        [padded(27), fields(7, g.extended)],
        kept=2,
        load=FLIGHT,
    )
    post, parcels = relay(post, along_y, 1, 30)
    post, second, state1, staged, field = call(
        "middle_second",
        lambda grid, _post, _out, _state, b, a, source, *refs: middle_second_kernel(
            grid, source, *refs, b, a
        ),
        [post, second, state1, *along_x, adjoint_in],
        [stage, padded(27)],
        kept=3,
        load=FLIGHT,
    )
    _, second, state1, staged, field, *parcels = call(
        "side_seed",
        side_seed_kernel,
        [post, second, state1, staged, field, *parcels, adjoint_in],
        y_faces(27, -1),
        kept=5,
    )
    along_y = swap_faces("gy", ny, parcels)
    staged, field, *parcels = call(
        "rim_seed",
        rim_seed_kernel,
        [staged, field, second, adjoint_in],
        x_faces(27),
        kept=2,
        load=FLIGHT,
    )
    along_x = swap_faces("gx", nx, parcels)
    staged, field, pulled, before, final = call(
        "inner_seed",
        lambda grid, kept, into, buf, *refs: inner_seed_kernel(grid, buf, kept, into, *refs),
        [staged, field, second, state1, adjoint_in],
        [padded(27), fields(1, g.extended), whole],
        [sems],
        kept=2,
        load=FLIGHT,
    )
    field, parcels = relay(field, along_y, -1, 27)
    field, pulled, before, total, parts, final = call(
        "middle_adjoint",
        lambda grid, _field, _out, _before, *refs: middle_adjoint_kernel(grid, *refs),
        [field, pulled, before, state1, state0, *along_x, staged],
        [fields(1, g.local), fields(5, g.local), whole],
        [sems],
        kept=3,
        load=FLIGHT,
        result=final,
    )
    _, pulled, _, total, parts, peak = call(
        "total",
        total_kernel,
        [field, pulled, before, total, parts, state1, state0, *parcels],
        [vmem(8, LANES)],
        kept=5,
    )
    half = g.cols // 2
    scratch = [vmem(half, 27, rows, LANES), pltpu.SemaphoreType.DMA((half,))]
    halves = []

    def first_half(peak):
        def kernel(grid, buf, fields, near, echo, *refs):
            echo[...] = near[...]
            adjoint_kernel(grid, 1, half, buf, fields, *refs)

        echo, result = call(
            "adjoint_low",
            kernel,
            [pulled, parts, peak],
            [vmem(8, LANES), whole],
            scratch,
            load=FLIGHT // 2,
        )
        halves.append(result)
        return echo

    largest = largest_of_all(peak, sizes, first_half)
    (adjoint_out,) = call(
        "adjoint_high",
        lambda grid, buf, fields, _, *refs: adjoint_kernel(
            grid, 1 + half, g.cols, buf, fields, *refs
        ),
        [pulled, parts],
        [whole],
        scratch,
        load=FLIGHT // 2,
        result=halves[0],
    )
    (sensitivity,) = call(
        "normalize",
        scale_kernel,
        [total, largest],
        [jax.ShapeDtypeStruct(porosity.shape, F32)],
    )
    return final, adjoint_out, sensitivity


def solution(mesh):
    sizes = (mesh.shape["gx"], mesh.shape["gy"])
    whole, flat = P(None, "gx", "gy"), P("gx", "gy")
    return jax.shard_map(
        functools.partial(on_device, sizes),
        mesh=mesh,
        in_specs=(whole, whole, flat, flat, flat),
        out_specs=(whole, whole, flat),
        check_vma=False,
    )
```

```python
import functools

import jax
import jax.numpy as jnp
from jax import lax
from jax.experimental import pallas as pl
from jax.experimental.pallas import tpu as pltpu
from jax.sharding import PartitionSpec as P

NZ = 64
RELAX = 0.8
PUSH = 0.2
EPS = 1e-06
LANES = 128
VELOCITY = [(a, b, c) for a in (-1, 0, 1) for b in (-1, 0, 1) for c in (-1, 0, 1)]
INDEX = {v: i for i, v in enumerate(VELOCITY)}
WEIGHT = [
    [8.0 / 27, 2.0 / 27, 1.0 / 54, 1.0 / 216][abs(v[0]) + abs(v[1]) + abs(v[2])]
    for v in VELOCITY
]
NORM = [abs(v[0]) + abs(v[1]) + abs(v[2]) for v in VELOCITY]
F32 = jnp.float32
VMEM_LIMIT = 6 * 1024 * 1024
FLIGHT = 12 * 1024 * 1024


class Grid:
    def __init__(self, rows, width):
        self.rows = rows
        self.cols = width // LANES
        self.panel = rows + 16
        self.halo = self.cols + 1
        self.local = self.cols * rows
        self.extended = self.halo * rows + 24
        self.outer = ((0, 8), (rows - 8, 8))
        self.inner = tuple(((r, 16),) for r in range(8, rows - 8, 16))

    def at(self, i, k, r):
        return self.field(i) + k * self.panel + r

    def field(self, i):
        return i * (self.cols + 2) * self.panel + 8

    def padded(self, fields):
        return (fields * (self.cols + 2) * self.panel + 64, LANES)


def velocity(i, sign):
    return tuple(sign * n for n in VELOCITY[i]) if i < 27 else (0, 0, 0)


def moving(fields, sign, axis, side):
    return [i for i in range(fields) if velocity(i, sign)[axis] == side]


def lane_masks(height):
    lane = lax.broadcasted_iota(jnp.int32, (height, LANES), 1)
    return lane >= NZ, lane % NZ == 0, lane % NZ == NZ - 1


def halves(load, d, masks):
    high = masks[0]
    if d[1] == 1:
        return jnp.where(high, load(-1), load(0))
    if d[1] == -1:
        return jnp.where(high, load(0), load(1))
    return load(0)


def turns(dz):
    return (1, NZ + 1) if dz == 1 else (LANES - 1, NZ - 1)


def shift_pair(flat, steep, dz, masks):
    edge, source = (masks[1], masks[2]) if dz == 1 else (masks[2], masks[1])
    near, far = turns(dz)
    one = pltpu.roll(jnp.where(source, steep, flat), near, 1)
    two = pltpu.roll(jnp.where(source, flat, steep), far, 1)
    return jnp.where(edge, two, one), jnp.where(edge, one, two)


def shift_steep(tile, dz, masks):
    if dz == 0:
        return pltpu.roll(tile, NZ, 1)
    near, far = turns(dz)
    edge = masks[1] if dz == 1 else masks[2]
    return jnp.where(edge, pltpu.roll(tile, near, 1), pltpu.roll(tile, far, 1))


def shift_lanes(tiles, sign, masks):
    out = list(tiles)
    place = {velocity(i, sign): i for i in range(27)}
    for dx in (-1, 0, 1):
        for dy in (-1, 1):
            i = place[dx, dy, 0]
            out[i] = shift_steep(tiles[i], 0, masks)
        for dz in (-1, 1):
            i, j, k = (place[dx, dy, dz] for dy in (0, 1, -1))
            out[i], out[j] = shift_pair(tiles[i], tiles[j], dz, masks)
            out[k] = shift_steep(tiles[k], dz, masks)
    return out


def stacked(parts):
    return parts[0] if len(parts) == 1 else jnp.concatenate(parts, 0)


def read_rows(ref, base, pieces):
    return stacked([ref[pl.ds(base + r, n), :] for r, n in pieces])


def write_rows(ref, base, pieces, value):
    done = 0
    for r, n in pieces:
        ref[pl.ds(base + r, n), :] = value[done : done + n]
        done += n


def pull_block(g, buf, sign, k, pieces, masks, fields=27):
    base = pl.multiple_of(k * g.panel, 8)
    after = pl.multiple_of(jnp.where(k == g.halo, g.panel, base + g.panel), 8)
    out = []
    for i in range(fields):
        d = velocity(i, sign)

        def load(n, i=i, d=d):
            start = {-1: base - g.panel, 0: base, 1: after}[n]
            return read_rows(buf, start + (g.field(i) - d[0]), pieces)

        out.append(halves(load, d, masks))
    return shift_lanes(out, sign, masks)


def pull_edge(g, buf, sign, side, masks, fields=27):
    out = []
    for i in range(fields):
        d = velocity(i, sign)
        if side == 1:
            row = g.rows - d[0]
        else:
            row = {1: g.rows, 0: g.rows + 1, -1: 0}[d[0]]

        def load(n, i=i, row=row):
            return buf[pl.ds(g.at(i, 1 + n, row), g.cols, stride=g.panel), :]

        out.append(halves(load, d, masks))
    return shift_lanes(out, sign, masks)


def moments(f):
    flat = {}
    along_z = None
    for a in (-1, 0, 1):
        for b in (-1, 0, 1):
            lo, mid, hi = (f[INDEX[(a, b, c)]] for c in (-1, 0, 1))
            flat[a, b] = lo + mid + hi
            diff = hi - lo
            along_z = diff if along_z is None else along_z + diff
    line = {}
    along_y = None
    for a in (-1, 0, 1):
        line[a] = flat[a, -1] + flat[a, 0] + flat[a, 1]
        diff = flat[a, 1] - flat[a, -1]
        along_y = diff if along_y is None else along_y + diff
    return line[-1] + line[0] + line[1], line[1] - line[-1], along_y, along_z


def combos(x, y, z):
    plane = {}
    for a in (-1, 0, 1):
        for b in (-1, 0, 1):
            if (a, b) > (0, 0):
                continue
            if a == 0:
                plane[a, b] = -y if b else None
            else:
                plane[a, b] = -x if b == 0 else (-x - y if b < 0 else y - x)
    out = []
    for a, b, c in VELOCITY[:13]:
        base = plane[a, b]
        if base is None:
            out.append(-z)
        else:
            out.append(base if c == 0 else (base - z if c < 0 else base + z))
    return out


def relax(f, rho, wx, wy, wz, damp, push, solid):
    ux, uy, uz = (wx + push) * damp, wy * damp, wz * damp
    base = 1.0 - 1.5 * (ux * ux + uy * uy + uz * uz)
    keep = 1.0 - 1.0 / RELAX
    gain = rho * (1.0 / RELAX)
    level = [gain * w for w in (8.0 / 27, 2.0 / 27, 1.0 / 54, 1.0 / 216)]
    along = combos(3.0 * ux, 3.0 * uy, 3.0 * uz)
    out = [None] * 27
    for i in range(13):
        j = 26 - i
        even = base + 0.5 * (along[i] * along[i])
        lift = level[NORM[i]]
        out[i] = jnp.where(solid, f[j], keep * f[i] + lift * (even + along[i]))
        out[j] = jnp.where(solid, f[i], keep * f[j] + lift * (even - along[i]))
    out[13] = jnp.where(solid, f[13], keep * f[13] + level[0] * base)
    return out


def pulled_moments(p):
    first = {}
    for a in (-1, 0, 1):
        for b in (-1, 0, 1):
            lo, mid, hi = (p[INDEX[(a, b, c)]] for c in (-1, 0, 1))
            both = lo + hi
            first[a, b] = (4.0 * mid + both, hi - lo, both)
    second = {}
    for a in (-1, 0, 1):
        lo, mid, hi = (first[a, b] for b in (-1, 0, 1))
        b0 = lo[0] + hi[0]
        b1 = lo[1] + hi[1]
        second[a] = dict(
            one=4.0 * mid[0] + b0,
            y=hi[0] - lo[0],
            yy=b0,
            z=4.0 * mid[1] + b1,
            yz=hi[1] - lo[1],
            zz=4.0 * mid[2] + lo[2] + hi[2],
        )
    lo, mid, hi = (second[a] for a in (-1, 0, 1))

    def full(key):
        return 4.0 * mid[key] + lo[key] + hi[key]

    xx = lo["one"] + hi["one"]
    return dict(
        one=4.0 * mid["one"] + xx,
        x=hi["one"] - lo["one"],
        xx=xx,
        y=full("y"),
        xy=hi["y"] - lo["y"],
        yy=full("yy"),
        z=full("z"),
        xz=hi["z"] - lo["z"],
        yz=full("yz"),
        zz=full("zz"),
    )


def adjoint_scalars(p, rho, wx, wy, wz, damp, push, solid):
    ux, uy, uz = (wx + push) * damp, wy * damp, wz * damp
    s = pulled_moments(p)
    scale = 1.0 / (216.0 * RELAX)
    one = s["one"] * scale
    b = [s[k] * (3.0 * scale) for k in ("x", "y", "z")]
    d = {k: s[k] * (9.0 * scale) for k in ("xx", "xy", "yy", "xz", "yz", "zz")}
    qx = d["xx"] * ux + d["xy"] * uy + d["xz"] * uz
    qy = d["xy"] * ux + d["yy"] * uy + d["yz"] * uz
    qz = d["xz"] * ux + d["yz"] * uy + d["zz"] * uz
    linear = b[0] * ux + b[1] * uy + b[2] * uz
    square = ux * ux + uy * uy + uz * uz
    even = one + linear + 0.5 * (qx * ux + qy * uy + qz * uz) - 1.5 * one * square
    three = 3.0 * one
    gx = (b[0] + qx - three * ux) * damp
    gy = (b[1] + qy - three * uy) * damp
    gz = (b[2] + qz - three * uz) * damp
    even = even - (gx * wx + gy * wy + gz * wz)
    porous = jnp.where(solid, 0.0, -rho * (gx * ux + gy * uy + gz * uz))
    return even, gx, gy, gz, porous


def adjoint_spread(p, even, gx, gy, gz, solid):
    keep = 1.0 - 1.0 / RELAX
    along = combos(gx, gy, gz)
    out = [None] * 27
    for i in range(13):
        j = 26 - i
        out[i] = jnp.where(solid, p[j], keep * p[i] + (even + along[i]))
        out[j] = jnp.where(solid, p[i], keep * p[j] + (even - along[i]))
    out[13] = jnp.where(solid, p[13], keep * p[13] + even)
    return out


def x_lines(g, sign, fields, side):
    lines = []
    for i in moving(fields, sign, 0, side):
        if side == 1:
            lines.append((i, g.rows - 1, (-1, g.rows + 1)))
            lines.append((i, g.rows - 2, (g.rows,)))
        else:
            lines += [(i, 0, (g.rows,)), (i, 1, (g.rows + 1,))]
    edge, target = (g.rows - 1, g.rows + 1) if side == 1 else (0, g.rows)
    return lines + [(i, edge, (target,)) for i in moving(fields, sign, 0, 0)]


def pack_x(g, buf, sign, fields, up, down):
    for side, ref in ((1, up), (-1, down)):
        for n, (i, r, _) in enumerate(x_lines(g, sign, fields, side)):
            ref[n * g.cols : (n + 1) * g.cols, :] = buf[
                pl.ds(g.at(i, 1, r), g.cols, stride=g.panel), :
            ]


def unpack_x(g, buf, sign, fields, up, down):
    for side, ref in ((1, up), (-1, down)):
        for n, (i, _, targets) in enumerate(x_lines(g, sign, fields, side)):
            value = ref[n * g.cols : (n + 1) * g.cols, :]
            for r in targets:
                buf[pl.ds(g.at(i, 1, r), g.cols, stride=g.panel), :] = value
    for i in moving(fields, sign, 0, -1):
        buf[pl.ds(g.at(i, 1, g.rows + 2), g.cols, stride=g.panel), :] = buf[
            pl.ds(g.at(i, 1, 0), g.cols, stride=g.panel), :
        ]


def halo_panels(g, i, sign):
    return (0, g.halo) if velocity(i, sign)[1] == 1 else (g.halo,)


def pack_corners(g, buf, sign, fields, up, down):
    for side, ref in ((1, up), (-1, down)):
        for n, (i, r, _) in enumerate(x_lines(g, sign, fields, side)):
            ref[n : n + 1, :] = buf[pl.ds(g.at(i, g.halo, r), 1), :]


def unpack_corners(g, buf, sign, fields, up, down):
    for side, ref in ((1, up), (-1, down)):
        for n, (i, _, targets) in enumerate(x_lines(g, sign, fields, side)):
            value = ref[n : n + 1, :]
            for r in targets:
                for k in halo_panels(g, i, sign):
                    buf[pl.ds(g.at(i, k, r), 1), :] = value
    for i in moving(fields, sign, 0, -1):
        for k in halo_panels(g, i, sign):
            buf[pl.ds(g.at(i, k, g.rows + 2), 1), :] = buf[pl.ds(g.at(i, k, 0), 1), :]


def still_pairs(fields, sign):
    still = moving(fields, sign, 1, 0)
    half = (len(still) + 1) // 2
    return [(still[n], still[n + half] if n + half < len(still) else None) for n in range(half)]


def y_slots(fields, sign):
    return 9 + len(still_pairs(fields, sign))


def pack_y(g, buf, sign, fields, up, down):
    high = lane_masks(g.rows)[0]
    for side, ref in ((1, up), (-1, down)):
        k = g.cols if side == 1 else 1
        for n, i in enumerate(moving(fields, sign, 1, side)):
            ref[n * g.rows : (n + 1) * g.rows, :] = buf[pl.ds(g.at(i, k, 0), g.rows), :]
        for n, (i, j) in enumerate(still_pairs(fields, sign)):
            value = buf[pl.ds(g.at(i, k, 0), g.rows), :]
            if j is not None:
                other = pltpu.roll(buf[pl.ds(g.at(j, k, 0), g.rows), :], NZ, 1)
                pair = (value, other) if side == 1 else (other, value)
                value = jnp.where(high, *pair)
            ref[(9 + n) * g.rows : (10 + n) * g.rows, :] = value


def unpack_y(g, buf, sign, fields, high, up, down):
    for side, ref in ((1, up), (-1, down)):
        for n, i in enumerate(moving(fields, sign, 1, side)):
            value = ref[n * g.rows : (n + 1) * g.rows, :]
            for k in halo_panels(g, i, sign):
                buf[pl.ds(g.at(i, k, 0), g.rows), :] = value
    for n, (i, j) in enumerate(still_pairs(fields, sign)):
        spot = slice((9 + n) * g.rows, (10 + n) * g.rows)
        before, after = up[spot, :], down[spot, :]
        buf[pl.ds(g.at(i, g.halo, 0), g.rows), :] = jnp.where(high, before, after)
        if j is not None:
            value = pltpu.roll(jnp.where(high, after, before), NZ, 1)
            buf[pl.ds(g.at(j, g.halo, 0), g.rows), :] = value


def by_parity(axis, first, second, act):
    even = lax.rem(lax.axis_index(axis), 2) == 0

    @pl.when(even)
    def _():
        act(first, second)

    @pl.when(jnp.logical_not(even))
    def _():
        act(second, first)


def load_fields(ref, rows, base, pieces, count):
    return [read_rows(ref, base + n * rows, pieces) for n in range(count)]


def save_fields(ref, rows, base, pieces, values):
    for n, value in enumerate(values):
        write_rows(ref, base + n * rows, pieces, value)


def save_populations(g, out, k, pieces, values):
    base = pl.multiple_of(k * g.panel, 8)
    for i, value in enumerate(values):
        write_rows(out, base + g.field(i), pieces, value)


def spot_of(g, k):
    return pl.multiple_of((k - 1) * g.rows, 8)


def lanes_of(k):
    return pl.ds(pl.multiple_of((k - 1) * LANES, LANES), LANES)


def every(first, last, act):
    def step(k, carry):
        act(k)
        return carry

    count = last + 1 - first
    unroll = max(n for n in (1, 2, 3, 4, 6, 8) if count % n == 0)
    lax.fori_loop(first, last + 1, step, 0, unroll=unroll)


def side_panels(g, act, count):
    def step(n, carry):
        act(jnp.where(n == 0, 1, g.cols - 1 + n))
        return carry

    lax.fori_loop(0, count, step, 0, unroll=count)


def interior_tiles(g, act):
    for pieces in g.inner:
        every(2, g.cols - 1, functools.partial(act, pieces=pieces))


def middle_tiles(g, act):
    for pieces in g.inner:
        side_panels(g, functools.partial(act, pieces=pieces), 3)
    every(2, g.cols - 1, functools.partial(act, pieces=g.outer))


def core_tiles(g, act):
    for pieces in g.inner:
        every(3, g.cols - 2, functools.partial(act, pieces=pieces))


def near_core_tiles(g, act):
    def step(n, carry):
        for pieces in g.inner:
            act(jnp.where(n == 0, 2, g.cols - 1), pieces=pieces)
        return carry

    lax.fori_loop(0, 2, step, 0, unroll=2)


def rim_tiles(g, act):
    every(1, g.cols, functools.partial(act, pieces=g.outer))
    for pieces in g.inner:
        side_panels(g, functools.partial(act, pieces=pieces), 2)


def step_tile(g, buf, out, sign, fields, masks, compute):
    def act(k, pieces):
        values = compute(
            pull_block(g, buf, sign, k, pieces, masks, fields), spot_of(g, k), pieces
        )
        save_populations(g, out, k, pieces, values)

    return act


def corner_tiles(g, buf, out, sign, fields, masks, compute):
    small = tuple(mask[:8] for mask in masks)
    act = step_tile(g, buf, out, sign, fields, masks, compute)
    side_panels(g, functools.partial(act, pieces=g.outer), 3)
    spot = g.halo * g.rows
    pieces = ((g.rows, 8),)
    values = compute(pull_block(g, buf, sign, g.halo, pieces, small, fields), spot, ((0, 8),))
    for i in range(27):
        dx = velocity(i, sign)[0]
        if dx == -1:
            out[pl.ds(g.at(i, g.halo, g.rows), 1), :] = values[i][0:1]
        elif dx == 1:
            out[pl.ds(g.at(i, g.halo, -1), 1), :] = values[i][1:2]
    edges = [pull_edge(g, buf, sign, side, small, fields) for side in (1, -1)]
    both = [stacked(pair) for pair in zip(*edges)]
    values = compute(both, spot, ((8, 16),))
    for i in moving(27, sign, 0, -1):
        out[pl.ds(g.at(i, 1, g.rows), g.cols, stride=g.panel), :] = values[i][:8]
    for i in moving(27, sign, 0, 1):
        out[pl.ds(g.at(i, 1, -1), g.cols, stride=g.panel), :] = values[i][8:]
    for i in moving(27, sign, 1, 1):
        out[pl.ds(g.at(i, 0, 0), g.rows), :] = out[pl.ds(g.at(i, g.halo, 0), g.rows), :]
        for r in (-1, g.rows):
            out[pl.ds(g.at(i, 0, r), 1), :] = out[pl.ds(g.at(i, g.halo, r), 1), :]


def flow_of(f):
    rho, mx, my, mz = moments(f)
    inverse = 1.0 / rho
    return inverse, rho, mx * inverse, my * inverse, mz * inverse


def collide_first(g, state, out):
    def act(k, pieces, f):
        base = pl.multiple_of(k * g.panel, 8)
        damp, push, wall = (read_rows(out, base + g.field(i), pieces) for i in (27, 28, 29))
        flow = flow_of(f)[1:] + (damp, push)
        save_fields(state, g.local, spot_of(g, k), pieces, flow + (wall,))
        save_populations(g, out, k, pieces, relax(f, *flow, wall > 0.5))

    return act


def collide_second(g, state):
    def compute(values, spot, pieces):
        f, (damp, push, wall) = values[:27], values[27:]
        flow = flow_of(f)[1:] + (damp, push)
        save_fields(state, g.extended, spot, pieces, flow + (wall,))
        return relax(f, *flow, wall > 0.5)

    return compute


def adjoint_second(g, state, total):
    def compute(p, spot, pieces):
        *flow, wall = load_fields(state, g.extended, spot, pieces, 7)
        *spread, porous = adjoint_scalars(p, *flow, wall > 0.5)
        save_fields(total, g.extended, spot, pieces, [porous])
        return adjoint_spread(p, *spread, wall > 0.5)

    return compute


def seed_tile(g, buf, adjoint, stage, out, masks):
    def act(k, pieces):
        f = pull_block(g, buf, 1, k, pieces, masks)
        for i in range(27):
            write_rows(stage.at[k - 1, i], 0, pieces, f[i])
        inverse, _, wx, wy, wz = flow_of(f)
        even = -(wx * wx + wy * wy + wz * wz) * inverse
        along = combos(wx * inverse, wy * inverse, wz * inverse)
        lanes = lanes_of(k)
        seeded = [
            stacked([adjoint[i, pl.ds(r, n), lanes] for r, n in pieces]) + even for i in range(27)
        ]
        for i in range(13):
            seeded[i] = seeded[i] + along[i]
            seeded[26 - i] = seeded[26 - i] - along[i]
        save_populations(g, out, k, pieces, seeded)

    return act


def block_of(ref, k):
    return ref.at[:, :, lanes_of(k)]


def flat_fields(g, out, near, k):
    porosity, solid, labels = near
    lanes = lanes_of(k)
    label = labels[:, lanes]
    damp = 1.0 / (1.0 + porosity[:, lanes])
    push = jnp.where(label == 1, PUSH, jnp.where(label == 2, -PUSH, 0.0))
    base = pl.multiple_of(k * g.panel, 8)
    for i, value in ((27, damp), (28, push), (29, solid[:, lanes].astype(F32))):
        out[pl.ds(base + g.field(i), g.rows), :] = value


def staged_tile(g, collide, stage):
    def act(k, pieces):
        collide(k, pieces, [read_rows(stage.at[k - 1, i], 0, pieces) for i in range(27)])

    return act


def side_tiles(g, act):
    for pieces in (g.outer,) + g.inner:
        side_panels(g, functools.partial(act, pieces=pieces), 2)


def side_first_kernel(g, pops, *refs):
    flat, (out, state, stage), near, faces, (sems, flat_sems) = (
        refs[:3],
        refs[3:6],
        refs[6:9],
        refs[9:11],
        refs[11:],
    )

    def copy(k):
        return pltpu.make_async_copy(block_of(pops, k), stage.at[k - 1], sems.at[k - 1])

    flat_copies = [
        pltpu.make_async_copy(source, target, flat_sems.at[n])
        for n, (source, target) in enumerate(zip(flat, near))
    ]
    for each in flat_copies:
        each.start()
    for k in (1, g.cols, *range(2, g.cols)):
        copy(k).start()
    for each in flat_copies:
        each.wait()
    for k in (1, g.cols):
        flat_fields(g, out, near, k)
    copy(1).wait()
    copy(g.cols).wait()
    side_tiles(g, staged_tile(g, collide_first(g, state, out), stage))
    by_parity("gy", *faces, functools.partial(pack_y, g, out, 1, 30))
    for k in range(2, g.cols):
        copy(k).wait()


def rim_first_kernel(g, _out, _state, stage, *refs):
    near, (out, state), faces = refs[:3], refs[3:5], refs[5:]
    every(2, g.cols - 1, functools.partial(flat_fields, g, out, near))
    act = staged_tile(g, collide_first(g, state, out), stage)
    every(2, g.cols - 1, functools.partial(act, pieces=g.outer))
    by_parity("gx", *faces, functools.partial(pack_x, g, out, 1, 30))


def inner_first_kernel(g, _, _state, stage, post, state0, out, state1):
    masks = lane_masks(16)
    interior_tiles(g, staged_tile(g, collide_first(g, state0, post), stage))
    interior_tiles(g, step_tile(g, post, out, 1, 30, masks, collide_second(g, state1)))


def relay_kernel(g, sign, fields, _, y_second, y_first, buf, first, second):
    high = lane_masks(g.rows)[0]
    by_parity("gy", y_second, y_first, functools.partial(unpack_y, g, buf, sign, fields, high))
    by_parity("gx", first, second, functools.partial(pack_corners, g, buf, sign, fields))


def middle_second_kernel(g, adjoint, post, out, state1, stage, field, x_second, x_first):
    masks = lane_masks(16)
    by_parity("gx", x_second, x_first, functools.partial(unpack_x, g, post, 1, 30))
    middle_tiles(g, step_tile(g, post, out, 1, 30, masks, collide_second(g, state1)))
    core_tiles(g, seed_tile(g, out, adjoint, stage, field, masks))


def side_seed_kernel(g, _post, _out, _state, _stage, _field, second, first, adjoint, *refs):
    post, out, state1, stage, field, *faces = refs
    masks = lane_masks(16)
    by_parity("gx", second, first, functools.partial(unpack_corners, g, post, 1, 30))
    corner_tiles(g, post, out, 1, 30, masks, collide_second(g, state1))
    side_tiles(g, seed_tile(g, out, adjoint, stage, field, masks))
    by_parity("gy", *faces, functools.partial(pack_y, g, field, -1, 27))


def rim_seed_kernel(g, _stage, _field, out, adjoint, stage, field, *faces):
    seed = seed_tile(g, out, adjoint, stage, field, lane_masks(16))
    every(2, g.cols - 1, functools.partial(seed, pieces=g.outer))
    by_parity("gx", *faces, functools.partial(pack_x, g, field, -1, 27))


def early_panels(g):
    return (1, g.cols, *range(3, g.cols // 2 + 1))


def inner_seed_kernel(
    g, post, _stage, _field, state1, adjoint, stage, field, out, total, final, sems
):
    masks = lane_masks(16)

    def copy(k):
        return pltpu.make_async_copy(stage.at[k - 1], block_of(final, k), sems.at[k - 1])

    for k in early_panels(g):
        copy(k).start()
    seed = seed_tile(g, post, adjoint, stage, field, masks)

    near_core_tiles(g, seed)
    interior_tiles(g, step_tile(g, field, out, -1, 27, masks, adjoint_second(g, state1, total)))
    for k in early_panels(g):
        copy(k).wait()


def total_tile(g, out, before, state0, total, parts, masks):
    def act(k, pieces):
        p = pull_block(g, out, -1, k, pieces, masks)
        spot = spot_of(g, k)
        *flow, wall = load_fields(state0, g.local, spot, pieces, 7)
        *spread, porous = adjoint_scalars(p, *flow, wall > 0.5)
        here = load_fields(before, g.extended, spot, pieces, 1)[0] + porous
        save_fields(total, g.local, spot, pieces, [here])
        save_fields(parts, g.local, spot, pieces, spread + [wall])

    return act


def middle_adjoint_kernel(
    g, state1, state0, x_second, x_first, stage, _, field, out, before, total, parts, final, sems
):
    masks = lane_masks(16)
    copies = [
        pltpu.make_async_copy(stage.at[k - 1], block_of(final, k), sems.at[k - 1])
        for k in range(1, g.cols + 1)
        if k not in early_panels(g)
    ]
    for each in copies:
        each.start()
    by_parity("gx", x_second, x_first, functools.partial(unpack_x, g, field, -1, 27))
    middle_tiles(g, step_tile(g, field, out, -1, 27, masks, adjoint_second(g, state1, before)))
    core_tiles(g, total_tile(g, out, before, state0, total, parts, masks))
    for each in copies:
        each.wait()


def total_kernel(g, *refs):
    state1, state0, second, first, field, out, before, total, parts, peak = refs[5:]
    masks = lane_masks(16)
    by_parity("gx", second, first, functools.partial(unpack_corners, g, field, -1, 27))
    corner_tiles(g, field, out, -1, 27, masks, adjoint_second(g, state1, before))
    act = total_tile(g, out, before, state0, total, parts, masks)
    near_core_tiles(g, act)
    rim_tiles(g, act)
    size = 8 * (g.local // 64)
    largest = jnp.zeros((8, LANES), F32)
    for start in range(0, g.local, size):
        value = jnp.abs(total[start : start + size, :]).reshape(-1, 8, LANES)
        largest = jnp.maximum(largest, jnp.max(value, 0))
    peak[...] = largest


def adjoint_kernel(g, first, last, buf, parts, result, stage, sems):
    masks = lane_masks(16)

    def copy(k):
        return pltpu.make_async_copy(stage.at[k - first], block_of(result, k), sems.at[k - first])

    def column(k):
        for pieces in (g.outer,) + g.inner:
            p = pull_block(g, buf, -1, k, pieces, masks)
            *spread, wall = load_fields(parts, g.local, spot_of(g, k), pieces, 5)
            for i, value in enumerate(adjoint_spread(p, *spread, wall > 0.5)):
                write_rows(stage.at[k - first, i], 0, pieces, value)
        copy(k).start()

    every(first, last, column)
    every(first, last, lambda k: copy(k).wait())


def scale_kernel(g, total, peak, out):
    largest = jnp.max(peak[...])
    factor = 1.0 / (jnp.full((g.rows, LANES), largest, F32) + EPS)
    for c in range(g.cols):
        value = total[c * g.rows : (c + 1) * g.rows, :] * factor
        out[:, c * LANES : (c + 1) * LANES] = value


def swap_pairs(count, start):
    pairs = []
    for i in range(start, count, 2):
        j = (i + 1) % count
        pairs += [(i, j), (j, i)]
    return pairs


def swap(axis, count, first, second):
    return (
        lax.ppermute(first, axis, swap_pairs(count, 0)),
        lax.ppermute(second, axis, swap_pairs(count, 1)),
    )


def largest_of_all(peak, sizes, beside):
    nx, ny = sizes
    peak = jnp.maximum(peak, lax.ppermute(peak, "gy", [(i, i ^ 1) for i in range(ny)]))
    groups = 0
    for axis, count, first, widths in (("gy", ny, 2, (4, 4)), ("gx", nx, 1, (4, 2))):
        step = first
        for width in widths:
            width = min(width, count // step)
            parts = []
            for n in range(1, width):
                if axis == "gy":
                    pairs = [(i, i ^ (n * step) ^ 1) for i in range(ny)]
                    parts.append(lax.ppermute(peak, "gy", pairs))
                else:
                    pairs = [
                        (i * ny + y, (i ^ (n * step)) * ny + (y ^ 1))
                        for i in range(nx)
                        for y in range(ny)
                    ]
                    parts.append(lax.ppermute(peak, ("gx", "gy"), pairs))
            groups += 1
            if groups == 1:
                peak = beside(peak)
            peak = functools.reduce(jnp.maximum, parts, peak)
            step *= width
    return peak


def on_device(sizes, populations, adjoint_in, porosity, solid, labels):
    rows, width = porosity.shape
    g = Grid(rows, width)
    in_vmem = pl.BlockSpec(memory_space=pltpu.VMEM)
    in_hbm = pl.BlockSpec(memory_space=pltpu.HBM)
    nx, ny = sizes

    def vmem(*shape):
        return pltpu.VMEM(shape, F32)

    def fields(count, size):
        return vmem(count * size, LANES)

    def padded(count):
        return vmem(*g.padded(count))

    def x_faces(count):
        return [vmem(count * g.cols, LANES)] * 2

    def y_faces(count, sign):
        return [vmem(y_slots(count, sign) * rows, LANES)] * 2

    def corners(count):
        return [vmem(-(-count // 8) * 8, LANES)] * 2

    whole = pltpu.HBM(populations.shape, F32)
    stage = vmem(g.cols, 27, rows, LANES)
    sems = pltpu.SemaphoreType.DMA((g.cols,))

    def call(name, kernel, operands, out_shape, scratch=(), kept=0, load=0, result=None):
        out_shape = [pltpu.VMEM(x.shape, x.dtype) for x in operands[:kept]] + out_shape
        aliases = {n: n for n in range(kept)}
        space = pltpu.HBM if name == "side_first" else pltpu.VMEM
        pinned = [pltpu.with_memory_space_constraint(x, space) for x in operands]
        in_specs = [pl.BlockSpec(memory_space=space)] * len(operands)
        if result is not None:
            aliases[len(operands)] = len(out_shape) - 1
            pinned.append(pltpu.with_memory_space_constraint(result, pltpu.HBM))
            in_specs.append(in_hbm)
        return pl.pallas_call(
            functools.partial(kernel, g),
            in_specs=in_specs,
            out_shape=out_shape,
            out_specs=[in_hbm if x is whole else in_vmem for x in out_shape],
            scratch_shapes=list(scratch),
            input_output_aliases=aliases,
            compiler_params=pltpu.CompilerParams(vmem_limit_bytes=VMEM_LIMIT),
            cost_estimate=pl.CostEstimate(flops=0, bytes_accessed=load, transcendentals=0)
            if load
            else None,
            name=name,
        )(*pinned)

    def swap_faces(axis, count, parcels):
        return swap(axis, count, *parcels)[::-1]

    def relay(buf, parcels, sign, count):
        def kernel(grid, *refs):
            relay_kernel(grid, sign, count, *refs)

        buf, *parcels = call("relay", kernel, [buf, *parcels], corners(count), kept=1)
        return buf, swap("gx", nx, *parcels)[::-1]

    flat_space = [vmem(*porosity.shape)] + [pltpu.VMEM(porosity.shape, jnp.int32)] * 2
    post, state0, staged, *rest = call(
        "side_first",
        side_first_kernel,
        [populations, porosity, solid, labels],
        [padded(30), fields(7, g.local), stage] + flat_space + y_faces(30, 1),
        [sems, pltpu.SemaphoreType.DMA((3,))],
    )
    along_y = swap_faces("gy", ny, rest[3:])
    post, state0, *parcels = call(
        "rim_first",
        rim_first_kernel,
        [post, state0, staged, *rest[:3]],
        x_faces(30),
        kept=2,
        load=FLIGHT,
    )
    along_x = swap_faces("gx", nx, parcels)
    post, state0, second, state1 = call(
        "inner_first",
        inner_first_kernel,
        [post, state0, staged],
        [padded(27), fields(7, g.extended)],
        kept=2,
        load=FLIGHT,
    )
    post, parcels = relay(post, along_y, 1, 30)
    post, second, state1, staged, field = call(
        "middle_second",
        lambda grid, _post, _out, _state, b, a, source, *refs: middle_second_kernel(
            grid, source, *refs, b, a
        ),
        [post, second, state1, *along_x, adjoint_in],
        [stage, padded(27)],
        kept=3,
        load=FLIGHT,
    )
    _, second, state1, staged, field, *parcels = call(
        "side_seed",
        side_seed_kernel,
        [post, second, state1, staged, field, *parcels, adjoint_in],
        y_faces(27, -1),
        kept=5,
    )
    along_y = swap_faces("gy", ny, parcels)
    staged, field, *parcels = call(
        "rim_seed",
        rim_seed_kernel,
        [staged, field, second, adjoint_in],
        x_faces(27),
        kept=2,
        load=FLIGHT,
    )
    along_x = swap_faces("gx", nx, parcels)
    staged, field, pulled, before, final = call(
        "inner_seed",
        lambda grid, kept, into, buf, *refs: inner_seed_kernel(grid, buf, kept, into, *refs),
        [staged, field, second, state1, adjoint_in],
        [padded(27), fields(1, g.extended), whole],
        [sems],
        kept=2,
        load=FLIGHT,
    )
    field, parcels = relay(field, along_y, -1, 27)
    field, pulled, before, total, parts, final = call(
        "middle_adjoint",
        lambda grid, _field, _out, _before, *refs: middle_adjoint_kernel(grid, *refs),
        [field, pulled, before, state1, state0, *along_x, staged],
        [fields(1, g.local), fields(5, g.local), whole],
        [sems],
        kept=3,
        load=FLIGHT,
        result=final,
    )
    _, pulled, _, total, parts, peak = call(
        "total",
        total_kernel,
        [field, pulled, before, total, parts, state1, state0, *parcels],
        [vmem(8, LANES)],
        kept=5,
    )
    half = g.cols // 2
    scratch = [vmem(half, 27, rows, LANES), pltpu.SemaphoreType.DMA((half,))]
    halves = []

    def first_half(peak):
        def kernel(grid, buf, fields, near, echo, *refs):
            echo[...] = near[...]
            adjoint_kernel(grid, 1, half, buf, fields, *refs)

        echo, result = call(
            "adjoint_low",
            kernel,
            [pulled, parts, peak],
            [vmem(8, LANES), whole],
            scratch,
            load=FLIGHT // 2,
        )
        halves.append(result)
        return echo

    largest = largest_of_all(peak, sizes, first_half)
    (adjoint_out,) = call(
        "adjoint_high",
        lambda grid, buf, fields, _, *refs: adjoint_kernel(
            grid, 1 + half, g.cols, buf, fields, *refs
        ),
        [pulled, parts],
        [whole],
        scratch,
        load=FLIGHT // 2,
        result=halves[0],
    )
    (sensitivity,) = call(
        "normalize",
        scale_kernel,
        [total, largest],
        [jax.ShapeDtypeStruct(porosity.shape, F32)],
    )
    return final, adjoint_out, sensitivity


def solution(mesh):
    sizes = (mesh.shape["gx"], mesh.shape["gy"])
    whole, flat = P(None, "gx", "gy"), P("gx", "gy")
    return jax.shard_map(
        functools.partial(on_device, sizes),
        mesh=mesh,
        in_specs=(whole, whole, flat, flat, flat),
        out_specs=(whole, whole, flat),
        check_vma=False,
    )
```

```python
import functools

import jax
import jax.numpy as jnp
from jax import lax
from jax.experimental import pallas as pl
from jax.experimental.pallas import tpu as pltpu
from jax.sharding import PartitionSpec as P

NZ = 64
RELAX = 0.8
PUSH = 0.2
EPS = 1e-06
LANES = 128
VELOCITY = [(a, b, c) for a in (-1, 0, 1) for b in (-1, 0, 1) for c in (-1, 0, 1)]
INDEX = {v: i for i, v in enumerate(VELOCITY)}
WEIGHT = [
    [8.0 / 27, 2.0 / 27, 1.0 / 54, 1.0 / 216][abs(v[0]) + abs(v[1]) + abs(v[2])]
    for v in VELOCITY
]
NORM = [abs(v[0]) + abs(v[1]) + abs(v[2]) for v in VELOCITY]
F32 = jnp.float32
VMEM_LIMIT = 6 * 1024 * 1024
FLIGHT = 12 * 1024 * 1024


class Grid:
    def __init__(self, rows, width):
        self.rows = rows
        self.cols = width // LANES
        self.panel = rows + 16
        self.halo = self.cols + 1
        self.local = self.cols * rows
        self.extended = self.halo * rows + 24
        self.outer = ((0, 8), (rows - 8, 8))
        self.inner = tuple(((r, 16),) for r in range(8, rows - 8, 16))

    def at(self, i, k, r):
        return self.field(i) + k * self.panel + r

    def field(self, i):
        return i * (self.cols + 2) * self.panel + 8

    def padded(self, fields):
        return (fields * (self.cols + 2) * self.panel + 64, LANES)


def velocity(i, sign):
    return tuple(sign * n for n in VELOCITY[i]) if i < 27 else (0, 0, 0)


def moving(fields, sign, axis, side):
    return [i for i in range(fields) if velocity(i, sign)[axis] == side]


def lane_masks(height):
    lane = lax.broadcasted_iota(jnp.int32, (height, LANES), 1)
    return lane >= NZ, lane % NZ == 0, lane % NZ == NZ - 1


def halves(load, d, masks):
    high = masks[0]
    if d[1] == 1:
        return jnp.where(high, load(-1), load(0))
    if d[1] == -1:
        return jnp.where(high, load(0), load(1))
    return load(0)


def turns(dz):
    return (1, NZ + 1) if dz == 1 else (LANES - 1, NZ - 1)


def shift_pair(flat, steep, dz, masks):
    edge, source = (masks[1], masks[2]) if dz == 1 else (masks[2], masks[1])
    near, far = turns(dz)
    one = pltpu.roll(jnp.where(source, steep, flat), near, 1)
    two = pltpu.roll(jnp.where(source, flat, steep), far, 1)
    return jnp.where(edge, two, one), jnp.where(edge, one, two)


def shift_steep(tile, dz, masks):
    if dz == 0:
        return pltpu.roll(tile, NZ, 1)
    near, far = turns(dz)
    edge = masks[1] if dz == 1 else masks[2]
    return jnp.where(edge, pltpu.roll(tile, near, 1), pltpu.roll(tile, far, 1))


def shift_lanes(tiles, sign, masks):
    out = list(tiles)
    place = {velocity(i, sign): i for i in range(27)}
    for dx in (-1, 0, 1):
        for dy in (-1, 1):
            i = place[dx, dy, 0]
            out[i] = shift_steep(tiles[i], 0, masks)
        for dz in (-1, 1):
            i, j, k = (place[dx, dy, dz] for dy in (0, 1, -1))
            out[i], out[j] = shift_pair(tiles[i], tiles[j], dz, masks)
            out[k] = shift_steep(tiles[k], dz, masks)
    return out


def stacked(parts):
    return parts[0] if len(parts) == 1 else jnp.concatenate(parts, 0)


def read_rows(ref, base, pieces):
    return stacked([ref[pl.ds(base + r, n), :] for r, n in pieces])


def write_rows(ref, base, pieces, value):
    done = 0
    for r, n in pieces:
        ref[pl.ds(base + r, n), :] = value[done : done + n]
        done += n


def pull_block(g, buf, sign, k, pieces, masks, fields=27):
    base = pl.multiple_of(k * g.panel, 8)
    after = pl.multiple_of(jnp.where(k == g.halo, g.panel, base + g.panel), 8)
    out = []
    for i in range(fields):
        d = velocity(i, sign)

        def load(n, i=i, d=d):
            start = {-1: base - g.panel, 0: base, 1: after}[n]
            return read_rows(buf, start + (g.field(i) - d[0]), pieces)

        out.append(halves(load, d, masks))
    return shift_lanes(out, sign, masks)


def pull_edge(g, buf, sign, side, masks, fields=27):
    out = []
    for i in range(fields):
        d = velocity(i, sign)
        if side == 1:
            row = g.rows - d[0]
        else:
            row = {1: g.rows, 0: g.rows + 1, -1: 0}[d[0]]

        def load(n, i=i, row=row):
            return buf[pl.ds(g.at(i, 1 + n, row), g.cols, stride=g.panel), :]

        out.append(halves(load, d, masks))
    return shift_lanes(out, sign, masks)


def moments(f):
    flat = {}
    along_z = None
    for a in (-1, 0, 1):
        for b in (-1, 0, 1):
            lo, mid, hi = (f[INDEX[(a, b, c)]] for c in (-1, 0, 1))
            flat[a, b] = lo + mid + hi
            diff = hi - lo
            along_z = diff if along_z is None else along_z + diff
    line = {}
    along_y = None
    for a in (-1, 0, 1):
        line[a] = flat[a, -1] + flat[a, 0] + flat[a, 1]
        diff = flat[a, 1] - flat[a, -1]
        along_y = diff if along_y is None else along_y + diff
    return line[-1] + line[0] + line[1], line[1] - line[-1], along_y, along_z


def combos(x, y, z):
    plane = {}
    for a in (-1, 0, 1):
        for b in (-1, 0, 1):
            if (a, b) > (0, 0):
                continue
            if a == 0:
                plane[a, b] = -y if b else None
            else:
                plane[a, b] = -x if b == 0 else (-x - y if b < 0 else y - x)
    out = []
    for a, b, c in VELOCITY[:13]:
        base = plane[a, b]
        if base is None:
            out.append(-z)
        else:
            out.append(base if c == 0 else (base - z if c < 0 else base + z))
    return out


def relax(f, rho, wx, wy, wz, damp, push, solid):
    ux, uy, uz = (wx + push) * damp, wy * damp, wz * damp
    base = 1.0 - 1.5 * (ux * ux + uy * uy + uz * uz)
    keep = 1.0 - 1.0 / RELAX
    gain = rho * (1.0 / RELAX)
    level = [gain * w for w in (8.0 / 27, 2.0 / 27, 1.0 / 54, 1.0 / 216)]
    along = combos(3.0 * ux, 3.0 * uy, 3.0 * uz)
    out = [None] * 27
    for i in range(13):
        j = 26 - i
        even = base + 0.5 * (along[i] * along[i])
        lift = level[NORM[i]]
        out[i] = jnp.where(solid, f[j], keep * f[i] + lift * (even + along[i]))
        out[j] = jnp.where(solid, f[i], keep * f[j] + lift * (even - along[i]))
    out[13] = jnp.where(solid, f[13], keep * f[13] + level[0] * base)
    return out


def pulled_moments(p):
    first = {}
    for a in (-1, 0, 1):
        for b in (-1, 0, 1):
            lo, mid, hi = (p[INDEX[(a, b, c)]] for c in (-1, 0, 1))
            both = lo + hi
            first[a, b] = (4.0 * mid + both, hi - lo, both)
    second = {}
    for a in (-1, 0, 1):
        lo, mid, hi = (first[a, b] for b in (-1, 0, 1))
        b0 = lo[0] + hi[0]
        b1 = lo[1] + hi[1]
        second[a] = dict(
            one=4.0 * mid[0] + b0,
            y=hi[0] - lo[0],
            yy=b0,
            z=4.0 * mid[1] + b1,
            yz=hi[1] - lo[1],
            zz=4.0 * mid[2] + lo[2] + hi[2],
        )
    lo, mid, hi = (second[a] for a in (-1, 0, 1))

    def full(key):
        return 4.0 * mid[key] + lo[key] + hi[key]

    xx = lo["one"] + hi["one"]
    return dict(
        one=4.0 * mid["one"] + xx,
        x=hi["one"] - lo["one"],
        xx=xx,
        y=full("y"),
        xy=hi["y"] - lo["y"],
        yy=full("yy"),
        z=full("z"),
        xz=hi["z"] - lo["z"],
        yz=full("yz"),
        zz=full("zz"),
    )


def adjoint_scalars(p, rho, wx, wy, wz, damp, push, solid):
    ux, uy, uz = (wx + push) * damp, wy * damp, wz * damp
    s = pulled_moments(p)
    scale = 1.0 / (216.0 * RELAX)
    one = s["one"] * scale
    b = [s[k] * (3.0 * scale) for k in ("x", "y", "z")]
    d = {k: s[k] * (9.0 * scale) for k in ("xx", "xy", "yy", "xz", "yz", "zz")}
    qx = d["xx"] * ux + d["xy"] * uy + d["xz"] * uz
    qy = d["xy"] * ux + d["yy"] * uy + d["yz"] * uz
    qz = d["xz"] * ux + d["yz"] * uy + d["zz"] * uz
    linear = b[0] * ux + b[1] * uy + b[2] * uz
    square = ux * ux + uy * uy + uz * uz
    even = one + linear + 0.5 * (qx * ux + qy * uy + qz * uz) - 1.5 * one * square
    three = 3.0 * one
    gx = (b[0] + qx - three * ux) * damp
    gy = (b[1] + qy - three * uy) * damp
    gz = (b[2] + qz - three * uz) * damp
    even = even - (gx * wx + gy * wy + gz * wz)
    porous = jnp.where(solid, 0.0, -rho * (gx * ux + gy * uy + gz * uz))
    return even, gx, gy, gz, porous


def adjoint_spread(p, even, gx, gy, gz, solid):
    keep = 1.0 - 1.0 / RELAX
    along = combos(gx, gy, gz)
    out = [None] * 27
    for i in range(13):
        j = 26 - i
        out[i] = jnp.where(solid, p[j], keep * p[i] + (even + along[i]))
        out[j] = jnp.where(solid, p[i], keep * p[j] + (even - along[i]))
    out[13] = jnp.where(solid, p[13], keep * p[13] + even)
    return out


def x_lines(g, sign, fields, side):
    lines = []
    for i in moving(fields, sign, 0, side):
        if side == 1:
            lines.append((i, g.rows - 1, (-1, g.rows + 1)))
            lines.append((i, g.rows - 2, (g.rows,)))
        else:
            lines += [(i, 0, (g.rows,)), (i, 1, (g.rows + 1,))]
    edge, target = (g.rows - 1, g.rows + 1) if side == 1 else (0, g.rows)
    return lines + [(i, edge, (target,)) for i in moving(fields, sign, 0, 0)]


def pack_x(g, buf, sign, fields, up, down):
    for side, ref in ((1, up), (-1, down)):
        for n, (i, r, _) in enumerate(x_lines(g, sign, fields, side)):
            ref[n * g.cols : (n + 1) * g.cols, :] = buf[
                pl.ds(g.at(i, 1, r), g.cols, stride=g.panel), :
            ]


def unpack_x(g, buf, sign, fields, up, down):
    for side, ref in ((1, up), (-1, down)):
        for n, (i, _, targets) in enumerate(x_lines(g, sign, fields, side)):
            value = ref[n * g.cols : (n + 1) * g.cols, :]
            for r in targets:
                buf[pl.ds(g.at(i, 1, r), g.cols, stride=g.panel), :] = value
    for i in moving(fields, sign, 0, -1):
        buf[pl.ds(g.at(i, 1, g.rows + 2), g.cols, stride=g.panel), :] = buf[
            pl.ds(g.at(i, 1, 0), g.cols, stride=g.panel), :
        ]


def halo_panels(g, i, sign):
    return (0, g.halo) if velocity(i, sign)[1] == 1 else (g.halo,)


def pack_corners(g, buf, sign, fields, up, down):
    for side, ref in ((1, up), (-1, down)):
        for n, (i, r, _) in enumerate(x_lines(g, sign, fields, side)):
            ref[n : n + 1, :] = buf[pl.ds(g.at(i, g.halo, r), 1), :]


def unpack_corners(g, buf, sign, fields, up, down):
    for side, ref in ((1, up), (-1, down)):
        for n, (i, _, targets) in enumerate(x_lines(g, sign, fields, side)):
            value = ref[n : n + 1, :]
            for r in targets:
                for k in halo_panels(g, i, sign):
                    buf[pl.ds(g.at(i, k, r), 1), :] = value
    for i in moving(fields, sign, 0, -1):
        for k in halo_panels(g, i, sign):
            buf[pl.ds(g.at(i, k, g.rows + 2), 1), :] = buf[pl.ds(g.at(i, k, 0), 1), :]


def still_pairs(fields, sign):
    still = moving(fields, sign, 1, 0)
    half = (len(still) + 1) // 2
    return [(still[n], still[n + half] if n + half < len(still) else None) for n in range(half)]


def y_slots(fields, sign):
    return 9 + len(still_pairs(fields, sign))


def pack_y(g, buf, sign, fields, up, down):
    high = lane_masks(g.rows)[0]
    for side, ref in ((1, up), (-1, down)):
        k = g.cols if side == 1 else 1
        for n, i in enumerate(moving(fields, sign, 1, side)):
            ref[n * g.rows : (n + 1) * g.rows, :] = buf[pl.ds(g.at(i, k, 0), g.rows), :]
        for n, (i, j) in enumerate(still_pairs(fields, sign)):
            value = buf[pl.ds(g.at(i, k, 0), g.rows), :]
            if j is not None:
                other = pltpu.roll(buf[pl.ds(g.at(j, k, 0), g.rows), :], NZ, 1)
                pair = (value, other) if side == 1 else (other, value)
                value = jnp.where(high, *pair)
            ref[(9 + n) * g.rows : (10 + n) * g.rows, :] = value


def unpack_y(g, buf, sign, fields, high, up, down):
    for side, ref in ((1, up), (-1, down)):
        for n, i in enumerate(moving(fields, sign, 1, side)):
            value = ref[n * g.rows : (n + 1) * g.rows, :]
            for k in halo_panels(g, i, sign):
                buf[pl.ds(g.at(i, k, 0), g.rows), :] = value
    for n, (i, j) in enumerate(still_pairs(fields, sign)):
        spot = slice((9 + n) * g.rows, (10 + n) * g.rows)
        before, after = up[spot, :], down[spot, :]
        buf[pl.ds(g.at(i, g.halo, 0), g.rows), :] = jnp.where(high, before, after)
        if j is not None:
            value = pltpu.roll(jnp.where(high, after, before), NZ, 1)
            buf[pl.ds(g.at(j, g.halo, 0), g.rows), :] = value


def by_parity(axis, first, second, act):
    even = lax.rem(lax.axis_index(axis), 2) == 0

    @pl.when(even)
    def _():
        act(first, second)

    @pl.when(jnp.logical_not(even))
    def _():
        act(second, first)


def load_fields(ref, rows, base, pieces, count):
    return [read_rows(ref, base + n * rows, pieces) for n in range(count)]


def save_fields(ref, rows, base, pieces, values):
    for n, value in enumerate(values):
        write_rows(ref, base + n * rows, pieces, value)


def save_populations(g, out, k, pieces, values):
    base = pl.multiple_of(k * g.panel, 8)
    for i, value in enumerate(values):
        write_rows(out, base + g.field(i), pieces, value)


def spot_of(g, k):
    return pl.multiple_of((k - 1) * g.rows, 8)


def lanes_of(k):
    return pl.ds(pl.multiple_of((k - 1) * LANES, LANES), LANES)


def every(first, last, act):
    def step(k, carry):
        act(k)
        return carry

    count = last + 1 - first
    unroll = max(n for n in (1, 2, 3, 4, 6, 8) if count % n == 0)
    lax.fori_loop(first, last + 1, step, 0, unroll=unroll)


def side_panels(g, act, count):
    def step(n, carry):
        act(jnp.where(n == 0, 1, g.cols - 1 + n))
        return carry

    lax.fori_loop(0, count, step, 0, unroll=count)


def interior_tiles(g, act):
    for pieces in g.inner:
        every(2, g.cols - 1, functools.partial(act, pieces=pieces))


def middle_tiles(g, act):
    for pieces in g.inner:
        side_panels(g, functools.partial(act, pieces=pieces), 3)
    every(2, g.cols - 1, functools.partial(act, pieces=g.outer))


def core_tiles(g, act):
    for pieces in g.inner:
        every(3, g.cols - 2, functools.partial(act, pieces=pieces))


def near_core_tiles(g, act):
    def step(n, carry):
        for pieces in g.inner:
            act(jnp.where(n == 0, 2, g.cols - 1), pieces=pieces)
        return carry

    lax.fori_loop(0, 2, step, 0, unroll=2)


def rim_tiles(g, act):
    every(1, g.cols, functools.partial(act, pieces=g.outer))
    for pieces in g.inner:
        side_panels(g, functools.partial(act, pieces=pieces), 2)


def step_tile(g, buf, out, sign, fields, masks, compute):
    def act(k, pieces):
        values = compute(
            pull_block(g, buf, sign, k, pieces, masks, fields), spot_of(g, k), pieces
        )
        save_populations(g, out, k, pieces, values)

    return act


def corner_tiles(g, buf, out, sign, fields, masks, compute):
    small = tuple(mask[:8] for mask in masks)
    act = step_tile(g, buf, out, sign, fields, masks, compute)
    side_panels(g, functools.partial(act, pieces=g.outer), 3)
    spot = g.halo * g.rows
    pieces = ((g.rows, 8),)
    values = compute(pull_block(g, buf, sign, g.halo, pieces, small, fields), spot, ((0, 8),))
    for i in range(27):
        dx = velocity(i, sign)[0]
        if dx == -1:
            out[pl.ds(g.at(i, g.halo, g.rows), 1), :] = values[i][0:1]
        elif dx == 1:
            out[pl.ds(g.at(i, g.halo, -1), 1), :] = values[i][1:2]
    edges = [pull_edge(g, buf, sign, side, small, fields) for side in (1, -1)]
    both = [stacked(pair) for pair in zip(*edges)]
    values = compute(both, spot, ((8, 16),))
    for i in moving(27, sign, 0, -1):
        out[pl.ds(g.at(i, 1, g.rows), g.cols, stride=g.panel), :] = values[i][:8]
    for i in moving(27, sign, 0, 1):
        out[pl.ds(g.at(i, 1, -1), g.cols, stride=g.panel), :] = values[i][8:]
    for i in moving(27, sign, 1, 1):
        out[pl.ds(g.at(i, 0, 0), g.rows), :] = out[pl.ds(g.at(i, g.halo, 0), g.rows), :]
        for r in (-1, g.rows):
            out[pl.ds(g.at(i, 0, r), 1), :] = out[pl.ds(g.at(i, g.halo, r), 1), :]


def flow_of(f):
    rho, mx, my, mz = moments(f)
    inverse = 1.0 / rho
    return inverse, rho, mx * inverse, my * inverse, mz * inverse


def collide_first(g, state, out):
    def act(k, pieces, f):
        base = pl.multiple_of(k * g.panel, 8)
        damp, push, wall = (read_rows(out, base + g.field(i), pieces) for i in (27, 28, 29))
        flow = flow_of(f)[1:] + (damp, push)
        save_fields(state, g.local, spot_of(g, k), pieces, flow + (wall,))
        save_populations(g, out, k, pieces, relax(f, *flow, wall > 0.5))

    return act


def collide_second(g, state):
    def compute(values, spot, pieces):
        f, (damp, push, wall) = values[:27], values[27:]
        flow = flow_of(f)[1:] + (damp, push)
        save_fields(state, g.extended, spot, pieces, flow + (wall,))
        return relax(f, *flow, wall > 0.5)

    return compute


def adjoint_second(g, state, total):
    def compute(p, spot, pieces):
        *flow, wall = load_fields(state, g.extended, spot, pieces, 7)
        *spread, porous = adjoint_scalars(p, *flow, wall > 0.5)
        save_fields(total, g.extended, spot, pieces, [porous])
        return adjoint_spread(p, *spread, wall > 0.5)

    return compute


def seed_tile(g, buf, adjoint, stage, out, masks):
    def act(k, pieces):
        f = pull_block(g, buf, 1, k, pieces, masks)
        for i in range(27):
            write_rows(stage.at[k - 1, i], 0, pieces, f[i])
        inverse, _, wx, wy, wz = flow_of(f)
        even = -(wx * wx + wy * wy + wz * wz) * inverse
        along = combos(wx * inverse, wy * inverse, wz * inverse)
        lanes = lanes_of(k)
        seeded = [
            stacked([adjoint[i, pl.ds(r, n), lanes] for r, n in pieces]) + even for i in range(27)
        ]
        for i in range(13):
            seeded[i] = seeded[i] + along[i]
            seeded[26 - i] = seeded[26 - i] - along[i]
        save_populations(g, out, k, pieces, seeded)

    return act


def block_of(ref, k):
    return ref.at[:, :, lanes_of(k)]


def flat_fields(g, out, near, k):
    porosity, solid, labels = near
    lanes = lanes_of(k)
    label = labels[:, lanes]
    damp = 1.0 / (1.0 + porosity[:, lanes])
    push = jnp.where(label == 1, PUSH, jnp.where(label == 2, -PUSH, 0.0))
    base = pl.multiple_of(k * g.panel, 8)
    for i, value in ((27, damp), (28, push), (29, solid[:, lanes].astype(F32))):
        out[pl.ds(base + g.field(i), g.rows), :] = value


def staged_tile(g, collide, stage):
    def act(k, pieces):
        collide(k, pieces, [read_rows(stage.at[k - 1, i], 0, pieces) for i in range(27)])

    return act


def side_tiles(g, act):
    for pieces in (g.outer,) + g.inner:
        side_panels(g, functools.partial(act, pieces=pieces), 2)


def side_first_kernel(g, pops, *refs):
    flat, (out, state, stage), near, faces, (sems, flat_sems) = (
        refs[:3],
        refs[3:6],
        refs[6:9],
        refs[9:11],
        refs[11:],
    )

    def copy(k, r, n):
        rows = pl.ds(r, n)
        source = pops.at[:, rows, lanes_of(k)]
        part = 1 if r else 0
        return pltpu.make_async_copy(source, stage.at[k - 1, :, rows], sems.at[k - 1, part])

    flat_copies = [
        pltpu.make_async_copy(source, target, flat_sems.at[n])
        for n, (source, target) in enumerate(zip(flat, near))
    ]
    for each in flat_copies:
        each.start()
    for k in (1, g.cols):
        copy(k, 0, g.rows).start()
    for k in range(2, g.cols):
        for piece in g.outer:
            copy(k, *piece).start()
    for each in flat_copies:
        each.wait()
    for k in (1, g.cols):
        flat_fields(g, out, near, k)
    for k in (1, g.cols):
        copy(k, 0, g.rows).wait()
    side_tiles(g, staged_tile(g, collide_first(g, state, out), stage))
    by_parity("gy", *faces, functools.partial(pack_y, g, out, 1, 30))
    for k in range(2, g.cols):
        for piece in g.outer:
            copy(k, *piece).wait()


def rim_first_kernel(g, _out, _state, stage, *refs):
    near, (out, state), faces = refs[:3], refs[3:5], refs[5:]
    every(2, g.cols - 1, functools.partial(flat_fields, g, out, near))
    act = staged_tile(g, collide_first(g, state, out), stage)
    every(2, g.cols - 1, functools.partial(act, pieces=g.outer))
    by_parity("gx", *faces, functools.partial(pack_x, g, out, 1, 30))


def inner_first_kernel(g, _, _state, pops, post, state0, out, state1):
    masks = lane_masks(16)
    collide = collide_first(g, state0, post)

    def act(k, pieces):
        lanes = lanes_of(k)
        f = [stacked([pops[i, pl.ds(r, n), lanes] for r, n in pieces]) for i in range(27)]
        collide(k, pieces, f)

    interior_tiles(g, act)
    interior_tiles(g, step_tile(g, post, out, 1, 30, masks, collide_second(g, state1)))


def relay_kernel(g, sign, fields, _, y_second, y_first, buf, first, second):
    high = lane_masks(g.rows)[0]
    by_parity("gy", y_second, y_first, functools.partial(unpack_y, g, buf, sign, fields, high))
    by_parity("gx", first, second, functools.partial(pack_corners, g, buf, sign, fields))


def middle_second_kernel(g, adjoint, post, out, state1, stage, field, x_second, x_first):
    masks = lane_masks(16)
    by_parity("gx", x_second, x_first, functools.partial(unpack_x, g, post, 1, 30))
    middle_tiles(g, step_tile(g, post, out, 1, 30, masks, collide_second(g, state1)))
    core_tiles(g, seed_tile(g, out, adjoint, stage, field, masks))


def side_seed_kernel(g, _post, _out, _state, _stage, _field, second, first, adjoint, *refs):
    post, out, state1, stage, field, *faces = refs
    masks = lane_masks(16)
    by_parity("gx", second, first, functools.partial(unpack_corners, g, post, 1, 30))
    corner_tiles(g, post, out, 1, 30, masks, collide_second(g, state1))
    side_tiles(g, seed_tile(g, out, adjoint, stage, field, masks))
    by_parity("gy", *faces, functools.partial(pack_y, g, field, -1, 27))


def rim_seed_kernel(g, _stage, _field, out, adjoint, stage, field, *faces):
    seed = seed_tile(g, out, adjoint, stage, field, lane_masks(16))
    every(2, g.cols - 1, functools.partial(seed, pieces=g.outer))
    by_parity("gx", *faces, functools.partial(pack_x, g, field, -1, 27))


def early_panels(g):
    return (1, g.cols, *range(3, g.cols // 2 + 1))


def inner_seed_kernel(
    g, post, _stage, _field, state1, adjoint, stage, field, out, total, final, sems
):
    masks = lane_masks(16)

    def copy(k):
        return pltpu.make_async_copy(stage.at[k - 1], block_of(final, k), sems.at[k - 1])

    for k in early_panels(g):
        copy(k).start()
    seed = seed_tile(g, post, adjoint, stage, field, masks)

    near_core_tiles(g, seed)
    interior_tiles(g, step_tile(g, field, out, -1, 27, masks, adjoint_second(g, state1, total)))
    for k in early_panels(g):
        copy(k).wait()


def total_tile(g, out, before, state0, total, parts, masks):
    def act(k, pieces):
        p = pull_block(g, out, -1, k, pieces, masks)
        spot = spot_of(g, k)
        *flow, wall = load_fields(state0, g.local, spot, pieces, 7)
        *spread, porous = adjoint_scalars(p, *flow, wall > 0.5)
        here = load_fields(before, g.extended, spot, pieces, 1)[0] + porous
        save_fields(total, g.local, spot, pieces, [here])
        save_fields(parts, g.local, spot, pieces, spread + [wall])

    return act


def middle_adjoint_kernel(
    g, state1, state0, x_second, x_first, stage, _, field, out, before, total, parts, final, sems
):
    masks = lane_masks(16)
    copies = [
        pltpu.make_async_copy(stage.at[k - 1], block_of(final, k), sems.at[k - 1])
        for k in range(1, g.cols + 1)
        if k not in early_panels(g)
    ]
    for each in copies:
        each.start()
    by_parity("gx", x_second, x_first, functools.partial(unpack_x, g, field, -1, 27))
    middle_tiles(g, step_tile(g, field, out, -1, 27, masks, adjoint_second(g, state1, before)))
    core_tiles(g, total_tile(g, out, before, state0, total, parts, masks))
    for each in copies:
        each.wait()


def total_kernel(g, *refs):
    state1, state0, second, first, field, out, before, total, parts, peak = refs[5:]
    masks = lane_masks(16)
    by_parity("gx", second, first, functools.partial(unpack_corners, g, field, -1, 27))
    corner_tiles(g, field, out, -1, 27, masks, adjoint_second(g, state1, before))
    act = total_tile(g, out, before, state0, total, parts, masks)
    near_core_tiles(g, act)
    rim_tiles(g, act)
    size = 8 * (g.local // 64)
    largest = jnp.zeros((8, LANES), F32)
    for start in range(0, g.local, size):
        value = jnp.abs(total[start : start + size, :]).reshape(-1, 8, LANES)
        largest = jnp.maximum(largest, jnp.max(value, 0))
    peak[...] = largest


def adjoint_kernel(g, first, last, buf, parts, result, stage, sems):
    masks = lane_masks(16)

    def copy(k):
        return pltpu.make_async_copy(stage.at[k - first], block_of(result, k), sems.at[k - first])

    def column(k):
        for pieces in (g.outer,) + g.inner:
            p = pull_block(g, buf, -1, k, pieces, masks)
            *spread, wall = load_fields(parts, g.local, spot_of(g, k), pieces, 5)
            for i, value in enumerate(adjoint_spread(p, *spread, wall > 0.5)):
                write_rows(stage.at[k - first, i], 0, pieces, value)
        copy(k).start()

    every(first, last, column)
    every(first, last, lambda k: copy(k).wait())


def scale_kernel(g, total, peak, out):
    largest = jnp.max(peak[...])
    factor = 1.0 / (jnp.full((g.rows, LANES), largest, F32) + EPS)
    for c in range(g.cols):
        value = total[c * g.rows : (c + 1) * g.rows, :] * factor
        out[:, c * LANES : (c + 1) * LANES] = value


def swap_pairs(count, start):
    pairs = []
    for i in range(start, count, 2):
        j = (i + 1) % count
        pairs += [(i, j), (j, i)]
    return pairs


def swap(axis, count, first, second):
    return (
        lax.ppermute(first, axis, swap_pairs(count, 0)),
        lax.ppermute(second, axis, swap_pairs(count, 1)),
    )


def largest_of_all(peak, sizes, beside):
    nx, ny = sizes
    peak = jnp.maximum(peak, lax.ppermute(peak, "gy", [(i, i ^ 1) for i in range(ny)]))
    groups = 0
    for axis, count, first, widths in (("gy", ny, 2, (4, 4)), ("gx", nx, 1, (4, 2))):
        step = first
        for width in widths:
            width = min(width, count // step)
            parts = []
            for n in range(1, width):
                if axis == "gy":
                    pairs = [(i, i ^ (n * step) ^ 1) for i in range(ny)]
                    parts.append(lax.ppermute(peak, "gy", pairs))
                else:
                    pairs = [
                        (i * ny + y, (i ^ (n * step)) * ny + (y ^ 1))
                        for i in range(nx)
                        for y in range(ny)
                    ]
                    parts.append(lax.ppermute(peak, ("gx", "gy"), pairs))
            groups += 1
            if groups == 1:
                peak = beside(peak)
            peak = functools.reduce(jnp.maximum, parts, peak)
            step *= width
    return peak


def on_device(sizes, populations, adjoint_in, porosity, solid, labels):
    rows, width = porosity.shape
    g = Grid(rows, width)
    in_vmem = pl.BlockSpec(memory_space=pltpu.VMEM)
    in_hbm = pl.BlockSpec(memory_space=pltpu.HBM)
    nx, ny = sizes

    def vmem(*shape):
        return pltpu.VMEM(shape, F32)

    def fields(count, size):
        return vmem(count * size, LANES)

    def padded(count):
        return vmem(*g.padded(count))

    def x_faces(count):
        return [vmem(count * g.cols, LANES)] * 2

    def y_faces(count, sign):
        return [vmem(y_slots(count, sign) * rows, LANES)] * 2

    def corners(count):
        return [vmem(-(-count // 8) * 8, LANES)] * 2

    whole = pltpu.HBM(populations.shape, F32)
    stage = vmem(g.cols, 27, rows, LANES)
    sems = pltpu.SemaphoreType.DMA((g.cols,))

    def call(name, kernel, operands, out_shape, scratch=(), kept=0, load=0, result=None):
        out_shape = [pltpu.VMEM(x.shape, x.dtype) for x in operands[:kept]] + out_shape
        aliases = {n: n for n in range(kept)}
        space = pltpu.HBM if name == "side_first" else pltpu.VMEM
        pinned = [pltpu.with_memory_space_constraint(x, space) for x in operands]
        in_specs = [pl.BlockSpec(memory_space=space)] * len(operands)
        if result is not None:
            aliases[len(operands)] = len(out_shape) - 1
            pinned.append(pltpu.with_memory_space_constraint(result, pltpu.HBM))
            in_specs.append(in_hbm)
        return pl.pallas_call(
            functools.partial(kernel, g),
            in_specs=in_specs,
            out_shape=out_shape,
            out_specs=[in_hbm if x is whole else in_vmem for x in out_shape],
            scratch_shapes=list(scratch),
            input_output_aliases=aliases,
            compiler_params=pltpu.CompilerParams(vmem_limit_bytes=VMEM_LIMIT),
            cost_estimate=pl.CostEstimate(flops=0, bytes_accessed=load, transcendentals=0)
            if load
            else None,
            name=name,
        )(*pinned)

    def swap_faces(axis, count, parcels):
        return swap(axis, count, *parcels)[::-1]

    def relay(buf, parcels, sign, count):
        def kernel(grid, *refs):
            relay_kernel(grid, sign, count, *refs)

        buf, *parcels = call("relay", kernel, [buf, *parcels], corners(count), kept=1)
        return buf, swap("gx", nx, *parcels)[::-1]

    flat_space = [vmem(*porosity.shape)] + [pltpu.VMEM(porosity.shape, jnp.int32)] * 2
    post, state0, staged, *rest = call(
        "side_first",
        side_first_kernel,
        [populations, porosity, solid, labels],
        [padded(30), fields(7, g.local), stage] + flat_space + y_faces(30, 1),
        [pltpu.SemaphoreType.DMA((g.cols, 2)), pltpu.SemaphoreType.DMA((3,))],
    )
    along_y = swap_faces("gy", ny, rest[3:])
    post, state0, *parcels = call(
        "rim_first",
        rim_first_kernel,
        [post, state0, staged, *rest[:3]],
        x_faces(30),
        kept=2,
        load=FLIGHT,
    )
    along_x = swap_faces("gx", nx, parcels)
    post, state0, second, state1 = call(
        "inner_first",
        inner_first_kernel,
        [post, state0, populations],
        [padded(27), fields(7, g.extended)],
        kept=2,
        load=FLIGHT,
    )
    post, parcels = relay(post, along_y, 1, 30)
    post, second, state1, staged, field = call(
        "middle_second",
        lambda grid, _post, _out, _state, b, a, source, *refs: middle_second_kernel(
            grid, source, *refs, b, a
        ),
        [post, second, state1, *along_x, adjoint_in],
        [stage, padded(27)],
        kept=3,
        load=FLIGHT,
    )
    _, second, state1, staged, field, *parcels = call(
        "side_seed",
        side_seed_kernel,
        [post, second, state1, staged, field, *parcels, adjoint_in],
        y_faces(27, -1),
        kept=5,
    )
    along_y = swap_faces("gy", ny, parcels)
    staged, field, *parcels = call(
        "rim_seed",
        rim_seed_kernel,
        [staged, field, second, adjoint_in],
        x_faces(27),
        kept=2,
        load=FLIGHT,
    )
    along_x = swap_faces("gx", nx, parcels)
    staged, field, pulled, before, final = call(
        "inner_seed",
        lambda grid, kept, into, buf, *refs: inner_seed_kernel(grid, buf, kept, into, *refs),
        [staged, field, second, state1, adjoint_in],
        [padded(27), fields(1, g.extended), whole],
        [sems],
        kept=2,
        load=FLIGHT,
    )
    field, parcels = relay(field, along_y, -1, 27)
    field, pulled, before, total, parts, final = call(
        "middle_adjoint",
        lambda grid, _field, _out, _before, *refs: middle_adjoint_kernel(grid, *refs),
        [field, pulled, before, state1, state0, *along_x, staged],
        [fields(1, g.local), fields(5, g.local), whole],
        [sems],
        kept=3,
        load=FLIGHT,
        result=final,
    )
    _, pulled, _, total, parts, peak = call(
        "total",
        total_kernel,
        [field, pulled, before, total, parts, state1, state0, *parcels],
        [vmem(8, LANES)],
        kept=5,
    )
    half = g.cols // 2
    scratch = [vmem(half, 27, rows, LANES), pltpu.SemaphoreType.DMA((half,))]
    halves = []

    def first_half(peak):
        def kernel(grid, buf, fields, near, echo, *refs):
            echo[...] = near[...]
            adjoint_kernel(grid, 1, half, buf, fields, *refs)

        echo, result = call(
            "adjoint_low",
            kernel,
            [pulled, parts, peak],
            [vmem(8, LANES), whole],
            scratch,
            load=FLIGHT // 2,
        )
        halves.append(result)
        return echo

    largest = largest_of_all(peak, sizes, first_half)
    (adjoint_out,) = call(
        "adjoint_high",
        lambda grid, buf, fields, _, *refs: adjoint_kernel(
            grid, 1 + half, g.cols, buf, fields, *refs
        ),
        [pulled, parts],
        [whole],
        scratch,
        load=FLIGHT // 2,
        result=halves[0],
    )
    (sensitivity,) = call(
        "normalize",
        scale_kernel,
        [total, largest],
        [jax.ShapeDtypeStruct(porosity.shape, F32)],
    )
    return final, adjoint_out, sensitivity


def solution(mesh):
    sizes = (mesh.shape["gx"], mesh.shape["gy"])
    whole, flat = P(None, "gx", "gy"), P("gx", "gy")
    return jax.shard_map(
        functools.partial(on_device, sizes),
        mesh=mesh,
        in_specs=(whole, whole, flat, flat, flat),
        out_specs=(whole, whole, flat),
        check_vma=False,
    )
```
